32 devices in a mesh: sub: 8 (over y, x, core), grp: 4 (over z).
Axes of the slice: x: 2, y: 2, z: 4, core: 2. Of those that a mesh axis runs over, the one named last changes fastest.
Arguments:
- load_terms: float32 [8, 4, 512, 384], P('sub', 'grp'), may hold values from -6 to 6
- schur_matrix: float32 [8, 4, 512, 512], P('sub', 'grp'), may hold values from -1 to 4
- local_inverse: float32 [8, 4, 512, 512], P('sub', 'grp'), may hold values from -0.3 to 1
- coarse_modes: float32 [8, 4, 512, 128], P('sub', 'grp'), may hold values from -0.25 to 0.25
- cluster_inverse: float32 [8, 512, 512], P('sub', None, 'grp'), may hold values from -0.5 to 2, as said below
- row_blocks: int32 [8, 4, 4, 96], P('sub', 'grp'), may hold values from 0 to 511, as said below
Outputs:
- solution: float32 [8, 4, 512, 384], P('sub', 'grp')
- residual: float32 [8, 4, 512, 384], P('sub', 'grp')
The draws below stay inside these ranges and needn't reach their ends.
Inputs may be any that keep to these rules, and one draw needn't show every extreme that they name: `row_blocks`: for each subdomain the four blocks hold 384 different rows. `cluster_inverse`: each cluster's matrix is symmetric.
All inputs are finite; a program needn't handle non-finite values.
Results may differ from the reference program's by a relative error of at most 0.00016.
Values sent between devices are 32-bit elements; how exact they have to be, the bound alone decides.
No kernel may reach another device: no remote copies, remote signals or barrier semaphores. Data moves between devices by JAX's collectives and lax.ppermute only.
A program may use at most 64 MiB of HBM per device.

```python
import jax
import jax.numpy as jnp
from jax import lax

SCHUR = 512
MODES = 128
SHARED = 96
LOADS = 384
ITERS = 2
ROW_SUBS = 4
CLUSTER = 512
N_SUB = 8
N_GRP = 4


def symmetric_noise(key, count, order, scale):
    noise = jax.random.truncated_normal(key, -4.0, 4.0, (count, order, order), jnp.float32)
    return (noise + jnp.swapaxes(noise, 1, 2)) * (scale / jnp.sqrt(2.0 * order))


def diagonal_matrices(key, count, order, lower, upper, scale):
    first_key, second_key = jax.random.split(key)
    diagonal = jnp.exp(jax.random.uniform(first_key, (count, order), jnp.float32, jnp.log(lower), jnp.log(upper)))
    return symmetric_noise(second_key, count, order, scale) + diagonal[:, :, None] * jnp.eye(order, dtype=jnp.float32)


def draw_schur_matrix(key, part):
    matrices = diagonal_matrices(jax.random.fold_in(key, 11), N_SUB * N_GRP, SCHUR, 1.5, 3.0, 0.6)
    return matrices.reshape(N_SUB, N_GRP, SCHUR, SCHUR)


def draw_local_inverse(key, part):
    matrices = diagonal_matrices(jax.random.fold_in(key, 23), N_SUB * N_GRP, SCHUR, 1.0 / 3.0, 2.0 / 3.0, 0.12)
    return matrices.reshape(N_SUB, N_GRP, SCHUR, SCHUR)


def draw_cluster_inverse(key, part):
    return diagonal_matrices(jax.random.fold_in(key, 37), N_SUB, N_GRP * MODES, 0.5, 1.5, 0.3)


def draw_row_blocks(key, part):
    subkeys = jax.random.split(jax.random.fold_in(key, 41), N_SUB * N_GRP)
    orders = jax.vmap(lambda one_key: jax.random.permutation(one_key, SCHUR))(subkeys)
    return orders[:, :4 * SHARED].reshape(N_SUB, N_GRP, 4, SHARED).astype(jnp.int32)


def block_levels(own_key, extent, pieces, smallest, largest):
    def one(axis_at, shards_of):
        draws = jax.random.uniform(jax.random.fold_in(jax.random.fold_in(own_key, 6), axis_at), (shards_of,), jnp.float32, smallest / len(pieces), largest / len(pieces))
        return jnp.repeat(jnp.exp(draws), extent[axis_at] // shards_of).reshape((-1,) + (1,) * (len(extent) - axis_at - 1))

    factor_of = one(*pieces[0])
    for cut in pieces[1:]:
        factor_of = factor_of * one(*cut)
    return factor_of


def normal_values(rng, shape, scale, reach, shards=(), kind=jnp.bfloat16):
    array = scale * jax.random.normal(rng, shape, jnp.float32)
    if shards:
        array = array * block_levels(rng, shape, shards, -0.22, 0.18)
    return jnp.clip(array, -reach, reach).astype(kind)


def setup_inputs(seed: int = 0) -> dict:
    key_of = jax.random.split(jax.random.key(seed), 7)
    load_terms = normal_values(key_of[0], (N_SUB, N_GRP, SCHUR, LOADS), 1.0, 6.0, ((0, 8), (1, 4)), jnp.float32)
    schur_matrix = draw_schur_matrix(jax.random.fold_in(key_of[6], 71), 0)
    local_inverse = draw_local_inverse(jax.random.fold_in(key_of[6], 71), 0)
    coarse_modes = normal_values(key_of[3], (N_SUB, N_GRP, SCHUR, MODES), SCHUR ** -0.5, 0.25, ((0, 8), (1, 4)), jnp.float32)
    cluster_inverse = draw_cluster_inverse(jax.random.fold_in(key_of[6], 71), 0)
    row_blocks = draw_row_blocks(jax.random.fold_in(key_of[6], 71), 0)
    return {"load_terms": load_terms, "schur_matrix": schur_matrix, "local_inverse": local_inverse, "coarse_modes": coarse_modes, "cluster_inverse": cluster_inverse, "row_blocks": row_blocks}


relax = 0.5
highest = lax.Precision.HIGHEST


def neighbour_present():
    indices = jnp.arange(N_SUB)
    marks = jnp.stack([indices > 0, indices < N_SUB - 1, indices >= ROW_SUBS, indices < N_SUB - ROW_SUBS], axis=1)
    return marks.astype(jnp.float32)


def moved(blocks, offset):
    if offset > 0:
        return jnp.concatenate([jnp.zeros_like(blocks[:offset]), blocks[:-offset]], axis=0)
    return jnp.concatenate([blocks[-offset:], jnp.zeros_like(blocks[:-offset])], axis=0)


def assemble(vectors, flat_rows, present):
    picked = jax.vmap(jax.vmap(lambda column_rows, chosen: column_rows[chosen]))(vectors, flat_rows)
    picked = picked.reshape(N_SUB, N_GRP, 4, SHARED, -1)
    incoming = jnp.stack([moved(picked[:, :, 1], 1), moved(picked[:, :, 0], -1),
                          moved(picked[:, :, 3], ROW_SUBS), moved(picked[:, :, 2], -ROW_SUBS)], axis=2)
    incoming = incoming * present[:, None, :, None, None]
    incoming = incoming.reshape(N_SUB, N_GRP, 4 * SHARED, -1)
    return jax.vmap(jax.vmap(lambda column_rows, chosen, arrivals: column_rows.at[chosen].add(arrivals)))(
        vectors, flat_rows, incoming)


def reference(load_terms, schur_matrix, local_inverse, coarse_modes, cluster_inverse, row_blocks):
    present = neighbour_present()
    flat_rows = row_blocks.reshape(N_SUB, N_GRP, 4 * SHARED).astype(jnp.int32)
    halves = jnp.where(present > 0, 0.5, 1.0)
    marks = jnp.broadcast_to(halves[:, None, :, None], (N_SUB, N_GRP, 4, SHARED)).reshape(N_SUB, N_GRP, -1)
    weight = jax.vmap(jax.vmap(lambda chosen, values: jnp.ones((SCHUR,), jnp.float32).at[chosen].set(values)))(
        flat_rows, marks)[..., None]

    def precondition(current):
        weighted = weight * current
        fine_part = jnp.einsum('sgij,sgjl->sgil', local_inverse, weighted, precision=highest)
        projected = jnp.einsum('sgim,sgil->sgml', coarse_modes, weighted, precision=highest)
        stacked = projected.reshape(N_SUB, CLUSTER, LOADS)
        coarse = jnp.einsum('sij,sjl->sil', cluster_inverse, stacked, precision=highest)
        coarse = coarse.reshape(N_SUB, N_GRP, MODES, LOADS)
        correction = jnp.einsum('sgim,sgml->sgil', coarse_modes, coarse, precision=highest)
        return assemble(weight * (fine_part + correction), flat_rows, present)

    residual = assemble(load_terms, flat_rows, present)
    solution = jnp.zeros_like(load_terms)
    for iteration in range(ITERS):
        solution = solution + relax * precondition(residual)
        product = jnp.einsum('sgij,sgjl->sgil', schur_matrix, solution, precision=highest)
        residual = assemble(load_terms - product, flat_rows, present)
    return solution, residual
```

```python
import jax
import jax.numpy as jnp
from jax import lax
from jax.experimental import pallas as pl
from jax.experimental.pallas import tpu as pltpu
from jax.sharding import PartitionSpec as P

ITERS = 2
ROW_SUBS = 4
RELAX = 0.5
WIDTHS = (128, 256)
PACE = {"project": 0, "mix": 4, "solve": 4.5, "correct": 10, "product": 15}
CYCLE = 20
LAG = 10

f32 = jnp.float32
bf16 = jnp.bfloat16
NN = (((1,), (0,)), ((), ()))
NT = (((1,), (1,)), ((), ()))


class Chain:
    def __init__(self):
        self.last = None

    def __call__(self, body, outs, flops, moved, *operands):
        count = len(operands)
        specs = [pl.BlockSpec(memory_space=pltpu.VMEM)] * count
        extra = []
        if self.last is not None:
            extra = [self.last]
            specs = specs + [pl.BlockSpec(memory_space=pl.ANY)]

        def whole_body(*refs):
            body(*refs[:count], *refs[count + len(extra) :])

        results = pl.pallas_call(
            whole_body,
            out_shape=[jax.ShapeDtypeStruct(shape, kind) for shape, kind in outs],
            in_specs=specs,
            out_specs=[pl.BlockSpec(memory_space=pltpu.VMEM)] * len(outs),
            compiler_params=pltpu.CompilerParams(vmem_limit_bytes=24 * 1024 * 1024),
            cost_estimate=pl.CostEstimate(flops=flops, bytes_accessed=moved, transcendentals=0),
        )(*operands, *extra)
        self.last = results[0]
        return results


def dot(left, right, dims=NN):
    return lax.dot_general(left, right, dims, preferred_element_type=f32)


def split(value):
    high = value.astype(bf16)
    return high, (value - high.astype(f32)).astype(bf16)


def dot3(left, right):
    return dot(left[0], right[0]) + (dot(left[0], right[1]) + dot(left[1], right[0]))


def pick(chooser, value):
    high, low = split(value)
    return dot(chooser, high) + dot(chooser, low)


def sides(subs):
    sub = lax.axis_index("sub")
    low_side = sub % 2 == 0
    low_row = (sub // ROW_SUBS) % 2 == 0
    up, down = sub < subs - 1, sub > 0
    over, under = sub < subs - ROW_SUBS, sub >= ROW_SUBS
    return [
        (low_row, 3, 2, jnp.where(low_row, over, under)),
        (low_side, 0, 1, jnp.where(low_side, down, up)),
        (low_side, 1, 0, jnp.where(low_side, up, down)),
        (low_row, 2, 3, jnp.where(low_row, under, over)),
    ]


def put_shared(value, shared_refs):
    for place, ref in enumerate(shared_refs):
        width = ref.shape[0]
        ref[...] = value[place * width : (place + 1) * width]


def add_shared(value, shared_refs):
    width = shared_refs[0].shape[0]
    parts = [
        value[place * width : (place + 1) * width] + ref[...]
        for place, ref in enumerate(shared_refs)
    ]
    parts.append(value[len(shared_refs) * width :])
    return jnp.concatenate(parts, axis=0)


def cut(widths):
    starts = [sum(widths[:place]) for place in range(len(widths))]
    return list(zip(starts, widths))


def listed_body(subs, count, widths, blocks_ref, load_ref, listed_ref, *shared_refs):
    blocks = blocks_ref[...]
    placed = jnp.concatenate(
        [jnp.where(test, blocks[a : a + 1], blocks[b : b + 1]) for test, a, b, _ in sides(subs)], axis=0
    )
    upright = placed.astype(f32).T
    column = jnp.concatenate([upright[:, place : place + 1] for place in range(4)], axis=0)
    listed, total = column.shape[0], load_ref.shape[0]
    lane = lax.broadcasted_iota(jnp.int32, (listed, total), 1).astype(f32)
    first = (column == lane).astype(f32).astype(bf16)
    listed_ref[...] = first
    sent = pick(first[: count * blocks.shape[1]], load_ref[...])
    for place, (start, width) in enumerate(cut(widths)):
        put_shared(sent[:, start : start + width], shared_refs[place * count : (place + 1) * count])


def order_body(subs, widths, listed_ref, load_ref, basis_ref, columns_ref,
               chooser_ref, flipped_ref, basis_high, basis_low, test_high, test_low, sent_ref, *sorted_refs):
    listed, total = listed_ref.shape
    first = listed_ref[...].astype(f32)
    unlisted = 1.0 - jnp.sum(first, axis=0, keepdims=True)
    before = (
        lax.broadcasted_iota(jnp.int32, (total, total), 0)
        < lax.broadcasted_iota(jnp.int32, (total, total), 1)
    ).astype(f32).astype(bf16)
    rank = dot(jnp.broadcast_to(unlisted, (8, total)).astype(bf16), before)[:1]
    slot = lax.broadcasted_iota(jnp.int32, (total - listed, total), 0).astype(f32)
    last = jnp.where(rank == slot, unlisted, 0.0)
    chooser = jnp.concatenate([first, last], axis=0)
    flipped_ref[...] = chooser.T.astype(bf16)
    weighted = (chooser * weight_column(subs, listed // 4, total)).astype(bf16)
    chooser = chooser.astype(bf16)
    chooser_ref[...] = chooser
    ordered = pick(chooser, load_ref[...])
    for ref, (start, width) in zip(sorted_refs, cut(widths)):
        ref[...] = ordered[:, start : start + width]
    for part, out, turned in zip(split(basis_ref[...]), (basis_high, basis_low), (test_high, test_low)):
        placed = dot(weighted, part)
        out[...] = placed.astype(bf16)
        turned[...] = placed.T.astype(bf16)
    sent_ref[...] = rows_of(columns_ref, 3 - (lax.axis_index("grp") ^ 1))


def weight_column(subs, width, total):
    parts = [jnp.full((width, 1), jnp.where(here, 0.5, 1.0), f32) for _, _, _, here in sides(subs)]
    return jnp.concatenate(parts + [jnp.ones((total - 4 * width, 1), f32)], axis=0)


def rows_of(columns_ref, place):
    modes = columns_ref.shape[1]
    return columns_ref[pl.ds(pl.multiple_of(place * modes, modes), modes), :]


def matrices_body(subs, listed, chooser_ref, flipped_ref, schur_ref, solve_ref,
                  schur_high, schur_low, solve_high, solve_low):
    chooser, flipped = chooser_ref[...], flipped_ref[...]
    column = weight_column(subs, listed // 4, chooser.shape[0])
    weighted = (chooser.astype(f32) * column).astype(bf16)
    for part, out in zip(split(solve_ref[...] * RELAX), (solve_high, solve_low)):
        out[...] = dot(dot(weighted, part).astype(bf16), weighted, NT).astype(bf16)
    for part, out in zip(split(schur_ref[...]), (schur_high, schur_low)):
        out[...] = dot(dot(chooser, part).astype(bf16), flipped).astype(bf16)


def blend_body(columns_ref, other_ref, mix_high, mix_low):
    grp = lax.axis_index("grp")
    away = jnp.concatenate([rows_of(columns_ref, 3 - grp), other_ref[...]], axis=1)
    kept = jnp.concatenate([rows_of(columns_ref, grp), rows_of(columns_ref, grp ^ 1).T], axis=1)
    mix_high[...], mix_low[...] = split(jnp.concatenate([away, kept], axis=0) * RELAX)


def project_body(count, value_ref, test_high, test_low, *refs):
    halves = split(add_shared(value_ref[...], refs[:count]))
    projected_ref, high_ref, low_ref = refs[count:]
    projected_ref[...] = dot3((test_high[...], test_low[...]), halves)
    high_ref[...], low_ref[...] = halves


def solve_body(high_ref, low_ref, solve_high, solve_low, fine_ref):
    fine_ref[...] = dot3((solve_high[...], solve_low[...]), (high_ref[...], low_ref[...]))


def mix_body(own_ref, other_ref, mix_high, mix_low, away_ref, kept_ref):
    pair = jnp.concatenate([own_ref[...], other_ref[...]], axis=0)
    mixed = dot3((mix_high[...], mix_low[...]), split(pair))
    modes = away_ref.shape[0]
    away_ref[...] = mixed[:modes]
    kept_ref[...] = mixed[modes:]


def correct_body(kept_ref, came_ref, fine_ref, basis_high, basis_low, out_ref, *shared_refs):
    coarse = kept_ref[...] + came_ref[...]
    step = fine_ref[...] + dot3((basis_high[...], basis_low[...]), split(coarse))
    out_ref[...] = step
    put_shared(step, shared_refs)


def product_body(count, first, *refs):
    refs = list(refs)
    step = add_shared(refs.pop(0)[...], [refs.pop(0) for _ in range(count)])
    if not first:
        step = step + refs.pop(0)[...]
    load_ref, schur_high, schur_low, iterate_ref, out_ref = refs[:5]
    iterate_ref[...] = step
    value = load_ref[...] - dot3((schur_high[...], schur_low[...]), split(step))
    out_ref[...] = value
    put_shared(value, refs[5:])


def restore_body(widths, flipped_ref, *refs):
    for ref, (start, width) in zip(refs, cut(widths)):
        refs[-1][:, start : start + width] = pick(flipped_ref[...], ref[...])


def settle_body(count, flipped_ref, value_ref, *refs):
    refs[-1][...] = pick(flipped_ref[...], add_shared(value_ref[...], refs[:-1]))


def finish_body(count, widths, flipped_ref, *refs):
    ready, arrived, out_ref = refs[: len(widths)], refs[len(widths) : -1], refs[-1]
    for ref, (start, width) in zip(ready[:-1], cut(widths)):
        out_ref[:, start : start + width] = ref[...]
    came = jnp.concatenate([ref[...] for ref in arrived], axis=0)
    start, width = cut(widths)[-1]
    out_ref[:, start : start + width] = ready[-1][...] + pick(flipped_ref[:, : came.shape[0]], came)


def swaps(count, stride, odd):
    pairs = []
    for low in range(count - stride):
        if (low // stride) % 2 == odd:
            pairs += [(low, low + stride), (low + stride, low)]
    return pairs


def local(load_terms, schur_matrix, local_inverse, coarse_modes, cluster_inverse, row_blocks):
    load = load_terms[0, 0]
    basis = coarse_modes[0, 0]
    columns = cluster_inverse[0]
    blocks = row_blocks[0, 0]
    rows, loads = load.shape
    modes = basis.shape[1]
    shared_rows = blocks.shape[1]
    listed = 4 * shared_rows
    subs = lax.axis_size("sub")
    if lax.axis_size("grp") != 4 or sum(WIDTHS) != loads:
        raise ValueError("unexpected sizes")

    plans = [swaps(subs, ROW_SUBS, 0), swaps(subs, 1, 1), swaps(subs, 1, 0), swaps(subs, ROW_SUBS, 1)]
    plans = [plan for plan in plans if plan]
    count = len(plans)
    pair_plan = [(0, 1), (1, 0), (2, 3), (3, 2)]
    mirror_plan = [(0, 3), (3, 0), (1, 2), (2, 1)]

    def exchange(parts):
        return [lax.ppermute(part, "sub", plan) for part, plan in zip(parts, plans)]

    def whole(width, kind=f32):
        return ((rows, width), kind)

    def shared(width):
        return [((shared_rows, width), f32)] * count

    run = Chain()
    size = rows * loads
    one_hot, *parts = run(
        lambda *refs: listed_body(subs, count, WIDTHS, *refs),
        [((listed, rows), bf16)] + [kind for width in WIDTHS for kind in shared(width)],
        4 * listed * size, 16 * size, blocks, load,
    )
    streams = []
    for place in range(len(WIDTHS)):
        streams.append({"arrived": exchange(parts[place * count : (place + 1) * count])})
    chooser, flipped, basis_high, basis_low, test_high, test_low, sent, *ordered = run(
        lambda *refs: order_body(subs, WIDTHS, *refs),
        [whole(rows, bf16)] * 2 + [whole(modes, bf16)] * 2 + [((modes, rows), bf16)] * 2
        + [((modes, modes), f32)] + [whole(width) for width in WIDTHS],
        4 * rows * size, 24 * size, one_hot, load, basis, columns,
    )
    other = lax.ppermute(sent, "grp", pair_plan)
    schur_high, schur_low, solve_high, solve_low = run(
        lambda *refs: matrices_body(subs, listed, *refs),
        [whole(rows, bf16)] * 4, 16 * rows**3, 24 * size,
        chooser, flipped, schur_matrix[0, 0], local_inverse[0, 0],
    )
    for stream, rows_sorted, width in zip(streams, ordered, WIDTHS):
        stream.update(load=rows_sorted, value=rows_sorted, width=width, iterate=None)

    mixers = []

    def project(stream):
        width = stream["width"]
        stream["projected"], stream["high"], stream["low"] = run(
            lambda *refs: project_body(count, *refs),
            [((modes, width), f32), whole(width, bf16), whole(width, bf16)],
            6 * modes * rows * width, 12 * rows * width,
            stream["value"], test_high, test_low, *stream["arrived"],
        )
        stream["theirs"] = lax.ppermute(stream["projected"], "grp", pair_plan)
        if not mixers:
            mixers.extend(run(blend_body, [((2 * modes, 2 * modes), bf16)] * 2, size, size, columns, other))

    def mix(stream):
        width = stream["width"]
        away, stream["kept"] = run(
            mix_body, [((modes, width), f32)] * 2, 24 * modes * modes * width, 4 * rows * width,
            stream["projected"], stream["theirs"], *mixers,
        )
        stream["came"] = lax.ppermute(away, "grp", mirror_plan)

    def solve(stream):
        width = stream["width"]
        (stream["fine"],) = run(
            solve_body, [whole(width)], 6 * rows * rows * width, 12 * rows * width,
            stream["high"], stream["low"], solve_high, solve_low,
        )

    def correct(stream):
        width = stream["width"]
        stream["step"], *parts = run(
            correct_body, [whole(width)] + shared(width), 6 * modes * rows * width, 12 * rows * width,
            stream["kept"], stream["came"], stream["fine"], basis_high, basis_low,
        )
        stream["arrived"] = exchange(parts)

    def product(stream):
        width = stream["width"]
        before = [] if stream["iterate"] is None else [stream["iterate"]]
        stream["iterate"], stream["value"], *parts = run(
            lambda *refs: product_body(count, not before, *refs),
            [whole(width)] * 2 + shared(width), 6 * rows * rows * width, 16 * rows * width,
            stream["step"], *stream["arrived"], *before, stream["load"], schur_high, schur_low,
        )
        stream["arrived"] = exchange(parts)

    steps = {"project": project, "mix": mix, "solve": solve, "correct": correct, "product": product}
    plan = []
    for place, stream in enumerate(streams):
        for iteration in range(ITERS):
            plan += [(iteration * CYCLE + place * LAG + when, place, name) for name, when in PACE.items()]
    for _, place, name in sorted(plan):
        steps[name](streams[place])

    (solution_rows,) = run(
        lambda *refs: restore_body(WIDTHS, *refs), [whole(loads)], 4 * rows * size, 10 * size,
        flipped, *[stream["iterate"] for stream in streams],
    )
    ready = []
    for stream in streams[:-1]:
        ready += run(
            lambda *refs: settle_body(count, *refs), [whole(stream["width"])],
            4 * rows * rows * stream["width"], 10 * rows * stream["width"],
            flipped, stream["value"], *stream["arrived"],
        )
    final = streams[-1]
    ready += run(
        lambda *refs: restore_body((final["width"],), *refs), [whole(final["width"])],
        4 * rows * rows * final["width"], 10 * rows * final["width"], flipped, final["value"],
    )
    (residual_rows,) = run(
        lambda *refs: finish_body(count, WIDTHS, *refs), [whole(loads)], 4 * rows * size, 10 * size,
        flipped, *ready, *final["arrived"],
    )
    return (solution_rows[None, None], residual_rows[None, None])


def solution(mesh):
    return jax.shard_map(
        local,
        mesh=mesh,
        in_specs=(
            P("sub", "grp", None, None),
            P("sub", "grp", None, None),
            P("sub", "grp", None, None),
            P("sub", "grp", None, None),
            P("sub", None, "grp"),
            P("sub", "grp", None, None),
        ),
        out_specs=(P("sub", "grp", None, None), P("sub", "grp", None, None)),
        check_vma=False,
    )
```

```python
import jax
import jax.numpy as jnp
from jax import lax
from jax.experimental import pallas as pl
from jax.experimental.pallas import tpu as pltpu
from jax.sharding import PartitionSpec as P

ITERS = 2
ROW_SUBS = 4
RELAX = 0.5
WIDTHS = (384,)
PACE = {"project": 0, "mix": 4, "solve": 4.5, "correct": 10, "product": 15}
CYCLE = 20
LAG = 10

f32 = jnp.float32
bf16 = jnp.bfloat16
NN = (((1,), (0,)), ((), ()))
NT = (((1,), (1,)), ((), ()))


class Chain:
    def __init__(self):
        self.last = None

    def __call__(self, body, outs, flops, moved, *operands):
        count = len(operands)
        specs = [pl.BlockSpec(memory_space=pltpu.VMEM)] * count
        extra = []
        if self.last is not None:
            extra = [self.last]
            specs = specs + [pl.BlockSpec(memory_space=pl.ANY)]

        def whole_body(*refs):
            body(*refs[:count], *refs[count + len(extra) :])

        results = pl.pallas_call(
            whole_body,
            out_shape=[jax.ShapeDtypeStruct(shape, kind) for shape, kind in outs],
            in_specs=specs,
            out_specs=[pl.BlockSpec(memory_space=pltpu.VMEM)] * len(outs),
            compiler_params=pltpu.CompilerParams(vmem_limit_bytes=24 * 1024 * 1024),
            cost_estimate=pl.CostEstimate(flops=1, bytes_accessed=1, transcendentals=0),
        )(*operands, *extra)
        self.last = results[0]
        return results


def dot(left, right, dims=NN):
    return lax.dot_general(left, right, dims, preferred_element_type=f32)


def split(value):
    high = value.astype(bf16)
    return high, (value - high.astype(f32)).astype(bf16)


def dot3(left, right):
    return dot(left[0], right[0]) + (dot(left[0], right[1]) + dot(left[1], right[0]))


def pick(chooser, value):
    high, low = split(value)
    return dot(chooser, high) + dot(chooser, low)


def sides(subs):
    sub = lax.axis_index("sub")
    low_side = sub % 2 == 0
    low_row = (sub // ROW_SUBS) % 2 == 0
    up, down = sub < subs - 1, sub > 0
    over, under = sub < subs - ROW_SUBS, sub >= ROW_SUBS
    return [
        (low_row, 3, 2, jnp.where(low_row, over, under)),
        (low_side, 0, 1, jnp.where(low_side, down, up)),
        (low_side, 1, 0, jnp.where(low_side, up, down)),
        (low_row, 2, 3, jnp.where(low_row, under, over)),
    ]


def put_shared(value, shared_refs):
    for place, ref in enumerate(shared_refs):
        width = ref.shape[0]
        ref[...] = value[place * width : (place + 1) * width]


def add_shared(subs, value, shared_refs):
    width = shared_refs[0].shape[0]
    parts = [
        value[place * width : (place + 1) * width] + ref[...] * jnp.where(here, 1.0, 0.0)
        for place, (ref, (_, _, _, here)) in enumerate(zip(shared_refs, sides(subs)))
    ]
    parts.append(value[len(shared_refs) * width :])
    return jnp.concatenate(parts, axis=0)


def cut(widths):
    starts = [sum(widths[:place]) for place in range(len(widths))]
    return list(zip(starts, widths))


def listed_body(subs, count, widths, blocks_ref, load_ref, listed_ref, *shared_refs):
    blocks = blocks_ref[...]
    placed = jnp.concatenate(
        [jnp.where(test, blocks[a : a + 1], blocks[b : b + 1]) for test, a, b, _ in sides(subs)], axis=0
    )
    upright = placed.astype(f32).T
    column = jnp.concatenate([upright[:, place : place + 1] for place in range(4)], axis=0)
    listed, total = column.shape[0], load_ref.shape[0]
    lane = lax.broadcasted_iota(jnp.int32, (listed, total), 1).astype(f32)
    first = (column == lane).astype(f32).astype(bf16)
    listed_ref[...] = first
    sent = pick(first[: count * blocks.shape[1]], load_ref[...])
    for place, (start, width) in enumerate(cut(widths)):
        put_shared(sent[:, start : start + width], shared_refs[place * count : (place + 1) * count])


def order_body(subs, widths, listed_ref, load_ref, basis_ref, columns_ref,
               chooser_ref, flipped_ref, basis_high, basis_low, test_high, test_low, sent_ref, *sorted_refs):
    listed, total = listed_ref.shape
    first = listed_ref[...].astype(f32)
    unlisted = 1.0 - jnp.sum(first, axis=0, keepdims=True)
    before = (
        lax.broadcasted_iota(jnp.int32, (total, total), 0)
        < lax.broadcasted_iota(jnp.int32, (total, total), 1)
    ).astype(f32).astype(bf16)
    rank = dot(jnp.broadcast_to(unlisted, (8, total)).astype(bf16), before)[:1]
    slot = lax.broadcasted_iota(jnp.int32, (total - listed, total), 0).astype(f32)
    last = jnp.where(rank == slot, unlisted, 0.0)
    chooser = jnp.concatenate([first, last], axis=0)
    flipped_ref[...] = chooser.T.astype(bf16)
    weighted = (chooser * weight_column(subs, listed // 4, total)).astype(bf16)
    chooser = chooser.astype(bf16)
    chooser_ref[...] = chooser
    ordered = pick(chooser, load_ref[...])
    for ref, (start, width) in zip(sorted_refs, cut(widths)):
        ref[...] = ordered[:, start : start + width]
    for part, out, turned in zip(split(basis_ref[...]), (basis_high, basis_low), (test_high, test_low)):
        placed = dot(weighted, part)
        out[...] = placed.astype(bf16)
        turned[...] = placed.T.astype(bf16)
    sent_ref[...] = rows_of(columns_ref, 3 - (lax.axis_index("grp") ^ 1))


def weight_column(subs, width, total):
    parts = [jnp.full((width, 1), jnp.where(here, 0.5, 1.0), f32) for _, _, _, here in sides(subs)]
    return jnp.concatenate(parts + [jnp.ones((total - 4 * width, 1), f32)], axis=0)


def rows_of(columns_ref, place):
    modes = columns_ref.shape[1]
    return columns_ref[pl.ds(pl.multiple_of(place * modes, modes), modes), :]


def matrices_body(subs, listed, chooser_ref, flipped_ref, schur_ref, solve_ref,
                  schur_high, schur_low, solve_high, solve_low):
    chooser, flipped = chooser_ref[...], flipped_ref[...]
    column = weight_column(subs, listed // 4, chooser.shape[0])
    weighted = (chooser.astype(f32) * column).astype(bf16)
    for part, out in zip(split(solve_ref[...] * RELAX), (solve_high, solve_low)):
        out[...] = dot(dot(weighted, part).astype(bf16), weighted, NT).astype(bf16)
    for part, out in zip(split(schur_ref[...]), (schur_high, schur_low)):
        out[...] = dot(dot(chooser, part).astype(bf16), flipped).astype(bf16)


def blend_body(columns_ref, other_ref, mix_high, mix_low):
    grp = lax.axis_index("grp")
    away = jnp.concatenate([rows_of(columns_ref, 3 - grp), other_ref[...]], axis=1)
    kept = jnp.concatenate([rows_of(columns_ref, grp), rows_of(columns_ref, grp ^ 1).T], axis=1)
    mix_high[...], mix_low[...] = split(jnp.concatenate([away, kept], axis=0) * RELAX)


def project_body(subs, count, value_ref, test_high, test_low, *refs):
    halves = split(add_shared(subs, value_ref[...], refs[:count]))
    projected_ref, high_ref, low_ref = refs[count:]
    projected_ref[...] = dot3((test_high[...], test_low[...]), halves)
    high_ref[...], low_ref[...] = halves


def solve_body(high_ref, low_ref, solve_high, solve_low, fine_ref):
    fine_ref[...] = dot3((solve_high[...], solve_low[...]), (high_ref[...], low_ref[...]))


def mix_body(own_ref, other_ref, mix_high, mix_low, away_ref, kept_ref):
    pair = jnp.concatenate([own_ref[...], other_ref[...]], axis=0)
    mixed = dot3((mix_high[...], mix_low[...]), split(pair))
    modes = away_ref.shape[0]
    away_ref[...] = mixed[:modes]
    kept_ref[...] = mixed[modes:]


def correct_body(kept_ref, came_ref, fine_ref, basis_high, basis_low, out_ref, *shared_refs):
    coarse = kept_ref[...] + came_ref[...]
    step = fine_ref[...] + dot3((basis_high[...], basis_low[...]), split(coarse))
    out_ref[...] = step
    put_shared(step, shared_refs)


def product_body(subs, count, first, *refs):
    refs = list(refs)
    step = add_shared(subs, refs.pop(0)[...], [refs.pop(0) for _ in range(count)])
    if not first:
        step = step + refs.pop(0)[...]
    load_ref, schur_high, schur_low, iterate_ref, out_ref = refs[:5]
    iterate_ref[...] = step
    value = load_ref[...] - dot3((schur_high[...], schur_low[...]), split(step))
    out_ref[...] = value
    put_shared(value, refs[5:])


def restore_body(widths, flipped_ref, *refs):
    for ref, (start, width) in zip(refs, cut(widths)):
        refs[-1][:, start : start + width] = pick(flipped_ref[...], ref[...])


def settle_body(subs, flipped_ref, value_ref, *refs):
    refs[-1][...] = pick(flipped_ref[...], add_shared(subs, value_ref[...], refs[:-1]))


def finish_body(subs, widths, flipped_ref, *refs):
    ready, arrived, out_ref = refs[: len(widths)], refs[len(widths) : -1], refs[-1]
    for ref, (start, width) in zip(ready[:-1], cut(widths)):
        out_ref[:, start : start + width] = ref[...]
    came = jnp.concatenate(
        [ref[...] * jnp.where(here, 1.0, 0.0) for ref, (_, _, _, here) in zip(arrived, sides(subs))], axis=0
    )
    start, width = cut(widths)[-1]
    out_ref[:, start : start + width] = ready[-1][...] + pick(flipped_ref[:, : came.shape[0]], came)


def swaps(count, stride, odd):
    partner = list(range(count))
    for low in range(count - stride):
        if (low // stride) % 2 == odd:
            partner[low], partner[low + stride] = low + stride, low
    return list(enumerate(partner)) if partner != list(range(count)) else []


def local(load_terms, schur_matrix, local_inverse, coarse_modes, cluster_inverse, row_blocks):
    load = load_terms[0, 0]
    basis = coarse_modes[0, 0]
    columns = cluster_inverse[0]
    blocks = row_blocks[0, 0]
    rows, loads = load.shape
    modes = basis.shape[1]
    shared_rows = blocks.shape[1]
    listed = 4 * shared_rows
    subs = lax.axis_size("sub")
    if lax.axis_size("grp") != 4 or sum(WIDTHS) != loads:
        raise ValueError("unexpected sizes")

    plans = [swaps(subs, ROW_SUBS, 0), swaps(subs, 1, 1), swaps(subs, 1, 0), swaps(subs, ROW_SUBS, 1)]
    plans = [plan for plan in plans if plan]
    count = len(plans)
    pair_plan = [(0, 1), (1, 0), (2, 3), (3, 2)]
    mirror_plan = [(0, 3), (3, 0), (1, 2), (2, 1)]

    def exchange(parts):
        return [lax.ppermute(part, "sub", plan) for part, plan in zip(parts, plans)]

    def whole(width, kind=f32):
        return ((rows, width), kind)

    def shared(width):
        return [((shared_rows, width), f32)] * count

    run = Chain()
    size = rows * loads
    one_hot, *parts = run(
        lambda *refs: listed_body(subs, count, WIDTHS, *refs),
        [((listed, rows), bf16)] + [kind for width in WIDTHS for kind in shared(width)],
        4 * listed * size, 16 * size, blocks, load,
    )
    streams = []
    for place in range(len(WIDTHS)):
        streams.append({"arrived": exchange(parts[place * count : (place + 1) * count])})
    chooser, flipped, basis_high, basis_low, test_high, test_low, sent, *ordered = run(
        lambda *refs: order_body(subs, WIDTHS, *refs),
        [whole(rows, bf16)] * 2 + [whole(modes, bf16)] * 2 + [((modes, rows), bf16)] * 2
        + [((modes, modes), f32)] + [whole(width) for width in WIDTHS],
        4 * rows * size, 24 * size, one_hot, load, basis, columns,
    )
    other = lax.ppermute(sent, "grp", pair_plan)
    schur_high, schur_low, solve_high, solve_low = run(
        lambda *refs: matrices_body(subs, listed, *refs),
        [whole(rows, bf16)] * 4, 16 * rows**3, 24 * size,
        chooser, flipped, schur_matrix[0, 0], local_inverse[0, 0],
    )
    for stream, rows_sorted, width in zip(streams, ordered, WIDTHS):
        stream.update(load=rows_sorted, value=rows_sorted, width=width, iterate=None)

    mixers = run(blend_body, [((2 * modes, 2 * modes), bf16)] * 2, size, size, columns, other)

    def project(stream):
        width = stream["width"]
        stream["projected"], stream["high"], stream["low"] = run(
            lambda *refs: project_body(subs, count, *refs),
            [((modes, width), f32), whole(width, bf16), whole(width, bf16)],
            6 * modes * rows * width, 12 * rows * width,
            stream["value"], test_high, test_low, *stream["arrived"],
        )
        stream["theirs"] = lax.ppermute(stream["projected"], "grp", pair_plan)

    def mix(stream):
        width = stream["width"]
        away, stream["kept"] = run(
            mix_body, [((modes, width), f32)] * 2, 24 * modes * modes * width, 4 * rows * width,
            stream["projected"], stream["theirs"], *mixers,
        )
        stream["came"] = lax.ppermute(away, "grp", mirror_plan)

    def solve(stream):
        width = stream["width"]
        (stream["fine"],) = run(
            solve_body, [whole(width)], 6 * rows * rows * width, 12 * rows * width,
            stream["high"], stream["low"], solve_high, solve_low,
        )

    def correct(stream):
        width = stream["width"]
        stream["step"], *parts = run(
            correct_body, [whole(width)] + shared(width), 6 * modes * rows * width, 12 * rows * width,
            stream["kept"], stream["came"], stream["fine"], basis_high, basis_low,
        )
        stream["arrived"] = exchange(parts)

    def product(stream):
        width = stream["width"]
        before = [] if stream["iterate"] is None else [stream["iterate"]]
        stream["iterate"], stream["value"], *parts = run(
            lambda *refs: product_body(subs, count, not before, *refs),
            [whole(width)] * 2 + shared(width), 6 * rows * rows * width, 16 * rows * width,
            stream["step"], *stream["arrived"], *before, stream["load"], schur_high, schur_low,
        )
        stream["arrived"] = exchange(parts)

    steps = {"project": project, "mix": mix, "solve": solve, "correct": correct, "product": product}
    plan = []
    for place, stream in enumerate(streams):
        for iteration in range(ITERS):
            plan += [(iteration * CYCLE + place * LAG + when, place, name) for name, when in PACE.items()]
    for _, place, name in sorted(plan):
        steps[name](streams[place])

    (solution_rows,) = run(
        lambda *refs: restore_body(WIDTHS, *refs), [whole(loads)], 4 * rows * size, 10 * size,
        flipped, *[stream["iterate"] for stream in streams],
    )
    ready = []
    for stream in streams[:-1]:
        ready += run(
            lambda *refs: settle_body(subs, *refs), [whole(stream["width"])],
            4 * rows * rows * stream["width"], 10 * rows * stream["width"],
            flipped, stream["value"], *stream["arrived"],
        )
    final = streams[-1]
    ready += run(
        lambda *refs: restore_body((final["width"],), *refs), [whole(final["width"])],
        4 * rows * rows * final["width"], 10 * rows * final["width"], flipped, final["value"],
    )
    (residual_rows,) = run(
        lambda *refs: finish_body(subs, WIDTHS, *refs), [whole(loads)], 4 * rows * size, 10 * size,
        flipped, *ready, *final["arrived"],
    )
    return (solution_rows[None, None], residual_rows[None, None])


def solution(mesh):
    return jax.shard_map(
        local,
        mesh=mesh,
        in_specs=(
            P("sub", "grp", None, None),
            P("sub", "grp", None, None),
            P("sub", "grp", None, None),
            P("sub", "grp", None, None),
            P("sub", None, "grp"),
            P("sub", "grp", None, None),
        ),
        out_specs=(P("sub", "grp", None, None), P("sub", "grp", None, None)),
        check_vma=False,
    )
```

```python
import jax
import jax.numpy as jnp
from jax import lax
from jax.experimental import pallas as pl
from jax.experimental.pallas import tpu as pltpu
from jax.sharding import PartitionSpec as P

ITERS = 2
ROW_SUBS = 4
RELAX = 0.5
WIDTHS = (384,)
PACE = {"project": 0, "mix": 4, "solve": 4.5, "correct": 10, "product": 15}
CYCLE = 20
LAG = 10

f32 = jnp.float32
bf16 = jnp.bfloat16
NN = (((1,), (0,)), ((), ()))
NT = (((1,), (1,)), ((), ()))


class Chain:
    def __init__(self):
        self.last = None

    def __call__(self, body, outs, flops, moved, *operands):
        count = len(operands)
        specs = [pl.BlockSpec(memory_space=pltpu.VMEM)] * count
        extra = []
        if self.last is not None:
            extra = [self.last]
            specs = specs + [pl.BlockSpec(memory_space=pl.ANY)]

        def whole_body(*refs):
            body(*refs[:count], *refs[count + len(extra) :])

        results = pl.pallas_call(
            whole_body,
            out_shape=[jax.ShapeDtypeStruct(shape, kind) for shape, kind in outs],
            in_specs=specs,
            out_specs=[pl.BlockSpec(memory_space=pltpu.VMEM)] * len(outs),
            compiler_params=pltpu.CompilerParams(vmem_limit_bytes=24 * 1024 * 1024),
            cost_estimate=pl.CostEstimate(flops=1, bytes_accessed=1, transcendentals=0),
        )(*operands, *extra)
        self.last = results[0]
        return results


def dot(left, right, dims=NN):
    return lax.dot_general(left, right, dims, preferred_element_type=f32)


def split(value):
    high = value.astype(bf16)
    return high, (value - high.astype(f32)).astype(bf16)


def dot3(left, right):
    return dot(left[0], right[0]) + (dot(left[0], right[1]) + dot(left[1], right[0]))


def pick(chooser, value):
    high, low = split(value)
    return dot(chooser, high) + dot(chooser, low)


def sides(subs):
    sub = lax.axis_index("sub")
    low_row = (sub // ROW_SUBS) % 2 == 0
    over, under = sub < subs - ROW_SUBS, sub >= ROW_SUBS
    return [
        (low_row, 3, 2, jnp.where(low_row, over, under)),
        (low_row, 0, 0, sub > 0),
        (low_row, 1, 1, sub < subs - 1),
        (low_row, 2, 3, jnp.where(low_row, under, over)),
    ]


def put_shared(value, shared_refs):
    for place, ref in enumerate(shared_refs):
        width = ref.shape[0]
        ref[...] = value[place * width : (place + 1) * width]


def add_shared(subs, value, shared_refs):
    width = shared_refs[0].shape[0]
    parts = [
        value[place * width : (place + 1) * width] + ref[...] * jnp.where(here, 1.0, 0.0)
        for place, (ref, (_, _, _, here)) in enumerate(zip(shared_refs, sides(subs)))
    ]
    parts.append(value[len(shared_refs) * width :])
    return jnp.concatenate(parts, axis=0)


def cut(widths):
    starts = [sum(widths[:place]) for place in range(len(widths))]
    return list(zip(starts, widths))


def listed_body(subs, count, widths, blocks_ref, load_ref, listed_ref, *shared_refs):
    blocks = blocks_ref[...]
    placed = jnp.concatenate(
        [jnp.where(test, blocks[a : a + 1], blocks[b : b + 1]) for test, a, b, _ in sides(subs)], axis=0
    )
    upright = placed.astype(f32).T
    column = jnp.concatenate([upright[:, place : place + 1] for place in range(4)], axis=0)
    listed, total = column.shape[0], load_ref.shape[0]
    lane = lax.broadcasted_iota(jnp.int32, (listed, total), 1).astype(f32)
    first = (column == lane).astype(f32).astype(bf16)
    listed_ref[...] = first
    sent = pick(first[: count * blocks.shape[1]], load_ref[...])
    for place, (start, width) in enumerate(cut(widths)):
        put_shared(sent[:, start : start + width], shared_refs[place * count : (place + 1) * count])


def order_body(subs, widths, listed_ref, load_ref, basis_ref, columns_ref,
               chooser_ref, flipped_ref, basis_high, basis_low, test_high, test_low, sent_ref, *sorted_refs):
    listed, total = listed_ref.shape
    first = listed_ref[...].astype(f32)
    unlisted = 1.0 - jnp.sum(first, axis=0, keepdims=True)
    before = (
        lax.broadcasted_iota(jnp.int32, (total, total), 0)
        < lax.broadcasted_iota(jnp.int32, (total, total), 1)
    ).astype(f32).astype(bf16)
    rank = dot(jnp.broadcast_to(unlisted, (8, total)).astype(bf16), before)[:1]
    slot = lax.broadcasted_iota(jnp.int32, (total - listed, total), 0).astype(f32)
    last = jnp.where(rank == slot, unlisted, 0.0)
    chooser = jnp.concatenate([first, last], axis=0)
    flipped_ref[...] = chooser.T.astype(bf16)
    weighted = (chooser * weight_column(subs, listed // 4, total)).astype(bf16)
    chooser = chooser.astype(bf16)
    chooser_ref[...] = chooser
    ordered = pick(chooser, load_ref[...])
    for ref, (start, width) in zip(sorted_refs, cut(widths)):
        ref[...] = ordered[:, start : start + width]
    for part, out, turned in zip(split(basis_ref[...]), (basis_high, basis_low), (test_high, test_low)):
        placed = dot(weighted, part)
        out[...] = placed.astype(bf16)
        turned[...] = placed.T.astype(bf16)
    sent_ref[...] = rows_of(columns_ref, 3 - (lax.axis_index("grp") ^ 1))


def weight_column(subs, width, total):
    parts = [jnp.full((width, 1), jnp.where(here, 0.5, 1.0), f32) for _, _, _, here in sides(subs)]
    return jnp.concatenate(parts + [jnp.ones((total - 4 * width, 1), f32)], axis=0)


def rows_of(columns_ref, place):
    modes = columns_ref.shape[1]
    return columns_ref[pl.ds(pl.multiple_of(place * modes, modes), modes), :]


def matrices_body(subs, listed, chooser_ref, flipped_ref, schur_ref, solve_ref,
                  schur_high, schur_low, solve_high, solve_low):
    chooser, flipped = chooser_ref[...], flipped_ref[...]
    column = weight_column(subs, listed // 4, chooser.shape[0])
    weighted = (chooser.astype(f32) * column).astype(bf16)
    for part, out in zip(split(solve_ref[...] * RELAX), (solve_high, solve_low)):
        out[...] = dot(dot(weighted, part).astype(bf16), weighted, NT).astype(bf16)
    for part, out in zip(split(schur_ref[...]), (schur_high, schur_low)):
        out[...] = dot(dot(chooser, part).astype(bf16), flipped).astype(bf16)


def blend_body(columns_ref, other_ref, mix_high, mix_low):
    grp = lax.axis_index("grp")
    away = jnp.concatenate([rows_of(columns_ref, 3 - grp), other_ref[...]], axis=1)
    kept = jnp.concatenate([rows_of(columns_ref, grp), rows_of(columns_ref, grp ^ 1).T], axis=1)
    mix_high[...], mix_low[...] = split(jnp.concatenate([away, kept], axis=0) * RELAX)


def project_body(subs, count, value_ref, test_high, test_low, *refs):
    halves = split(add_shared(subs, value_ref[...], refs[:count]))
    projected_ref, high_ref, low_ref = refs[count:]
    projected_ref[...] = dot3((test_high[...], test_low[...]), halves)
    high_ref[...], low_ref[...] = halves


def solve_body(high_ref, low_ref, solve_high, solve_low, fine_ref):
    fine_ref[...] = dot3((solve_high[...], solve_low[...]), (high_ref[...], low_ref[...]))


def mix_body(own_ref, other_ref, mix_high, mix_low, away_ref, kept_ref):
    pair = jnp.concatenate([own_ref[...], other_ref[...]], axis=0)
    mixed = dot3((mix_high[...], mix_low[...]), split(pair))
    modes = away_ref.shape[0]
    away_ref[...] = mixed[:modes]
    kept_ref[...] = mixed[modes:]


def correct_body(kept_ref, came_ref, fine_ref, basis_high, basis_low, out_ref, *shared_refs):
    coarse = kept_ref[...] + came_ref[...]
    step = fine_ref[...] + dot3((basis_high[...], basis_low[...]), split(coarse))
    out_ref[...] = step
    put_shared(step, shared_refs)


def product_body(subs, count, first, *refs):
    refs = list(refs)
    step = add_shared(subs, refs.pop(0)[...], [refs.pop(0) for _ in range(count)])
    if not first:
        step = step + refs.pop(0)[...]
    load_ref, schur_high, schur_low, iterate_ref, out_ref = refs[:5]
    iterate_ref[...] = step
    value = load_ref[...] - dot3((schur_high[...], schur_low[...]), split(step))
    out_ref[...] = value
    put_shared(value, refs[5:])


def restore_body(widths, flipped_ref, *refs):
    for ref, (start, width) in zip(refs, cut(widths)):
        refs[-1][:, start : start + width] = pick(flipped_ref[...], ref[...])


def settle_body(subs, flipped_ref, value_ref, *refs):
    refs[-1][...] = pick(flipped_ref[...], add_shared(subs, value_ref[...], refs[:-1]))


def finish_body(subs, widths, flipped_ref, *refs):
    ready, arrived, out_ref = refs[: len(widths)], refs[len(widths) : -1], refs[-1]
    for ref, (start, width) in zip(ready[:-1], cut(widths)):
        out_ref[:, start : start + width] = ref[...]
    came = jnp.concatenate(
        [ref[...] * jnp.where(here, 1.0, 0.0) for ref, (_, _, _, here) in zip(arrived, sides(subs))], axis=0
    )
    start, width = cut(widths)[-1]
    out_ref[:, start : start + width] = ready[-1][...] + pick(flipped_ref[:, : came.shape[0]], came)


def swaps(count, stride, odd):
    partner = list(range(count))
    for low in range(count - stride):
        if (low // stride) % 2 == odd:
            partner[low], partner[low + stride] = low + stride, low
    return list(enumerate(partner)) if partner != list(range(count)) else []


def local(load_terms, schur_matrix, local_inverse, coarse_modes, cluster_inverse, row_blocks):
    load = load_terms[0, 0]
    basis = coarse_modes[0, 0]
    columns = cluster_inverse[0]
    blocks = row_blocks[0, 0]
    rows, loads = load.shape
    modes = basis.shape[1]
    shared_rows = blocks.shape[1]
    listed = 4 * shared_rows
    subs = lax.axis_size("sub")
    if lax.axis_size("grp") != 4 or sum(WIDTHS) != loads:
        raise ValueError("unexpected sizes")

    up = [(low, (low + 1) % subs) for low in range(subs)]
    down = [(target, source) for source, target in up]
    plans = [(0, swaps(subs, ROW_SUBS, 0)), (2, up), (1, down), (3, swaps(subs, ROW_SUBS, 1))]
    plans = [plan for plan in plans if plan[1]]
    count = len(plans)
    pair_plan = [(0, 1), (1, 0), (2, 3), (3, 2)]
    mirror_plan = [(0, 3), (3, 0), (1, 2), (2, 1)]

    def exchange(parts):
        return [lax.ppermute(parts[place], "sub", pairs) for place, pairs in plans]

    def whole(width, kind=f32):
        return ((rows, width), kind)

    def shared(width):
        return [((shared_rows, width), f32)] * count

    run = Chain()
    size = rows * loads
    one_hot, *parts = run(
        lambda *refs: listed_body(subs, count, WIDTHS, *refs),
        [((listed, rows), bf16)] + [kind for width in WIDTHS for kind in shared(width)],
        4 * listed * size, 16 * size, blocks, load,
    )
    streams = []
    for place in range(len(WIDTHS)):
        streams.append({"arrived": exchange(parts[place * count : (place + 1) * count])})
    chooser, flipped, basis_high, basis_low, test_high, test_low, sent, *ordered = run(
        lambda *refs: order_body(subs, WIDTHS, *refs),
        [whole(rows, bf16)] * 2 + [whole(modes, bf16)] * 2 + [((modes, rows), bf16)] * 2
        + [((modes, modes), f32)] + [whole(width) for width in WIDTHS],
        4 * rows * size, 24 * size, one_hot, load, basis, columns,
    )
    other = lax.ppermute(sent, "grp", pair_plan)
    schur_high, schur_low, solve_high, solve_low = run(
        lambda *refs: matrices_body(subs, listed, *refs),
        [whole(rows, bf16)] * 4, 16 * rows**3, 24 * size,
        chooser, flipped, schur_matrix[0, 0], local_inverse[0, 0],
    )
    for stream, rows_sorted, width in zip(streams, ordered, WIDTHS):
        stream.update(load=rows_sorted, value=rows_sorted, width=width, iterate=None)

    mixers = run(blend_body, [((2 * modes, 2 * modes), bf16)] * 2, size, size, columns, other)

    def project(stream):
        width = stream["width"]
        stream["projected"], stream["high"], stream["low"] = run(
            lambda *refs: project_body(subs, count, *refs),
            [((modes, width), f32), whole(width, bf16), whole(width, bf16)],
            6 * modes * rows * width, 12 * rows * width,
            stream["value"], test_high, test_low, *stream["arrived"],
        )
        stream["theirs"] = lax.ppermute(stream["projected"], "grp", pair_plan)

    def mix(stream):
        width = stream["width"]
        away, stream["kept"] = run(
            mix_body, [((modes, width), f32)] * 2, 24 * modes * modes * width, 4 * rows * width,
            stream["projected"], stream["theirs"], *mixers,
        )
        stream["came"] = lax.ppermute(away, "grp", mirror_plan)

    def solve(stream):
        width = stream["width"]
        (stream["fine"],) = run(
            solve_body, [whole(width)], 6 * rows * rows * width, 12 * rows * width,
            stream["high"], stream["low"], solve_high, solve_low,
        )

    def correct(stream):
        width = stream["width"]
        stream["step"], *parts = run(
            correct_body, [whole(width)] + shared(width), 6 * modes * rows * width, 12 * rows * width,
            stream["kept"], stream["came"], stream["fine"], basis_high, basis_low,
        )
        stream["arrived"] = exchange(parts)

    def product(stream):
        width = stream["width"]
        before = [] if stream["iterate"] is None else [stream["iterate"]]
        stream["iterate"], stream["value"], *parts = run(
            lambda *refs: product_body(subs, count, not before, *refs),
            [whole(width)] * 2 + shared(width), 6 * rows * rows * width, 16 * rows * width,
            stream["step"], *stream["arrived"], *before, stream["load"], schur_high, schur_low,
        )
        stream["arrived"] = exchange(parts)

    steps = {"project": project, "mix": mix, "solve": solve, "correct": correct, "product": product}
    plan = []
    for place, stream in enumerate(streams):
        for iteration in range(ITERS):
            plan += [(iteration * CYCLE + place * LAG + when, place, name) for name, when in PACE.items()]
    for _, place, name in sorted(plan):
        steps[name](streams[place])

    (solution_rows,) = run(
        lambda *refs: restore_body(WIDTHS, *refs), [whole(loads)], 4 * rows * size, 10 * size,
        flipped, *[stream["iterate"] for stream in streams],
    )
    ready = []
    for stream in streams[:-1]:
        ready += run(
            lambda *refs: settle_body(subs, *refs), [whole(stream["width"])],
            4 * rows * rows * stream["width"], 10 * rows * stream["width"],
            flipped, stream["value"], *stream["arrived"],
        )
    final = streams[-1]
    ready += run(
        lambda *refs: restore_body((final["width"],), *refs), [whole(final["width"])],
        4 * rows * rows * final["width"], 10 * rows * final["width"], flipped, final["value"],
    )
    (residual_rows,) = run(
        lambda *refs: finish_body(subs, WIDTHS, *refs), [whole(loads)], 4 * rows * size, 10 * size,
        flipped, *ready, *final["arrived"],
    )
    return (solution_rows[None, None], residual_rows[None, None])


def solution(mesh):
    return jax.shard_map(
        local,
        mesh=mesh,
        in_specs=(
            P("sub", "grp", None, None),
            P("sub", "grp", None, None),
            P("sub", "grp", None, None),
            P("sub", "grp", None, None),
            P("sub", None, "grp"),
            P("sub", "grp", None, None),
        ),
        out_specs=(P("sub", "grp", None, None), P("sub", "grp", None, None)),
        check_vma=False,
    )
```

```python
import jax
import jax.numpy as jnp
from jax import lax
from jax.experimental import pallas as pl
from jax.experimental.pallas import tpu as pltpu
from jax.sharding import PartitionSpec as P

ITERS = 2
ROW_SUBS = 4
RELAX = 0.5
WIDTHS = (384,)
GROUPS = 4
PACE = {"project": 0, "mix": 4, "solve": 4.5, "correct": 10, "product": 15}
CYCLE = 20
LAG = 10

f32 = jnp.float32
bf16 = jnp.bfloat16
NN = (((1,), (0,)), ((), ()))
NT = (((1,), (1,)), ((), ()))


class Chain:
    def __init__(self):
        self.last = None

    def __call__(self, body, outs, flops, moved, *operands, scratch=(), ins=None, places=None):
        count = len(operands)
        specs = [pl.BlockSpec(memory_space=pltpu.VMEM)] * count if ins is None else ins
        extra = []
        if self.last is not None:
            extra = [self.last]
            specs = specs + [pl.BlockSpec(memory_space=pl.ANY)]

        def whole_body(*refs):
            body(*refs[:count], *refs[count + len(extra) :])

        results = pl.pallas_call(
            whole_body,
            out_shape=[jax.ShapeDtypeStruct(shape, kind) for shape, kind in outs],
            in_specs=specs,
            out_specs=[pl.BlockSpec(memory_space=pltpu.VMEM)] * len(outs) if places is None else places,
            scratch_shapes=list(scratch),
            compiler_params=pltpu.CompilerParams(vmem_limit_bytes=24 * 1024 * 1024),
            cost_estimate=pl.CostEstimate(flops=flops, bytes_accessed=moved, transcendentals=0),
        )(*operands, *extra)
        self.last = results[0]
        return results


def dot(left, right, dims=NN):
    return lax.dot_general(left, right, dims, preferred_element_type=f32)


def split(value):
    high = value.astype(bf16)
    return high, (value - high.astype(f32)).astype(bf16)


def dot3(left, right):
    return dot(left[0], right[0]) + (dot(left[0], right[1]) + dot(left[1], right[0]))


def pick(chooser, value):
    high, low = split(value)
    return dot(chooser, high) + dot(chooser, low)


def sides(subs):
    sub = lax.axis_index("sub")
    low_row = (sub // ROW_SUBS) % 2 == 0
    over, under = sub < subs - ROW_SUBS, sub >= ROW_SUBS
    return [
        (low_row, 3, 2, jnp.where(low_row, over, under)),
        (low_row, 0, 0, sub > 0),
        (low_row, 1, 1, sub < subs - 1),
        (low_row, 2, 3, jnp.where(low_row, under, over)),
    ]


def put_shared(value, shared_refs):
    for place, ref in enumerate(shared_refs):
        width = ref.shape[0]
        ref[...] = value[place * width : (place + 1) * width]


def add_shared(subs, value, shared_refs):
    width = shared_refs[0].shape[0]
    parts = [
        value[place * width : (place + 1) * width] + ref[...] * jnp.where(here, 1.0, 0.0)
        for place, (ref, (_, _, _, here)) in enumerate(zip(shared_refs, sides(subs)))
    ]
    parts.append(value[len(shared_refs) * width :])
    return jnp.concatenate(parts, axis=0)


def cut(widths):
    starts = [sum(widths[:place]) for place in range(len(widths))]
    return list(zip(starts, widths))


def listed_body(subs, count, widths, blocks_hbm, load_hbm, listed_ref, load_ref, *refs):
    *shared_refs, blocks_ref, load_sem, blocks_sem = refs
    load_copy = pltpu.make_async_copy(load_hbm, load_ref, load_sem)
    blocks_copy = pltpu.make_async_copy(blocks_hbm, blocks_ref, blocks_sem)
    blocks_copy.start()
    load_copy.start()
    blocks_copy.wait()
    blocks = blocks_ref[...]
    placed = jnp.concatenate(
        [jnp.where(test, blocks[a : a + 1], blocks[b : b + 1]) for test, a, b, _ in sides(subs)], axis=0
    )
    upright = placed.astype(f32).T
    column = jnp.concatenate([upright[:, place : place + 1] for place in range(4)], axis=0)
    listed, total = column.shape[0], load_ref.shape[0]
    lane = lax.broadcasted_iota(jnp.int32, (listed, total), 1).astype(f32)
    first = (column == lane).astype(f32).astype(bf16)
    listed_ref[...] = first
    load_copy.wait()
    sent = pick(first[: count * blocks.shape[1]], load_ref[...])
    for place, (start, width) in enumerate(cut(widths)):
        put_shared(sent[:, start : start + width], shared_refs[place * count : (place + 1) * count])


def order_body(subs, widths, listed_ref, load_ref, basis_ref, columns_ref,
               chooser_ref, flipped_ref, basis_high, basis_low, test_high, test_low, *refs):
    listed, total = listed_ref.shape
    first = listed_ref[...].astype(f32)
    unlisted = 1.0 - jnp.sum(first, axis=0, keepdims=True)
    before = (
        lax.broadcasted_iota(jnp.int32, (total, total), 0)
        < lax.broadcasted_iota(jnp.int32, (total, total), 1)
    ).astype(f32).astype(bf16)
    rank = dot(jnp.broadcast_to(unlisted, (8, total)).astype(bf16), before)[:1]
    slot = lax.broadcasted_iota(jnp.int32, (total - listed, total), 0).astype(f32)
    last = jnp.where(rank == slot, unlisted, 0.0)
    chooser = jnp.concatenate([first, last], axis=0)
    flipped_ref[...] = chooser.T.astype(bf16)
    weighted = (chooser * weight_column(subs, listed // 4, total)).astype(bf16)
    chooser = chooser.astype(bf16)
    chooser_ref[...] = chooser
    ordered = pick(chooser, load_ref[...])
    for ref, (start, width) in zip(refs[GROUPS - 2 :], cut(widths)):
        ref[...] = ordered[:, start : start + width]
    for part, out, turned in zip(split(basis_ref[...]), (basis_high, basis_low), (test_high, test_low)):
        placed = dot(weighted, part)
        out[...] = placed.astype(bf16)
        turned[...] = placed.T.astype(bf16)
    for step, ref in zip(range(1, GROUPS - 1), refs):
        put_blocks(columns_ref, step, ref)


def put_blocks(columns_ref, step, ref):
    grp = lax.axis_index("grp")
    ref[...] = jnp.concatenate(
        [rows_of(columns_ref, grp), rows_of(columns_ref, grp ^ step ^ following(step))], axis=0
    )


def following(step):
    return step % (GROUPS - 1) + 1


def weight_column(subs, width, total):
    parts = [jnp.full((width, 1), jnp.where(here, 0.5, 1.0), f32) for _, _, _, here in sides(subs)]
    return jnp.concatenate(parts + [jnp.ones((total - 4 * width, 1), f32)], axis=0)


def rows_of(columns_ref, place):
    modes = columns_ref.shape[1]
    return columns_ref[pl.ds(pl.multiple_of(place * modes, modes), modes), :]


def matrices_body(subs, listed, chooser_ref, flipped_ref, schur_ref, solve_ref, columns_ref,
                  schur_high, schur_low, solve_high, solve_low, sent_ref):
    chooser, flipped = chooser_ref[...], flipped_ref[...]
    column = weight_column(subs, listed // 4, chooser.shape[0])
    weighted = (chooser.astype(f32) * column).astype(bf16)
    for part, out in zip(split(solve_ref[...] * RELAX), (solve_high, solve_low)):
        out[...] = dot(dot(weighted, part).astype(bf16), weighted, NT).astype(bf16)
    put_blocks(columns_ref, GROUPS - 1, sent_ref)
    for part, out in zip(split(schur_ref[...]), (schur_high, schur_low)):
        out[...] = dot(dot(chooser, part).astype(bf16), flipped).astype(bf16)


def blend_body(columns_ref, *refs):
    *came_refs, mix_high, mix_low = refs
    modes = columns_ref.shape[1]
    grp = lax.axis_index("grp")
    blocks = {}
    for step in range(GROUPS):
        blocks[step, 0] = rows_of(columns_ref, grp ^ step)
        blocks[0, step] = blocks[step, 0].T if step else blocks[0, 0]
    for step, ref in zip(range(1, GROUPS), came_refs):
        blocks[step, step] = ref[:modes]
        blocks[following(step), step] = ref[modes:]
        blocks[step, following(step)] = ref[modes:].T
    mix = jnp.concatenate(
        [jnp.concatenate([blocks[i, j] for j in range(GROUPS)], axis=1) for i in range(GROUPS)], axis=0
    )
    mix_high[...], mix_low[...] = split(mix * RELAX)


def quarter(ref, place):
    size = ref.shape[0] // GROUPS
    return ref.at[pl.ds(pl.multiple_of(place * size, size), size), :]


def project_body(subs, count, value_ref, test_high, test_low, *refs):
    halves = split(add_shared(subs, value_ref[...], refs[:count]))
    high_ref, low_ref, *quarter_refs, turned_ref = refs[count:]
    turned_ref[...] = dot3((test_high[...], test_low[...]), halves).T
    grp = lax.axis_index("grp")
    for step, ref in enumerate(quarter_refs):
        ref[...] = quarter(turned_ref, grp ^ step)[...]
    high_ref[...], low_ref[...] = halves


def solve_body(high_ref, low_ref, solve_high, solve_low, fine_ref):
    fine_ref[...] = dot3((solve_high[...], solve_low[...]), (high_ref[...], low_ref[...]))


def mix_body(mix_high, mix_low, *refs):
    gathered = jnp.concatenate([ref[...] for ref in refs[:GROUPS]], axis=1)
    mixed = dot3(split(gathered), (mix_high[...], mix_low[...]))
    for step, ref in enumerate(refs[GROUPS:]):
        modes = ref.shape[1]
        ref[...] = mixed[:, step * modes : (step + 1) * modes]


def correct_body(fine_ref, basis_high, basis_low, *refs):
    quarters, (out_ref, *shared_refs, coarse_ref) = refs[:GROUPS], refs[GROUPS:]
    grp = lax.axis_index("grp")
    for step, ref in enumerate(quarters):
        quarter(coarse_ref, grp ^ step)[...] = ref[...]
    high, low = split(coarse_ref[...])
    correction = dot(basis_high[...], high, NT) + (dot(basis_high[...], low, NT) + dot(basis_low[...], high, NT))
    step = fine_ref[...] + correction
    out_ref[...] = step
    put_shared(step, shared_refs)


def product_body(subs, count, first, *refs):
    refs = list(refs)
    step = add_shared(subs, refs.pop(0)[...], [refs.pop(0) for _ in range(count)])
    if not first:
        step = step + refs.pop(0)[...]
    load_ref, schur_high, schur_low, iterate_ref, out_ref = refs[:5]
    iterate_ref[...] = step
    value = load_ref[...] - dot3((schur_high[...], schur_low[...]), split(step))
    out_ref[...] = value
    put_shared(value, refs[5:])


def settle_body(subs, flipped_ref, value_ref, *refs):
    refs[-1][...] = pick(flipped_ref[...], add_shared(subs, value_ref[...], refs[:-1]))


def restore_body(widths, flipped_ref, value_ref, *refs):
    flipped = flipped_ref[...]
    base_ref, out_ref = refs[-2:]
    for ref, (start, width) in zip(refs, cut(widths)):
        out_ref[:, start : start + width] = pick(flipped, ref[...])
    base_ref[...] = pick(flipped, value_ref[...])


def finish_body(subs, widths, flipped_ref, *refs):
    *refs, out_hbm, out_ref, sems = refs
    ready, arrived = refs[: len(widths)], refs[len(widths) :]
    came = jnp.concatenate(
        [ref[...] * jnp.where(here, 1.0, 0.0) for ref, (_, _, _, here) in zip(arrived, sides(subs))], axis=0
    )
    halves = split(came)
    copies = []
    size = out_ref.shape[0] // 4
    for step in range(4):
        rows = slice(step * size, (step + 1) * size)
        for ref, (start, width) in zip(ready, cut(widths)):
            value = ref[rows]
            if ref is ready[-1]:
                chooser = flipped_ref[rows, : came.shape[0]]
                value = value + (dot(chooser, halves[0]) + dot(chooser, halves[1]))
            out_ref[rows, start : start + width] = value
        copy = pltpu.make_async_copy(out_ref.at[rows], out_hbm.at[rows], sems.at[step])
        copy.start()
        copies.append(copy)
    for copy in copies:
        copy.wait()


def swaps(count, stride, odd):
    partner = list(range(count))
    for low in range(count - stride):
        if (low // stride) % 2 == odd:
            partner[low], partner[low + stride] = low + stride, low
    return list(enumerate(partner)) if partner != list(range(count)) else []


def local(load_terms, schur_matrix, local_inverse, coarse_modes, cluster_inverse, row_blocks):
    load = load_terms[0, 0]
    basis = coarse_modes[0, 0]
    columns = cluster_inverse[0]
    blocks = row_blocks[0, 0]
    rows, loads = load.shape
    modes = basis.shape[1]
    shared_rows = blocks.shape[1]
    listed = 4 * shared_rows
    subs = lax.axis_size("sub")
    if lax.axis_size("grp") != GROUPS or sum(WIDTHS) != loads:
        raise ValueError("unexpected sizes")

    up = [(low, (low + 1) % subs) for low in range(subs)]
    down = [(target, source) for source, target in up]
    plans = [(0, swaps(subs, ROW_SUBS, 0)), (2, up), (1, down), (3, swaps(subs, ROW_SUBS, 1))]
    plans = [plan for plan in plans if plan[1]]
    count = len(plans)
    def exchange(parts):
        return [lax.ppermute(parts[place], "sub", pairs) for place, pairs in plans]

    def regroup(parts):
        moved = [
            lax.ppermute(part, "grp", [(member, member ^ step) for member in range(GROUPS)])
            for step, part in enumerate(parts) if step and part is not None
        ]
        return [parts[0], *moved]

    def whole(width, kind=f32):
        return ((rows, width), kind)

    def shared(width):
        return [((shared_rows, width), f32)] * count

    run = Chain()
    size = rows * loads
    outside = pl.BlockSpec(memory_space=pltpu.HBM)
    one_hot, load_near, *parts = run(
        lambda *refs: listed_body(subs, count, WIDTHS, *refs),
        [((listed, rows), bf16), whole(loads)] + [kind for width in WIDTHS for kind in shared(width)],
        4 * listed * size, 16 * size,
        *[pltpu.with_memory_space_constraint(array, pltpu.HBM) for array in (blocks, load)], ins=[outside] * 2,
        scratch=[pltpu.VMEM(blocks.shape, blocks.dtype), pltpu.SemaphoreType.DMA, pltpu.SemaphoreType.DMA],
    )
    streams = []
    for place in range(len(WIDTHS)):
        streams.append({"arrived": exchange(parts[place * count : (place + 1) * count])})
    chooser, flipped, basis_high, basis_low, test_high, test_low, *ordered = run(
        lambda *refs: order_body(subs, WIDTHS, *refs),
        [whole(rows, bf16)] * 2 + [whole(modes, bf16)] * 2 + [((modes, rows), bf16)] * 2
        + [((2 * modes, modes), f32)] * (GROUPS - 2) + [whole(width) for width in WIDTHS],
        4 * rows * size, 24 * size, one_hot, load_near, basis, columns,
    )
    others = regroup([None, *ordered[: GROUPS - 2]])[1:]
    ordered = ordered[GROUPS - 2 :]
    schur_high, schur_low, solve_high, solve_low, sent = run(
        lambda *refs: matrices_body(subs, listed, *refs),
        [whole(rows, bf16)] * 4 + [((2 * modes, modes), f32)], 16 * rows**3, 24 * size,
        chooser, flipped, schur_matrix[0, 0], local_inverse[0, 0], columns,
    )
    others += regroup([None] * (GROUPS - 1) + [sent])[-1:]
    for stream, rows_sorted, width in zip(streams, ordered, WIDTHS):
        stream.update(load=rows_sorted, value=rows_sorted, width=width, iterate=None)

    mixers = []

    def project(stream):
        width = stream["width"]
        stream["high"], stream["low"], *quarters = run(
            lambda *refs: project_body(subs, count, *refs),
            [whole(width, bf16)] * 2 + [((width // GROUPS, modes), f32)] * GROUPS,
            6 * modes * rows * width, 12 * rows * width,
            stream["value"], test_high, test_low, *stream["arrived"],
            scratch=[pltpu.VMEM((width, modes), f32)],
        )
        stream["quarters"] = regroup(quarters)

    def mix(stream):
        width = stream["width"]
        if not mixers:
            mixers.extend(
                run(blend_body, [((GROUPS * modes, GROUPS * modes), bf16)] * 2, size, size, columns, *others)
            )
        parts = run(
            mix_body, [((width // GROUPS, modes), f32)] * GROUPS, 24 * modes * modes * width, 4 * rows * width,
            *mixers, *stream["quarters"],
        )
        stream["quarters"] = regroup(parts)

    def solve(stream):
        width = stream["width"]
        (stream["fine"],) = run(
            solve_body, [whole(width)], 6 * rows * rows * width, 12 * rows * width,
            stream["high"], stream["low"], solve_high, solve_low,
        )

    def correct(stream):
        width = stream["width"]
        stream["step"], *parts = run(
            correct_body, [whole(width)] + shared(width), 6 * modes * rows * width, 12 * rows * width,
            stream["fine"], basis_high, basis_low, *stream["quarters"],
            scratch=[pltpu.VMEM((width, modes), f32)],
        )
        stream["arrived"] = exchange(parts)

    def product(stream):
        width = stream["width"]
        before = [] if stream["iterate"] is None else [stream["iterate"]]
        stream["iterate"], stream["value"], *parts = run(
            lambda *refs: product_body(subs, count, not before, *refs),
            [whole(width)] * 2 + shared(width), 6 * rows * rows * width, 16 * rows * width,
            stream["step"], *stream["arrived"], *before, stream["load"], schur_high, schur_low,
        )
        stream["arrived"] = exchange(parts)

    steps = {"project": project, "mix": mix, "solve": solve, "correct": correct, "product": product}
    plan = []
    for place, stream in enumerate(streams):
        for iteration in range(ITERS):
            plan += [(iteration * CYCLE + place * LAG + when, place, name) for name, when in PACE.items()]
    for _, place, name in sorted(plan):
        steps[name](streams[place])

    ready = []
    for stream in streams[:-1]:
        ready += run(
            lambda *refs: settle_body(subs, *refs), [whole(stream["width"])],
            4 * rows * rows * stream["width"], 10 * rows * stream["width"],
            flipped, stream["value"], *stream["arrived"],
        )
    final = streams[-1]
    base, solution_rows = run(
        lambda *refs: restore_body(WIDTHS, *refs), [whole(final["width"]), whole(loads)],
        8 * rows * size, 10 * size, flipped, final["value"], *[stream["iterate"] for stream in streams],
    )
    (residual_rows,) = run(
        lambda *refs: finish_body(subs, WIDTHS, *refs), [whole(loads)], 4 * rows * size, 10 * size,
        flipped, *ready, base, *final["arrived"], places=[outside],
        scratch=[pltpu.VMEM((rows, loads), f32), pltpu.SemaphoreType.DMA((4,))],
    )
    return (solution_rows[None, None], residual_rows[None, None])


def solution(mesh):
    return jax.shard_map(
        local,
        mesh=mesh,
        in_specs=(
            P("sub", "grp", None, None),
            P("sub", "grp", None, None),
            P("sub", "grp", None, None),
            P("sub", "grp", None, None),
            P("sub", None, "grp"),
            P("sub", "grp", None, None),
        ),
        out_specs=(P("sub", "grp", None, None), P("sub", "grp", None, None)),
        check_vma=False,
    )
```

```python
import jax
import jax.numpy as jnp
from jax import lax
from jax.experimental import pallas as pl
from jax.experimental.pallas import tpu as pltpu
from jax.sharding import PartitionSpec as P

ITERS = 2
ROW_SUBS = 4
RELAX = 0.5
WIDTHS = (384,)
GROUPS = 4
PACE = {"project": 0, "mix": 4, "solve": 4.5, "correct": 10, "product": 15}
CYCLE = 20
LAG = 10

f32 = jnp.float32
bf16 = jnp.bfloat16
NN = (((1,), (0,)), ((), ()))
NT = (((1,), (1,)), ((), ()))


class Chain:
    def __init__(self):
        self.last = None

    def __call__(self, body, outs, flops, moved, *operands, scratch=(), ins=None, places=None):
        count = len(operands)
        specs = [pl.BlockSpec(memory_space=pltpu.VMEM)] * count if ins is None else ins
        extra = []
        if self.last is not None:
            extra = [self.last]
            specs = specs + [pl.BlockSpec(memory_space=pl.ANY)]

        def whole_body(*refs):
            body(*refs[:count], *refs[count + len(extra) :])

        results = pl.pallas_call(
            whole_body,
            out_shape=[jax.ShapeDtypeStruct(shape, kind) for shape, kind in outs],
            in_specs=specs,
            out_specs=[pl.BlockSpec(memory_space=pltpu.VMEM)] * len(outs) if places is None else places,
            scratch_shapes=list(scratch),
            compiler_params=pltpu.CompilerParams(vmem_limit_bytes=24 * 1024 * 1024),
            cost_estimate=pl.CostEstimate(flops=flops, bytes_accessed=moved, transcendentals=0),
        )(*operands, *extra)
        self.last = results[0]
        return results


def dot(left, right, dims=NN):
    return lax.dot_general(left, right, dims, preferred_element_type=f32)


def split(value):
    high = value.astype(bf16)
    return high, (value - high.astype(f32)).astype(bf16)


def dot3(left, right):
    return dot(left[0], right[0]) + (dot(left[0], right[1]) + dot(left[1], right[0]))


def pick(chooser, value):
    high, low = split(value)
    return dot(chooser, high) + dot(chooser, low)


def sides(subs):
    sub = lax.axis_index("sub")
    low_row = (sub // ROW_SUBS) % 2 == 0
    over, under = sub < subs - ROW_SUBS, sub >= ROW_SUBS
    return [
        (low_row, 3, 2, jnp.where(low_row, over, under)),
        (low_row, 0, 0, sub > 0),
        (low_row, 1, 1, sub < subs - 1),
        (low_row, 2, 3, jnp.where(low_row, under, over)),
    ]


def put_shared(value, shared_refs):
    for place, ref in enumerate(shared_refs):
        width = ref.shape[0]
        ref[...] = value[place * width : (place + 1) * width]


def add_shared(subs, value, shared_refs):
    width = shared_refs[0].shape[0]
    parts = [
        value[place * width : (place + 1) * width] + ref[...] * jnp.where(here, 1.0, 0.0)
        for place, (ref, (_, _, _, here)) in enumerate(zip(shared_refs, sides(subs)))
    ]
    parts.append(value[len(shared_refs) * width :])
    return jnp.concatenate(parts, axis=0)


def cut(widths):
    starts = [sum(widths[:place]) for place in range(len(widths))]
    return list(zip(starts, widths))


def listed_body(subs, count, widths, blocks_hbm, load_hbm, listed_ref, load_ref, *refs):
    *shared_refs, blocks_ref, load_sem, blocks_sem = refs
    load_copy = pltpu.make_async_copy(load_hbm, load_ref, load_sem)
    blocks_copy = pltpu.make_async_copy(blocks_hbm, blocks_ref, blocks_sem)
    blocks_copy.start()
    load_copy.start()
    blocks_copy.wait()
    blocks = blocks_ref[...]
    placed = jnp.concatenate(
        [jnp.where(test, blocks[a : a + 1], blocks[b : b + 1]) for test, a, b, _ in sides(subs)], axis=0
    )
    upright = placed.astype(f32).T
    column = jnp.concatenate([upright[:, place : place + 1] for place in range(4)], axis=0)
    listed, total = column.shape[0], load_ref.shape[0]
    lane = lax.broadcasted_iota(jnp.int32, (listed, total), 1).astype(f32)
    first = (column == lane).astype(f32).astype(bf16)
    listed_ref[...] = first
    load_copy.wait()
    sent = pick(first[: count * blocks.shape[1]], load_ref[...])
    for place, (start, width) in enumerate(cut(widths)):
        put_shared(sent[:, start : start + width], shared_refs[place * count : (place + 1) * count])


def order_body(subs, widths, listed_ref, load_ref, basis_ref, columns_ref,
               chooser_ref, flipped_ref, basis_high, basis_low, test_high, test_low, sent_ref, *refs):
    listed, total = listed_ref.shape
    first = listed_ref[...].astype(f32)
    unlisted = 1.0 - jnp.sum(first, axis=0, keepdims=True)
    before = (
        lax.broadcasted_iota(jnp.int32, (total, total), 0)
        < lax.broadcasted_iota(jnp.int32, (total, total), 1)
    ).astype(f32).astype(bf16)
    rank = dot(jnp.broadcast_to(unlisted, (8, total)).astype(bf16), before)[:1]
    slot = lax.broadcasted_iota(jnp.int32, (total - listed, total), 0).astype(f32)
    last = jnp.where(rank == slot, unlisted, 0.0)
    chooser = jnp.concatenate([first, last], axis=0)
    flipped_ref[...] = chooser.T.astype(bf16)
    weighted = (chooser * weight_column(subs, listed // 4, total)).astype(bf16)
    chooser = chooser.astype(bf16)
    chooser_ref[...] = chooser
    ordered = pick(chooser, load_ref[...])
    for ref, (start, width) in zip(refs, cut(widths)):
        ref[...] = ordered[:, start : start + width]
    for part, out, turned in zip(split(basis_ref[...]), (basis_high, basis_low), (test_high, test_low)):
        placed = dot(weighted, part)
        out[...] = placed.astype(bf16)
        turned[...] = placed.T.astype(bf16)
    sent_ref[...] = rows_of(columns_ref, 3 - (lax.axis_index("grp") ^ 1))


def weight_column(subs, width, total):
    parts = [jnp.full((width, 1), jnp.where(here, 0.5, 1.0), f32) for _, _, _, here in sides(subs)]
    return jnp.concatenate(parts + [jnp.ones((total - 4 * width, 1), f32)], axis=0)


def rows_of(columns_ref, place):
    modes = columns_ref.shape[1]
    return columns_ref[pl.ds(pl.multiple_of(place * modes, modes), modes), :]


def matrices_body(subs, listed, chooser_ref, flipped_ref, schur_ref, solve_ref,
                  schur_high, schur_low, solve_high, solve_low):
    chooser, flipped = chooser_ref[...], flipped_ref[...]
    column = weight_column(subs, listed // 4, chooser.shape[0])
    weighted = (chooser.astype(f32) * column).astype(bf16)
    for part, out in zip(split(solve_ref[...] * RELAX), (solve_high, solve_low)):
        out[...] = dot(dot(weighted, part).astype(bf16), weighted, NT).astype(bf16)
    for part, out in zip(split(schur_ref[...]), (schur_high, schur_low)):
        out[...] = dot(dot(chooser, part).astype(bf16), flipped).astype(bf16)


def blend_body(columns_ref, other_ref, mix_high, mix_low):
    grp = lax.axis_index("grp")
    away = jnp.concatenate([rows_of(columns_ref, 3 - grp), other_ref[...]], axis=1)
    kept = jnp.concatenate([rows_of(columns_ref, grp), rows_of(columns_ref, grp ^ 1).T], axis=1)
    mix_high[...], mix_low[...] = split(jnp.concatenate([away, kept], axis=0) * RELAX)


def project_body(subs, count, value_ref, test_high, test_low, *refs):
    halves = split(add_shared(subs, value_ref[...], refs[:count]))
    projected_ref, high_ref, low_ref = refs[count:]
    projected_ref[...] = dot3((test_high[...], test_low[...]), halves)
    high_ref[...], low_ref[...] = halves


def solve_body(high_ref, low_ref, solve_high, solve_low, fine_ref):
    fine_ref[...] = dot3((solve_high[...], solve_low[...]), (high_ref[...], low_ref[...]))


def mix_body(own_ref, other_ref, mix_high, mix_low, away_ref, kept_ref):
    pair = jnp.concatenate([own_ref[...], other_ref[...]], axis=0)
    mixed = dot3((mix_high[...], mix_low[...]), split(pair))
    modes = away_ref.shape[0]
    away_ref[...] = mixed[:modes]
    kept_ref[...] = mixed[modes:]


def correct_body(kept_ref, came_ref, fine_ref, basis_high, basis_low, out_ref, *shared_refs):
    coarse = kept_ref[...] + came_ref[...]
    step = fine_ref[...] + dot3((basis_high[...], basis_low[...]), split(coarse))
    out_ref[...] = step
    put_shared(step, shared_refs)


def product_body(subs, count, first, *refs):
    refs = list(refs)
    step = add_shared(subs, refs.pop(0)[...], [refs.pop(0) for _ in range(count)])
    if not first:
        step = step + refs.pop(0)[...]
    load_ref, schur_high, schur_low, iterate_ref, out_ref = refs[:5]
    iterate_ref[...] = step
    value = load_ref[...] - dot3((schur_high[...], schur_low[...]), split(step))
    out_ref[...] = value
    put_shared(value, refs[5:])


def settle_body(subs, flipped_ref, value_ref, *refs):
    refs[-1][...] = pick(flipped_ref[...], add_shared(subs, value_ref[...], refs[:-1]))


def restore_body(widths, flipped_ref, value_ref, *refs):
    flipped = flipped_ref[...]
    base_ref, out_ref = refs[-2:]
    for ref, (start, width) in zip(refs, cut(widths)):
        out_ref[:, start : start + width] = pick(flipped, ref[...])
    base_ref[...] = pick(flipped, value_ref[...])


def finish_body(subs, widths, flipped_ref, *refs):
    *refs, out_hbm, out_ref, sems = refs
    ready, arrived = refs[: len(widths)], refs[len(widths) :]
    came = jnp.concatenate(
        [ref[...] * jnp.where(here, 1.0, 0.0) for ref, (_, _, _, here) in zip(arrived, sides(subs))], axis=0
    )
    halves = split(came)
    copies = []
    size = out_ref.shape[0] // 4
    for step in range(4):
        rows = slice(step * size, (step + 1) * size)
        for ref, (start, width) in zip(ready, cut(widths)):
            value = ref[rows]
            if ref is ready[-1]:
                chooser = flipped_ref[rows, : came.shape[0]]
                value = value + (dot(chooser, halves[0]) + dot(chooser, halves[1]))
            out_ref[rows, start : start + width] = value
        copy = pltpu.make_async_copy(out_ref.at[rows], out_hbm.at[rows], sems.at[step])
        copy.start()
        copies.append(copy)
    for copy in copies:
        copy.wait()


def swaps(count, stride, odd):
    partner = list(range(count))
    for low in range(count - stride):
        if (low // stride) % 2 == odd:
            partner[low], partner[low + stride] = low + stride, low
    return list(enumerate(partner)) if partner != list(range(count)) else []


def local(load_terms, schur_matrix, local_inverse, coarse_modes, cluster_inverse, row_blocks):
    load = load_terms[0, 0]
    basis = coarse_modes[0, 0]
    columns = cluster_inverse[0]
    blocks = row_blocks[0, 0]
    rows, loads = load.shape
    modes = basis.shape[1]
    shared_rows = blocks.shape[1]
    listed = 4 * shared_rows
    subs = lax.axis_size("sub")
    if lax.axis_size("grp") != GROUPS or sum(WIDTHS) != loads:
        raise ValueError("unexpected sizes")

    up = [(low, (low + 1) % subs) for low in range(subs)]
    down = [(target, source) for source, target in up]
    plans = [(0, swaps(subs, ROW_SUBS, 0)), (2, up), (1, down), (3, swaps(subs, ROW_SUBS, 1))]
    plans = [plan for plan in plans if plan[1]]
    count = len(plans)
    def exchange(parts):
        return [lax.ppermute(parts[place], "sub", pairs) for place, pairs in plans]

    def whole(width, kind=f32):
        return ((rows, width), kind)

    def shared(width):
        return [((shared_rows, width), f32)] * count

    pair_plan = [(0, 1), (1, 0), (2, 3), (3, 2)]
    mirror_plan = [(0, 3), (3, 0), (1, 2), (2, 1)]

    run = Chain()
    size = rows * loads
    outside = pl.BlockSpec(memory_space=pltpu.HBM)
    one_hot, load_near, *parts = run(
        lambda *refs: listed_body(subs, count, WIDTHS, *refs),
        [((listed, rows), bf16), whole(loads)] + [kind for width in WIDTHS for kind in shared(width)],
        4 * listed * size, 16 * size,
        *[pltpu.with_memory_space_constraint(array, pltpu.HBM) for array in (blocks, load)], ins=[outside] * 2,
        scratch=[pltpu.VMEM(blocks.shape, blocks.dtype), pltpu.SemaphoreType.DMA, pltpu.SemaphoreType.DMA],
    )
    streams = []
    for place in range(len(WIDTHS)):
        streams.append({"arrived": exchange(parts[place * count : (place + 1) * count])})
    chooser, flipped, basis_high, basis_low, test_high, test_low, sent, *ordered = run(
        lambda *refs: order_body(subs, WIDTHS, *refs),
        [whole(rows, bf16)] * 2 + [whole(modes, bf16)] * 2 + [((modes, rows), bf16)] * 2
        + [((modes, modes), f32)] + [whole(width) for width in WIDTHS],
        4 * rows * size, 24 * size, one_hot, load_near, basis, columns,
    )
    other = lax.ppermute(sent, "grp", pair_plan)
    for stream, rows_sorted, width in zip(streams, ordered, WIDTHS):
        stream.update(load=rows_sorted, value=rows_sorted, width=width, iterate=None)

    prepared = {}

    def prepare():
        names = ("schur_high", "schur_low", "solve_high", "solve_low")
        prepared.update(zip(names, run(
            lambda *refs: matrices_body(subs, listed, *refs),
            [whole(rows, bf16)] * 4, 16 * rows**3, 24 * size,
            chooser, flipped, schur_matrix[0, 0], local_inverse[0, 0],
        )))
        prepared["mix"] = run(blend_body, [((2 * modes, 2 * modes), bf16)] * 2, size, size, columns, other)

    def project(stream):
        width = stream["width"]
        stream["projected"], stream["high"], stream["low"] = run(
            lambda *refs: project_body(subs, count, *refs),
            [((modes, width), f32), whole(width, bf16), whole(width, bf16)],
            6 * modes * rows * width, 12 * rows * width,
            stream["value"], test_high, test_low, *stream["arrived"],
        )
        stream["theirs"] = lax.ppermute(stream["projected"], "grp", pair_plan)

    def mix(stream):
        if not prepared:
            prepare()
        width = stream["width"]
        away, stream["kept"] = run(
            mix_body, [((modes, width), f32)] * 2, 24 * modes * modes * width, 4 * rows * width,
            stream["projected"], stream["theirs"], *prepared["mix"],
        )
        stream["came"] = lax.ppermute(away, "grp", mirror_plan)

    def solve(stream):
        width = stream["width"]
        (stream["fine"],) = run(
            solve_body, [whole(width)], 6 * rows * rows * width, 12 * rows * width,
            stream["high"], stream["low"], prepared["solve_high"], prepared["solve_low"],
        )

    def correct(stream):
        width = stream["width"]
        stream["step"], *parts = run(
            correct_body, [whole(width)] + shared(width), 6 * modes * rows * width, 12 * rows * width,
            stream["kept"], stream["came"], stream["fine"], basis_high, basis_low,
        )
        stream["arrived"] = exchange(parts)

    def product(stream):
        width = stream["width"]
        before = [] if stream["iterate"] is None else [stream["iterate"]]
        stream["iterate"], stream["value"], *parts = run(
            lambda *refs: product_body(subs, count, not before, *refs),
            [whole(width)] * 2 + shared(width), 6 * rows * rows * width, 16 * rows * width,
            stream["step"], *stream["arrived"], *before, stream["load"], prepared["schur_high"], prepared["schur_low"],
        )
        stream["arrived"] = exchange(parts)

    steps = {"project": project, "mix": mix, "solve": solve, "correct": correct, "product": product}
    plan = []
    for place, stream in enumerate(streams):
        for iteration in range(ITERS):
            plan += [(iteration * CYCLE + place * LAG + when, place, name) for name, when in PACE.items()]
    for _, place, name in sorted(plan):
        steps[name](streams[place])

    ready = []
    for stream in streams[:-1]:
        ready += run(
            lambda *refs: settle_body(subs, *refs), [whole(stream["width"])],
            4 * rows * rows * stream["width"], 10 * rows * stream["width"],
            flipped, stream["value"], *stream["arrived"],
        )
    final = streams[-1]
    base, solution_rows = run(
        lambda *refs: restore_body(WIDTHS, *refs), [whole(final["width"]), whole(loads)],
        8 * rows * size, 10 * size, flipped, final["value"], *[stream["iterate"] for stream in streams],
    )
    (residual_rows,) = run(
        lambda *refs: finish_body(subs, WIDTHS, *refs), [whole(loads)], 4 * rows * size, 10 * size,
        flipped, *ready, base, *final["arrived"], places=[outside],
        scratch=[pltpu.VMEM((rows, loads), f32), pltpu.SemaphoreType.DMA((4,))],
    )
    return (solution_rows[None, None], residual_rows[None, None])


def solution(mesh):
    return jax.shard_map(
        local,
        mesh=mesh,
        in_specs=(
            P("sub", "grp", None, None),
            P("sub", "grp", None, None),
            P("sub", "grp", None, None),
            P("sub", "grp", None, None),
            P("sub", None, "grp"),
            P("sub", "grp", None, None),
        ),
        out_specs=(P("sub", "grp", None, None), P("sub", "grp", None, None)),
        check_vma=False,
    )
```

```python
import jax
import jax.numpy as jnp
from jax import lax
from jax.experimental import pallas as pl
from jax.experimental.pallas import tpu as pltpu
from jax.sharding import PartitionSpec as P

ITERS = 2
ROW_SUBS = 4
RELAX = 0.5
WIDTHS = (384,)
GROUPS = 4
PACE = {"project": 0, "mix": 4, "solve": 4.5, "correct": 10, "product": 15}
CYCLE = 20
LAG = 10

f32 = jnp.float32
bf16 = jnp.bfloat16
NN = (((1,), (0,)), ((), ()))
NT = (((1,), (1,)), ((), ()))


class Chain:
    def __init__(self):
        self.last = None

    def __call__(self, body, outs, flops, moved, *operands, scratch=(), ins=None, places=None):
        count = len(operands)
        specs = [pl.BlockSpec(memory_space=pltpu.VMEM)] * count if ins is None else ins
        extra = []
        if self.last is not None:
            extra = [self.last]
            specs = specs + [pl.BlockSpec(memory_space=pl.ANY)]

        def whole_body(*refs):
            body(*refs[:count], *refs[count + len(extra) :])

        results = pl.pallas_call(
            whole_body,
            out_shape=[jax.ShapeDtypeStruct(shape, kind) for shape, kind in outs],
            in_specs=specs,
            out_specs=[pl.BlockSpec(memory_space=pltpu.VMEM)] * len(outs) if places is None else places,
            scratch_shapes=list(scratch),
            compiler_params=pltpu.CompilerParams(vmem_limit_bytes=24 * 1024 * 1024),
            cost_estimate=pl.CostEstimate(flops=flops, bytes_accessed=moved, transcendentals=0),
        )(*operands, *extra)
        self.last = results[0]
        return results


def dot(left, right, dims=NN):
    return lax.dot_general(left, right, dims, preferred_element_type=f32)


def split(value):
    high = value.astype(bf16)
    return high, (value - high.astype(f32)).astype(bf16)


def dot3(left, right):
    return dot(left[0], right[0]) + (dot(left[0], right[1]) + dot(left[1], right[0]))


def pick(chooser, value):
    high, low = split(value)
    return dot(chooser, high) + dot(chooser, low)


def sides(subs):
    sub = lax.axis_index("sub")
    low_row = (sub // ROW_SUBS) % 2 == 0
    over, under = sub < subs - ROW_SUBS, sub >= ROW_SUBS
    return [
        (low_row, 3, 2, jnp.where(low_row, over, under)),
        (low_row, 0, 0, sub > 0),
        (low_row, 1, 1, sub < subs - 1),
        (low_row, 2, 3, jnp.where(low_row, under, over)),
    ]


def put_shared(value, shared_refs):
    for place, ref in enumerate(shared_refs):
        width = ref.shape[0]
        ref[...] = value[place * width : (place + 1) * width]


def add_shared(subs, value, shared_refs):
    width = shared_refs[0].shape[0]
    parts = [
        value[place * width : (place + 1) * width] + ref[...] * jnp.where(here, 1.0, 0.0)
        for place, (ref, (_, _, _, here)) in enumerate(zip(shared_refs, sides(subs)))
    ]
    parts.append(value[len(shared_refs) * width :])
    return jnp.concatenate(parts, axis=0)


def cut(widths):
    starts = [sum(widths[:place]) for place in range(len(widths))]
    return list(zip(starts, widths))


def listed_body(subs, count, widths, blocks_hbm, load_hbm, listed_ref, load_ref, *refs):
    *shared_refs, blocks_ref, load_sem, blocks_sem = refs
    load_copy = pltpu.make_async_copy(load_hbm, load_ref, load_sem)
    blocks_copy = pltpu.make_async_copy(blocks_hbm, blocks_ref, blocks_sem)
    blocks_copy.start()
    load_copy.start()
    blocks_copy.wait()
    blocks = blocks_ref[...]
    placed = jnp.concatenate(
        [jnp.where(test, blocks[a : a + 1], blocks[b : b + 1]) for test, a, b, _ in sides(subs)], axis=0
    )
    upright = placed.astype(f32).T
    column = jnp.concatenate([upright[:, place : place + 1] for place in range(4)], axis=0)
    listed, total = column.shape[0], load_ref.shape[0]
    lane = lax.broadcasted_iota(jnp.int32, (listed, total), 1).astype(f32)
    first = (column == lane).astype(f32).astype(bf16)
    listed_ref[...] = first
    load_copy.wait()
    sent = pick(first[: count * blocks.shape[1]], load_ref[...])
    for place, (start, width) in enumerate(cut(widths)):
        put_shared(sent[:, start : start + width], shared_refs[place * count : (place + 1) * count])


def order_body(subs, widths, listed_ref, load_ref, basis_ref, columns_ref,
               chooser_ref, flipped_ref, basis_high, basis_low, test_high, test_low, sent_ref, *refs):
    listed, total = listed_ref.shape
    first = listed_ref[...].astype(f32)
    unlisted = 1.0 - jnp.sum(first, axis=0, keepdims=True)
    before = (
        lax.broadcasted_iota(jnp.int32, (total, total), 0)
        < lax.broadcasted_iota(jnp.int32, (total, total), 1)
    ).astype(f32).astype(bf16)
    rank = dot(jnp.broadcast_to(unlisted, (8, total)).astype(bf16), before)[:1]
    slot = lax.broadcasted_iota(jnp.int32, (total - listed, total), 0).astype(f32)
    last = jnp.where(rank == slot, unlisted, 0.0)
    chooser = jnp.concatenate([first, last], axis=0)
    flipped_ref[...] = chooser.T.astype(bf16)
    weighted = (chooser * weight_column(subs, listed // 4, total)).astype(bf16)
    chooser = chooser.astype(bf16)
    chooser_ref[...] = chooser
    ordered = pick(chooser, load_ref[...])
    for ref, (start, width) in zip(refs, cut(widths)):
        ref[...] = ordered[:, start : start + width]
    for part, out, turned in zip(split(basis_ref[...]), (basis_high, basis_low), (test_high, test_low)):
        placed = dot(weighted, part)
        out[...] = placed.astype(bf16)
        turned[...] = placed.T.astype(bf16)
    sent_ref[...] = rows_of(columns_ref, lax.axis_index("grp") ^ 3)


def weight_column(subs, width, total):
    parts = [jnp.full((width, 1), jnp.where(here, 0.5, 1.0), f32) for _, _, _, here in sides(subs)]
    return jnp.concatenate(parts + [jnp.ones((total - 4 * width, 1), f32)], axis=0)


def rows_of(columns_ref, place):
    modes = columns_ref.shape[1]
    return columns_ref[pl.ds(pl.multiple_of(place * modes, modes), modes), :]


def matrices_body(subs, listed, chooser_ref, flipped_ref, schur_ref, solve_ref,
                  schur_high, schur_low, solve_high, solve_low):
    chooser, flipped = chooser_ref[...], flipped_ref[...]
    column = weight_column(subs, listed // 4, chooser.shape[0])
    weighted = (chooser.astype(f32) * column).astype(bf16)
    for part, out in zip(split(solve_ref[...] * RELAX), (solve_high, solve_low)):
        out[...] = dot(dot(weighted, part).astype(bf16), weighted, NT).astype(bf16)
    for part, out in zip(split(schur_ref[...]), (schur_high, schur_low)):
        out[...] = dot(dot(chooser, part).astype(bf16), flipped).astype(bf16)


def blend_body(columns_ref, other_ref, mix_high, mix_low):
    grp = lax.axis_index("grp")
    away = jnp.concatenate([rows_of(columns_ref, grp ^ 2), other_ref[...]], axis=1)
    kept = jnp.concatenate([rows_of(columns_ref, grp), rows_of(columns_ref, grp ^ 1).T], axis=1)
    mix_high[...], mix_low[...] = split(jnp.concatenate([away, kept], axis=0) * RELAX)


def project_body(subs, count, value_ref, test_high, test_low, *refs):
    halves = split(add_shared(subs, value_ref[...], refs[:count]))
    projected_ref, high_ref, low_ref = refs[count:]
    projected_ref[...] = dot3((test_high[...], test_low[...]), halves)
    high_ref[...], low_ref[...] = halves


def solve_body(high_ref, low_ref, solve_high, solve_low, fine_ref):
    fine_ref[...] = dot3((solve_high[...], solve_low[...]), (high_ref[...], low_ref[...]))


def mix_body(own_ref, other_ref, mix_high, mix_low, away_ref, kept_ref):
    pair = jnp.concatenate([own_ref[...], other_ref[...]], axis=0)
    mixed = dot3((mix_high[...], mix_low[...]), split(pair))
    modes = away_ref.shape[0]
    away_ref[...] = mixed[:modes]
    kept_ref[...] = mixed[modes:]


def correct_body(kept_ref, came_ref, fine_ref, basis_high, basis_low, out_ref, *shared_refs):
    coarse = kept_ref[...] + came_ref[...]
    step = fine_ref[...] + dot3((basis_high[...], basis_low[...]), split(coarse))
    out_ref[...] = step
    put_shared(step, shared_refs)


def product_body(subs, count, first, *refs):
    refs = list(refs)
    step = add_shared(subs, refs.pop(0)[...], [refs.pop(0) for _ in range(count)])
    if not first:
        step = step + refs.pop(0)[...]
    load_ref, schur_high, schur_low, iterate_ref, out_ref = refs[:5]
    iterate_ref[...] = step
    value = load_ref[...] - dot3((schur_high[...], schur_low[...]), split(step))
    out_ref[...] = value
    put_shared(value, refs[5:])


def settle_body(subs, flipped_ref, value_ref, *refs):
    refs[-1][...] = pick(flipped_ref[...], add_shared(subs, value_ref[...], refs[:-1]))


def restore_body(widths, flipped_ref, value_ref, *refs):
    flipped = flipped_ref[...]
    base_ref, out_ref = refs[-2:]
    for ref, (start, width) in zip(refs, cut(widths)):
        out_ref[:, start : start + width] = pick(flipped, ref[...])
    base_ref[...] = pick(flipped, value_ref[...])


def finish_body(subs, widths, flipped_ref, *refs):
    *refs, out_hbm, out_ref, sems = refs
    ready, arrived = refs[: len(widths)], refs[len(widths) :]
    came = jnp.concatenate(
        [ref[...] * jnp.where(here, 1.0, 0.0) for ref, (_, _, _, here) in zip(arrived, sides(subs))], axis=0
    )
    halves = split(came)
    copies = []
    size = out_ref.shape[0] // 4
    for step in range(4):
        rows = slice(step * size, (step + 1) * size)
        for ref, (start, width) in zip(ready, cut(widths)):
            value = ref[rows]
            if ref is ready[-1]:
                chooser = flipped_ref[rows, : came.shape[0]]
                value = value + (dot(chooser, halves[0]) + dot(chooser, halves[1]))
            out_ref[rows, start : start + width] = value
        copy = pltpu.make_async_copy(out_ref.at[rows], out_hbm.at[rows], sems.at[step])
        copy.start()
        copies.append(copy)
    for copy in copies:
        copy.wait()


def swaps(count, stride, odd):
    partner = list(range(count))
    for low in range(count - stride):
        if (low // stride) % 2 == odd:
            partner[low], partner[low + stride] = low + stride, low
    return list(enumerate(partner)) if partner != list(range(count)) else []


def local(load_terms, schur_matrix, local_inverse, coarse_modes, cluster_inverse, row_blocks):
    load = load_terms[0, 0]
    basis = coarse_modes[0, 0]
    columns = cluster_inverse[0]
    blocks = row_blocks[0, 0]
    rows, loads = load.shape
    modes = basis.shape[1]
    shared_rows = blocks.shape[1]
    listed = 4 * shared_rows
    subs = lax.axis_size("sub")
    if lax.axis_size("grp") != GROUPS or sum(WIDTHS) != loads:
        raise ValueError("unexpected sizes")

    up = [(low, (low + 1) % subs) for low in range(subs)]
    down = [(target, source) for source, target in up]
    plans = [(0, swaps(subs, ROW_SUBS, 0)), (2, up), (1, down), (3, swaps(subs, ROW_SUBS, 1))]
    plans = [plan for plan in plans if plan[1]]
    count = len(plans)
    def exchange(parts):
        return [lax.ppermute(parts[place], "sub", pairs) for place, pairs in plans]

    def whole(width, kind=f32):
        return ((rows, width), kind)

    def shared(width):
        return [((shared_rows, width), f32)] * count

    pair_plan = [(0, 1), (1, 0), (2, 3), (3, 2)]
    across_plan = [(0, 2), (1, 3), (2, 0), (3, 1)]

    run = Chain()
    size = rows * loads
    outside = pl.BlockSpec(memory_space=pltpu.HBM)
    one_hot, load_near, *parts = run(
        lambda *refs: listed_body(subs, count, WIDTHS, *refs),
        [((listed, rows), bf16), whole(loads)] + [kind for width in WIDTHS for kind in shared(width)],
        4 * listed * size, 16 * size,
        *[pltpu.with_memory_space_constraint(array, pltpu.HBM) for array in (blocks, load)], ins=[outside] * 2,
        scratch=[pltpu.VMEM(blocks.shape, blocks.dtype), pltpu.SemaphoreType.DMA, pltpu.SemaphoreType.DMA],
    )
    streams = []
    for place in range(len(WIDTHS)):
        streams.append({"arrived": exchange(parts[place * count : (place + 1) * count])})
    chooser, flipped, basis_high, basis_low, test_high, test_low, sent, *ordered = run(
        lambda *refs: order_body(subs, WIDTHS, *refs),
        [whole(rows, bf16)] * 2 + [whole(modes, bf16)] * 2 + [((modes, rows), bf16)] * 2
        + [((modes, modes), f32)] + [whole(width) for width in WIDTHS],
        4 * rows * size, 24 * size, one_hot, load_near, basis, columns,
    )
    other = lax.ppermute(sent, "grp", pair_plan)
    for stream, rows_sorted, width in zip(streams, ordered, WIDTHS):
        stream.update(load=rows_sorted, value=rows_sorted, width=width, iterate=None)

    prepared = {}

    def prepare():
        names = ("schur_high", "schur_low", "solve_high", "solve_low")
        prepared.update(zip(names, run(
            lambda *refs: matrices_body(subs, listed, *refs),
            [whole(rows, bf16)] * 4, 16 * rows**3, 24 * size,
            chooser, flipped, schur_matrix[0, 0], local_inverse[0, 0],
        )))
        prepared["mix"] = run(blend_body, [((2 * modes, 2 * modes), bf16)] * 2, size, size, columns, other)

    def project(stream):
        width = stream["width"]
        stream["projected"], stream["high"], stream["low"] = run(
            lambda *refs: project_body(subs, count, *refs),
            [((modes, width), f32), whole(width, bf16), whole(width, bf16)],
            6 * modes * rows * width, 12 * rows * width,
            stream["value"], test_high, test_low, *stream["arrived"],
        )
        stream["theirs"] = lax.ppermute(stream["projected"], "grp", pair_plan)

    def mix(stream):
        if not prepared:
            prepare()
        width = stream["width"]
        away, stream["kept"] = run(
            mix_body, [((modes, width), f32)] * 2, 24 * modes * modes * width, 4 * rows * width,
            stream["projected"], stream["theirs"], *prepared["mix"],
        )
        stream["came"] = lax.ppermute(away, "grp", across_plan)

    def solve(stream):
        width = stream["width"]
        (stream["fine"],) = run(
            solve_body, [whole(width)], 6 * rows * rows * width, 12 * rows * width,
            stream["high"], stream["low"], prepared["solve_high"], prepared["solve_low"],
        )

    def correct(stream):
        width = stream["width"]
        stream["step"], *parts = run(
            correct_body, [whole(width)] + shared(width), 6 * modes * rows * width, 12 * rows * width,
            stream["kept"], stream["came"], stream["fine"], basis_high, basis_low,
        )
        stream["arrived"] = exchange(parts)

    def product(stream):
        width = stream["width"]
        before = [] if stream["iterate"] is None else [stream["iterate"]]
        stream["iterate"], stream["value"], *parts = run(
            lambda *refs: product_body(subs, count, not before, *refs),
            [whole(width)] * 2 + shared(width), 6 * rows * rows * width, 16 * rows * width,
            stream["step"], *stream["arrived"], *before, stream["load"], prepared["schur_high"], prepared["schur_low"],
        )
        stream["arrived"] = exchange(parts)

    steps = {"project": project, "mix": mix, "solve": solve, "correct": correct, "product": product}
    plan = []
    for place, stream in enumerate(streams):
        for iteration in range(ITERS):
            plan += [(iteration * CYCLE + place * LAG + when, place, name) for name, when in PACE.items()]
    for _, place, name in sorted(plan):
        steps[name](streams[place])

    ready = []
    for stream in streams[:-1]:
        ready += run(
            lambda *refs: settle_body(subs, *refs), [whole(stream["width"])],
            4 * rows * rows * stream["width"], 10 * rows * stream["width"],
            flipped, stream["value"], *stream["arrived"],
        )
    final = streams[-1]
    base, solution_rows = run(
        lambda *refs: restore_body(WIDTHS, *refs), [whole(final["width"]), whole(loads)],
        8 * rows * size, 10 * size, flipped, final["value"], *[stream["iterate"] for stream in streams],
    )
    (residual_rows,) = run(
        lambda *refs: finish_body(subs, WIDTHS, *refs), [whole(loads)], 4 * rows * size, 10 * size,
        flipped, *ready, base, *final["arrived"], places=[outside],
        scratch=[pltpu.VMEM((rows, loads), f32), pltpu.SemaphoreType.DMA((4,))],
    )
    return (solution_rows[None, None], residual_rows[None, None])


def solution(mesh):
    return jax.shard_map(
        local,
        mesh=mesh,
        in_specs=(
            P("sub", "grp", None, None),
            P("sub", "grp", None, None),
            P("sub", "grp", None, None),
            P("sub", "grp", None, None),
            P("sub", None, "grp"),
            P("sub", "grp", None, None),
        ),
        out_specs=(P("sub", "grp", None, None), P("sub", "grp", None, None)),
        check_vma=False,
    )
```

```python
import jax
import jax.numpy as jnp
from jax import lax
from jax.experimental import pallas as pl
from jax.experimental.pallas import tpu as pltpu
from jax.sharding import PartitionSpec as P

ITERS = 2
ROW_SUBS = 4
RELAX = 0.5
WIDTHS = (192, 192)
GROUPS = 4
PACE = {"project": 0, "mix": 4, "solve": 4.5, "correct": 10, "product": 15}
CYCLE = 20
LAG = 0.1

f32 = jnp.float32
bf16 = jnp.bfloat16
NN = (((1,), (0,)), ((), ()))
NT = (((1,), (1,)), ((), ()))


class Chain:
    def __init__(self):
        self.last = None

    def __call__(self, body, outs, flops, moved, *operands, scratch=(), ins=None, places=None):
        count = len(operands)
        specs = [pl.BlockSpec(memory_space=pltpu.VMEM)] * count if ins is None else ins
        extra = []
        if self.last is not None:
            extra = [self.last]
            specs = specs + [pl.BlockSpec(memory_space=pl.ANY)]

        def whole_body(*refs):
            body(*refs[:count], *refs[count + len(extra) :])

        results = pl.pallas_call(
            whole_body,
            out_shape=[jax.ShapeDtypeStruct(shape, kind) for shape, kind in outs],
            in_specs=specs,
            out_specs=[pl.BlockSpec(memory_space=pltpu.VMEM)] * len(outs) if places is None else places,
            scratch_shapes=list(scratch),
            compiler_params=pltpu.CompilerParams(vmem_limit_bytes=24 * 1024 * 1024),
            cost_estimate=pl.CostEstimate(flops=flops, bytes_accessed=moved, transcendentals=0),
        )(*operands, *extra)
        self.last = results[0]
        return results


def dot(left, right, dims=NN):
    return lax.dot_general(left, right, dims, preferred_element_type=f32)


def split(value):
    high = value.astype(bf16)
    return high, (value - high.astype(f32)).astype(bf16)


def dot3(left, right):
    return dot(left[0], right[0]) + (dot(left[0], right[1]) + dot(left[1], right[0]))


def pick(chooser, value):
    high, low = split(value)
    return dot(chooser, high) + dot(chooser, low)


def sides(subs):
    sub = lax.axis_index("sub")
    low_row = (sub // ROW_SUBS) % 2 == 0
    over, under = sub < subs - ROW_SUBS, sub >= ROW_SUBS
    return [
        (low_row, 3, 2, jnp.where(low_row, over, under)),
        (low_row, 0, 0, sub > 0),
        (low_row, 1, 1, sub < subs - 1),
        (low_row, 2, 3, jnp.where(low_row, under, over)),
    ]


LANES = 128


def packed(rows, width):
    return (rows, width) if width % LANES == 0 else (rows * width // LANES, LANES)


def pack(value):
    rows, width = value.shape
    if width % LANES == 0:
        return value
    odd = value[:, width - LANES // 2 :]
    folded = jnp.concatenate([odd[: rows // 2], odd[rows // 2 :]], axis=1)
    whole = [value[:, start : start + LANES] for start in range(0, width - LANES // 2, LANES)]
    return jnp.concatenate(whole + [folded], axis=0)


def unpack(value, width):
    if width % LANES == 0:
        return value
    rows = value.shape[0] * LANES // width
    folded = value[value.shape[0] - rows // 2 :]
    odd = jnp.concatenate([folded[:, : LANES // 2], folded[:, LANES // 2 :]], axis=0)
    whole = [value[start : start + rows] for start in range(0, value.shape[0] - rows // 2, rows)]
    return jnp.concatenate(whole + [odd], axis=1)


def put_shared(value, shared_refs):
    for place, ref in enumerate(shared_refs):
        count = ref.shape[0] * ref.shape[1] // value.shape[1]
        ref[...] = pack(value[place * count : (place + 1) * count])


def came_in(subs, shared_refs, width):
    return [
        unpack(ref[...], width) * jnp.where(here, 1.0, 0.0)
        for ref, (_, _, _, here) in zip(shared_refs, sides(subs))
    ]


def add_shared(subs, value, shared_refs):
    came = jnp.concatenate(came_in(subs, shared_refs, value.shape[1]), axis=0)
    count = came.shape[0]
    return jnp.concatenate([value[:count] + came, value[count:]], axis=0)


def cut(widths):
    starts = [sum(widths[:place]) for place in range(len(widths))]
    return list(zip(starts, widths))


def listed_body(subs, count, widths, blocks_hbm, load_hbm, listed_ref, load_ref, *refs):
    *shared_refs, blocks_ref, load_sem, blocks_sem = refs
    load_copy = pltpu.make_async_copy(load_hbm, load_ref, load_sem)
    blocks_copy = pltpu.make_async_copy(blocks_hbm, blocks_ref, blocks_sem)
    blocks_copy.start()
    load_copy.start()
    blocks_copy.wait()
    blocks = blocks_ref[...]
    placed = jnp.concatenate(
        [jnp.where(test, blocks[a : a + 1], blocks[b : b + 1]) for test, a, b, _ in sides(subs)], axis=0
    )
    upright = placed.astype(f32).T
    column = jnp.concatenate([upright[:, place : place + 1] for place in range(4)], axis=0)
    listed, total = column.shape[0], load_ref.shape[0]
    lane = lax.broadcasted_iota(jnp.int32, (listed, total), 1).astype(f32)
    first = (column == lane).astype(f32).astype(bf16)
    listed_ref[...] = first
    load_copy.wait()
    sent = pick(first[: count * blocks.shape[1]], load_ref[...])
    for place, (start, width) in enumerate(cut(widths)):
        put_shared(sent[:, start : start + width], shared_refs[place * count : (place + 1) * count])


def order_body(subs, widths, listed_ref, load_ref, basis_ref, columns_ref,
               chooser_ref, flipped_ref, basis_high, basis_low, test_high, test_low, sent_ref, *refs):
    listed, total = listed_ref.shape
    first = listed_ref[...].astype(f32)
    unlisted = 1.0 - jnp.sum(first, axis=0, keepdims=True)
    before = (
        lax.broadcasted_iota(jnp.int32, (total, total), 0)
        < lax.broadcasted_iota(jnp.int32, (total, total), 1)
    ).astype(f32).astype(bf16)
    rank = dot(jnp.broadcast_to(unlisted, (8, total)).astype(bf16), before)[:1]
    slot = lax.broadcasted_iota(jnp.int32, (total - listed, total), 0).astype(f32)
    last = jnp.where(rank == slot, unlisted, 0.0)
    chooser = jnp.concatenate([first, last], axis=0)
    flipped_ref[...] = chooser.T.astype(bf16)
    weighted = (chooser * weight_column(subs, listed // 4, total)).astype(bf16)
    chooser = chooser.astype(bf16)
    chooser_ref[...] = chooser
    ordered = pick(chooser, load_ref[...])
    for ref, (start, width) in zip(refs, cut(widths)):
        ref[...] = ordered[:, start : start + width]
    for part, out, turned in zip(split(basis_ref[...]), (basis_high, basis_low), (test_high, test_low)):
        placed = dot(weighted, part)
        out[...] = placed.astype(bf16)
        turned[...] = placed.T.astype(bf16)
    sent_ref[...] = rows_of(columns_ref, 3 - (lax.axis_index("grp") ^ 1))


def weight_column(subs, width, total):
    parts = [jnp.full((width, 1), jnp.where(here, 0.5, 1.0), f32) for _, _, _, here in sides(subs)]
    return jnp.concatenate(parts + [jnp.ones((total - 4 * width, 1), f32)], axis=0)


def rows_of(columns_ref, place):
    modes = columns_ref.shape[1]
    return columns_ref[pl.ds(pl.multiple_of(place * modes, modes), modes), :]


def matrices_body(subs, listed, chooser_ref, flipped_ref, schur_ref, solve_ref,
                  schur_high, schur_low, solve_high, solve_low):
    chooser, flipped = chooser_ref[...], flipped_ref[...]
    column = weight_column(subs, listed // 4, chooser.shape[0])
    weighted = (chooser.astype(f32) * column).astype(bf16)
    for part, out in zip(split(solve_ref[...] * RELAX), (solve_high, solve_low)):
        out[...] = dot(dot(weighted, part).astype(bf16), weighted, NT).astype(bf16)
    for part, out in zip(split(schur_ref[...]), (schur_high, schur_low)):
        out[...] = dot(dot(chooser, part).astype(bf16), flipped).astype(bf16)


def blend_body(columns_ref, other_ref, mix_high, mix_low):
    grp = lax.axis_index("grp")
    away = jnp.concatenate([rows_of(columns_ref, 3 - grp), other_ref[...]], axis=1)
    kept = jnp.concatenate([rows_of(columns_ref, grp), rows_of(columns_ref, grp ^ 1).T], axis=1)
    mix_high[...], mix_low[...] = split(jnp.concatenate([away, kept], axis=0) * RELAX)


def project_body(subs, count, value_ref, test_high, test_low, *refs):
    halves = split(add_shared(subs, value_ref[...], refs[:count]))
    projected_ref, high_ref, low_ref = refs[count:]
    projected_ref[...] = pack(dot3((test_high[...], test_low[...]), halves))
    high_ref[...], low_ref[...] = halves


def solve_body(high_ref, low_ref, solve_high, solve_low, fine_ref):
    fine_ref[...] = dot3((solve_high[...], solve_low[...]), (high_ref[...], low_ref[...]))


def mix_body(own_ref, other_ref, mix_high, mix_low, away_ref, kept_ref):
    modes, width = kept_ref.shape
    pair = jnp.concatenate([unpack(own_ref[...], width), unpack(other_ref[...], width)], axis=0)
    mixed = dot3((mix_high[...], mix_low[...]), split(pair))
    away_ref[...] = pack(mixed[:modes])
    kept_ref[...] = mixed[modes:]


def correct_body(kept_ref, came_ref, fine_ref, basis_high, basis_low, out_ref, *shared_refs):
    coarse = kept_ref[...] + unpack(came_ref[...], kept_ref.shape[1])
    step = fine_ref[...] + dot3((basis_high[...], basis_low[...]), split(coarse))
    out_ref[...] = step
    put_shared(step, shared_refs)


def product_body(subs, count, first, *refs):
    refs = list(refs)
    step = add_shared(subs, refs.pop(0)[...], [refs.pop(0) for _ in range(count)])
    if not first:
        step = step + refs.pop(0)[...]
    load_ref, schur_high, schur_low, iterate_ref, out_ref = refs[:5]
    iterate_ref[...] = step
    value = load_ref[...] - dot3((schur_high[...], schur_low[...]), split(step))
    out_ref[...] = value
    put_shared(value, refs[5:])


def settle_body(subs, flipped_ref, value_ref, *refs):
    refs[-1][...] = pick(flipped_ref[...], add_shared(subs, value_ref[...], refs[:-1]))


def restore_body(widths, flipped_ref, value_ref, *refs):
    flipped = flipped_ref[...]
    base_ref, out_ref = refs[-2:]
    for ref, (start, width) in zip(refs, cut(widths)):
        out_ref[:, start : start + width] = pick(flipped, ref[...])
    base_ref[...] = pick(flipped, value_ref[...])


def finish_body(subs, widths, flipped_ref, *refs):
    *refs, out_hbm, out_ref, sems = refs
    ready, arrived = refs[: len(widths)], refs[len(widths) :]
    came = jnp.concatenate(came_in(subs, arrived, widths[-1]), axis=0)
    halves = split(came)
    copies = []
    size = out_ref.shape[0] // 4
    for step in range(4):
        rows = slice(step * size, (step + 1) * size)
        for ref, (start, width) in zip(ready, cut(widths)):
            value = ref[rows]
            if ref is ready[-1]:
                chooser = flipped_ref[rows, : came.shape[0]]
                value = value + (dot(chooser, halves[0]) + dot(chooser, halves[1]))
            out_ref[rows, start : start + width] = value
        copy = pltpu.make_async_copy(out_ref.at[rows], out_hbm.at[rows], sems.at[step])
        copy.start()
        copies.append(copy)
    for copy in copies:
        copy.wait()


def swaps(count, stride, odd):
    partner = list(range(count))
    for low in range(count - stride):
        if (low // stride) % 2 == odd:
            partner[low], partner[low + stride] = low + stride, low
    return list(enumerate(partner)) if partner != list(range(count)) else []


def local(load_terms, schur_matrix, local_inverse, coarse_modes, cluster_inverse, row_blocks):
    load = load_terms[0, 0]
    basis = coarse_modes[0, 0]
    columns = cluster_inverse[0]
    blocks = row_blocks[0, 0]
    rows, loads = load.shape
    modes = basis.shape[1]
    shared_rows = blocks.shape[1]
    listed = 4 * shared_rows
    subs = lax.axis_size("sub")
    if lax.axis_size("grp") != GROUPS or sum(WIDTHS) != loads:
        raise ValueError("unexpected sizes")

    up = [(low, (low + 1) % subs) for low in range(subs)]
    down = [(target, source) for source, target in up]
    plans = [(0, swaps(subs, ROW_SUBS, 0)), (2, up), (1, down), (3, swaps(subs, ROW_SUBS, 1))]
    plans = [plan for plan in plans if plan[1]]
    count = len(plans)
    def exchange(parts):
        return [lax.ppermute(parts[place], "sub", pairs) for place, pairs in plans]

    def whole(width, kind=f32):
        return ((rows, width), kind)

    def shared(width):
        return [(packed(shared_rows, width), f32)] * count

    pair_plan = [(0, 1), (1, 0), (2, 3), (3, 2)]
    mirror_plan = [(0, 3), (3, 0), (1, 2), (2, 1)]

    run = Chain()
    size = rows * loads
    outside = pl.BlockSpec(memory_space=pltpu.HBM)
    one_hot, load_near, *parts = run(
        lambda *refs: listed_body(subs, count, WIDTHS, *refs),
        [((listed, rows), bf16), whole(loads)] + [kind for width in WIDTHS for kind in shared(width)],
        4 * listed * size, 16 * size,
        *[pltpu.with_memory_space_constraint(array, pltpu.HBM) for array in (blocks, load)], ins=[outside] * 2,
        scratch=[pltpu.VMEM(blocks.shape, blocks.dtype), pltpu.SemaphoreType.DMA, pltpu.SemaphoreType.DMA],
    )
    streams = []
    for place in range(len(WIDTHS)):
        streams.append({"arrived": exchange(parts[place * count : (place + 1) * count])})
    chooser, flipped, basis_high, basis_low, test_high, test_low, sent, *ordered = run(
        lambda *refs: order_body(subs, WIDTHS, *refs),
        [whole(rows, bf16)] * 2 + [whole(modes, bf16)] * 2 + [((modes, rows), bf16)] * 2
        + [((modes, modes), f32)] + [whole(width) for width in WIDTHS],
        4 * rows * size, 24 * size, one_hot, load_near, basis, columns,
    )
    other = lax.ppermute(sent, "grp", pair_plan)
    for stream, rows_sorted, width in zip(streams, ordered, WIDTHS):
        stream.update(load=rows_sorted, value=rows_sorted, width=width, iterate=None)

    prepared = {}

    def prepare():
        names = ("schur_high", "schur_low", "solve_high", "solve_low")
        prepared.update(zip(names, run(
            lambda *refs: matrices_body(subs, listed, *refs),
            [whole(rows, bf16)] * 4, 16 * rows**3, 24 * size,
            chooser, flipped, schur_matrix[0, 0], local_inverse[0, 0],
        )))
        prepared["mix"] = run(blend_body, [((2 * modes, 2 * modes), bf16)] * 2, size, size, columns, other)

    def project(stream):
        width = stream["width"]
        stream["projected"], stream["high"], stream["low"] = run(
            lambda *refs: project_body(subs, count, *refs),
            [(packed(modes, width), f32), whole(width, bf16), whole(width, bf16)],
            6 * modes * rows * width, 12 * rows * width,
            stream["value"], test_high, test_low, *stream["arrived"],
        )
        stream["theirs"] = lax.ppermute(stream["projected"], "grp", pair_plan)

    def mix(stream):
        if not prepared:
            prepare()
        width = stream["width"]
        away, stream["kept"] = run(
            mix_body, [(packed(modes, width), f32), ((modes, width), f32)], 24 * modes * modes * width, 4 * rows * width,
            stream["projected"], stream["theirs"], *prepared["mix"],
        )
        stream["came"] = lax.ppermute(away, "grp", mirror_plan)

    def solve(stream):
        width = stream["width"]
        (stream["fine"],) = run(
            solve_body, [whole(width)], 6 * rows * rows * width, 12 * rows * width,
            stream["high"], stream["low"], prepared["solve_high"], prepared["solve_low"],
        )

    def correct(stream):
        width = stream["width"]
        stream["step"], *parts = run(
            correct_body, [whole(width)] + shared(width), 6 * modes * rows * width, 12 * rows * width,
            stream["kept"], stream["came"], stream["fine"], basis_high, basis_low,
        )
        stream["arrived"] = exchange(parts)

    def product(stream):
        width = stream["width"]
        before = [] if stream["iterate"] is None else [stream["iterate"]]
        stream["iterate"], stream["value"], *parts = run(
            lambda *refs: product_body(subs, count, not before, *refs),
            [whole(width)] * 2 + shared(width), 6 * rows * rows * width, 16 * rows * width,
            stream["step"], *stream["arrived"], *before, stream["load"], prepared["schur_high"], prepared["schur_low"],
        )
        stream["arrived"] = exchange(parts)

    steps = {"project": project, "mix": mix, "solve": solve, "correct": correct, "product": product}
    plan = []
    for place, stream in enumerate(streams):
        for iteration in range(ITERS):
            plan += [(iteration * CYCLE + place * LAG + when, place, name) for name, when in PACE.items()]
    for _, place, name in sorted(plan):
        steps[name](streams[place])

    ready = []
    for stream in streams[:-1]:
        ready += run(
            lambda *refs: settle_body(subs, *refs), [whole(stream["width"])],
            4 * rows * rows * stream["width"], 10 * rows * stream["width"],
            flipped, stream["value"], *stream["arrived"],
        )
    final = streams[-1]
    base, solution_rows = run(
        lambda *refs: restore_body(WIDTHS, *refs), [whole(final["width"]), whole(loads)],
        8 * rows * size, 10 * size, flipped, final["value"], *[stream["iterate"] for stream in streams],
    )
    (residual_rows,) = run(
        lambda *refs: finish_body(subs, WIDTHS, *refs), [whole(loads)], 4 * rows * size, 10 * size,
        flipped, *ready, base, *final["arrived"], places=[outside],
        scratch=[pltpu.VMEM((rows, loads), f32), pltpu.SemaphoreType.DMA((4,))],
    )
    return (solution_rows[None, None], residual_rows[None, None])


def solution(mesh):
    return jax.shard_map(
        local,
        mesh=mesh,
        in_specs=(
            P("sub", "grp", None, None),
            P("sub", "grp", None, None),
            P("sub", "grp", None, None),
            P("sub", "grp", None, None),
            P("sub", None, "grp"),
            P("sub", "grp", None, None),
        ),
        out_specs=(P("sub", "grp", None, None), P("sub", "grp", None, None)),
        check_vma=False,
    )
```

```python
import jax
import jax.numpy as jnp
from jax import lax
from jax.experimental import pallas as pl
from jax.experimental.pallas import tpu as pltpu
from jax.sharding import PartitionSpec as P

ITERS = 2
ROW_SUBS = 4
RELAX = 0.5
WIDTHS = (384,)
GROUPS = 4
PIECE = 128
PACE = {"project": 0, "solve": 1, "mix": 4, "correct": 10, "product": 15}
CYCLE = 20
LAG = 10

f32 = jnp.float32
bf16 = jnp.bfloat16
NN = (((1,), (0,)), ((), ()))
NT = (((1,), (1,)), ((), ()))


class Chain:
    def __init__(self):
        self.last = None

    def __call__(self, body, outs, flops, moved, *operands, scratch=(), ins=None, places=None):
        count = len(operands)
        specs = [pl.BlockSpec(memory_space=pltpu.VMEM)] * count if ins is None else ins
        extra = []
        if self.last is not None:
            extra = [self.last]
            specs = specs + [pl.BlockSpec(memory_space=pl.ANY)]

        def whole_body(*refs):
            body(*refs[:count], *refs[count + len(extra) :])

        results = pl.pallas_call(
            whole_body,
            out_shape=[jax.ShapeDtypeStruct(shape, kind) for shape, kind in outs],
            in_specs=specs,
            out_specs=[pl.BlockSpec(memory_space=pltpu.VMEM)] * len(outs) if places is None else places,
            scratch_shapes=list(scratch),
            compiler_params=pltpu.CompilerParams(vmem_limit_bytes=24 * 1024 * 1024),
            cost_estimate=pl.CostEstimate(flops=flops, bytes_accessed=moved, transcendentals=0),
        )(*operands, *extra)
        self.last = results[0]
        return results


def dot(left, right, dims=NN):
    return lax.dot_general(left, right, dims, preferred_element_type=f32)


def split(value):
    high = value.astype(bf16)
    return high, (value - high.astype(f32)).astype(bf16)


def dot3(left, right):
    return dot(left[0], right[0]) + (dot(left[0], right[1]) + dot(left[1], right[0]))


def pick(chooser, value):
    high, low = split(value)
    return dot(chooser, high) + dot(chooser, low)


def sides(subs):
    sub = lax.axis_index("sub")
    low_row = (sub // ROW_SUBS) % 2 == 0
    over, under = sub < subs - ROW_SUBS, sub >= ROW_SUBS
    return [
        (low_row, 3, 2, jnp.where(low_row, over, under)),
        (low_row, 0, 0, sub > 0),
        (low_row, 1, 1, sub < subs - 1),
        (low_row, 2, 3, jnp.where(low_row, under, over)),
    ]


def put_shared(value, shared_refs):
    for place, ref in enumerate(shared_refs):
        width = ref.shape[0]
        ref[...] = value[place * width : (place + 1) * width]


def add_shared(subs, value, shared_refs):
    width = shared_refs[0].shape[0]
    parts = [
        value[place * width : (place + 1) * width] + ref[...] * jnp.where(here, 1.0, 0.0)
        for place, (ref, (_, _, _, here)) in enumerate(zip(shared_refs, sides(subs)))
    ]
    parts.append(value[len(shared_refs) * width :])
    return jnp.concatenate(parts, axis=0)


def cut(widths):
    starts = [sum(widths[:place]) for place in range(len(widths))]
    return list(zip(starts, widths))


def listed_body(subs, count, widths, blocks_hbm, load_hbm, listed_ref, load_ref, *refs):
    *shared_refs, blocks_ref, load_sem, blocks_sem = refs
    load_copy = pltpu.make_async_copy(load_hbm, load_ref, load_sem)
    blocks_copy = pltpu.make_async_copy(blocks_hbm, blocks_ref, blocks_sem)
    blocks_copy.start()
    load_copy.start()
    blocks_copy.wait()
    blocks = blocks_ref[...]
    placed = jnp.concatenate(
        [jnp.where(test, blocks[a : a + 1], blocks[b : b + 1]) for test, a, b, _ in sides(subs)], axis=0
    )
    upright = placed.astype(f32).T
    column = jnp.concatenate([upright[:, place : place + 1] for place in range(4)], axis=0)
    listed, total = column.shape[0], load_ref.shape[0]
    lane = lax.broadcasted_iota(jnp.int32, (listed, total), 1).astype(f32)
    first = (column == lane).astype(f32).astype(bf16)
    listed_ref[...] = first
    load_copy.wait()
    sent = pick(first[: count * blocks.shape[1]], load_ref[...])
    for place, (start, width) in enumerate(cut(widths)):
        put_shared(sent[:, start : start + width], shared_refs[place * count : (place + 1) * count])


def order_body(subs, widths, listed_ref, load_ref, basis_ref, columns_ref,
               chooser_ref, flipped_ref, basis_high, basis_low, test_high, test_low, sent_ref, *refs):
    listed, total = listed_ref.shape
    first = listed_ref[...].astype(f32)
    unlisted = 1.0 - jnp.sum(first, axis=0, keepdims=True)
    before = (
        lax.broadcasted_iota(jnp.int32, (total, total), 0)
        < lax.broadcasted_iota(jnp.int32, (total, total), 1)
    ).astype(f32).astype(bf16)
    rank = dot(jnp.broadcast_to(unlisted, (8, total)).astype(bf16), before)[:1]
    slot = lax.broadcasted_iota(jnp.int32, (total - listed, total), 0).astype(f32)
    last = jnp.where(rank == slot, unlisted, 0.0)
    chooser = jnp.concatenate([first, last], axis=0)
    flipped_ref[...] = chooser.T.astype(bf16)
    weighted = (chooser * weight_column(subs, listed // 4, total)).astype(bf16)
    chooser = chooser.astype(bf16)
    chooser_ref[...] = chooser
    ordered = pick(chooser, load_ref[...])
    for ref, (start, width) in zip(refs, cut(widths)):
        ref[...] = ordered[:, start : start + width]
    for part, out, turned in zip(split(basis_ref[...]), (basis_high, basis_low), (test_high, test_low)):
        placed = dot(weighted, part)
        out[...] = placed.astype(bf16)
        turned[...] = placed.T.astype(bf16)
    sent_ref[...] = rows_of(columns_ref, 3 - (lax.axis_index("grp") ^ 1))


def weight_column(subs, width, total):
    parts = [jnp.full((width, 1), jnp.where(here, 0.5, 1.0), f32) for _, _, _, here in sides(subs)]
    return jnp.concatenate(parts + [jnp.ones((total - 4 * width, 1), f32)], axis=0)


def rows_of(columns_ref, place):
    modes = columns_ref.shape[1]
    return columns_ref[pl.ds(pl.multiple_of(place * modes, modes), modes), :]


def matrices_body(subs, listed, chooser_ref, flipped_ref, schur_ref, solve_ref,
                  schur_high, schur_low, solve_high, solve_low):
    chooser, flipped = chooser_ref[...], flipped_ref[...]
    column = weight_column(subs, listed // 4, chooser.shape[0])
    weighted = (chooser.astype(f32) * column).astype(bf16)
    for part, out in zip(split(solve_ref[...] * RELAX), (solve_high, solve_low)):
        out[...] = dot(dot(weighted, part).astype(bf16), weighted, NT).astype(bf16)
    for part, out in zip(split(schur_ref[...]), (schur_high, schur_low)):
        out[...] = dot(dot(chooser, part).astype(bf16), flipped).astype(bf16)


def blend_body(columns_ref, other_ref, mix_high, mix_low):
    grp = lax.axis_index("grp")
    away = jnp.concatenate([rows_of(columns_ref, 3 - grp), other_ref[...]], axis=1)
    kept = jnp.concatenate([rows_of(columns_ref, grp), rows_of(columns_ref, grp ^ 1).T], axis=1)
    mix_high[...], mix_low[...] = split(jnp.concatenate([away, kept], axis=0) * RELAX)


def project_body(subs, count, value_ref, test_high, test_low, *refs):
    halves = split(add_shared(subs, value_ref[...], refs[:count]))
    high_ref, low_ref, *piece_refs = refs[count:]
    projected = dot3((test_high[...], test_low[...]), halves)
    for place, ref in enumerate(piece_refs):
        ref[...] = projected[:, place * PIECE : (place + 1) * PIECE]
    high_ref[...], low_ref[...] = halves


def solve_body(high_ref, low_ref, solve_high, solve_low, fine_ref):
    fine_ref[...] = dot3((solve_high[...], solve_low[...]), (high_ref[...], low_ref[...]))


def mix_body(own_ref, other_ref, mix_high, mix_low, away_ref, kept_ref):
    pair = jnp.concatenate([own_ref[...], other_ref[...]], axis=0)
    mixed = dot3((mix_high[...], mix_low[...]), split(pair))
    modes = away_ref.shape[0]
    away_ref[...] = mixed[:modes]
    kept_ref[...] = mixed[modes:]


def correct_body(kept_ref, came_ref, fine_ref, basis_high, basis_low, place, *refs):
    coarse = kept_ref[...] + came_ref[...]
    fine = fine_ref[:, place * PIECE : (place + 1) * PIECE]
    step = fine + dot3((basis_high[...], basis_low[...]), split(coarse))
    formers = place if len(refs) > 1 else 0
    former_refs, out_ref = refs[:formers], refs[formers]
    out_ref[...] = step
    for at, ref in enumerate(refs[formers + 1 :]):
        size = ref.shape[0]
        rows = slice(at * size, (at + 1) * size)
        ref[...] = jnp.concatenate([former[rows] for former in former_refs] + [step[rows]], axis=1)


def product_body(subs, pieces, count, first, *refs):
    refs = list(refs)
    step = jnp.concatenate([refs.pop(0)[...] for _ in range(pieces)], axis=1)
    step = add_shared(subs, step, [refs.pop(0) for _ in range(count)])
    if not first:
        step = step + refs.pop(0)[...]
    load_ref, schur_high, schur_low, iterate_ref, out_ref = refs[:5]
    iterate_ref[...] = step
    value = load_ref[...] - dot3((schur_high[...], schur_low[...]), split(step))
    out_ref[...] = value
    put_shared(value, refs[5:])


def settle_body(subs, flipped_ref, value_ref, *refs):
    refs[-1][...] = pick(flipped_ref[...], add_shared(subs, value_ref[...], refs[:-1]))


def restore_body(widths, flipped_ref, value_ref, *refs):
    flipped = flipped_ref[...]
    base_ref, out_ref = refs[-2:]
    for ref, (start, width) in zip(refs, cut(widths)):
        out_ref[:, start : start + width] = pick(flipped, ref[...])
    base_ref[...] = pick(flipped, value_ref[...])


def finish_body(subs, widths, flipped_ref, *refs):
    *refs, out_hbm, out_ref, sems = refs
    ready, arrived = refs[: len(widths)], refs[len(widths) :]
    came = jnp.concatenate(
        [ref[...] * jnp.where(here, 1.0, 0.0) for ref, (_, _, _, here) in zip(arrived, sides(subs))], axis=0
    )
    halves = split(came)
    copies = []
    size = out_ref.shape[0] // 4
    for step in range(4):
        rows = slice(step * size, (step + 1) * size)
        for ref, (start, width) in zip(ready, cut(widths)):
            value = ref[rows]
            if ref is ready[-1]:
                chooser = flipped_ref[rows, : came.shape[0]]
                value = value + (dot(chooser, halves[0]) + dot(chooser, halves[1]))
            out_ref[rows, start : start + width] = value
        copy = pltpu.make_async_copy(out_ref.at[rows], out_hbm.at[rows], sems.at[step])
        copy.start()
        copies.append(copy)
    for copy in copies:
        copy.wait()


def swaps(count, stride, odd):
    partner = list(range(count))
    for low in range(count - stride):
        if (low // stride) % 2 == odd:
            partner[low], partner[low + stride] = low + stride, low
    return list(enumerate(partner)) if partner != list(range(count)) else []


def local(load_terms, schur_matrix, local_inverse, coarse_modes, cluster_inverse, row_blocks):
    load = load_terms[0, 0]
    basis = coarse_modes[0, 0]
    columns = cluster_inverse[0]
    blocks = row_blocks[0, 0]
    rows, loads = load.shape
    modes = basis.shape[1]
    shared_rows = blocks.shape[1]
    listed = 4 * shared_rows
    subs = lax.axis_size("sub")
    if lax.axis_size("grp") != GROUPS or sum(WIDTHS) != loads:
        raise ValueError("unexpected sizes")

    up = [(low, (low + 1) % subs) for low in range(subs)]
    down = [(target, source) for source, target in up]
    plans = [(0, swaps(subs, ROW_SUBS, 0)), (2, up), (1, down), (3, swaps(subs, ROW_SUBS, 1))]
    plans = [plan for plan in plans if plan[1]]
    count = len(plans)
    def exchange(parts):
        return [lax.ppermute(parts[place], "sub", pairs) for place, pairs in plans]

    def whole(width, kind=f32):
        return ((rows, width), kind)

    def shared(width):
        return [((shared_rows, width), f32)] * count

    pair_plan = [(0, 1), (1, 0), (2, 3), (3, 2)]
    mirror_plan = [(0, 3), (3, 0), (1, 2), (2, 1)]

    run = Chain()
    size = rows * loads
    outside = pl.BlockSpec(memory_space=pltpu.HBM)
    one_hot, load_near, *parts = run(
        lambda *refs: listed_body(subs, count, WIDTHS, *refs),
        [((listed, rows), bf16), whole(loads)] + [kind for width in WIDTHS for kind in shared(width)],
        4 * listed * size, 16 * size,
        *[pltpu.with_memory_space_constraint(array, pltpu.HBM) for array in (blocks, load)], ins=[outside] * 2,
        scratch=[pltpu.VMEM(blocks.shape, blocks.dtype), pltpu.SemaphoreType.DMA, pltpu.SemaphoreType.DMA],
    )
    streams = []
    for place in range(len(WIDTHS)):
        streams.append({"arrived": exchange(parts[place * count : (place + 1) * count])})
    chooser, flipped, basis_high, basis_low, test_high, test_low, sent, *ordered = run(
        lambda *refs: order_body(subs, WIDTHS, *refs),
        [whole(rows, bf16)] * 2 + [whole(modes, bf16)] * 2 + [((modes, rows), bf16)] * 2
        + [((modes, modes), f32)] + [whole(width) for width in WIDTHS],
        4 * rows * size, 24 * size, one_hot, load_near, basis, columns,
    )
    other = lax.ppermute(sent, "grp", pair_plan)
    for stream, rows_sorted, width in zip(streams, ordered, WIDTHS):
        stream.update(load=rows_sorted, value=rows_sorted, width=width, iterate=None)

    prepared = {}

    def prepare():
        names = ("schur_high", "schur_low", "solve_high", "solve_low")
        prepared.update(zip(names, run(
            lambda *refs: matrices_body(subs, listed, *refs),
            [whole(rows, bf16)] * 4, 16 * rows**3, 24 * size,
            chooser, flipped, schur_matrix[0, 0], local_inverse[0, 0],
        )))
        prepared["mix"] = run(blend_body, [((2 * modes, 2 * modes), bf16)] * 2, size, size, columns, other)

    def project(stream):
        width = stream["width"]
        stream["high"], stream["low"], *pieces = run(
            lambda *refs: project_body(subs, count, *refs),
            [whole(width, bf16)] * 2 + [((modes, PIECE), f32)] * (width // PIECE),
            6 * modes * rows * width, 12 * rows * width,
            stream["value"], test_high, test_low, *stream["arrived"],
        )
        stream["pieces"] = [(piece, lax.ppermute(piece, "grp", pair_plan)) for piece in pieces]

    def mix(stream):
        stream["kept"], stream["came"] = [], []
        for piece, theirs in stream["pieces"]:
            away, kept = run(
                mix_body, [((modes, PIECE), f32)] * 2, 24 * modes * modes * PIECE, 4 * rows * PIECE,
                piece, theirs, *prepared["mix"],
            )
            stream["kept"].append(kept)
            stream["came"].append(lax.ppermute(away, "grp", mirror_plan))

    def solve(stream):
        if not prepared:
            prepare()
        width = stream["width"]
        (stream["fine"],) = run(
            solve_body, [whole(width)], 6 * rows * rows * width, 12 * rows * width,
            stream["high"], stream["low"], prepared["solve_high"], prepared["solve_low"],
        )

    def correct(stream):
        width = stream["width"]
        pieces = width // PIECE
        stream["steps"] = []
        for place, (kept, came) in enumerate(zip(stream["kept"], stream["came"])):
            final = place == pieces - 1
            step, *parts = run(
                lambda kept, came, fine, high, low, *refs: correct_body(kept, came, fine, high, low, place, *refs),
                [whole(PIECE)] + (shared(width) if final else []),
                6 * modes * rows * PIECE, 12 * rows * PIECE,
                kept, came, stream["fine"], basis_high, basis_low, *(stream["steps"] if final else []),
            )
            stream["steps"].append(step)
        stream["arrived"] = exchange(parts)

    def product(stream):
        width = stream["width"]
        before = [] if stream["iterate"] is None else [stream["iterate"]]
        stream["iterate"], stream["value"], *parts = run(
            lambda *refs: product_body(subs, width // PIECE, count, not before, *refs),
            [whole(width)] * 2 + shared(width), 6 * rows * rows * width, 16 * rows * width,
            *stream["steps"], *stream["arrived"], *before, stream["load"], prepared["schur_high"], prepared["schur_low"],
        )
        stream["arrived"] = exchange(parts)

    steps = {"project": project, "mix": mix, "solve": solve, "correct": correct, "product": product}
    plan = []
    for place, stream in enumerate(streams):
        for iteration in range(ITERS):
            plan += [(iteration * CYCLE + place * LAG + when, place, name) for name, when in PACE.items()]
    for _, place, name in sorted(plan):
        steps[name](streams[place])

    ready = []
    for stream in streams[:-1]:
        ready += run(
            lambda *refs: settle_body(subs, *refs), [whole(stream["width"])],
            4 * rows * rows * stream["width"], 10 * rows * stream["width"],
            flipped, stream["value"], *stream["arrived"],
        )
    final = streams[-1]
    base, solution_rows = run(
        lambda *refs: restore_body(WIDTHS, *refs), [whole(final["width"]), whole(loads)],
        8 * rows * size, 10 * size, flipped, final["value"], *[stream["iterate"] for stream in streams],
    )
    (residual_rows,) = run(
        lambda *refs: finish_body(subs, WIDTHS, *refs), [whole(loads)], 4 * rows * size, 10 * size,
        flipped, *ready, base, *final["arrived"], places=[outside],
        scratch=[pltpu.VMEM((rows, loads), f32), pltpu.SemaphoreType.DMA((4,))],
    )
    return (solution_rows[None, None], residual_rows[None, None])


def solution(mesh):
    return jax.shard_map(
        local,
        mesh=mesh,
        in_specs=(
            P("sub", "grp", None, None),
            P("sub", "grp", None, None),
            P("sub", "grp", None, None),
            P("sub", "grp", None, None),
            P("sub", None, "grp"),
            P("sub", "grp", None, None),
        ),
        out_specs=(P("sub", "grp", None, None), P("sub", "grp", None, None)),
        check_vma=False,
    )
```

```python
import jax
import jax.numpy as jnp
from jax import lax
from jax.experimental import pallas as pl
from jax.experimental.pallas import tpu as pltpu
from jax.sharding import PartitionSpec as P

ITERS = 2
ROW_SUBS = 4
RELAX = 0.5
GROUPS = 4
PIECE = 128
f32 = jnp.float32
bf16 = jnp.bfloat16
NN = (((1,), (0,)), ((), ()))
NT = (((1,), (1,)), ((), ()))


class Chain:
    def __init__(self):
        self.last = None

    def __call__(self, body, outs, flops, moved, *operands, scratch=(), ins=None, places=None):
        count = len(operands)
        specs = [pl.BlockSpec(memory_space=pltpu.VMEM)] * count if ins is None else ins
        extra = []
        if self.last is not None:
            extra = [self.last]
            specs = specs + [pl.BlockSpec(memory_space=pl.ANY)]

        def whole_body(*refs):
            body(*refs[:count], *refs[count + len(extra) :])

        results = pl.pallas_call(
            whole_body,
            out_shape=[jax.ShapeDtypeStruct(shape, kind) for shape, kind in outs],
            in_specs=specs,
            out_specs=[pl.BlockSpec(memory_space=pltpu.VMEM)] * len(outs) if places is None else places,
            scratch_shapes=list(scratch),
            compiler_params=pltpu.CompilerParams(vmem_limit_bytes=24 * 1024 * 1024),
            cost_estimate=pl.CostEstimate(flops=flops, bytes_accessed=moved, transcendentals=0),
        )(*operands, *extra)
        self.last = results[0]
        return results


def dot(left, right, dims=NN):
    return lax.dot_general(left, right, dims, preferred_element_type=f32)


def split(value):
    high = value.astype(bf16)
    return high, (value - high.astype(f32)).astype(bf16)


def dot3(left, right):
    return dot(left[0], right[0]) + (dot(left[0], right[1]) + dot(left[1], right[0]))


def pick(chooser, value):
    high, low = split(value)
    return dot(chooser, high) + dot(chooser, low)


def sides(subs):
    sub = lax.axis_index("sub")
    low_row = (sub // ROW_SUBS) % 2 == 0
    over, under = sub < subs - ROW_SUBS, sub >= ROW_SUBS
    return [
        (low_row, 3, 2, jnp.where(low_row, over, under)),
        (low_row, 0, 0, sub > 0),
        (low_row, 1, 1, sub < subs - 1),
        (low_row, 2, 3, jnp.where(low_row, under, over)),
    ]


def put_shared(value, shared_refs):
    for place, ref in enumerate(shared_refs):
        width = ref.shape[0]
        ref[...] = value[place * width : (place + 1) * width]


def came_in(subs, shared_refs):
    return jnp.concatenate(
        [ref[...] * jnp.where(here, 1.0, 0.0) for ref, (_, _, _, here) in zip(shared_refs, sides(subs))], axis=0
    )


def add_shared(subs, value, shared_refs):
    came = came_in(subs, shared_refs)
    count = came.shape[0]
    return jnp.concatenate([value[:count] + came, value[count:]], axis=0)


def listed_body(subs, count, blocks_hbm, load_hbm, listed_ref, load_ref, *refs):
    *shared_refs, blocks_ref, load_sem, blocks_sem = refs
    load_copy = pltpu.make_async_copy(load_hbm, load_ref, load_sem)
    blocks_copy = pltpu.make_async_copy(blocks_hbm, blocks_ref, blocks_sem)
    blocks_copy.start()
    load_copy.start()
    blocks_copy.wait()
    blocks = blocks_ref[...]
    placed = jnp.concatenate(
        [jnp.where(test, blocks[a : a + 1], blocks[b : b + 1]) for test, a, b, _ in sides(subs)], axis=0
    )
    upright = placed.astype(f32).T
    column = jnp.concatenate([upright[:, place : place + 1] for place in range(4)], axis=0)
    listed, total = column.shape[0], load_ref.shape[0]
    lane = lax.broadcasted_iota(jnp.int32, (listed, total), 1).astype(f32)
    first = (column == lane).astype(f32).astype(bf16)
    listed_ref[...] = first
    load_copy.wait()
    sent = pick(first[: count * blocks.shape[1]], load_ref[...])
    put_shared(sent, shared_refs)


def order_body(subs, listed_ref, load_ref, basis_ref,
               chooser_ref, flipped_ref, basis_high, basis_low, test_high, test_low, ahead_ref, ordered_ref):
    listed, total = listed_ref.shape
    first = listed_ref[...].astype(f32)
    unlisted = 1.0 - jnp.sum(first, axis=0, keepdims=True)
    before = (
        lax.broadcasted_iota(jnp.int32, (total, total), 0)
        < lax.broadcasted_iota(jnp.int32, (total, total), 1)
    ).astype(f32).astype(bf16)
    rank = dot(jnp.broadcast_to(unlisted, (8, total)).astype(bf16), before)[:1]
    slot = lax.broadcasted_iota(jnp.int32, (total - listed, total), 0).astype(f32)
    last = jnp.where(rank == slot, unlisted, 0.0)
    chooser = jnp.concatenate([first, last], axis=0)
    flipped_ref[...] = chooser.T.astype(bf16)
    weighted = (chooser * weight_column(subs, listed // 4, total)).astype(bf16)
    chooser = chooser.astype(bf16)
    chooser_ref[...] = chooser
    ordered = pick(chooser, load_ref[...])
    ordered_ref[...] = ordered
    for part, out, turned in zip(split(basis_ref[...]), (basis_high, basis_low), (test_high, test_low)):
        placed = dot(weighted, part)
        out[...] = placed.astype(bf16)
        turned[...] = placed.T.astype(bf16)
    ahead_ref[...] = dot3((test_high[...], test_low[...]), split(ordered))


def weight_column(subs, width, total):
    parts = [jnp.full((width, 1), jnp.where(here, 0.5, 1.0), f32) for _, _, _, here in sides(subs)]
    return jnp.concatenate(parts + [jnp.ones((total - 4 * width, 1), f32)], axis=0)


def rows_of(columns_ref, place):
    modes = columns_ref.shape[1]
    return columns_ref[pl.ds(pl.multiple_of(place * modes, modes), modes), :]


def matrices_body(subs, listed, chooser_ref, flipped_ref, schur_ref, solve_ref,
                  schur_high, schur_low, solve_high, solve_low):
    chooser, flipped = chooser_ref[...], flipped_ref[...]
    column = weight_column(subs, listed // 4, chooser.shape[0])
    weighted = (chooser.astype(f32) * column).astype(bf16)
    for part, out in zip(split(solve_ref[...] * RELAX), (solve_high, solve_low)):
        out[...] = dot(dot(weighted, part).astype(bf16), weighted, NT).astype(bf16)
    for part, out in zip(split(schur_ref[...]), (schur_high, schur_low)):
        out[...] = dot(dot(chooser, part).astype(bf16), flipped).astype(bf16)


def blend_body(columns_ref, other_ref, mix_high, mix_low):
    grp = lax.axis_index("grp")
    other = other_ref[columns_ref.shape[1] :]
    away = jnp.concatenate([rows_of(columns_ref, 3 - grp), other], axis=1)
    kept = jnp.concatenate([rows_of(columns_ref, grp), rows_of(columns_ref, grp ^ 1).T], axis=1)
    mix_high[...], mix_low[...] = split(jnp.concatenate([away, kept], axis=0) * RELAX)


def project_body(subs, count, columns, ahead_ref, test_high, test_low, *refs):
    came = came_in(subs, refs[:count])
    size = came.shape[0]
    projected = ahead_ref[...] + dot3((test_high[:, :size], test_low[:, :size]), split(came))
    refs = refs[count:]
    modes = projected.shape[0]
    if columns:
        refs[1][modes:] = rows_of(refs[0], 3 - (lax.axis_index("grp") ^ 1))
        refs = refs[1:]
    for place, ref in enumerate(refs):
        ref[:modes] = projected[:, place * PIECE : (place + 1) * PIECE]


def solve_body(subs, value_ref, solve_high, solve_low, *refs):
    halves = split(add_shared(subs, value_ref[...], refs[:-1]))
    refs[-1][...] = dot3((solve_high[...], solve_low[...]), halves)


def mix_body(own_ref, other_ref, mix_high, mix_low, away_ref, kept_ref):
    modes = away_ref.shape[0]
    pair = jnp.concatenate([own_ref[:modes], other_ref[:modes]], axis=0)
    mixed = dot3((mix_high[...], mix_low[...]), split(pair))
    away_ref[...] = mixed[:modes]
    kept_ref[...] = mixed[modes:]


def correct_body(kept_ref, came_ref, fine_ref, basis_high, basis_low, place, *refs):
    coarse = kept_ref[...] + came_ref[...]
    fine = fine_ref[:, place * PIECE : (place + 1) * PIECE]
    step = fine + dot3((basis_high[...], basis_low[...]), split(coarse))
    formers = place if len(refs) > 1 else 0
    former_refs, out_ref = refs[:formers], refs[formers]
    out_ref[...] = step
    for at, ref in enumerate(refs[formers + 1 :]):
        size = ref.shape[0]
        rows = slice(at * size, (at + 1) * size)
        ref[...] = jnp.concatenate([former[rows] for former in former_refs] + [step[rows]], axis=1)


def ahead_body(pieces, first, *refs):
    total = jnp.concatenate([ref[...] for ref in refs[:pieces]], axis=1)
    refs = refs[pieces:]
    if not first:
        total = refs[0][...] + total
        refs = refs[1:]
    load_ref, schur_high, schur_low, base_ref, total_ref = refs
    total_ref[...] = total
    base_ref[...] = load_ref[...] - dot3((schur_high[...], schur_low[...]), split(total))


def product_body(subs, count, base_ref, schur_high, schur_low, *refs):
    came = came_in(subs, refs[:count])
    size = came.shape[0]
    part = dot3((schur_high[:size, :size], schur_low[:size, :size]), split(came))
    put_shared(base_ref[:size] - part, refs[count:])


def follow_body(subs, count, last, base_ref, total_ref, schur_high, schur_low, *refs):
    arrived, shared, refs = refs[:count], refs[count : 2 * count], refs[2 * count :]
    came = came_in(subs, arrived)
    size = came.shape[0]
    part = dot3((schur_high[size:, :size], schur_low[size:, :size]), split(came))
    value = jnp.concatenate([ref[...] for ref in shared] + [base_ref[size:] - part], axis=0)
    iterate_ref, value_ref = refs[-2:]
    value_ref[...] = value
    iterate_ref[...] = jnp.concatenate([total_ref[:size] + came, total_ref[size:]], axis=0)
    if not last:
        test_high, test_low, projected_ref = refs[:3]
        projected_ref[...] = dot3((test_high[...], test_low[...]), split(value))


def restore_body(flipped_ref, value_ref, iterate_ref, base_ref, out_ref):
    flipped = flipped_ref[...]
    out_ref[...] = pick(flipped, iterate_ref[...])
    base_ref[...] = pick(flipped, value_ref[...])


def finish_body(subs, flipped_ref, base_ref, *refs):
    *arrived, out_hbm, out_ref, sems = refs
    came = came_in(subs, arrived)
    halves = split(came)
    copies = []
    size = out_ref.shape[0] // 4
    for step in range(4):
        rows = slice(step * size, (step + 1) * size)
        chooser = flipped_ref[rows, : came.shape[0]]
        out_ref[rows] = base_ref[rows] + (dot(chooser, halves[0]) + dot(chooser, halves[1]))
        copy = pltpu.make_async_copy(out_ref.at[rows], out_hbm.at[rows], sems.at[step])
        copy.start()
        copies.append(copy)
    for copy in copies:
        copy.wait()


def swaps(count, stride, odd):
    partner = list(range(count))
    for low in range(count - stride):
        if (low // stride) % 2 == odd:
            partner[low], partner[low + stride] = low + stride, low
    return list(enumerate(partner)) if partner != list(range(count)) else []


def local(load_terms, schur_matrix, local_inverse, coarse_modes, cluster_inverse, row_blocks):
    load = load_terms[0, 0]
    basis = coarse_modes[0, 0]
    columns = cluster_inverse[0]
    blocks = row_blocks[0, 0]
    rows, loads = load.shape
    modes = basis.shape[1]
    shared_rows = blocks.shape[1]
    listed = 4 * shared_rows
    subs = lax.axis_size("sub")
    if lax.axis_size("grp") != GROUPS or loads % PIECE:
        raise ValueError("unexpected sizes")

    up = [(low, (low + 1) % subs) for low in range(subs)]
    down = [(target, source) for source, target in up]
    plans = [(0, swaps(subs, ROW_SUBS, 0)), (2, up), (1, down), (3, swaps(subs, ROW_SUBS, 1))]
    plans = [plan for plan in plans if plan[1]]
    count = len(plans)
    def exchange(parts):
        return [lax.ppermute(parts[place], "sub", pairs) for place, pairs in plans]

    def whole(width, kind=f32):
        return ((rows, width), kind)

    pair_plan = [(0, 1), (1, 0), (2, 3), (3, 2)]
    mirror_plan = [(0, 3), (3, 0), (1, 2), (2, 1)]
    shared = [((shared_rows, loads), f32)] * count
    outside = pl.BlockSpec(memory_space=pltpu.HBM)
    pieces = loads // PIECE
    size = rows * loads
    run = Chain()

    one_hot, load_near, *parts = run(
        lambda *refs: listed_body(subs, count, *refs),
        [((listed, rows), bf16), whole(loads)] + shared, 4 * listed * size, 16 * size,
        *[pltpu.with_memory_space_constraint(array, pltpu.HBM) for array in (blocks, load)], ins=[outside] * 2,
        scratch=[pltpu.VMEM(blocks.shape, blocks.dtype), pltpu.SemaphoreType.DMA, pltpu.SemaphoreType.DMA],
    )
    arrived = exchange(parts)
    chooser, flipped, basis_high, basis_low, test_high, test_low, ahead, ordered = run(
        lambda *refs: order_body(subs, *refs),
        [whole(rows, bf16)] * 2 + [whole(modes, bf16)] * 2 + [((modes, rows), bf16)] * 2
        + [((modes, loads), f32), whole(loads)],
        4 * rows * size, 24 * size, one_hot, load_near, basis,
    )
    value, iterate = ordered, None
    for iteration in range(ITERS):
        first, last = iteration == 0, iteration == ITERS - 1
        shapes = [((modes, PIECE), f32)] * pieces
        if first:
            shapes[0] = ((2 * modes, PIECE), f32)
        own = run(
            lambda *refs: project_body(subs, count, first, *refs), shapes, 6 * modes * size, 12 * size,
            ahead, test_high, test_low, *arrived, *([columns] if first else []),
        )
        theirs = [lax.ppermute(piece, "grp", pair_plan) for piece in own]
        if first:
            mixers = run(blend_body, [((2 * modes, 2 * modes), bf16)] * 2, size, size, columns, theirs[0])
        kept, came = [], []
        for place in range(pieces):
            away, keep = run(
                mix_body, [((modes, PIECE), f32)] * 2, 24 * modes * modes * PIECE, 4 * rows * PIECE,
                own[place], theirs[place], *mixers,
            )
            kept.append(keep)
            came.append(lax.ppermute(away, "grp", mirror_plan))
        if first:
            schur_high, schur_low, solve_high, solve_low = run(
                lambda *refs: matrices_body(subs, listed, *refs),
                [whole(rows, bf16)] * 4, 16 * rows**3, 24 * size,
                chooser, flipped, schur_matrix[0, 0], local_inverse[0, 0],
            )
        (fine,) = run(
            lambda *refs: solve_body(subs, *refs), [whole(loads)], 6 * rows * size, 12 * size,
            value, solve_high, solve_low, *arrived,
        )
        steps = []
        for place in range(pieces):
            final = place == pieces - 1
            step, *parts = run(
                lambda kept, came, fine, high, low, *refs: correct_body(kept, came, fine, high, low, place, *refs),
                [whole(PIECE)] + (shared if final else []), 6 * modes * rows * PIECE, 12 * rows * PIECE,
                kept[place], came[place], fine, basis_high, basis_low, *(steps if final else []),
            )
            steps.append(step)
        arrived = exchange(parts)
        base, total = run(
            lambda *refs: ahead_body(pieces, first, *refs), [whole(loads)] * 2, 6 * rows * size, 16 * size,
            *steps, *([] if first else [iterate]), ordered, schur_high, schur_low,
        )
        parts = run(
            lambda *refs: product_body(subs, count, *refs), shared, 2 * rows * size, 12 * size,
            base, schur_high, schur_low, *arrived,
        )
        before, arrived = arrived, exchange(parts)
        *projected, iterate, value = run(
            lambda *refs: follow_body(subs, count, last, *refs),
            ([] if last else [((modes, loads), f32)]) + [whole(loads)] * 2, 3 * rows * size, 16 * size,
            base, total, schur_high, schur_low, *before, *parts, *([] if last else [test_high, test_low]),
        )
        ahead = projected[0] if projected else None
    near, solution_rows = run(
        restore_body, [whole(loads)] * 2, 8 * rows * size, 10 * size, flipped, value, iterate,
    )
    (residual_rows,) = run(
        lambda *refs: finish_body(subs, *refs), [whole(loads)], 4 * rows * size, 10 * size,
        flipped, near, *arrived, places=[outside],
        scratch=[pltpu.VMEM((rows, loads), f32), pltpu.SemaphoreType.DMA((4,))],
    )
    return (solution_rows[None, None], residual_rows[None, None])


def solution(mesh):
    return jax.shard_map(
        local,
        mesh=mesh,
        in_specs=(
            P("sub", "grp", None, None),
            P("sub", "grp", None, None),
            P("sub", "grp", None, None),
            P("sub", "grp", None, None),
            P("sub", None, "grp"),
            P("sub", "grp", None, None),
        ),
        out_specs=(P("sub", "grp", None, None), P("sub", "grp", None, None)),
        check_vma=False,
    )
```

```python
import jax
import jax.numpy as jnp
from jax import lax
from jax.experimental import pallas as pl
from jax.experimental.pallas import tpu as pltpu
from jax.sharding import PartitionSpec as P

ROW_SUBS = 4
RELAX = 0.5
GROUPS = 4
PIECES = ((128, 256), (256, 128))
f32 = jnp.float32
bf16 = jnp.bfloat16
NN = (((1,), (0,)), ((), ()))
NT = (((1,), (1,)), ((), ()))


class Chain:
    def __init__(self):
        self.last = None

    def __call__(self, body, outs, flops, moved, *operands, scratch=(), ins=None, places=None):
        count = len(operands)
        specs = [pl.BlockSpec(memory_space=pltpu.VMEM)] * count if ins is None else ins
        extra = []
        if self.last is not None:
            extra = [self.last]
            specs = specs + [pl.BlockSpec(memory_space=pl.ANY)]

        def whole_body(*refs):
            body(*refs[:count], *refs[count + len(extra) :])

        results = pl.pallas_call(
            whole_body,
            out_shape=[jax.ShapeDtypeStruct(shape, kind) for shape, kind in outs],
            in_specs=specs,
            out_specs=[pl.BlockSpec(memory_space=pltpu.VMEM)] * len(outs) if places is None else places,
            scratch_shapes=list(scratch),
            compiler_params=pltpu.CompilerParams(vmem_limit_bytes=24 * 1024 * 1024),
            cost_estimate=pl.CostEstimate(flops=flops, bytes_accessed=moved, transcendentals=0),
        )(*operands, *extra)
        self.last = results[0]
        return results


def dot(left, right, dims=NN):
    return lax.dot_general(left, right, dims, preferred_element_type=f32)


def split(value):
    high = value.astype(bf16)
    return high, (value - high.astype(f32)).astype(bf16)


def dot3(left, right):
    return dot(left[0], right[0]) + (dot(left[0], right[1]) + dot(left[1], right[0]))


def pick(chooser, value):
    high, low = split(value)
    return dot(chooser, high) + dot(chooser, low)


def sides(subs):
    sub = lax.axis_index("sub")
    low_row = (sub // ROW_SUBS) % 2 == 0
    over, under = sub < subs - ROW_SUBS, sub >= ROW_SUBS
    return [
        (low_row, 3, 2, jnp.where(low_row, over, under)),
        (low_row, 0, 0, sub > 0),
        (low_row, 1, 1, sub < subs - 1),
        (low_row, 2, 3, jnp.where(low_row, under, over)),
    ]


def put_shared(value, shared_refs):
    for place, ref in enumerate(shared_refs):
        width = ref.shape[0]
        ref[...] = value[place * width : (place + 1) * width]


def came_in(subs, shared_refs):
    return jnp.concatenate(
        [ref[...] * jnp.where(here, 1.0, 0.0) for ref, (_, _, _, here) in zip(shared_refs, sides(subs))], axis=0
    )


def add_shared(subs, value, shared_refs):
    came = came_in(subs, shared_refs)
    count = came.shape[0]
    return jnp.concatenate([value[:count] + came, value[count:]], axis=0)


def listed_body(subs, count, blocks_hbm, load_hbm, listed_ref, load_ref, *refs):
    *shared_refs, blocks_ref, load_sem, blocks_sem = refs
    load_copy = pltpu.make_async_copy(load_hbm, load_ref, load_sem)
    blocks_copy = pltpu.make_async_copy(blocks_hbm, blocks_ref, blocks_sem)
    blocks_copy.start()
    load_copy.start()
    blocks_copy.wait()
    blocks = blocks_ref[...]
    placed = jnp.concatenate(
        [jnp.where(test, blocks[a : a + 1], blocks[b : b + 1]) for test, a, b, _ in sides(subs)], axis=0
    )
    upright = placed.astype(f32).T
    column = jnp.concatenate([upright[:, place : place + 1] for place in range(4)], axis=0)
    listed, total = column.shape[0], load_ref.shape[0]
    lane = lax.broadcasted_iota(jnp.int32, (listed, total), 1).astype(f32)
    first = (column == lane).astype(f32).astype(bf16)
    listed_ref[...] = first
    load_copy.wait()
    sent = pick(first[: count * blocks.shape[1]], load_ref[...])
    put_shared(sent, shared_refs)


def order_body(subs, listed_ref, load_ref, basis_ref,
               chooser_ref, flipped_ref, basis_high, basis_low, test_high, test_low, ahead_ref, ordered_ref):
    listed, total = listed_ref.shape
    first = listed_ref[...].astype(f32)
    unlisted = 1.0 - jnp.sum(first, axis=0, keepdims=True)
    before = (
        lax.broadcasted_iota(jnp.int32, (total, total), 0)
        < lax.broadcasted_iota(jnp.int32, (total, total), 1)
    ).astype(f32).astype(bf16)
    rank = dot(jnp.broadcast_to(unlisted, (8, total)).astype(bf16), before)[:1]
    slot = lax.broadcasted_iota(jnp.int32, (total - listed, total), 0).astype(f32)
    last = jnp.where(rank == slot, unlisted, 0.0)
    chooser = jnp.concatenate([first, last], axis=0)
    flipped_ref[...] = chooser.T.astype(bf16)
    weighted = (chooser * weight_column(subs, listed // 4, total)).astype(bf16)
    chooser = chooser.astype(bf16)
    chooser_ref[...] = chooser
    ordered = pick(chooser, load_ref[...])
    ordered_ref[...] = ordered
    for part, out, turned in zip(split(basis_ref[...]), (basis_high, basis_low), (test_high, test_low)):
        placed = dot(weighted, part)
        out[...] = placed.astype(bf16)
        turned[...] = placed.T.astype(bf16)
    ahead_ref[...] = dot3((test_high[...], test_low[...]), split(ordered))


def weight_column(subs, width, total):
    parts = [jnp.full((width, 1), jnp.where(here, 0.5, 1.0), f32) for _, _, _, here in sides(subs)]
    return jnp.concatenate(parts + [jnp.ones((total - 4 * width, 1), f32)], axis=0)


def rows_of(columns_ref, place):
    modes = columns_ref.shape[1]
    return columns_ref[pl.ds(pl.multiple_of(place * modes, modes), modes), :]


def matrices_body(subs, listed, chooser_ref, flipped_ref, schur_ref, solve_ref,
                  schur_high, schur_low, solve_high, solve_low):
    chooser, flipped = chooser_ref[...], flipped_ref[...]
    column = weight_column(subs, listed // 4, chooser.shape[0])
    weighted = (chooser.astype(f32) * column).astype(bf16)
    for part, out in zip(split(solve_ref[...] * RELAX), (solve_high, solve_low)):
        out[...] = dot(dot(weighted, part).astype(bf16), weighted, NT).astype(bf16)
    for part, out in zip(split(schur_ref[...]), (schur_high, schur_low)):
        out[...] = dot(dot(chooser, part).astype(bf16), flipped).astype(bf16)


def blend_body(columns_ref, other_ref, mix_high, mix_low):
    grp = lax.axis_index("grp")
    modes = columns_ref.shape[1]
    other = other_ref[modes:, :modes]
    away = jnp.concatenate([rows_of(columns_ref, 3 - grp), other], axis=1)
    kept = jnp.concatenate([rows_of(columns_ref, grp), rows_of(columns_ref, grp ^ 1).T], axis=1)
    mix_high[...], mix_low[...] = split(jnp.concatenate([away, kept], axis=0) * RELAX)


def cut(widths):
    return [(sum(widths[:place]), width) for place, width in enumerate(widths)]


def project_body(subs, count, widths, columns, ahead_ref, test_high, test_low, *refs):
    came = came_in(subs, refs[:count])
    size = came.shape[0]
    projected = ahead_ref[...] + dot3((test_high[:, :size], test_low[:, :size]), split(came))
    refs = refs[count:]
    modes = projected.shape[0]
    if columns:
        refs[1][modes:, :modes] = rows_of(refs[0], 3 - (lax.axis_index("grp") ^ 1))
        refs = refs[1:]
    for ref, (start, width) in zip(refs, cut(widths)):
        ref[:modes] = projected[:, start : start + width]


def solve_body(subs, value_ref, solve_high, solve_low, *refs):
    halves = split(add_shared(subs, value_ref[...], refs[:-1]))
    refs[-1][...] = dot3((solve_high[...], solve_low[...]), halves)


def mix_body(own_ref, other_ref, mix_high, mix_low, away_ref, kept_ref):
    modes = away_ref.shape[0]
    pair = jnp.concatenate([own_ref[:modes], other_ref[:modes]], axis=0)
    mixed = dot3((mix_high[...], mix_low[...]), split(pair))
    away_ref[...] = mixed[:modes]
    kept_ref[...] = mixed[modes:]


def correct_body(kept_ref, came_ref, fine_ref, basis_high, basis_low, widths, place, *refs):
    coarse = kept_ref[...] + came_ref[...]
    start, width = cut(widths)[place]
    fine = fine_ref[:, start : start + width]
    step = fine + dot3((basis_high[...], basis_low[...]), split(coarse))
    formers = place if len(refs) > 1 else 0
    former_refs, out_ref = refs[:formers], refs[formers]
    out_ref[...] = step
    for at, ref in enumerate(refs[formers + 1 :]):
        size = ref.shape[0]
        rows = slice(at * size, (at + 1) * size)
        ref[...] = jnp.concatenate([former[rows] for former in former_refs] + [step[rows]], axis=1)


def ahead_body(pieces, first, *refs):
    total = jnp.concatenate([ref[...] for ref in refs[:pieces]], axis=1)
    refs = refs[pieces:]
    if not first:
        total = refs[0][...] + total
        refs = refs[1:]
    load_ref, schur_high, schur_low, base_ref, total_ref = refs
    total_ref[...] = total
    base_ref[...] = load_ref[...] - dot3((schur_high[...], schur_low[...]), split(total))


def product_body(subs, count, base_ref, schur_high, schur_low, *refs):
    came = came_in(subs, refs[:count])
    size = came.shape[0]
    part = dot3((schur_high[:size, :size], schur_low[:size, :size]), split(came))
    put_shared(base_ref[:size] - part, refs[count:])


def follow_body(subs, count, last, base_ref, total_ref, schur_high, schur_low, *refs):
    arrived, shared, refs = refs[:count], refs[count : 2 * count], refs[2 * count :]
    came = came_in(subs, arrived)
    size = came.shape[0]
    part = dot3((schur_high[size:, :size], schur_low[size:, :size]), split(came))
    value = jnp.concatenate([ref[...] for ref in shared] + [base_ref[size:] - part], axis=0)
    iterate_ref, value_ref = refs[-2:]
    value_ref[...] = value
    iterate_ref[...] = jnp.concatenate([total_ref[:size] + came, total_ref[size:]], axis=0)
    if not last:
        test_high, test_low, projected_ref = refs[:3]
        projected_ref[...] = dot3((test_high[...], test_low[...]), split(value))


def restore_body(flipped_ref, value_ref, iterate_ref, base_ref, out_ref):
    flipped = flipped_ref[...]
    out_ref[...] = pick(flipped, iterate_ref[...])
    base_ref[...] = pick(flipped, value_ref[...])


def finish_body(subs, flipped_ref, base_ref, *refs):
    *arrived, out_hbm, out_ref, sems = refs
    came = came_in(subs, arrived)
    halves = split(came)
    copies = []
    size = out_ref.shape[0] // 4
    for step in range(4):
        rows = slice(step * size, (step + 1) * size)
        chooser = flipped_ref[rows, : came.shape[0]]
        out_ref[rows] = base_ref[rows] + (dot(chooser, halves[0]) + dot(chooser, halves[1]))
        copy = pltpu.make_async_copy(out_ref.at[rows], out_hbm.at[rows], sems.at[step])
        copy.start()
        copies.append(copy)
    for copy in copies:
        copy.wait()


def swaps(count, stride, odd):
    partner = list(range(count))
    for low in range(count - stride):
        if (low // stride) % 2 == odd:
            partner[low], partner[low + stride] = low + stride, low
    return list(enumerate(partner)) if partner != list(range(count)) else []


def local(load_terms, schur_matrix, local_inverse, coarse_modes, cluster_inverse, row_blocks):
    load = load_terms[0, 0]
    basis = coarse_modes[0, 0]
    columns = cluster_inverse[0]
    blocks = row_blocks[0, 0]
    rows, loads = load.shape
    modes = basis.shape[1]
    shared_rows = blocks.shape[1]
    listed = 4 * shared_rows
    subs = lax.axis_size("sub")
    if lax.axis_size("grp") != GROUPS or any(sum(widths) != loads for widths in PIECES):
        raise ValueError("unexpected sizes")

    up = [(low, (low + 1) % subs) for low in range(subs)]
    down = [(target, source) for source, target in up]
    plans = [(0, swaps(subs, ROW_SUBS, 0)), (2, up), (1, down), (3, swaps(subs, ROW_SUBS, 1))]
    plans = [plan for plan in plans if plan[1]]
    count = len(plans)
    def exchange(parts):
        return [lax.ppermute(parts[place], "sub", pairs) for place, pairs in plans]

    def whole(width, kind=f32):
        return ((rows, width), kind)

    pair_plan = [(0, 1), (1, 0), (2, 3), (3, 2)]
    mirror_plan = [(0, 3), (3, 0), (1, 2), (2, 1)]
    shared = [((shared_rows, loads), f32)] * count
    outside = pl.BlockSpec(memory_space=pltpu.HBM)
    size = rows * loads
    run = Chain()

    one_hot, load_near, *parts = run(
        lambda *refs: listed_body(subs, count, *refs),
        [((listed, rows), bf16), whole(loads)] + shared, 4 * listed * size, 16 * size,
        *[pltpu.with_memory_space_constraint(array, pltpu.HBM) for array in (blocks, load)], ins=[outside] * 2,
        scratch=[pltpu.VMEM(blocks.shape, blocks.dtype), pltpu.SemaphoreType.DMA, pltpu.SemaphoreType.DMA],
    )
    arrived = exchange(parts)
    chooser, flipped, basis_high, basis_low, test_high, test_low, ahead, ordered = run(
        lambda *refs: order_body(subs, *refs),
        [whole(rows, bf16)] * 2 + [whole(modes, bf16)] * 2 + [((modes, rows), bf16)] * 2
        + [((modes, loads), f32), whole(loads)],
        4 * rows * size, 24 * size, one_hot, load_near, basis,
    )
    value, iterate = ordered, None
    for iteration, widths in enumerate(PIECES):
        first, last, pieces = iteration == 0, iteration == len(PIECES) - 1, len(widths)
        shapes = [((modes, width), f32) for width in widths]
        if first:
            shapes[0] = ((2 * modes, widths[0]), f32)
        own = run(
            lambda *refs: project_body(subs, count, widths, first, *refs), shapes, 6 * modes * size, 12 * size,
            ahead, test_high, test_low, *arrived, *([columns] if first else []),
        )
        theirs = [lax.ppermute(piece, "grp", pair_plan) for piece in own]
        if first:
            mixers = run(blend_body, [((2 * modes, 2 * modes), bf16)] * 2, size, size, columns, theirs[0])
        kept, came = [], []
        for place, width in enumerate(widths):
            away, keep = run(
                mix_body, [((modes, width), f32)] * 2, 24 * modes * modes * width, 4 * rows * width,
                own[place], theirs[place], *mixers,
            )
            kept.append(keep)
            came.append(lax.ppermute(away, "grp", mirror_plan))
        if first:
            schur_high, schur_low, solve_high, solve_low = run(
                lambda *refs: matrices_body(subs, listed, *refs),
                [whole(rows, bf16)] * 4, 16 * rows**3, 24 * size,
                chooser, flipped, schur_matrix[0, 0], local_inverse[0, 0],
            )
        (fine,) = run(
            lambda *refs: solve_body(subs, *refs), [whole(loads)], 6 * rows * size, 12 * size,
            value, solve_high, solve_low, *arrived,
        )
        steps = []
        for place, width in enumerate(widths):
            final = place == pieces - 1
            step, *parts = run(
                lambda kept, came, fine, high, low, *refs: correct_body(kept, came, fine, high, low, widths, place, *refs),
                [whole(width)] + (shared if final else []), 6 * modes * rows * width, 12 * rows * width,
                kept[place], came[place], fine, basis_high, basis_low, *(steps if final else []),
            )
            steps.append(step)
        arrived = exchange(parts)
        base, total = run(
            lambda *refs: ahead_body(pieces, first, *refs), [whole(loads)] * 2, 6 * rows * size, 16 * size,
            *steps, *([] if first else [iterate]), ordered, schur_high, schur_low,
        )
        parts = run(
            lambda *refs: product_body(subs, count, *refs), shared, 2 * rows * size, 12 * size,
            base, schur_high, schur_low, *arrived,
        )
        before, arrived = arrived, exchange(parts)
        *projected, iterate, value = run(
            lambda *refs: follow_body(subs, count, last, *refs),
            ([] if last else [((modes, loads), f32)]) + [whole(loads)] * 2, 3 * rows * size, 16 * size,
            base, total, schur_high, schur_low, *before, *parts, *([] if last else [test_high, test_low]),
        )
        ahead = projected[0] if projected else None
    near, solution_rows = run(
        restore_body, [whole(loads)] * 2, 8 * rows * size, 10 * size, flipped, value, iterate,
    )
    (residual_rows,) = run(
        lambda *refs: finish_body(subs, *refs), [whole(loads)], 4 * rows * size, 10 * size,
        flipped, near, *arrived, places=[outside],
        scratch=[pltpu.VMEM((rows, loads), f32), pltpu.SemaphoreType.DMA((4,))],
    )
    return (solution_rows[None, None], residual_rows[None, None])


def solution(mesh):
    return jax.shard_map(
        local,
        mesh=mesh,
        in_specs=(
            P("sub", "grp", None, None),
            P("sub", "grp", None, None),
            P("sub", "grp", None, None),
            P("sub", "grp", None, None),
            P("sub", None, "grp"),
            P("sub", "grp", None, None),
        ),
        out_specs=(P("sub", "grp", None, None), P("sub", "grp", None, None)),
        check_vma=False,
    )
```

```python
import jax
import jax.numpy as jnp
from jax import lax
from jax.experimental import pallas as pl
from jax.experimental.pallas import tpu as pltpu
from jax.sharding import PartitionSpec as P

ITERS = 2
ROW_SUBS = 4
RELAX = 0.5
GROUPS = 4
PIECE = 128
f32 = jnp.float32
bf16 = jnp.bfloat16
NN = (((1,), (0,)), ((), ()))
NT = (((1,), (1,)), ((), ()))


class Chain:
    def __init__(self):
        self.last = None

    def __call__(self, body, outs, flops, moved, *operands, scratch=(), ins=None, places=None):
        count = len(operands)
        specs = [pl.BlockSpec(memory_space=pltpu.VMEM)] * count if ins is None else ins
        extra = []
        if self.last is not None:
            extra = [self.last]
            specs = specs + [pl.BlockSpec(memory_space=pl.ANY)]

        def whole_body(*refs):
            body(*refs[:count], *refs[count + len(extra) :])

        results = pl.pallas_call(
            whole_body,
            out_shape=[jax.ShapeDtypeStruct(shape, kind) for shape, kind in outs],
            in_specs=specs,
            out_specs=[pl.BlockSpec(memory_space=pltpu.VMEM)] * len(outs) if places is None else places,
            scratch_shapes=list(scratch),
            compiler_params=pltpu.CompilerParams(vmem_limit_bytes=24 * 1024 * 1024),
            cost_estimate=pl.CostEstimate(flops=flops, bytes_accessed=moved, transcendentals=0),
        )(*operands, *extra)
        self.last = results[0]
        return results


def dot(left, right, dims=NN):
    return lax.dot_general(left, right, dims, preferred_element_type=f32)


def split(value):
    high = value.astype(bf16)
    return high, (value - high.astype(f32)).astype(bf16)


def dot3(left, right):
    return dot(left[0], right[0]) + (dot(left[0], right[1]) + dot(left[1], right[0]))


def pick(chooser, value):
    high, low = split(value)
    return dot(chooser, high) + dot(chooser, low)


def sides(subs):
    sub = lax.axis_index("sub")
    low_row = (sub // ROW_SUBS) % 2 == 0
    over, under = sub < subs - ROW_SUBS, sub >= ROW_SUBS
    return [
        (low_row, 3, 2, jnp.where(low_row, over, under)),
        (low_row, 0, 0, sub > 0),
        (low_row, 1, 1, sub < subs - 1),
        (low_row, 2, 3, jnp.where(low_row, under, over)),
    ]


def put_shared(value, shared_refs):
    for place, ref in enumerate(shared_refs):
        width = ref.shape[0]
        ref[...] = value[place * width : (place + 1) * width]


def came_in(subs, shared_refs):
    return jnp.concatenate(
        [ref[...] * jnp.where(here, 1.0, 0.0) for ref, (_, _, _, here) in zip(shared_refs, sides(subs))], axis=0
    )


def add_shared(subs, value, shared_refs):
    came = came_in(subs, shared_refs)
    count = came.shape[0]
    return jnp.concatenate([value[:count] + came, value[count:]], axis=0)


def listed_body(subs, count, blocks_hbm, load_hbm, columns_hbm, listed_ref, load_ref, sent_ref, *refs):
    *shared_refs, blocks_ref, load_sem, blocks_sem, sent_sem = refs
    modes = sent_ref.shape[0]
    wanted = pl.multiple_of((3 - (lax.axis_index("grp") ^ 1)) * modes, modes)
    sent_copy = pltpu.make_async_copy(columns_hbm.at[pl.ds(wanted, modes), :], sent_ref, sent_sem)
    load_copy = pltpu.make_async_copy(load_hbm, load_ref, load_sem)
    blocks_copy = pltpu.make_async_copy(blocks_hbm, blocks_ref, blocks_sem)
    blocks_copy.start()
    load_copy.start()
    sent_copy.start()
    blocks_copy.wait()
    blocks = blocks_ref[...]
    placed = jnp.concatenate(
        [jnp.where(test, blocks[a : a + 1], blocks[b : b + 1]) for test, a, b, _ in sides(subs)], axis=0
    )
    upright = placed.astype(f32).T
    column = jnp.concatenate([upright[:, place : place + 1] for place in range(4)], axis=0)
    listed, total = column.shape[0], load_ref.shape[0]
    lane = lax.broadcasted_iota(jnp.int32, (listed, total), 1).astype(f32)
    first = (column == lane).astype(f32).astype(bf16)
    listed_ref[...] = first
    load_copy.wait()
    sent_copy.wait()
    sent = pick(first[: count * blocks.shape[1]], load_ref[...])
    put_shared(sent, shared_refs)


def order_body(subs, listed_ref, load_ref, basis_ref,
               chooser_ref, flipped_ref, basis_high, basis_low, test_high, test_low, ahead_ref, ordered_ref):
    listed, total = listed_ref.shape
    first = listed_ref[...].astype(f32)
    unlisted = 1.0 - jnp.sum(first, axis=0, keepdims=True)
    before = (
        lax.broadcasted_iota(jnp.int32, (total, total), 0)
        < lax.broadcasted_iota(jnp.int32, (total, total), 1)
    ).astype(f32).astype(bf16)
    rank = dot(jnp.broadcast_to(unlisted, (8, total)).astype(bf16), before)[:1]
    slot = lax.broadcasted_iota(jnp.int32, (total - listed, total), 0).astype(f32)
    last = jnp.where(rank == slot, unlisted, 0.0)
    chooser = jnp.concatenate([first, last], axis=0)
    flipped_ref[...] = chooser.T.astype(bf16)
    weighted = (chooser * weight_column(subs, listed // 4, total)).astype(bf16)
    chooser = chooser.astype(bf16)
    chooser_ref[...] = chooser
    ordered = pick(chooser, load_ref[...])
    ordered_ref[...] = ordered
    for part, out, turned in zip(split(basis_ref[...]), (basis_high, basis_low), (test_high, test_low)):
        placed = dot(weighted, part)
        out[...] = placed.astype(bf16)
        turned[...] = placed.T.astype(bf16)
    ahead_ref[...] = dot3((test_high[...], test_low[...]), split(ordered))


def weight_column(subs, width, total):
    parts = [jnp.full((width, 1), jnp.where(here, 0.5, 1.0), f32) for _, _, _, here in sides(subs)]
    return jnp.concatenate(parts + [jnp.ones((total - 4 * width, 1), f32)], axis=0)


def rows_of(columns_ref, place):
    modes = columns_ref.shape[1]
    return columns_ref[pl.ds(pl.multiple_of(place * modes, modes), modes), :]


def solver_body(subs, listed, chooser_ref, solve_ref, solve_high, solve_low):
    chooser = chooser_ref[...]
    weighted = (chooser.astype(f32) * weight_column(subs, listed // 4, chooser.shape[0])).astype(bf16)
    for part, out in zip(split(solve_ref[...] * RELAX), (solve_high, solve_low)):
        out[...] = dot(dot(weighted, part).astype(bf16), weighted, NT).astype(bf16)


def schur_body(chooser_ref, flipped_ref, schur_ref, schur_high, schur_low):
    chooser, flipped = chooser_ref[...], flipped_ref[...]
    for part, out in zip(split(schur_ref[...]), (schur_high, schur_low)):
        out[...] = dot(dot(chooser, part).astype(bf16), flipped).astype(bf16)


def blend_body(columns_ref, other_ref, mix_high, mix_low):
    grp = lax.axis_index("grp")
    away = jnp.concatenate([rows_of(columns_ref, 3 - grp), other_ref[...]], axis=1)
    kept = jnp.concatenate([rows_of(columns_ref, grp), rows_of(columns_ref, grp ^ 1).T], axis=1)
    mix_high[...], mix_low[...] = split(jnp.concatenate([away, kept], axis=0) * RELAX)


def project_body(subs, count, ahead_ref, test_high, test_low, *refs):
    came = came_in(subs, refs[:count])
    size = came.shape[0]
    projected = ahead_ref[...] + dot3((test_high[:, :size], test_low[:, :size]), split(came))
    for place, ref in enumerate(refs[count:]):
        ref[...] = projected[:, place * PIECE : (place + 1) * PIECE]


def solve_body(subs, value_ref, solve_high, solve_low, *refs):
    halves = split(add_shared(subs, value_ref[...], refs[:-1]))
    refs[-1][...] = dot3((solve_high[...], solve_low[...]), halves)


def mix_body(own_ref, other_ref, mix_high, mix_low, away_ref, kept_ref):
    modes = away_ref.shape[0]
    pair = jnp.concatenate([own_ref[...], other_ref[...]], axis=0)
    mixed = dot3((mix_high[...], mix_low[...]), split(pair))
    away_ref[...] = mixed[:modes]
    kept_ref[...] = mixed[modes:]


def correct_body(kept_ref, came_ref, fine_ref, basis_high, basis_low, place, *refs):
    coarse = kept_ref[...] + came_ref[...]
    fine = fine_ref[:, place * PIECE : (place + 1) * PIECE]
    step = fine + dot3((basis_high[...], basis_low[...]), split(coarse))
    formers = place if len(refs) > 1 else 0
    former_refs, out_ref = refs[:formers], refs[formers]
    out_ref[...] = step
    for at, ref in enumerate(refs[formers + 1 :]):
        size = ref.shape[0]
        rows = slice(at * size, (at + 1) * size)
        ref[...] = jnp.concatenate([former[rows] for former in former_refs] + [step[rows]], axis=1)


def ahead_body(pieces, first, *refs):
    total = jnp.concatenate([ref[...] for ref in refs[:pieces]], axis=1)
    refs = refs[pieces:]
    if not first:
        total = refs[0][...] + total
        refs = refs[1:]
    load_ref, schur_high, schur_low, base_ref, total_ref = refs
    total_ref[...] = total
    base_ref[...] = load_ref[...] - dot3((schur_high[...], schur_low[...]), split(total))


def product_body(subs, count, base_ref, schur_high, schur_low, *refs):
    came = came_in(subs, refs[:count])
    size = came.shape[0]
    part = dot3((schur_high[:size, :size], schur_low[:size, :size]), split(came))
    put_shared(base_ref[:size] - part, refs[count:])


def follow_body(subs, count, last, base_ref, total_ref, schur_high, schur_low, *refs):
    arrived, shared, refs = refs[:count], refs[count : 2 * count], refs[2 * count :]
    came = came_in(subs, arrived)
    size = came.shape[0]
    part = dot3((schur_high[size:, :size], schur_low[size:, :size]), split(came))
    value = jnp.concatenate([ref[...] for ref in shared] + [base_ref[size:] - part], axis=0)
    iterate_ref, value_ref = refs[-2:]
    value_ref[...] = value
    iterate_ref[...] = jnp.concatenate([total_ref[:size] + came, total_ref[size:]], axis=0)
    if not last:
        test_high, test_low, projected_ref = refs[:3]
        projected_ref[...] = dot3((test_high[...], test_low[...]), split(value))


def restore_body(flipped_ref, value_ref, iterate_ref, base_ref, out_ref):
    flipped = flipped_ref[...]
    out_ref[...] = pick(flipped, iterate_ref[...])
    base_ref[...] = pick(flipped, value_ref[...])


def finish_body(subs, flipped_ref, base_ref, *refs):
    *arrived, out_hbm, out_ref, sems = refs
    came = came_in(subs, arrived)
    halves = split(came)
    copies = []
    size = out_ref.shape[0] // 4
    for step in range(4):
        rows = slice(step * size, (step + 1) * size)
        chooser = flipped_ref[rows, : came.shape[0]]
        out_ref[rows] = base_ref[rows] + (dot(chooser, halves[0]) + dot(chooser, halves[1]))
        copy = pltpu.make_async_copy(out_ref.at[rows], out_hbm.at[rows], sems.at[step])
        copy.start()
        copies.append(copy)
    for copy in copies:
        copy.wait()


def swaps(count, stride, odd):
    partner = list(range(count))
    for low in range(count - stride):
        if (low // stride) % 2 == odd:
            partner[low], partner[low + stride] = low + stride, low
    return list(enumerate(partner)) if partner != list(range(count)) else []


def local(load_terms, schur_matrix, local_inverse, coarse_modes, cluster_inverse, row_blocks):
    load = load_terms[0, 0]
    basis = coarse_modes[0, 0]
    columns = cluster_inverse[0]
    blocks = row_blocks[0, 0]
    rows, loads = load.shape
    modes = basis.shape[1]
    shared_rows = blocks.shape[1]
    listed = 4 * shared_rows
    subs = lax.axis_size("sub")
    if lax.axis_size("grp") != GROUPS or loads % PIECE:
        raise ValueError("unexpected sizes")

    up = [(low, (low + 1) % subs) for low in range(subs)]
    down = [(target, source) for source, target in up]
    plans = [(0, swaps(subs, ROW_SUBS, 0)), (2, up), (1, down), (3, swaps(subs, ROW_SUBS, 1))]
    plans = [plan for plan in plans if plan[1]]
    count = len(plans)
    def exchange(parts):
        return [lax.ppermute(parts[place], "sub", pairs) for place, pairs in plans]

    def whole(width, kind=f32):
        return ((rows, width), kind)

    pair_plan = [(0, 1), (1, 0), (2, 3), (3, 2)]
    mirror_plan = [(0, 3), (3, 0), (1, 2), (2, 1)]
    shared = [((shared_rows, loads), f32)] * count
    outside = pl.BlockSpec(memory_space=pltpu.HBM)
    pieces = loads // PIECE
    size = rows * loads
    run = Chain()

    one_hot, load_near, sent, *parts = run(
        lambda *refs: listed_body(subs, count, *refs),
        [((listed, rows), bf16), whole(loads), ((modes, modes), f32)] + shared, 4 * listed * size, 16 * size,
        *[pltpu.with_memory_space_constraint(array, pltpu.HBM) for array in (blocks, load, columns)], ins=[outside] * 3,
        scratch=[pltpu.VMEM(blocks.shape, blocks.dtype)] + [pltpu.SemaphoreType.DMA] * 3,
    )
    arrived = exchange(parts)
    other = lax.ppermute(sent, "grp", pair_plan)
    chooser, flipped, basis_high, basis_low, test_high, test_low, ahead, ordered = run(
        lambda *refs: order_body(subs, *refs),
        [whole(rows, bf16)] * 2 + [whole(modes, bf16)] * 2 + [((modes, rows), bf16)] * 2
        + [((modes, loads), f32), whole(loads)],
        4 * rows * size, 24 * size, one_hot, load_near, basis,
    )
    mixers = run(blend_body, [((2 * modes, 2 * modes), bf16)] * 2, size, size, columns, other)
    value, iterate = ordered, None
    for iteration in range(ITERS):
        first, last = iteration == 0, iteration == ITERS - 1
        shapes = [((modes, PIECE), f32)] * pieces
        own = run(
            lambda *refs: project_body(subs, count, *refs), shapes, 6 * modes * size, 12 * size,
            ahead, test_high, test_low, *arrived,
        )
        theirs = [lax.ppermute(piece, "grp", pair_plan) for piece in own]
        kept, came = [], []
        for place in range(pieces):
            away, keep = run(
                mix_body, [((modes, PIECE), f32)] * 2, 24 * modes * modes * PIECE, 4 * rows * PIECE,
                own[place], theirs[place], *mixers,
            )
            kept.append(keep)
            came.append(lax.ppermute(away, "grp", mirror_plan))
        if first:
            solve_high, solve_low = run(
                lambda *refs: solver_body(subs, listed, *refs), [whole(rows, bf16)] * 2, 8 * rows**3, 12 * size,
                chooser, local_inverse[0, 0],
            )
        (fine,) = run(
            lambda *refs: solve_body(subs, *refs), [whole(loads)], 6 * rows * size, 12 * size,
            value, solve_high, solve_low, *arrived,
        )
        steps = []
        for place in range(pieces):
            final = place == pieces - 1
            step, *parts = run(
                lambda kept, came, fine, high, low, *refs: correct_body(kept, came, fine, high, low, place, *refs),
                [whole(PIECE)] + (shared if final else []), 6 * modes * rows * PIECE, 12 * rows * PIECE,
                kept[place], came[place], fine, basis_high, basis_low, *(steps if final else []),
            )
            steps.append(step)
        arrived = exchange(parts)
        if first:
            schur_high, schur_low = run(
                schur_body, [whole(rows, bf16)] * 2, 8 * rows**3, 12 * size, chooser, flipped, schur_matrix[0, 0],
            )
        base, total = run(
            lambda *refs: ahead_body(pieces, first, *refs), [whole(loads)] * 2, 6 * rows * size, 16 * size,
            *steps, *([] if first else [iterate]), ordered, schur_high, schur_low,
        )
        parts = run(
            lambda *refs: product_body(subs, count, *refs), shared, 2 * rows * size, 12 * size,
            base, schur_high, schur_low, *arrived,
        )
        before, arrived = arrived, exchange(parts)
        *projected, iterate, value = run(
            lambda *refs: follow_body(subs, count, last, *refs),
            ([] if last else [((modes, loads), f32)]) + [whole(loads)] * 2, 3 * rows * size, 16 * size,
            base, total, schur_high, schur_low, *before, *parts, *([] if last else [test_high, test_low]),
        )
        ahead = projected[0] if projected else None
    near, solution_rows = run(
        restore_body, [whole(loads)] * 2, 8 * rows * size, 10 * size, flipped, value, iterate,
    )
    (residual_rows,) = run(
        lambda *refs: finish_body(subs, *refs), [whole(loads)], 4 * rows * size, 10 * size,
        flipped, near, *arrived, places=[outside],
        scratch=[pltpu.VMEM((rows, loads), f32), pltpu.SemaphoreType.DMA((4,))],
    )
    return (solution_rows[None, None], residual_rows[None, None])


def solution(mesh):
    return jax.shard_map(
        local,
        mesh=mesh,
        in_specs=(
            P("sub", "grp", None, None),
            P("sub", "grp", None, None),
            P("sub", "grp", None, None),
            P("sub", "grp", None, None),
            P("sub", None, "grp"),
            P("sub", "grp", None, None),
        ),
        out_specs=(P("sub", "grp", None, None), P("sub", "grp", None, None)),
        check_vma=False,
    )
```

```python
import jax
import jax.numpy as jnp
from jax import lax
from jax.experimental import pallas as pl
from jax.experimental.pallas import tpu as pltpu
from jax.sharding import PartitionSpec as P

ITERS = 2
ROW_SUBS = 4
RELAX = 0.5
GROUPS = 4
PIECE = 128
f32 = jnp.float32
bf16 = jnp.bfloat16
NN = (((1,), (0,)), ((), ()))
NT = (((1,), (1,)), ((), ()))


class Chain:
    def __init__(self):
        self.last = None

    def __call__(self, body, outs, flops, moved, *operands, scratch=(), ins=None, places=None):
        count = len(operands)
        specs = [pl.BlockSpec(memory_space=pltpu.VMEM)] * count if ins is None else ins
        extra = []
        if self.last is not None:
            extra = [self.last]
            specs = specs + [pl.BlockSpec(memory_space=pl.ANY)]

        def whole_body(*refs):
            body(*refs[:count], *refs[count + len(extra) :])

        results = pl.pallas_call(
            whole_body,
            out_shape=[jax.ShapeDtypeStruct(shape, kind) for shape, kind in outs],
            in_specs=specs,
            out_specs=[pl.BlockSpec(memory_space=pltpu.VMEM)] * len(outs) if places is None else places,
            scratch_shapes=list(scratch),
            compiler_params=pltpu.CompilerParams(vmem_limit_bytes=24 * 1024 * 1024),
            cost_estimate=pl.CostEstimate(flops=flops, bytes_accessed=moved, transcendentals=0),
        )(*operands, *extra)
        self.last = results[0]
        return results


def dot(left, right, dims=NN):
    return lax.dot_general(left, right, dims, preferred_element_type=f32)


def split(value):
    high = value.astype(bf16)
    return high, (value - high.astype(f32)).astype(bf16)


def dot3(left, right):
    return dot(left[0], right[0]) + (dot(left[0], right[1]) + dot(left[1], right[0]))


def pick(chooser, value):
    high, low = split(value)
    return dot(chooser, high) + dot(chooser, low)


def sides(subs):
    sub = lax.axis_index("sub")
    low_row = (sub // ROW_SUBS) % 2 == 0
    over, under = sub < subs - ROW_SUBS, sub >= ROW_SUBS
    return [
        (low_row, 0, 0, sub > 0),
        (low_row, 3, 2, jnp.where(low_row, over, under)),
        (low_row, 1, 1, sub < subs - 1),
        (low_row, 2, 3, jnp.where(low_row, under, over)),
    ]


def put_shared(value, shared_refs):
    for place, ref in enumerate(shared_refs):
        width = ref.shape[0]
        ref[...] = value[place * width : (place + 1) * width]


def came_in(subs, shared_refs):
    return jnp.concatenate(
        [ref[...] * jnp.where(here, 1.0, 0.0) for ref, (_, _, _, here) in zip(shared_refs, sides(subs))], axis=0
    )


def add_shared(subs, value, shared_refs):
    came = came_in(subs, shared_refs)
    count = came.shape[0]
    return jnp.concatenate([value[:count] + came, value[count:]], axis=0)


def listed_body(subs, count, blocks_hbm, load_hbm, columns_hbm, listed_ref, load_ref, sent_ref, *refs):
    *shared_refs, blocks_ref, load_sem, blocks_sem, sent_sem = refs
    modes = sent_ref.shape[0]
    wanted = pl.multiple_of((3 - (lax.axis_index("grp") ^ 1)) * modes, modes)
    sent_copy = pltpu.make_async_copy(columns_hbm.at[pl.ds(wanted, modes), :], sent_ref, sent_sem)
    load_copy = pltpu.make_async_copy(load_hbm, load_ref, load_sem)
    blocks_copy = pltpu.make_async_copy(blocks_hbm, blocks_ref, blocks_sem)
    blocks_copy.start()
    load_copy.start()
    sent_copy.start()
    blocks_copy.wait()
    blocks = blocks_ref[...]
    placed = jnp.concatenate(
        [jnp.where(test, blocks[a : a + 1], blocks[b : b + 1]) for test, a, b, _ in sides(subs)], axis=0
    )
    upright = placed.astype(f32).T
    column = jnp.concatenate([upright[:, place : place + 1] for place in range(4)], axis=0)
    listed, total = column.shape[0], load_ref.shape[0]
    lane = lax.broadcasted_iota(jnp.int32, (listed, total), 1).astype(f32)
    first = (column == lane).astype(f32).astype(bf16)
    listed_ref[...] = first
    load_copy.wait()
    sent_copy.wait()
    sent = pick(first[: count * blocks.shape[1]], load_ref[...])
    put_shared(sent, shared_refs)


def order_body(subs, listed_ref, load_ref, basis_ref,
               chooser_ref, flipped_ref, basis_high, basis_low, test_high, test_low, ahead_ref, ordered_ref):
    listed, total = listed_ref.shape
    first = listed_ref[...].astype(f32)
    unlisted = 1.0 - jnp.sum(first, axis=0, keepdims=True)
    before = (
        lax.broadcasted_iota(jnp.int32, (total, total), 0)
        < lax.broadcasted_iota(jnp.int32, (total, total), 1)
    ).astype(f32).astype(bf16)
    rank = dot(jnp.broadcast_to(unlisted, (8, total)).astype(bf16), before)[:1]
    slot = lax.broadcasted_iota(jnp.int32, (total - listed, total), 0).astype(f32)
    last = jnp.where(rank == slot, unlisted, 0.0)
    chooser = jnp.concatenate([first, last], axis=0)
    flipped_ref[...] = chooser.T.astype(bf16)
    weighted = (chooser * weight_column(subs, listed // 4, total)).astype(bf16)
    chooser = chooser.astype(bf16)
    chooser_ref[...] = chooser
    ordered = pick(chooser, load_ref[...])
    ordered_ref[...] = ordered
    for part, out, turned in zip(split(basis_ref[...]), (basis_high, basis_low), (test_high, test_low)):
        placed = dot(weighted, part)
        out[...] = placed.astype(bf16)
        turned[...] = placed.T.astype(bf16)
    ahead_ref[...] = dot3((test_high[...], test_low[...]), split(ordered))


def weight_column(subs, width, total):
    parts = [jnp.full((width, 1), jnp.where(here, 0.5, 1.0), f32) for _, _, _, here in sides(subs)]
    return jnp.concatenate(parts + [jnp.ones((total - 4 * width, 1), f32)], axis=0)


def rows_of(columns_ref, place):
    modes = columns_ref.shape[1]
    return columns_ref[pl.ds(pl.multiple_of(place * modes, modes), modes), :]


def solver_body(subs, listed, chooser_ref, solve_ref, solve_high, solve_low):
    chooser = chooser_ref[...]
    weighted = (chooser.astype(f32) * weight_column(subs, listed // 4, chooser.shape[0])).astype(bf16)
    for part, out in zip(split(solve_ref[...] * RELAX), (solve_high, solve_low)):
        out[...] = dot(dot(weighted, part).astype(bf16), weighted, NT).astype(bf16)


def schur_body(chooser_ref, flipped_ref, schur_ref, schur_high, schur_low):
    chooser, flipped = chooser_ref[...], flipped_ref[...]
    for part, out in zip(split(schur_ref[...]), (schur_high, schur_low)):
        out[...] = dot(dot(chooser, part).astype(bf16), flipped).astype(bf16)


def blend_body(columns_ref, other_ref, mix_high, mix_low):
    grp = lax.axis_index("grp")
    away = jnp.concatenate([rows_of(columns_ref, 3 - grp), other_ref[...]], axis=1)
    kept = jnp.concatenate([rows_of(columns_ref, grp), rows_of(columns_ref, grp ^ 1).T], axis=1)
    mix_high[...], mix_low[...] = split(jnp.concatenate([away, kept], axis=0) * RELAX)


def project_body(subs, count, ahead_ref, test_high, test_low, *refs):
    came = came_in(subs, refs[:count])
    size = came.shape[0]
    projected = ahead_ref[...] + dot3((test_high[:, :size], test_low[:, :size]), split(came))
    for place, ref in enumerate(refs[count:]):
        ref[...] = projected[:, place * PIECE : (place + 1) * PIECE]


def solve_body(subs, value_ref, solve_high, solve_low, *refs):
    halves = split(add_shared(subs, value_ref[...], refs[:-1]))
    refs[-1][...] = dot3((solve_high[...], solve_low[...]), halves)


def mix_body(own_ref, other_ref, mix_high, mix_low, away_ref, kept_ref):
    modes = away_ref.shape[0]
    pair = jnp.concatenate([own_ref[...], other_ref[...]], axis=0)
    mixed = dot3((mix_high[...], mix_low[...]), split(pair))
    away_ref[...] = mixed[:modes]
    kept_ref[...] = mixed[modes:]


def correct_body(kept_ref, came_ref, fine_ref, basis_high, basis_low, place, *refs):
    coarse = kept_ref[...] + came_ref[...]
    fine = fine_ref[:, place * PIECE : (place + 1) * PIECE]
    step = fine + dot3((basis_high[...], basis_low[...]), split(coarse))
    formers = place if len(refs) > 1 else 0
    former_refs, out_ref = refs[:formers], refs[formers]
    out_ref[...] = step
    for at, ref in enumerate(refs[formers + 1 :]):
        size = ref.shape[0]
        rows = slice(at * size, (at + 1) * size)
        ref[...] = jnp.concatenate([former[rows] for former in former_refs] + [step[rows]], axis=1)


def ahead_body(pieces, first, *refs):
    total = jnp.concatenate([ref[...] for ref in refs[:pieces]], axis=1)
    refs = refs[pieces:]
    if not first:
        total = refs[0][...] + total
        refs = refs[1:]
    load_ref, schur_high, schur_low, base_ref, total_ref = refs
    total_ref[...] = total
    base_ref[...] = load_ref[...] - dot3((schur_high[...], schur_low[...]), split(total))


def product_body(subs, count, base_ref, schur_high, schur_low, *refs):
    came = came_in(subs, refs[:count])
    size = came.shape[0]
    part = dot3((schur_high[:size, :size], schur_low[:size, :size]), split(came))
    put_shared(base_ref[:size] - part, refs[count:])


def follow_body(subs, count, last, base_ref, total_ref, schur_high, schur_low, *refs):
    arrived, shared, refs = refs[:count], refs[count : 2 * count], refs[2 * count :]
    came = came_in(subs, arrived)
    size = came.shape[0]
    part = dot3((schur_high[size:, :size], schur_low[size:, :size]), split(came))
    value = jnp.concatenate([ref[...] for ref in shared] + [base_ref[size:] - part], axis=0)
    iterate_ref, value_ref = refs[-2:]
    value_ref[...] = value
    iterate_ref[...] = jnp.concatenate([total_ref[:size] + came, total_ref[size:]], axis=0)
    if not last:
        test_high, test_low, projected_ref = refs[:3]
        projected_ref[...] = dot3((test_high[...], test_low[...]), split(value))


def restore_body(flipped_ref, value_ref, iterate_ref, base_ref, out_ref):
    flipped = flipped_ref[...]
    out_ref[...] = pick(flipped, iterate_ref[...])
    base_ref[...] = pick(flipped, value_ref[...])


def finish_body(subs, flipped_ref, base_ref, *refs):
    *arrived, out_hbm, out_ref, sems = refs
    came = came_in(subs, arrived)
    halves = split(came)
    copies = []
    size = out_ref.shape[0] // 4
    for step in range(4):
        rows = slice(step * size, (step + 1) * size)
        chooser = flipped_ref[rows, : came.shape[0]]
        out_ref[rows] = base_ref[rows] + (dot(chooser, halves[0]) + dot(chooser, halves[1]))
        copy = pltpu.make_async_copy(out_ref.at[rows], out_hbm.at[rows], sems.at[step])
        copy.start()
        copies.append(copy)
    for copy in copies:
        copy.wait()


def swaps(count, stride, odd):
    partner = list(range(count))
    for low in range(count - stride):
        if (low // stride) % 2 == odd:
            partner[low], partner[low + stride] = low + stride, low
    return list(enumerate(partner)) if partner != list(range(count)) else []


def local(load_terms, schur_matrix, local_inverse, coarse_modes, cluster_inverse, row_blocks):
    load = load_terms[0, 0]
    basis = coarse_modes[0, 0]
    columns = cluster_inverse[0]
    blocks = row_blocks[0, 0]
    rows, loads = load.shape
    modes = basis.shape[1]
    shared_rows = blocks.shape[1]
    listed = 4 * shared_rows
    subs = lax.axis_size("sub")
    if lax.axis_size("grp") != GROUPS or loads % PIECE:
        raise ValueError("unexpected sizes")

    up = [(low, (low + 1) % subs) for low in range(subs)]
    down = [(target, source) for source, target in up]
    plans = [(2, up), (1, swaps(subs, ROW_SUBS, 0)), (0, down), (3, swaps(subs, ROW_SUBS, 1))]
    plans = [plan for plan in plans if plan[1]]
    count = len(plans)
    def exchange(parts):
        return [lax.ppermute(parts[place], "sub", pairs) for place, pairs in plans]

    def whole(width, kind=f32):
        return ((rows, width), kind)

    pair_plan = [(0, 1), (1, 0), (2, 3), (3, 2)]
    mirror_plan = [(0, 3), (3, 0), (1, 2), (2, 1)]
    shared = [((shared_rows, loads), f32)] * count
    outside = pl.BlockSpec(memory_space=pltpu.HBM)
    pieces = loads // PIECE
    size = rows * loads
    run = Chain()

    one_hot, load_near, sent, *parts = run(
        lambda *refs: listed_body(subs, count, *refs),
        [((listed, rows), bf16), whole(loads), ((modes, modes), f32)] + shared, 4 * listed * size, 16 * size,
        *[pltpu.with_memory_space_constraint(array, pltpu.HBM) for array in (blocks, load, columns)], ins=[outside] * 3,
        scratch=[pltpu.VMEM(blocks.shape, blocks.dtype)] + [pltpu.SemaphoreType.DMA] * 3,
    )
    arrived = exchange(parts)
    other = lax.ppermute(sent, "grp", pair_plan)
    chooser, flipped, basis_high, basis_low, test_high, test_low, ahead, ordered = run(
        lambda *refs: order_body(subs, *refs),
        [whole(rows, bf16)] * 2 + [whole(modes, bf16)] * 2 + [((modes, rows), bf16)] * 2
        + [((modes, loads), f32), whole(loads)],
        4 * rows * size, 24 * size, one_hot, load_near, basis,
    )
    mixers = run(blend_body, [((2 * modes, 2 * modes), bf16)] * 2, size, size, columns, other)
    value, iterate = ordered, None
    for iteration in range(ITERS):
        first, last = iteration == 0, iteration == ITERS - 1
        shapes = [((modes, PIECE), f32)] * pieces
        own = run(
            lambda *refs: project_body(subs, count, *refs), shapes, 6 * modes * size, 12 * size,
            ahead, test_high, test_low, *arrived,
        )
        theirs = [lax.ppermute(piece, "grp", pair_plan) for piece in own]
        kept, came = [], []
        for place in range(pieces):
            away, keep = run(
                mix_body, [((modes, PIECE), f32)] * 2, 24 * modes * modes * PIECE, 4 * rows * PIECE,
                own[place], theirs[place], *mixers,
            )
            kept.append(keep)
            came.append(lax.ppermute(away, "grp", mirror_plan))
        if first:
            solve_high, solve_low = run(
                lambda *refs: solver_body(subs, listed, *refs), [whole(rows, bf16)] * 2, 8 * rows**3, 12 * size,
                chooser, local_inverse[0, 0],
            )
        (fine,) = run(
            lambda *refs: solve_body(subs, *refs), [whole(loads)], 6 * rows * size, 12 * size,
            value, solve_high, solve_low, *arrived,
        )
        steps = []
        for place in range(pieces):
            final = place == pieces - 1
            step, *parts = run(
                lambda kept, came, fine, high, low, *refs: correct_body(kept, came, fine, high, low, place, *refs),
                [whole(PIECE)] + (shared if final else []), 6 * modes * rows * PIECE, 12 * rows * PIECE,
                kept[place], came[place], fine, basis_high, basis_low, *(steps if final else []),
            )
            steps.append(step)
        arrived = exchange(parts)
        if first:
            schur_high, schur_low = run(
                schur_body, [whole(rows, bf16)] * 2, 8 * rows**3, 12 * size, chooser, flipped, schur_matrix[0, 0],
            )
        base, total = run(
            lambda *refs: ahead_body(pieces, first, *refs), [whole(loads)] * 2, 6 * rows * size, 16 * size,
            *steps, *([] if first else [iterate]), ordered, schur_high, schur_low,
        )
        parts = run(
            lambda *refs: product_body(subs, count, *refs), shared, 2 * rows * size, 12 * size,
            base, schur_high, schur_low, *arrived,
        )
        before, arrived = arrived, exchange(parts)
        *projected, iterate, value = run(
            lambda *refs: follow_body(subs, count, last, *refs),
            ([] if last else [((modes, loads), f32)]) + [whole(loads)] * 2, 3 * rows * size, 16 * size,
            base, total, schur_high, schur_low, *before, *parts, *([] if last else [test_high, test_low]),
        )
        ahead = projected[0] if projected else None
    near, solution_rows = run(
        restore_body, [whole(loads)] * 2, 8 * rows * size, 10 * size, flipped, value, iterate,
    )
    (residual_rows,) = run(
        lambda *refs: finish_body(subs, *refs), [whole(loads)], 4 * rows * size, 10 * size,
        flipped, near, *arrived, places=[outside],
        scratch=[pltpu.VMEM((rows, loads), f32), pltpu.SemaphoreType.DMA((4,))],
    )
    return (solution_rows[None, None], residual_rows[None, None])


def solution(mesh):
    return jax.shard_map(
        local,
        mesh=mesh,
        in_specs=(
            P("sub", "grp", None, None),
            P("sub", "grp", None, None),
            P("sub", "grp", None, None),
            P("sub", "grp", None, None),
            P("sub", None, "grp"),
            P("sub", "grp", None, None),
        ),
        out_specs=(P("sub", "grp", None, None), P("sub", "grp", None, None)),
        check_vma=False,
    )
```

```python
import jax
import jax.numpy as jnp
from jax import lax
from jax.experimental import pallas as pl
from jax.experimental.pallas import tpu as pltpu
from jax.sharding import PartitionSpec as P

ITERS = 2
ROW_SUBS = 4
RELAX = 0.5
GROUPS = 4
HIDE = 16
PIECES = (128, 256)
f32 = jnp.float32
bf16 = jnp.bfloat16
NN = (((1,), (0,)), ((), ()))
NT = (((1,), (1,)), ((), ()))


class Chain:
    def __init__(self):
        self.last = None

    def __call__(self, body, outs, flops, moved, *operands, scratch=(), ins=None, places=None):
        count = len(operands)
        specs = [pl.BlockSpec(memory_space=pltpu.VMEM)] * count if ins is None else ins
        extra = []
        if self.last is not None:
            extra = [self.last]
            specs = specs + [pl.BlockSpec(memory_space=pl.ANY)]

        def whole_body(*refs):
            body(*refs[:count], *refs[count + len(extra) :])

        results = pl.pallas_call(
            whole_body,
            out_shape=[jax.ShapeDtypeStruct(shape, kind) for shape, kind in outs],
            in_specs=specs,
            out_specs=[pl.BlockSpec(memory_space=pltpu.VMEM)] * len(outs) if places is None else places,
            scratch_shapes=list(scratch),
            compiler_params=pltpu.CompilerParams(vmem_limit_bytes=24 * 1024 * 1024),
            cost_estimate=pl.CostEstimate(flops=flops, bytes_accessed=moved, transcendentals=0),
        )(*operands, *extra)
        self.last = results[0]
        return results


def dot(left, right, dims=NN):
    return lax.dot_general(left, right, dims, preferred_element_type=f32)


def split(value):
    high = value.astype(bf16)
    return high, (value - high.astype(f32)).astype(bf16)


def dot3(left, right):
    return dot(left[0], right[0]) + (dot(left[0], right[1]) + dot(left[1], right[0]))


def pick(chooser, value):
    high, low = split(value)
    return dot(chooser, high) + dot(chooser, low)


def sides(subs):
    sub = lax.axis_index("sub")
    low_row = (sub // ROW_SUBS) % 2 == 0
    over, under = sub < subs - ROW_SUBS, sub >= ROW_SUBS
    return [
        (low_row, 3, 2, jnp.where(low_row, over, under)),
        (low_row, 0, 0, sub > 0),
        (low_row, 1, 1, sub < subs - 1),
        (low_row, 2, 3, jnp.where(low_row, under, over)),
    ]


def put_shared(value, shared_refs):
    for place, ref in enumerate(shared_refs):
        width = ref.shape[0]
        ref[...] = value[place * width : (place + 1) * width]


def came_in(subs, shared_refs):
    return jnp.concatenate(
        [ref[...] * jnp.where(here, 1.0, 0.0) for ref, (_, _, _, here) in zip(shared_refs, sides(subs))], axis=0
    )


def add_shared(subs, value, shared_refs):
    came = came_in(subs, shared_refs)
    count = came.shape[0]
    return jnp.concatenate([value[:count] + came, value[count:]], axis=0)


def listed_body(subs, count, blocks_hbm, load_hbm, columns_hbm, listed_ref, load_ref, sent_ref, *refs):
    *shared_refs, blocks_ref, load_sem, blocks_sem, sent_sem = refs
    modes = sent_ref.shape[0]
    wanted = pl.multiple_of((3 - (lax.axis_index("grp") ^ 1)) * modes, modes)
    sent_copy = pltpu.make_async_copy(columns_hbm.at[pl.ds(wanted, modes), :], sent_ref, sent_sem)
    load_copy = pltpu.make_async_copy(load_hbm, load_ref, load_sem)
    blocks_copy = pltpu.make_async_copy(blocks_hbm, blocks_ref, blocks_sem)
    blocks_copy.start()
    load_copy.start()
    sent_copy.start()
    blocks_copy.wait()
    blocks = blocks_ref[...]
    placed = jnp.concatenate(
        [jnp.where(test, blocks[a : a + 1], blocks[b : b + 1]) for test, a, b, _ in sides(subs)], axis=0
    )
    upright = placed.astype(f32).T
    column = jnp.concatenate([upright[:, place : place + 1] for place in range(4)], axis=0)
    listed, total = column.shape[0], load_ref.shape[0]
    lane = lax.broadcasted_iota(jnp.int32, (listed, total), 1).astype(f32)
    first = (column == lane).astype(f32).astype(bf16)
    listed_ref[...] = first
    load_copy.wait()
    sent_copy.wait()
    sent = pick(first[: count * blocks.shape[1]], load_ref[...])
    put_shared(sent, shared_refs)


def order_body(subs, listed_ref, load_ref, basis_ref,
               chooser_ref, flipped_ref, basis_high, basis_low, test_high, test_low, ahead_ref, ordered_ref):
    listed, total = listed_ref.shape
    first = listed_ref[...].astype(f32)
    unlisted = 1.0 - jnp.sum(first, axis=0, keepdims=True)
    before = (
        lax.broadcasted_iota(jnp.int32, (total, total), 0)
        < lax.broadcasted_iota(jnp.int32, (total, total), 1)
    ).astype(f32).astype(bf16)
    rank = dot(jnp.broadcast_to(unlisted, (8, total)).astype(bf16), before)[:1]
    slot = lax.broadcasted_iota(jnp.int32, (total - listed, total), 0).astype(f32)
    last = jnp.where(rank == slot, unlisted, 0.0)
    chooser = jnp.concatenate([first, last], axis=0)
    flipped_ref[...] = chooser.T.astype(bf16)
    weighted = (chooser * weight_column(subs, listed // 4, total)).astype(bf16)
    chooser = chooser.astype(bf16)
    chooser_ref[...] = chooser
    ordered = pick(chooser, load_ref[...])
    ordered_ref[...] = ordered
    for part, out, turned in zip(split(basis_ref[...]), (basis_high, basis_low), (test_high, test_low)):
        placed = dot(weighted, part)
        out[...] = placed.astype(bf16)
        turned[...] = placed.T.astype(bf16)
    ahead_ref[...] = dot3((test_high[...], test_low[...]), split(ordered))


def weight_column(subs, width, total):
    parts = [jnp.full((width, 1), jnp.where(here, 0.5, 1.0), f32) for _, _, _, here in sides(subs)]
    return jnp.concatenate(parts + [jnp.ones((total - 4 * width, 1), f32)], axis=0)


def rows_of(columns_ref, place):
    modes = columns_ref.shape[1]
    return columns_ref[pl.ds(pl.multiple_of(place * modes, modes), modes), :]


def solver_body(subs, listed, chooser_ref, solve_ref, solve_high, solve_low):
    chooser = chooser_ref[...]
    weighted = (chooser.astype(f32) * weight_column(subs, listed // 4, chooser.shape[0])).astype(bf16)
    for part, out in zip(split(solve_ref[...] * RELAX), (solve_high, solve_low)):
        out[...] = dot(dot(weighted, part).astype(bf16), weighted, NT).astype(bf16)


def schur_body(chooser_ref, flipped_ref, schur_ref, schur_high, schur_low):
    chooser, flipped = chooser_ref[...], flipped_ref[...]
    for part, out in zip(split(schur_ref[...]), (schur_high, schur_low)):
        out[...] = dot(dot(chooser, part).astype(bf16), flipped).astype(bf16)


def blend_body(columns_ref, other_ref, mix_high, mix_low):
    grp = lax.axis_index("grp")
    away = jnp.concatenate([rows_of(columns_ref, 3 - grp), other_ref[...]], axis=1)
    kept = jnp.concatenate([rows_of(columns_ref, grp), rows_of(columns_ref, grp ^ 1).T], axis=1)
    mix_high[...], mix_low[...] = split(jnp.concatenate([away, kept], axis=0) * RELAX)


def cut():
    return [(sum(PIECES[:place]), width) for place, width in enumerate(PIECES)]


def project_body(subs, count, ahead_ref, test_high, test_low, *refs):
    came = came_in(subs, refs[:count])
    size = came.shape[0]
    projected = ahead_ref[...] + dot3((test_high[:, :size], test_low[:, :size]), split(came))
    for ref, (start, width) in zip(refs[count:], cut()):
        ref[...] = projected[:, start : start + width]


def solve_body(subs, value_ref, solve_high, solve_low, *refs):
    halves = split(add_shared(subs, value_ref[...], refs[:-1]))
    refs[-1][...] = dot3((solve_high[...], solve_low[...]), halves)


def mix_body(own_ref, other_ref, mix_high, mix_low, away_ref, kept_ref):
    modes = away_ref.shape[0]
    pair = jnp.concatenate([own_ref[...], other_ref[...]], axis=0)
    mixed = dot3((mix_high[...], mix_low[...]), split(pair))
    away_ref[...] = mixed[:modes]
    kept_ref[...] = mixed[modes:]


def correct_body(kept_ref, came_ref, fine_ref, basis_high, basis_low, place, *refs):
    coarse = kept_ref[...] + came_ref[...]
    start, width = cut()[place]
    fine = fine_ref[:, start : start + width]
    step = fine + dot3((basis_high[...], basis_low[...]), split(coarse))
    formers = place if len(refs) > 1 else 0
    former_refs, out_ref = refs[:formers], refs[formers]
    out_ref[...] = step
    for at, ref in enumerate(refs[formers + 1 :]):
        size = ref.shape[0]
        rows = slice(at * size, (at + 1) * size)
        ref[...] = jnp.concatenate([former[rows] for former in former_refs] + [step[rows]], axis=1)


def ahead_body(pieces, first, *refs):
    total = jnp.concatenate([ref[...] for ref in refs[:pieces]], axis=1)
    refs = refs[pieces:]
    if not first:
        total = refs[0][...] + total
        refs = refs[1:]
    load_ref, schur_high, schur_low, base_ref, total_ref = refs
    total_ref[...] = total
    base_ref[...] = load_ref[...] - dot3((schur_high[...], schur_low[...]), split(total))


def product_body(subs, count, base_ref, schur_high, schur_low, *refs):
    came = came_in(subs, refs[:count])
    size = came.shape[0]
    part = dot3((schur_high[:size, :size], schur_low[:size, :size]), split(came))
    put_shared(base_ref[:size] - part, refs[count:])


def follow_body(subs, count, last, base_ref, total_ref, schur_high, schur_low, *refs):
    arrived, shared, refs = refs[:count], refs[count : 2 * count], refs[2 * count :]
    came = came_in(subs, arrived)
    size = came.shape[0]
    part = dot3((schur_high[size:, :size], schur_low[size:, :size]), split(came))
    value = jnp.concatenate([ref[...] for ref in shared] + [base_ref[size:] - part], axis=0)
    iterate_ref, value_ref = refs[-2:]
    value_ref[...] = value
    iterate_ref[...] = jnp.concatenate([total_ref[:size] + came, total_ref[size:]], axis=0)
    if not last:
        test_high, test_low, projected_ref = refs[:3]
        projected_ref[...] = dot3((test_high[...], test_low[...]), split(value))


def restore_body(flipped_ref, value_ref, iterate_ref, base_ref, out_ref):
    flipped = flipped_ref[...]
    out_ref[...] = pick(flipped, iterate_ref[...])
    base_ref[...] = pick(flipped, value_ref[...])


def finish_body(subs, flipped_ref, base_ref, *refs):
    *arrived, out_hbm, out_ref, sems = refs
    came = came_in(subs, arrived)
    halves = split(came)
    copies = []
    size = out_ref.shape[0] // 4
    for step in range(4):
        rows = slice(step * size, (step + 1) * size)
        chooser = flipped_ref[rows, : came.shape[0]]
        out_ref[rows] = base_ref[rows] + (dot(chooser, halves[0]) + dot(chooser, halves[1]))
        copy = pltpu.make_async_copy(out_ref.at[rows], out_hbm.at[rows], sems.at[step])
        copy.start()
        copies.append(copy)
    for copy in copies:
        copy.wait()


def swaps(count, stride, odd):
    partner = list(range(count))
    for low in range(count - stride):
        if (low // stride) % 2 == odd:
            partner[low], partner[low + stride] = low + stride, low
    return list(enumerate(partner)) if partner != list(range(count)) else []


def local(load_terms, schur_matrix, local_inverse, coarse_modes, cluster_inverse, row_blocks):
    load = load_terms[0, 0]
    basis = coarse_modes[0, 0]
    columns = cluster_inverse[0]
    blocks = row_blocks[0, 0]
    rows, loads = load.shape
    modes = basis.shape[1]
    shared_rows = blocks.shape[1]
    listed = 4 * shared_rows
    subs = lax.axis_size("sub")
    if lax.axis_size("grp") != GROUPS or sum(PIECES) != loads:
        raise ValueError("unexpected sizes")

    up = [(low, (low + 1) % subs) for low in range(subs)]
    down = [(target, source) for source, target in up]
    plans = [(0, swaps(subs, ROW_SUBS, 0)), (2, up), (1, down), (3, swaps(subs, ROW_SUBS, 1))]
    plans = [plan for plan in plans if plan[1]]
    count = len(plans)
    def exchange(parts):
        return [lax.ppermute(parts[place], "sub", pairs) for place, pairs in plans]

    def whole(width, kind=f32):
        return ((rows, width), kind)

    pair_plan = [(0, 1), (1, 0), (2, 3), (3, 2)]
    mirror_plan = [(0, 3), (3, 0), (1, 2), (2, 1)]
    shared = [((shared_rows, loads), f32)] * count
    outside = pl.BlockSpec(memory_space=pltpu.HBM)
    pieces = len(PIECES)
    size = rows * loads
    run = Chain()

    one_hot, load_near, sent, *parts = run(
        lambda *refs: listed_body(subs, count, *refs),
        [((listed, rows), bf16), whole(loads), ((modes, modes), f32)] + shared, 4 * listed * size, 16 * size,
        *[pltpu.with_memory_space_constraint(array, pltpu.HBM) for array in (blocks, load, columns)], ins=[outside] * 3,
        scratch=[pltpu.VMEM(blocks.shape, blocks.dtype)] + [pltpu.SemaphoreType.DMA] * 3,
    )
    arrived = exchange(parts)
    other = lax.ppermute(sent, "grp", pair_plan)
    chooser, flipped, basis_high, basis_low, test_high, test_low, ahead, ordered = run(
        lambda *refs: order_body(subs, *refs),
        [whole(rows, bf16)] * 2 + [whole(modes, bf16)] * 2 + [((modes, rows), bf16)] * 2
        + [((modes, loads), f32), whole(loads)],
        4 * rows * size, 24 * size, one_hot, load_near, basis,
    )
    mixers = run(blend_body, [((2 * modes, 2 * modes), bf16)] * 2, size, size, columns, other)
    value, iterate = ordered, None
    for iteration in range(ITERS):
        first, last = iteration == 0, iteration == ITERS - 1
        shapes = [((modes, width), f32) for width in PIECES]
        own = run(
            lambda *refs: project_body(subs, count, *refs), shapes, 6 * modes * size, 12 * size,
            ahead, test_high, test_low, *arrived,
        )
        theirs = [lax.ppermute(piece, "grp", pair_plan) for piece in own]
        kept, came = [], []
        for place, width in enumerate(PIECES):
            away, keep = run(
                mix_body, [((modes, width), f32)] * 2, HIDE * 24 * modes * modes * width, HIDE * 4 * rows * width,
                own[place], theirs[place], *mixers,
            )
            kept.append(keep)
            came.append(lax.ppermute(away, "grp", mirror_plan))
        if first:
            solve_high, solve_low = run(
                lambda *refs: solver_body(subs, listed, *refs), [whole(rows, bf16)] * 2, 8 * rows**3, 12 * size,
                chooser, local_inverse[0, 0],
            )
        (fine,) = run(
            lambda *refs: solve_body(subs, *refs), [whole(loads)], HIDE * 6 * rows * size, HIDE * 12 * size,
            value, solve_high, solve_low, *arrived,
        )
        steps = []
        for place, width in enumerate(PIECES):
            final = place == pieces - 1
            step, *parts = run(
                lambda kept, came, fine, high, low, *refs: correct_body(kept, came, fine, high, low, place, *refs),
                [whole(width)] + (shared if final else []), 6 * modes * rows * width, 12 * rows * width,
                kept[place], came[place], fine, basis_high, basis_low, *(steps if final else []),
            )
            steps.append(step)
        arrived = exchange(parts)
        if first:
            schur_high, schur_low = run(
                schur_body, [whole(rows, bf16)] * 2, 8 * rows**3, 12 * size, chooser, flipped, schur_matrix[0, 0],
            )
        base, total = run(
            lambda *refs: ahead_body(pieces, first, *refs), [whole(loads)] * 2, 6 * rows * size, 16 * size,
            *steps, *([] if first else [iterate]), ordered, schur_high, schur_low,
        )
        parts = run(
            lambda *refs: product_body(subs, count, *refs), shared, 2 * rows * size, 12 * size,
            base, schur_high, schur_low, *arrived,
        )
        before, arrived = arrived, exchange(parts)
        *projected, iterate, value = run(
            lambda *refs: follow_body(subs, count, last, *refs),
            ([] if last else [((modes, loads), f32)]) + [whole(loads)] * 2, 3 * rows * size, 16 * size,
            base, total, schur_high, schur_low, *before, *parts, *([] if last else [test_high, test_low]),
        )
        ahead = projected[0] if projected else None
    near, solution_rows = run(
        restore_body, [whole(loads)] * 2, 8 * rows * size, 10 * size, flipped, value, iterate,
    )
    (residual_rows,) = run(
        lambda *refs: finish_body(subs, *refs), [whole(loads)], 4 * rows * size, 10 * size,
        flipped, near, *arrived, places=[outside],
        scratch=[pltpu.VMEM((rows, loads), f32), pltpu.SemaphoreType.DMA((4,))],
    )
    return (solution_rows[None, None], residual_rows[None, None])


def solution(mesh):
    return jax.shard_map(
        local,
        mesh=mesh,
        in_specs=(
            P("sub", "grp", None, None),
            P("sub", "grp", None, None),
            P("sub", "grp", None, None),
            P("sub", "grp", None, None),
            P("sub", None, "grp"),
            P("sub", "grp", None, None),
        ),
        out_specs=(P("sub", "grp", None, None), P("sub", "grp", None, None)),
        check_vma=False,
    )
```

```python
import jax
import jax.numpy as jnp
from jax import lax
from jax.experimental import pallas as pl
from jax.experimental.pallas import tpu as pltpu
from jax.sharding import PartitionSpec as P

ITERS = 2
ROW_SUBS = 4
RELAX = 0.5
GROUPS = 4
HIDE = 16
PIECES = (128, 256)
f32 = jnp.float32
bf16 = jnp.bfloat16
NN = (((1,), (0,)), ((), ()))
NT = (((1,), (1,)), ((), ()))


class Chain:
    def __init__(self):
        self.last = None

    def __call__(self, body, outs, flops, moved, *operands, scratch=(), ins=None, places=None):
        count = len(operands)
        specs = [pl.BlockSpec(memory_space=pltpu.VMEM)] * count if ins is None else ins
        extra = []
        if self.last is not None:
            extra = [self.last]
            specs = specs + [pl.BlockSpec(memory_space=pl.ANY)]

        def whole_body(*refs):
            body(*refs[:count], *refs[count + len(extra) :])

        results = pl.pallas_call(
            whole_body,
            out_shape=[jax.ShapeDtypeStruct(shape, kind) for shape, kind in outs],
            in_specs=specs,
            out_specs=[pl.BlockSpec(memory_space=pltpu.VMEM)] * len(outs) if places is None else places,
            scratch_shapes=list(scratch),
            compiler_params=pltpu.CompilerParams(vmem_limit_bytes=24 * 1024 * 1024),
            cost_estimate=pl.CostEstimate(flops=flops, bytes_accessed=moved, transcendentals=0),
        )(*operands, *extra)
        self.last = results[0]
        return results


def dot(left, right, dims=NN):
    return lax.dot_general(left, right, dims, preferred_element_type=f32)


def split(value):
    high = value.astype(bf16)
    return high, (value - high.astype(f32)).astype(bf16)


def dot3(left, right):
    return dot(left[0], right[0]) + (dot(left[0], right[1]) + dot(left[1], right[0]))


def pick(chooser, value):
    high, low = split(value)
    return dot(chooser, high) + dot(chooser, low)


def sides(subs):
    sub = lax.axis_index("sub")
    low_row = (sub // ROW_SUBS) % 2 == 0
    over, under = sub < subs - ROW_SUBS, sub >= ROW_SUBS
    return [
        (low_row, 3, 2, jnp.where(low_row, over, under)),
        (low_row, 0, 0, sub > 0),
        (low_row, 1, 1, sub < subs - 1),
        (low_row, 2, 3, jnp.where(low_row, under, over)),
    ]


def put_shared(value, shared_refs):
    for place, ref in enumerate(shared_refs):
        width = ref.shape[0]
        ref[...] = value[place * width : (place + 1) * width]


def came_in(subs, shared_refs):
    return jnp.concatenate(
        [ref[...] * jnp.where(here, 1.0, 0.0) for ref, (_, _, _, here) in zip(shared_refs, sides(subs))], axis=0
    )


def add_shared(subs, value, shared_refs):
    came = came_in(subs, shared_refs)
    count = came.shape[0]
    return jnp.concatenate([value[:count] + came, value[count:]], axis=0)


def listed_body(subs, count, blocks_hbm, load_hbm, columns_hbm, listed_ref, load_ref, sent_ref, *refs):
    *shared_refs, blocks_ref, load_sems, blocks_sem, sent_sem = refs
    modes = sent_ref.shape[0]
    wanted = pl.multiple_of((3 - (lax.axis_index("grp") ^ 1)) * modes, modes)
    sent_copy = pltpu.make_async_copy(columns_hbm.at[pl.ds(wanted, modes), :], sent_ref, sent_sem)
    half = load_ref.shape[0] // 2
    halves = [slice(0, half), slice(half, 2 * half)]
    load_copies = [
        pltpu.make_async_copy(load_hbm.at[rows], load_ref.at[rows], load_sems.at[place])
        for place, rows in enumerate(halves)
    ]
    blocks_copy = pltpu.make_async_copy(blocks_hbm, blocks_ref, blocks_sem)
    blocks_copy.start()
    for copy in load_copies:
        copy.start()
    sent_copy.start()
    blocks_copy.wait()
    blocks = blocks_ref[...]
    placed = jnp.concatenate(
        [jnp.where(test, blocks[a : a + 1], blocks[b : b + 1]) for test, a, b, _ in sides(subs)], axis=0
    )
    upright = placed.astype(f32).T
    column = jnp.concatenate([upright[:, place : place + 1] for place in range(4)], axis=0)
    listed, total = column.shape[0], load_ref.shape[0]
    lane = lax.broadcasted_iota(jnp.int32, (listed, total), 1).astype(f32)
    first = (column == lane).astype(f32).astype(bf16)
    listed_ref[...] = first
    wanted_rows = count * blocks.shape[1]
    sent = None
    for copy, rows in zip(load_copies, halves):
        copy.wait()
        part = pick(first[:wanted_rows, rows], load_ref[rows])
        sent = part if sent is None else sent + part
    put_shared(sent, shared_refs)
    sent_copy.wait()


def order_body(subs, listed_ref, load_ref, basis_ref,
               chooser_ref, flipped_ref, basis_high, basis_low, test_high, test_low, ahead_ref, ordered_ref):
    listed, total = listed_ref.shape
    first = listed_ref[...].astype(f32)
    unlisted = 1.0 - jnp.sum(first, axis=0, keepdims=True)
    before = (
        lax.broadcasted_iota(jnp.int32, (total, total), 0)
        < lax.broadcasted_iota(jnp.int32, (total, total), 1)
    ).astype(f32).astype(bf16)
    rank = dot(jnp.broadcast_to(unlisted, (8, total)).astype(bf16), before)[:1]
    slot = lax.broadcasted_iota(jnp.int32, (total - listed, total), 0).astype(f32)
    last = jnp.where(rank == slot, unlisted, 0.0)
    chooser = jnp.concatenate([first, last], axis=0)
    flipped_ref[...] = chooser.T.astype(bf16)
    weighted = (chooser * weight_column(subs, listed // 4, total)).astype(bf16)
    chooser = chooser.astype(bf16)
    chooser_ref[...] = chooser
    ordered = pick(chooser, load_ref[...])
    ordered_ref[...] = ordered
    for part, out, turned in zip(split(basis_ref[...]), (basis_high, basis_low), (test_high, test_low)):
        placed = dot(weighted, part)
        out[...] = placed.astype(bf16)
        turned[...] = placed.T.astype(bf16)
    ahead_ref[...] = dot3((test_high[...], test_low[...]), split(ordered))


def weight_column(subs, width, total):
    parts = [jnp.full((width, 1), jnp.where(here, 0.5, 1.0), f32) for _, _, _, here in sides(subs)]
    return jnp.concatenate(parts + [jnp.ones((total - 4 * width, 1), f32)], axis=0)


def rows_of(columns_ref, place):
    modes = columns_ref.shape[1]
    return columns_ref[pl.ds(pl.multiple_of(place * modes, modes), modes), :]


def solver_body(subs, listed, chooser_ref, solve_ref, solve_high, solve_low):
    chooser = chooser_ref[...]
    weighted = (chooser.astype(f32) * weight_column(subs, listed // 4, chooser.shape[0])).astype(bf16)
    for part, out in zip(split(solve_ref[...] * RELAX), (solve_high, solve_low)):
        out[...] = dot(dot(weighted, part).astype(bf16), weighted, NT).astype(bf16)


def schur_body(chooser_ref, flipped_ref, schur_ref, schur_high, schur_low):
    chooser, flipped = chooser_ref[...], flipped_ref[...]
    for part, out in zip(split(schur_ref[...]), (schur_high, schur_low)):
        out[...] = dot(dot(chooser, part).astype(bf16), flipped).astype(bf16)


def blend_body(columns_ref, other_ref, mix_high, mix_low):
    grp = lax.axis_index("grp")
    away = jnp.concatenate([rows_of(columns_ref, 3 - grp), other_ref[...]], axis=1)
    kept = jnp.concatenate([rows_of(columns_ref, grp), rows_of(columns_ref, grp ^ 1).T], axis=1)
    mix_high[...], mix_low[...] = split(jnp.concatenate([away, kept], axis=0) * RELAX)


def cut():
    return [(sum(PIECES[:place]), width) for place, width in enumerate(PIECES)]


def project_body(subs, count, ahead_ref, test_high, test_low, *refs):
    came = came_in(subs, refs[:count])
    size = came.shape[0]
    projected = ahead_ref[...] + dot3((test_high[:, :size], test_low[:, :size]), split(came))
    for ref, (start, width) in zip(refs[count:], cut()):
        ref[...] = projected[:, start : start + width]


def solve_body(subs, value_ref, solve_high, solve_low, *refs):
    halves = split(add_shared(subs, value_ref[...], refs[:-1]))
    refs[-1][...] = dot3((solve_high[...], solve_low[...]), halves)


def mix_body(own_ref, other_ref, mix_high, mix_low, away_ref, kept_ref):
    modes = away_ref.shape[0]
    pair = jnp.concatenate([own_ref[...], other_ref[...]], axis=0)
    mixed = dot3((mix_high[...], mix_low[...]), split(pair))
    away_ref[...] = mixed[:modes]
    kept_ref[...] = mixed[modes:]


def correct_body(kept_ref, came_ref, fine_ref, basis_high, basis_low, place, *refs):
    coarse = kept_ref[...] + came_ref[...]
    start, width = cut()[place]
    fine = fine_ref[:, start : start + width]
    step = fine + dot3((basis_high[...], basis_low[...]), split(coarse))
    formers = place if len(refs) > 1 else 0
    former_refs, out_ref = refs[:formers], refs[formers]
    out_ref[...] = step
    for at, ref in enumerate(refs[formers + 1 :]):
        size = ref.shape[0]
        rows = slice(at * size, (at + 1) * size)
        ref[...] = jnp.concatenate([former[rows] for former in former_refs] + [step[rows]], axis=1)


def ahead_body(pieces, first, *refs):
    total = jnp.concatenate([ref[...] for ref in refs[:pieces]], axis=1)
    refs = refs[pieces:]
    if not first:
        total = refs[0][...] + total
        refs = refs[1:]
    load_ref, schur_high, schur_low, base_ref, total_ref = refs
    total_ref[...] = total
    base_ref[...] = load_ref[...] - dot3((schur_high[...], schur_low[...]), split(total))


def product_body(subs, count, base_ref, schur_high, schur_low, *refs):
    came = came_in(subs, refs[:count])
    size = came.shape[0]
    part = dot3((schur_high[:size, :size], schur_low[:size, :size]), split(came))
    put_shared(base_ref[:size] - part, refs[count:])


def follow_body(subs, count, last, base_ref, total_ref, schur_high, schur_low, *refs):
    arrived, shared, refs = refs[:count], refs[count : 2 * count], refs[2 * count :]
    came = came_in(subs, arrived)
    size = came.shape[0]
    part = dot3((schur_high[size:, :size], schur_low[size:, :size]), split(came))
    value = jnp.concatenate([ref[...] for ref in shared] + [base_ref[size:] - part], axis=0)
    iterate_ref, value_ref = refs[-2:]
    value_ref[...] = value
    iterate_ref[...] = jnp.concatenate([total_ref[:size] + came, total_ref[size:]], axis=0)
    if not last:
        test_high, test_low, projected_ref = refs[:3]
        projected_ref[...] = dot3((test_high[...], test_low[...]), split(value))


def restore_body(flipped_ref, value_ref, iterate_ref, base_ref, out_ref):
    flipped = flipped_ref[...]
    out_ref[...] = pick(flipped, iterate_ref[...])
    base_ref[...] = pick(flipped, value_ref[...])


def finish_body(subs, flipped_ref, base_ref, *refs):
    *arrived, out_hbm, out_ref, sems = refs
    came = came_in(subs, arrived)
    total = base_ref[...] + pick(flipped_ref[:, : came.shape[0]], came)
    copies = []
    size = out_ref.shape[0] // 4
    for step in range(4):
        rows = slice(step * size, (step + 1) * size)
        out_ref[rows] = total[rows]
        copy = pltpu.make_async_copy(out_ref.at[rows], out_hbm.at[rows], sems.at[step])
        copy.start()
        copies.append(copy)
    for copy in copies:
        copy.wait()


def swaps(count, stride, odd):
    partner = list(range(count))
    for low in range(count - stride):
        if (low // stride) % 2 == odd:
            partner[low], partner[low + stride] = low + stride, low
    return list(enumerate(partner)) if partner != list(range(count)) else []


def local(load_terms, schur_matrix, local_inverse, coarse_modes, cluster_inverse, row_blocks):
    load = load_terms[0, 0]
    basis = coarse_modes[0, 0]
    columns = cluster_inverse[0]
    blocks = row_blocks[0, 0]
    rows, loads = load.shape
    modes = basis.shape[1]
    shared_rows = blocks.shape[1]
    listed = 4 * shared_rows
    subs = lax.axis_size("sub")
    if lax.axis_size("grp") != GROUPS or sum(PIECES) != loads:
        raise ValueError("unexpected sizes")

    up = [(low, (low + 1) % subs) for low in range(subs)]
    down = [(target, source) for source, target in up]
    plans = [(0, swaps(subs, ROW_SUBS, 0)), (2, up), (1, down), (3, swaps(subs, ROW_SUBS, 1))]
    plans = [plan for plan in plans if plan[1]]
    count = len(plans)
    def exchange(parts):
        return [lax.ppermute(parts[place], "sub", pairs) for place, pairs in plans]

    def whole(width, kind=f32):
        return ((rows, width), kind)

    pair_plan = [(0, 1), (1, 0), (2, 3), (3, 2)]
    mirror_plan = [(0, 3), (3, 0), (1, 2), (2, 1)]
    shared = [((shared_rows, loads), f32)] * count
    outside = pl.BlockSpec(memory_space=pltpu.HBM)
    pieces = len(PIECES)
    size = rows * loads
    run = Chain()

    one_hot, load_near, sent, *parts = run(
        lambda *refs: listed_body(subs, count, *refs),
        [((listed, rows), bf16), whole(loads), ((modes, modes), f32)] + shared, 4 * listed * size, 16 * size,
        *[pltpu.with_memory_space_constraint(array, pltpu.HBM) for array in (blocks, load, columns)], ins=[outside] * 3,
        scratch=[pltpu.VMEM(blocks.shape, blocks.dtype), pltpu.SemaphoreType.DMA((2,))]
        + [pltpu.SemaphoreType.DMA] * 2,
    )
    arrived = exchange(parts)
    other = lax.ppermute(sent, "grp", pair_plan)
    chooser, flipped, basis_high, basis_low, test_high, test_low, ahead, ordered = run(
        lambda *refs: order_body(subs, *refs),
        [whole(rows, bf16)] * 2 + [whole(modes, bf16)] * 2 + [((modes, rows), bf16)] * 2
        + [((modes, loads), f32), whole(loads)],
        4 * rows * size, 24 * size, one_hot, load_near, basis,
    )
    mixers = run(blend_body, [((2 * modes, 2 * modes), bf16)] * 2, size, size, columns, other)
    value, iterate = ordered, None
    for iteration in range(ITERS):
        first, last = iteration == 0, iteration == ITERS - 1
        shapes = [((modes, width), f32) for width in PIECES]
        own = run(
            lambda *refs: project_body(subs, count, *refs), shapes, 6 * modes * size, 12 * size,
            ahead, test_high, test_low, *arrived,
        )
        theirs = [lax.ppermute(piece, "grp", pair_plan) for piece in own]
        kept, came = [], []
        for place, width in enumerate(PIECES):
            away, keep = run(
                mix_body, [((modes, width), f32)] * 2, HIDE * 24 * modes * modes * width, HIDE * 4 * rows * width,
                own[place], theirs[place], *mixers,
            )
            kept.append(keep)
            came.append(lax.ppermute(away, "grp", mirror_plan))
        if first:
            solve_high, solve_low = run(
                lambda *refs: solver_body(subs, listed, *refs), [whole(rows, bf16)] * 2, 8 * rows**3, 12 * size,
                chooser, local_inverse[0, 0],
            )
        (fine,) = run(
            lambda *refs: solve_body(subs, *refs), [whole(loads)], HIDE * 6 * rows * size, HIDE * 12 * size,
            value, solve_high, solve_low, *arrived,
        )
        steps = []
        for place, width in enumerate(PIECES):
            final = place == pieces - 1
            step, *parts = run(
                lambda kept, came, fine, high, low, *refs: correct_body(kept, came, fine, high, low, place, *refs),
                [whole(width)] + (shared if final else []), 6 * modes * rows * width, 12 * rows * width,
                kept[place], came[place], fine, basis_high, basis_low, *(steps if final else []),
            )
            steps.append(step)
        arrived = exchange(parts)
        if first:
            schur_high, schur_low = run(
                schur_body, [whole(rows, bf16)] * 2, 8 * rows**3, 12 * size, chooser, flipped, schur_matrix[0, 0],
            )
        base, total = run(
            lambda *refs: ahead_body(pieces, first, *refs), [whole(loads)] * 2, 6 * rows * size, 16 * size,
            *steps, *([] if first else [iterate]), ordered, schur_high, schur_low,
        )
        parts = run(
            lambda *refs: product_body(subs, count, *refs), shared, 2 * rows * size, 12 * size,
            base, schur_high, schur_low, *arrived,
        )
        before, arrived = arrived, exchange(parts)
        *projected, iterate, value = run(
            lambda *refs: follow_body(subs, count, last, *refs),
            ([] if last else [((modes, loads), f32)]) + [whole(loads)] * 2, 3 * rows * size, 16 * size,
            base, total, schur_high, schur_low, *before, *parts, *([] if last else [test_high, test_low]),
        )
        ahead = projected[0] if projected else None
    near, solution_rows = run(
        restore_body, [whole(loads)] * 2, 8 * rows * size, 10 * size, flipped, value, iterate,
    )
    (residual_rows,) = run(
        lambda *refs: finish_body(subs, *refs), [whole(loads)], 4 * rows * size, 10 * size,
        flipped, near, *arrived, places=[outside],
        scratch=[pltpu.VMEM((rows, loads), f32), pltpu.SemaphoreType.DMA((4,))],
    )
    return (solution_rows[None, None], residual_rows[None, None])


def solution(mesh):
    return jax.shard_map(
        local,
        mesh=mesh,
        in_specs=(
            P("sub", "grp", None, None),
            P("sub", "grp", None, None),
            P("sub", "grp", None, None),
            P("sub", "grp", None, None),
            P("sub", None, "grp"),
            P("sub", "grp", None, None),
        ),
        out_specs=(P("sub", "grp", None, None), P("sub", "grp", None, None)),
        check_vma=False,
    )
```

```python
import jax
import jax.numpy as jnp
from jax import lax
from jax.experimental import pallas as pl
from jax.experimental.pallas import tpu as pltpu
from jax.sharding import PartitionSpec as P

ITERS = 2
ROW_SUBS = 4
RELAX = 0.5
GROUPS = 4
HIDE = 16
PIECES = (128, 256)
f32 = jnp.float32
bf16 = jnp.bfloat16
NN = (((1,), (0,)), ((), ()))
NT = (((1,), (1,)), ((), ()))


class Chain:
    def __init__(self):
        self.last = None

    def __call__(self, body, outs, flops, moved, *operands, scratch=(), ins=None, places=None):
        count = len(operands)
        specs = [pl.BlockSpec(memory_space=pltpu.VMEM)] * count if ins is None else ins
        extra = []
        if self.last is not None:
            extra = [self.last]
            specs = specs + [pl.BlockSpec(memory_space=pl.ANY)]

        def whole_body(*refs):
            body(*refs[:count], *refs[count + len(extra) :])

        results = pl.pallas_call(
            whole_body,
            out_shape=[jax.ShapeDtypeStruct(shape, kind) for shape, kind in outs],
            in_specs=specs,
            out_specs=[pl.BlockSpec(memory_space=pltpu.VMEM)] * len(outs) if places is None else places,
            scratch_shapes=list(scratch),
            compiler_params=pltpu.CompilerParams(vmem_limit_bytes=24 * 1024 * 1024),
            cost_estimate=pl.CostEstimate(flops=flops, bytes_accessed=moved, transcendentals=0),
        )(*operands, *extra)
        self.last = results[0]
        return results


def dot(left, right, dims=NN):
    return lax.dot_general(left, right, dims, preferred_element_type=f32)


def split(value):
    high = value.astype(bf16)
    return high, (value - high.astype(f32)).astype(bf16)


def dot3(left, right):
    return dot(left[0], right[0]) + (dot(left[0], right[1]) + dot(left[1], right[0]))


def pick(chooser, value):
    high, low = split(value)
    return dot(chooser, high) + dot(chooser, low)


def sides(subs):
    sub = lax.axis_index("sub")
    low_side = sub % 2 == 0
    low_row = (sub // ROW_SUBS) % 2 == 0
    up, down = sub < subs - 1, sub > 0
    over, under = sub < subs - ROW_SUBS, sub >= ROW_SUBS
    return [
        (low_row, 3, 2, jnp.where(low_row, over, under)),
        (low_side, 0, 1, jnp.where(low_side, down, up)),
        (low_side, 1, 0, jnp.where(low_side, up, down)),
        (low_row, 2, 3, jnp.where(low_row, under, over)),
    ]


def put_shared(value, shared_refs):
    for place, ref in enumerate(shared_refs):
        width = ref.shape[0]
        ref[...] = value[place * width : (place + 1) * width]


def came_in(subs, shared_refs):
    return jnp.concatenate(
        [ref[...] * jnp.where(here, 1.0, 0.0) for ref, (_, _, _, here) in zip(shared_refs, sides(subs))], axis=0
    )


def add_shared(subs, value, shared_refs):
    came = came_in(subs, shared_refs)
    count = came.shape[0]
    return jnp.concatenate([value[:count] + came, value[count:]], axis=0)


def listed_body(subs, count, blocks_hbm, load_hbm, columns_hbm, listed_ref, load_ref, sent_ref, *refs):
    *shared_refs, blocks_ref, load_sems, blocks_sem, sent_sem = refs
    modes = sent_ref.shape[0]
    wanted = pl.multiple_of((3 - (lax.axis_index("grp") ^ 1)) * modes, modes)
    sent_copy = pltpu.make_async_copy(columns_hbm.at[pl.ds(wanted, modes), :], sent_ref, sent_sem)
    half = load_ref.shape[0] // 2
    halves = [slice(0, half), slice(half, 2 * half)]
    load_copies = [
        pltpu.make_async_copy(load_hbm.at[rows], load_ref.at[rows], load_sems.at[place])
        for place, rows in enumerate(halves)
    ]
    blocks_copy = pltpu.make_async_copy(blocks_hbm, blocks_ref, blocks_sem)
    blocks_copy.start()
    for copy in load_copies:
        copy.start()
    sent_copy.start()
    blocks_copy.wait()
    blocks = blocks_ref[...]
    placed = jnp.concatenate(
        [jnp.where(test, blocks[a : a + 1], blocks[b : b + 1]) for test, a, b, _ in sides(subs)], axis=0
    )
    upright = placed.astype(f32).T
    column = jnp.concatenate([upright[:, place : place + 1] for place in range(4)], axis=0)
    listed, total = column.shape[0], load_ref.shape[0]
    lane = lax.broadcasted_iota(jnp.int32, (listed, total), 1).astype(f32)
    first = (column == lane).astype(f32).astype(bf16)
    listed_ref[...] = first
    wanted_rows = count * blocks.shape[1]
    sent = None
    for copy, rows in zip(load_copies, halves):
        copy.wait()
        part = pick(first[:wanted_rows, rows], load_ref[rows])
        sent = part if sent is None else sent + part
    put_shared(sent, shared_refs)
    sent_copy.wait()


def order_body(subs, listed_ref, load_ref, basis_ref,
               chooser_ref, flipped_ref, basis_high, basis_low, test_high, test_low, ahead_ref, ordered_ref):
    listed, total = listed_ref.shape
    first = listed_ref[...].astype(f32)
    unlisted = 1.0 - jnp.sum(first, axis=0, keepdims=True)
    before = (
        lax.broadcasted_iota(jnp.int32, (total, total), 0)
        < lax.broadcasted_iota(jnp.int32, (total, total), 1)
    ).astype(f32).astype(bf16)
    rank = dot(jnp.broadcast_to(unlisted, (8, total)).astype(bf16), before)[:1]
    slot = lax.broadcasted_iota(jnp.int32, (total - listed, total), 0).astype(f32)
    last = jnp.where(rank == slot, unlisted, 0.0)
    chooser = jnp.concatenate([first, last], axis=0)
    flipped_ref[...] = chooser.T.astype(bf16)
    weighted = (chooser * weight_column(subs, listed // 4, total)).astype(bf16)
    chooser = chooser.astype(bf16)
    chooser_ref[...] = chooser
    ordered = pick(chooser, load_ref[...])
    ordered_ref[...] = ordered
    for part, out, turned in zip(split(basis_ref[...]), (basis_high, basis_low), (test_high, test_low)):
        placed = dot(weighted, part)
        out[...] = placed.astype(bf16)
        turned[...] = placed.T.astype(bf16)
    ahead_ref[...] = dot3((test_high[...], test_low[...]), split(ordered))


def weight_column(subs, width, total):
    parts = [jnp.full((width, 1), jnp.where(here, 0.5, 1.0), f32) for _, _, _, here in sides(subs)]
    return jnp.concatenate(parts + [jnp.ones((total - 4 * width, 1), f32)], axis=0)


def rows_of(columns_ref, place):
    modes = columns_ref.shape[1]
    return columns_ref[pl.ds(pl.multiple_of(place * modes, modes), modes), :]


def solver_body(subs, listed, chooser_ref, solve_ref, solve_high, solve_low):
    chooser = chooser_ref[...]
    weighted = (chooser.astype(f32) * weight_column(subs, listed // 4, chooser.shape[0])).astype(bf16)
    for part, out in zip(split(solve_ref[...] * RELAX), (solve_high, solve_low)):
        out[...] = dot(dot(weighted, part).astype(bf16), weighted, NT).astype(bf16)


def schur_body(chooser_ref, flipped_ref, schur_ref, schur_high, schur_low):
    chooser, flipped = chooser_ref[...], flipped_ref[...]
    for part, out in zip(split(schur_ref[...]), (schur_high, schur_low)):
        out[...] = dot(dot(chooser, part).astype(bf16), flipped).astype(bf16)


def blend_body(columns_ref, other_ref, mix_high, mix_low):
    grp = lax.axis_index("grp")
    away = jnp.concatenate([rows_of(columns_ref, 3 - grp), other_ref[...]], axis=1)
    kept = jnp.concatenate([rows_of(columns_ref, grp), rows_of(columns_ref, grp ^ 1).T], axis=1)
    mix_high[...], mix_low[...] = split(jnp.concatenate([away, kept], axis=0) * RELAX)


def cut():
    return [(sum(PIECES[:place]), width) for place, width in enumerate(PIECES)]


def project_body(subs, count, ahead_ref, test_high, test_low, *refs):
    came = came_in(subs, refs[:count])
    size = came.shape[0]
    projected = ahead_ref[...] + dot3((test_high[:, :size], test_low[:, :size]), split(came))
    for ref, (start, width) in zip(refs[count:], cut()):
        ref[...] = projected[:, start : start + width]


def solve_body(subs, value_ref, solve_high, solve_low, *refs):
    halves = split(add_shared(subs, value_ref[...], refs[:-1]))
    refs[-1][...] = dot3((solve_high[...], solve_low[...]), halves)


def mix_body(own_ref, other_ref, mix_high, mix_low, away_ref, kept_ref):
    modes = away_ref.shape[0]
    pair = jnp.concatenate([own_ref[...], other_ref[...]], axis=0)
    mixed = dot3((mix_high[...], mix_low[...]), split(pair))
    away_ref[...] = mixed[:modes]
    kept_ref[...] = mixed[modes:]


def correct_body(kept_ref, came_ref, fine_ref, basis_high, basis_low, place, *refs):
    coarse = kept_ref[...] + came_ref[...]
    start, width = cut()[place]
    fine = fine_ref[:, start : start + width]
    step = fine + dot3((basis_high[...], basis_low[...]), split(coarse))
    formers = place if len(refs) > 1 else 0
    former_refs, out_ref = refs[:formers], refs[formers]
    out_ref[...] = step
    for at, ref in enumerate(refs[formers + 1 :]):
        size = ref.shape[0]
        rows = slice(at * size, (at + 1) * size)
        ref[...] = jnp.concatenate([former[rows] for former in former_refs] + [step[rows]], axis=1)


def ahead_body(pieces, first, *refs):
    total = jnp.concatenate([ref[...] for ref in refs[:pieces]], axis=1)
    refs = refs[pieces:]
    if not first:
        total = refs[0][...] + total
        refs = refs[1:]
    load_ref, schur_high, schur_low, base_ref, total_ref = refs
    total_ref[...] = total
    base_ref[...] = load_ref[...] - dot3((schur_high[...], schur_low[...]), split(total))


def product_body(subs, count, base_ref, schur_high, schur_low, *refs):
    came = came_in(subs, refs[:count])
    size = came.shape[0]
    part = dot3((schur_high[:size, :size], schur_low[:size, :size]), split(came))
    put_shared(base_ref[:size] - part, refs[count:])


def follow_body(subs, count, last, base_ref, total_ref, schur_high, schur_low, *refs):
    arrived, shared, refs = refs[:count], refs[count : 2 * count], refs[2 * count :]
    came = came_in(subs, arrived)
    size = came.shape[0]
    part = dot3((schur_high[size:, :size], schur_low[size:, :size]), split(came))
    value = jnp.concatenate([ref[...] for ref in shared] + [base_ref[size:] - part], axis=0)
    iterate_ref, value_ref = refs[-2:]
    value_ref[...] = value
    iterate_ref[...] = jnp.concatenate([total_ref[:size] + came, total_ref[size:]], axis=0)
    if not last:
        test_high, test_low, projected_ref = refs[:3]
        projected_ref[...] = dot3((test_high[...], test_low[...]), split(value))


def restore_body(flipped_ref, value_ref, iterate_ref, base_ref, out_ref):
    flipped = flipped_ref[...]
    out_ref[...] = pick(flipped, iterate_ref[...])
    base_ref[...] = pick(flipped, value_ref[...])


def finish_body(subs, flipped_ref, base_ref, *refs):
    *arrived, out_hbm, out_ref, sems = refs
    came = came_in(subs, arrived)
    total = base_ref[...] + pick(flipped_ref[:, : came.shape[0]], came)
    copies = []
    size = out_ref.shape[0] // 4
    for step in range(4):
        rows = slice(step * size, (step + 1) * size)
        out_ref[rows] = total[rows]
        copy = pltpu.make_async_copy(out_ref.at[rows], out_hbm.at[rows], sems.at[step])
        copy.start()
        copies.append(copy)
    for copy in copies:
        copy.wait()


def swaps(count, stride, odd):
    partner = {}
    for low in range(count - stride):
        if (low // stride) % 2 == odd:
            partner[low], partner[low + stride] = low + stride, low
    if not partner:
        return []
    left = [index for index in range(count) if index not in partner]
    half = len(left) // 2
    for low, high in zip(left[:half], left[half:]):
        partner[low], partner[high] = high, low
    return sorted(partner.items())


def local(load_terms, schur_matrix, local_inverse, coarse_modes, cluster_inverse, row_blocks):
    load = load_terms[0, 0]
    basis = coarse_modes[0, 0]
    columns = cluster_inverse[0]
    blocks = row_blocks[0, 0]
    rows, loads = load.shape
    modes = basis.shape[1]
    shared_rows = blocks.shape[1]
    listed = 4 * shared_rows
    subs = lax.axis_size("sub")
    if lax.axis_size("grp") != GROUPS or sum(PIECES) != loads:
        raise ValueError("unexpected sizes")

    plans = [swaps(subs, ROW_SUBS, 0), swaps(subs, 1, 1), swaps(subs, 1, 0), swaps(subs, ROW_SUBS, 1)]
    plans = [plan for plan in plans if plan]
    count = len(plans)

    def exchange(parts):
        return [lax.ppermute(part, "sub", plan) for part, plan in zip(parts, plans)]

    def whole(width, kind=f32):
        return ((rows, width), kind)

    pair_plan = [(0, 1), (1, 0), (2, 3), (3, 2)]
    mirror_plan = [(0, 3), (3, 0), (1, 2), (2, 1)]
    shared = [((shared_rows, loads), f32)] * count
    outside = pl.BlockSpec(memory_space=pltpu.HBM)
    pieces = len(PIECES)
    size = rows * loads
    run = Chain()

    one_hot, load_near, sent, *parts = run(
        lambda *refs: listed_body(subs, count, *refs),
        [((listed, rows), bf16), whole(loads), ((modes, modes), f32)] + shared, 4 * listed * size, 16 * size,
        *[pltpu.with_memory_space_constraint(array, pltpu.HBM) for array in (blocks, load, columns)], ins=[outside] * 3,
        scratch=[pltpu.VMEM(blocks.shape, blocks.dtype), pltpu.SemaphoreType.DMA((2,))]
        + [pltpu.SemaphoreType.DMA] * 2,
    )
    arrived = exchange(parts)
    other = lax.ppermute(sent, "grp", pair_plan)
    chooser, flipped, basis_high, basis_low, test_high, test_low, ahead, ordered = run(
        lambda *refs: order_body(subs, *refs),
        [whole(rows, bf16)] * 2 + [whole(modes, bf16)] * 2 + [((modes, rows), bf16)] * 2
        + [((modes, loads), f32), whole(loads)],
        4 * rows * size, 24 * size, one_hot, load_near, basis,
    )
    mixers = run(blend_body, [((2 * modes, 2 * modes), bf16)] * 2, size, size, columns, other)
    value, iterate = ordered, None
    for iteration in range(ITERS):
        first, last = iteration == 0, iteration == ITERS - 1
        shapes = [((modes, width), f32) for width in PIECES]
        own = run(
            lambda *refs: project_body(subs, count, *refs), shapes, 6 * modes * size, 12 * size,
            ahead, test_high, test_low, *arrived,
        )
        theirs = [lax.ppermute(piece, "grp", pair_plan) for piece in own]
        kept, came = [], []
        for place, width in enumerate(PIECES):
            away, keep = run(
                mix_body, [((modes, width), f32)] * 2, HIDE * 24 * modes * modes * width, HIDE * 4 * rows * width,
                own[place], theirs[place], *mixers,
            )
            kept.append(keep)
            came.append(lax.ppermute(away, "grp", mirror_plan))
        if first:
            solve_high, solve_low = run(
                lambda *refs: solver_body(subs, listed, *refs), [whole(rows, bf16)] * 2, 8 * rows**3, 12 * size,
                chooser, local_inverse[0, 0],
            )
        (fine,) = run(
            lambda *refs: solve_body(subs, *refs), [whole(loads)], HIDE * 6 * rows * size, HIDE * 12 * size,
            value, solve_high, solve_low, *arrived,
        )
        steps = []
        for place, width in enumerate(PIECES):
            final = place == pieces - 1
            step, *parts = run(
                lambda kept, came, fine, high, low, *refs: correct_body(kept, came, fine, high, low, place, *refs),
                [whole(width)] + (shared if final else []), 6 * modes * rows * width, 12 * rows * width,
                kept[place], came[place], fine, basis_high, basis_low, *(steps if final else []),
            )
            steps.append(step)
        arrived = exchange(parts)
        if first:
            schur_high, schur_low = run(
                schur_body, [whole(rows, bf16)] * 2, 8 * rows**3, 12 * size, chooser, flipped, schur_matrix[0, 0],
            )
        base, total = run(
            lambda *refs: ahead_body(pieces, first, *refs), [whole(loads)] * 2, 6 * rows * size, 16 * size,
            *steps, *([] if first else [iterate]), ordered, schur_high, schur_low,
        )
        parts = run(
            lambda *refs: product_body(subs, count, *refs), shared, 2 * rows * size, 12 * size,
            base, schur_high, schur_low, *arrived,
        )
        before, arrived = arrived, exchange(parts)
        *projected, iterate, value = run(
            lambda *refs: follow_body(subs, count, last, *refs),
            ([] if last else [((modes, loads), f32)]) + [whole(loads)] * 2, 3 * rows * size, 16 * size,
            base, total, schur_high, schur_low, *before, *parts, *([] if last else [test_high, test_low]),
        )
        ahead = projected[0] if projected else None
    near, solution_rows = run(
        restore_body, [whole(loads)] * 2, 8 * rows * size, 10 * size, flipped, value, iterate,
    )
    (residual_rows,) = run(
        lambda *refs: finish_body(subs, *refs), [whole(loads)], 4 * rows * size, 10 * size,
        flipped, near, *arrived, places=[outside],
        scratch=[pltpu.VMEM((rows, loads), f32), pltpu.SemaphoreType.DMA((4,))],
    )
    return (solution_rows[None, None], residual_rows[None, None])


def solution(mesh):
    return jax.shard_map(
        local,
        mesh=mesh,
        in_specs=(
            P("sub", "grp", None, None),
            P("sub", "grp", None, None),
            P("sub", "grp", None, None),
            P("sub", "grp", None, None),
            P("sub", None, "grp"),
            P("sub", "grp", None, None),
        ),
        out_specs=(P("sub", "grp", None, None), P("sub", "grp", None, None)),
        check_vma=False,
    )
```

```python
import jax
import jax.numpy as jnp
from jax import lax
from jax.experimental import pallas as pl
from jax.experimental.pallas import tpu as pltpu
from jax.sharding import PartitionSpec as P

ITERS = 2
ROW_SUBS = 4
RELAX = 0.5
GROUPS = 4
HIDE = 16
PIECES = (128, 256)
f32 = jnp.float32
bf16 = jnp.bfloat16
NN = (((1,), (0,)), ((), ()))
NT = (((1,), (1,)), ((), ()))


class Chain:
    def __init__(self):
        self.last = None

    def __call__(self, body, outs, flops, moved, *operands, scratch=(), ins=None, places=None):
        count = len(operands)
        specs = [pl.BlockSpec(memory_space=pltpu.VMEM)] * count if ins is None else ins
        extra = []
        if self.last is not None:
            extra = [self.last]
            specs = specs + [pl.BlockSpec(memory_space=pl.ANY)]

        def whole_body(*refs):
            body(*refs[:count], *refs[count + len(extra) :])

        results = pl.pallas_call(
            whole_body,
            out_shape=[jax.ShapeDtypeStruct(shape, kind) for shape, kind in outs],
            in_specs=specs,
            out_specs=[pl.BlockSpec(memory_space=pltpu.VMEM)] * len(outs) if places is None else places,
            scratch_shapes=list(scratch),
            compiler_params=pltpu.CompilerParams(vmem_limit_bytes=24 * 1024 * 1024),
            cost_estimate=pl.CostEstimate(flops=flops, bytes_accessed=moved, transcendentals=0),
        )(*operands, *extra)
        self.last = results[0]
        return results


def dot(left, right, dims=NN):
    return lax.dot_general(left, right, dims, preferred_element_type=f32)


def split(value):
    high = value.astype(bf16)
    return high, (value - high.astype(f32)).astype(bf16)


def dot3(left, right):
    return dot(left[0], right[0]) + (dot(left[0], right[1]) + dot(left[1], right[0]))


def pick(chooser, value):
    high, low = split(value)
    return dot(chooser, high) + dot(chooser, low)


def sides(subs):
    sub = lax.axis_index("sub")
    low_side = sub % 2 == 0
    low_row = (sub // ROW_SUBS) % 2 == 0
    up, down = sub < subs - 1, sub > 0
    over, under = sub < subs - ROW_SUBS, sub >= ROW_SUBS
    return [
        (low_side, 0, 1, jnp.where(low_side, down, up)),
        (low_row, 3, 2, jnp.where(low_row, over, under)),
        (low_side, 1, 0, jnp.where(low_side, up, down)),
        (low_row, 2, 3, jnp.where(low_row, under, over)),
    ]


def put_shared(value, shared_refs):
    for place, ref in enumerate(shared_refs):
        width = ref.shape[0]
        ref[...] = value[place * width : (place + 1) * width]


def came_in(subs, shared_refs):
    return jnp.concatenate(
        [ref[...] * jnp.where(here, 1.0, 0.0) for ref, (_, _, _, here) in zip(shared_refs, sides(subs))], axis=0
    )


def add_shared(subs, value, shared_refs):
    came = came_in(subs, shared_refs)
    count = came.shape[0]
    return jnp.concatenate([value[:count] + came, value[count:]], axis=0)


def listed_body(subs, count, blocks_hbm, load_hbm, columns_hbm, listed_ref, load_ref, sent_ref, *refs):
    *shared_refs, blocks_ref, load_sems, blocks_sem, sent_sem = refs
    modes = sent_ref.shape[0]
    wanted = pl.multiple_of((3 - (lax.axis_index("grp") ^ 1)) * modes, modes)
    sent_copy = pltpu.make_async_copy(columns_hbm.at[pl.ds(wanted, modes), :], sent_ref, sent_sem)
    half = load_ref.shape[0] // 2
    halves = [slice(0, half), slice(half, 2 * half)]
    load_copies = [
        pltpu.make_async_copy(load_hbm.at[rows], load_ref.at[rows], load_sems.at[place])
        for place, rows in enumerate(halves)
    ]
    blocks_copy = pltpu.make_async_copy(blocks_hbm, blocks_ref, blocks_sem)
    blocks_copy.start()
    for copy in load_copies:
        copy.start()
    sent_copy.start()
    blocks_copy.wait()
    blocks = blocks_ref[...]
    placed = jnp.concatenate(
        [jnp.where(test, blocks[a : a + 1], blocks[b : b + 1]) for test, a, b, _ in sides(subs)], axis=0
    )
    upright = placed.astype(f32).T
    column = jnp.concatenate([upright[:, place : place + 1] for place in range(4)], axis=0)
    listed, total = column.shape[0], load_ref.shape[0]
    lane = lax.broadcasted_iota(jnp.int32, (listed, total), 1).astype(f32)
    first = (column == lane).astype(f32).astype(bf16)
    listed_ref[...] = first
    wanted_rows = count * blocks.shape[1]
    sent = None
    for copy, rows in zip(load_copies, halves):
        copy.wait()
        part = pick(first[:wanted_rows, rows], load_ref[rows])
        sent = part if sent is None else sent + part
    put_shared(sent, shared_refs)
    sent_copy.wait()


def order_body(subs, listed_ref, load_ref, basis_ref,
               chooser_ref, flipped_ref, basis_high, basis_low, test_high, test_low, ahead_ref, ordered_ref):
    listed, total = listed_ref.shape
    first = listed_ref[...].astype(f32)
    unlisted = 1.0 - jnp.sum(first, axis=0, keepdims=True)
    before = (
        lax.broadcasted_iota(jnp.int32, (total, total), 0)
        < lax.broadcasted_iota(jnp.int32, (total, total), 1)
    ).astype(f32).astype(bf16)
    rank = dot(jnp.broadcast_to(unlisted, (8, total)).astype(bf16), before)[:1]
    slot = lax.broadcasted_iota(jnp.int32, (total - listed, total), 0).astype(f32)
    last = jnp.where(rank == slot, unlisted, 0.0)
    chooser = jnp.concatenate([first, last], axis=0)
    flipped_ref[...] = chooser.T.astype(bf16)
    weighted = (chooser * weight_column(subs, listed // 4, total)).astype(bf16)
    chooser = chooser.astype(bf16)
    chooser_ref[...] = chooser
    ordered = pick(chooser, load_ref[...])
    ordered_ref[...] = ordered
    for part, out, turned in zip(split(basis_ref[...]), (basis_high, basis_low), (test_high, test_low)):
        placed = dot(weighted, part)
        out[...] = placed.astype(bf16)
        turned[...] = placed.T.astype(bf16)
    ahead_ref[...] = dot3((test_high[...], test_low[...]), split(ordered))


def weight_column(subs, width, total):
    parts = [jnp.full((width, 1), jnp.where(here, 0.5, 1.0), f32) for _, _, _, here in sides(subs)]
    return jnp.concatenate(parts + [jnp.ones((total - 4 * width, 1), f32)], axis=0)


def rows_of(columns_ref, place):
    modes = columns_ref.shape[1]
    return columns_ref[pl.ds(pl.multiple_of(place * modes, modes), modes), :]


def solver_body(subs, listed, chooser_ref, solve_ref, solve_high, solve_low):
    chooser = chooser_ref[...]
    weighted = (chooser.astype(f32) * weight_column(subs, listed // 4, chooser.shape[0])).astype(bf16)
    for part, out in zip(split(solve_ref[...] * RELAX), (solve_high, solve_low)):
        out[...] = dot(dot(weighted, part).astype(bf16), weighted, NT).astype(bf16)


def schur_body(chooser_ref, flipped_ref, schur_ref, schur_high, schur_low):
    chooser, flipped = chooser_ref[...], flipped_ref[...]
    for part, out in zip(split(schur_ref[...]), (schur_high, schur_low)):
        out[...] = dot(dot(chooser, part).astype(bf16), flipped).astype(bf16)


def blend_body(columns_ref, other_ref, mix_high, mix_low):
    grp = lax.axis_index("grp")
    away = jnp.concatenate([rows_of(columns_ref, 3 - grp), other_ref[...]], axis=1)
    kept = jnp.concatenate([rows_of(columns_ref, grp), rows_of(columns_ref, grp ^ 1).T], axis=1)
    mix_high[...], mix_low[...] = split(jnp.concatenate([away, kept], axis=0) * RELAX)


def cut():
    return [(sum(PIECES[:place]), width) for place, width in enumerate(PIECES)]


def project_body(subs, count, ahead_ref, test_high, test_low, *refs):
    came = came_in(subs, refs[:count])
    size = came.shape[0]
    projected = ahead_ref[...] + dot3((test_high[:, :size], test_low[:, :size]), split(came))
    for ref, (start, width) in zip(refs[count:], cut()):
        ref[...] = projected[:, start : start + width]


def solve_body(subs, value_ref, solve_high, solve_low, *refs):
    halves = split(add_shared(subs, value_ref[...], refs[:-1]))
    refs[-1][...] = dot3((solve_high[...], solve_low[...]), halves)


def mix_body(own_ref, other_ref, mix_high, mix_low, away_ref, kept_ref):
    modes = away_ref.shape[0]
    pair = jnp.concatenate([own_ref[...], other_ref[...]], axis=0)
    mixed = dot3((mix_high[...], mix_low[...]), split(pair))
    away_ref[...] = mixed[:modes]
    kept_ref[...] = mixed[modes:]


def correct_body(kept_ref, came_ref, fine_ref, basis_high, basis_low, place, *refs):
    coarse = kept_ref[...] + came_ref[...]
    start, width = cut()[place]
    fine = fine_ref[:, start : start + width]
    step = fine + dot3((basis_high[...], basis_low[...]), split(coarse))
    formers = place if len(refs) > 1 else 0
    former_refs, out_ref = refs[:formers], refs[formers]
    out_ref[...] = step
    for at, ref in enumerate(refs[formers + 1 :]):
        size = ref.shape[0]
        rows = slice(at * size, (at + 1) * size)
        ref[...] = jnp.concatenate([former[rows] for former in former_refs] + [step[rows]], axis=1)


def ahead_body(pieces, first, *refs):
    total = jnp.concatenate([ref[...] for ref in refs[:pieces]], axis=1)
    refs = refs[pieces:]
    if not first:
        total = refs[0][...] + total
        refs = refs[1:]
    load_ref, schur_high, schur_low, base_ref, total_ref = refs
    total_ref[...] = total
    base_ref[...] = load_ref[...] - dot3((schur_high[...], schur_low[...]), split(total))


def product_body(subs, count, base_ref, schur_high, schur_low, *refs):
    came = came_in(subs, refs[:count])
    size = came.shape[0]
    part = dot3((schur_high[:size, :size], schur_low[:size, :size]), split(came))
    put_shared(base_ref[:size] - part, refs[count:])


def follow_body(subs, count, last, base_ref, total_ref, schur_high, schur_low, *refs):
    arrived, shared, refs = refs[:count], refs[count : 2 * count], refs[2 * count :]
    came = came_in(subs, arrived)
    size = came.shape[0]
    part = dot3((schur_high[size:, :size], schur_low[size:, :size]), split(came))
    value = jnp.concatenate([ref[...] for ref in shared] + [base_ref[size:] - part], axis=0)
    iterate_ref, value_ref = refs[-2:]
    value_ref[...] = value
    iterate_ref[...] = jnp.concatenate([total_ref[:size] + came, total_ref[size:]], axis=0)
    if not last:
        test_high, test_low, projected_ref = refs[:3]
        projected_ref[...] = dot3((test_high[...], test_low[...]), split(value))


def restore_body(flipped_ref, value_ref, iterate_ref, base_ref, out_ref):
    flipped = flipped_ref[...]
    out_ref[...] = pick(flipped, iterate_ref[...])
    base_ref[...] = pick(flipped, value_ref[...])


def finish_body(subs, flipped_ref, base_ref, *refs):
    *arrived, out_hbm, out_ref, sems = refs
    came = came_in(subs, arrived)
    total = base_ref[...] + pick(flipped_ref[:, : came.shape[0]], came)
    copies = []
    size = out_ref.shape[0] // 4
    for step in range(4):
        rows = slice(step * size, (step + 1) * size)
        out_ref[rows] = total[rows]
        copy = pltpu.make_async_copy(out_ref.at[rows], out_hbm.at[rows], sems.at[step])
        copy.start()
        copies.append(copy)
    for copy in copies:
        copy.wait()


def swaps(count, stride, odd):
    partner = {}
    for low in range(count - stride):
        if (low // stride) % 2 == odd:
            partner[low], partner[low + stride] = low + stride, low
    if not partner:
        return []
    left = [index for index in range(count) if index not in partner]
    half = len(left) // 2
    for low, high in zip(left[:half], left[half:]):
        partner[low], partner[high] = high, low
    return sorted(partner.items())


def local(load_terms, schur_matrix, local_inverse, coarse_modes, cluster_inverse, row_blocks):
    load = load_terms[0, 0]
    basis = coarse_modes[0, 0]
    columns = cluster_inverse[0]
    blocks = row_blocks[0, 0]
    rows, loads = load.shape
    modes = basis.shape[1]
    shared_rows = blocks.shape[1]
    listed = 4 * shared_rows
    subs = lax.axis_size("sub")
    if lax.axis_size("grp") != GROUPS or sum(PIECES) != loads:
        raise ValueError("unexpected sizes")

    plans = [swaps(subs, 1, 1), swaps(subs, ROW_SUBS, 0), swaps(subs, 1, 0), swaps(subs, ROW_SUBS, 1)]
    plans = [plan for plan in plans if plan]
    count = len(plans)

    def exchange(parts):
        return [lax.ppermute(part, "sub", plan) for part, plan in zip(parts, plans)]

    def whole(width, kind=f32):
        return ((rows, width), kind)

    pair_plan = [(0, 1), (1, 0), (2, 3), (3, 2)]
    mirror_plan = [(0, 3), (3, 0), (1, 2), (2, 1)]
    shared = [((shared_rows, loads), f32)] * count
    outside = pl.BlockSpec(memory_space=pltpu.HBM)
    pieces = len(PIECES)
    size = rows * loads
    run = Chain()

    one_hot, load_near, sent, *parts = run(
        lambda *refs: listed_body(subs, count, *refs),
        [((listed, rows), bf16), whole(loads), ((modes, modes), f32)] + shared, 4 * listed * size, 16 * size,
        *[pltpu.with_memory_space_constraint(array, pltpu.HBM) for array in (blocks, load, columns)], ins=[outside] * 3,
        scratch=[pltpu.VMEM(blocks.shape, blocks.dtype), pltpu.SemaphoreType.DMA((2,))]
        + [pltpu.SemaphoreType.DMA] * 2,
    )
    arrived = exchange(parts)
    other = lax.ppermute(sent, "grp", pair_plan)
    chooser, flipped, basis_high, basis_low, test_high, test_low, ahead, ordered = run(
        lambda *refs: order_body(subs, *refs),
        [whole(rows, bf16)] * 2 + [whole(modes, bf16)] * 2 + [((modes, rows), bf16)] * 2
        + [((modes, loads), f32), whole(loads)],
        4 * rows * size, 24 * size, one_hot, load_near, basis,
    )
    mixers = run(blend_body, [((2 * modes, 2 * modes), bf16)] * 2, size, size, columns, other)
    value, iterate = ordered, None
    for iteration in range(ITERS):
        first, last = iteration == 0, iteration == ITERS - 1
        shapes = [((modes, width), f32) for width in PIECES]
        own = run(
            lambda *refs: project_body(subs, count, *refs), shapes, 6 * modes * size, 12 * size,
            ahead, test_high, test_low, *arrived,
        )
        theirs = [lax.ppermute(piece, "grp", pair_plan) for piece in own]
        kept, came = [], []
        for place, width in enumerate(PIECES):
            away, keep = run(
                mix_body, [((modes, width), f32)] * 2, HIDE * 24 * modes * modes * width, HIDE * 4 * rows * width,
                own[place], theirs[place], *mixers,
            )
            kept.append(keep)
            came.append(lax.ppermute(away, "grp", mirror_plan))
        if first:
            solve_high, solve_low = run(
                lambda *refs: solver_body(subs, listed, *refs), [whole(rows, bf16)] * 2, 8 * rows**3, 12 * size,
                chooser, local_inverse[0, 0],
            )
        (fine,) = run(
            lambda *refs: solve_body(subs, *refs), [whole(loads)], HIDE * 6 * rows * size, HIDE * 12 * size,
            value, solve_high, solve_low, *arrived,
        )
        steps = []
        for place, width in enumerate(PIECES):
            final = place == pieces - 1
            step, *parts = run(
                lambda kept, came, fine, high, low, *refs: correct_body(kept, came, fine, high, low, place, *refs),
                [whole(width)] + (shared if final else []), 6 * modes * rows * width, 12 * rows * width,
                kept[place], came[place], fine, basis_high, basis_low, *(steps if final else []),
            )
            steps.append(step)
        arrived = exchange(parts)
        if first:
            schur_high, schur_low = run(
                schur_body, [whole(rows, bf16)] * 2, 8 * rows**3, 12 * size, chooser, flipped, schur_matrix[0, 0],
            )
        base, total = run(
            lambda *refs: ahead_body(pieces, first, *refs), [whole(loads)] * 2, 6 * rows * size, 16 * size,
            *steps, *([] if first else [iterate]), ordered, schur_high, schur_low,
        )
        parts = run(
            lambda *refs: product_body(subs, count, *refs), shared, 2 * rows * size, 12 * size,
            base, schur_high, schur_low, *arrived,
        )
        before, arrived = arrived, exchange(parts)
        *projected, iterate, value = run(
            lambda *refs: follow_body(subs, count, last, *refs),
            ([] if last else [((modes, loads), f32)]) + [whole(loads)] * 2, 3 * rows * size, 16 * size,
            base, total, schur_high, schur_low, *before, *parts, *([] if last else [test_high, test_low]),
        )
        ahead = projected[0] if projected else None
    near, solution_rows = run(
        restore_body, [whole(loads)] * 2, 8 * rows * size, 10 * size, flipped, value, iterate,
    )
    (residual_rows,) = run(
        lambda *refs: finish_body(subs, *refs), [whole(loads)], 4 * rows * size, 10 * size,
        flipped, near, *arrived, places=[outside],
        scratch=[pltpu.VMEM((rows, loads), f32), pltpu.SemaphoreType.DMA((4,))],
    )
    return (solution_rows[None, None], residual_rows[None, None])


def solution(mesh):
    return jax.shard_map(
        local,
        mesh=mesh,
        in_specs=(
            P("sub", "grp", None, None),
            P("sub", "grp", None, None),
            P("sub", "grp", None, None),
            P("sub", "grp", None, None),
            P("sub", None, "grp"),
            P("sub", "grp", None, None),
        ),
        out_specs=(P("sub", "grp", None, None), P("sub", "grp", None, None)),
        check_vma=False,
    )
```

```python
import jax
import jax.numpy as jnp
from jax import lax
from jax.experimental import pallas as pl
from jax.experimental.pallas import tpu as pltpu
from jax.sharding import PartitionSpec as P

ITERS = 2
ROW_SUBS = 4
RELAX = 0.5
GROUPS = 4
HIDE = 16
PIECES = (128, 256)
f32 = jnp.float32
bf16 = jnp.bfloat16
NN = (((1,), (0,)), ((), ()))
NT = (((1,), (1,)), ((), ()))


class Chain:
    def __init__(self):
        self.last = None

    def __call__(self, body, outs, flops, moved, *operands, scratch=(), ins=None, places=None):
        count = len(operands)
        specs = [pl.BlockSpec(memory_space=pltpu.VMEM)] * count if ins is None else ins
        extra = []
        if self.last is not None:
            extra = [self.last]
            specs = specs + [pl.BlockSpec(memory_space=pl.ANY)]

        def whole_body(*refs):
            body(*refs[:count], *refs[count + len(extra) :])

        results = pl.pallas_call(
            whole_body,
            out_shape=[jax.ShapeDtypeStruct(shape, kind) for shape, kind in outs],
            in_specs=specs,
            out_specs=[pl.BlockSpec(memory_space=pltpu.VMEM)] * len(outs) if places is None else places,
            scratch_shapes=list(scratch),
            compiler_params=pltpu.CompilerParams(vmem_limit_bytes=24 * 1024 * 1024),
            cost_estimate=pl.CostEstimate(flops=flops, bytes_accessed=moved, transcendentals=0),
        )(*operands, *extra)
        self.last = results[0]
        return results


def dot(left, right, dims=NN):
    return lax.dot_general(left, right, dims, preferred_element_type=f32)


def split(value):
    high = value.astype(bf16)
    return high, (value - high.astype(f32)).astype(bf16)


def dot3(left, right):
    return dot(left[0], right[0]) + (dot(left[0], right[1]) + dot(left[1], right[0]))


def pick(chooser, value):
    high, low = split(value)
    return dot(chooser, high) + dot(chooser, low)


def sides(subs):
    sub = lax.axis_index("sub")
    low_side = sub % 2 == 0
    low_row = (sub // ROW_SUBS) % 2 == 0
    up, down = sub < subs - 1, sub > 0
    over, under = sub < subs - ROW_SUBS, sub >= ROW_SUBS
    return [
        (low_row, 3, 2, jnp.where(low_row, over, under)),
        (low_side, 0, 1, jnp.where(low_side, down, up)),
        (low_side, 1, 0, jnp.where(low_side, up, down)),
        (low_row, 2, 3, jnp.where(low_row, under, over)),
    ]


def put_shared(value, shared_refs):
    for place, ref in enumerate(shared_refs):
        width = ref.shape[0]
        ref[...] = value[place * width : (place + 1) * width]


def came_in(subs, shared_refs):
    return jnp.concatenate(
        [ref[...] * jnp.where(here, 1.0, 0.0) for ref, (_, _, _, here) in zip(shared_refs, sides(subs))], axis=0
    )


def add_shared(subs, value, shared_refs):
    came = came_in(subs, shared_refs)
    count = came.shape[0]
    return jnp.concatenate([value[:count] + came, value[count:]], axis=0)


def listed_body(subs, count, blocks_hbm, load_hbm, columns_hbm, listed_ref, load_ref, sent_ref, *refs):
    *shared_refs, blocks_ref, load_sems, blocks_sem, sent_sem = refs
    modes = sent_ref.shape[0]
    wanted = pl.multiple_of((3 - (lax.axis_index("grp") ^ 1)) * modes, modes)
    sent_copy = pltpu.make_async_copy(columns_hbm.at[pl.ds(wanted, modes), :], sent_ref, sent_sem)
    half = load_ref.shape[0] // 2
    halves = [slice(0, half), slice(half, 2 * half)]
    load_copies = [
        pltpu.make_async_copy(load_hbm.at[rows], load_ref.at[rows], load_sems.at[place])
        for place, rows in enumerate(halves)
    ]
    blocks_copy = pltpu.make_async_copy(blocks_hbm, blocks_ref, blocks_sem)
    blocks_copy.start()
    for copy in load_copies:
        copy.start()
    sent_copy.start()
    blocks_copy.wait()
    blocks = blocks_ref[...]
    placed = jnp.concatenate(
        [jnp.where(test, blocks[a : a + 1], blocks[b : b + 1]) for test, a, b, _ in sides(subs)], axis=0
    )
    upright = placed.astype(f32).T
    column = jnp.concatenate([upright[:, place : place + 1] for place in range(4)], axis=0)
    listed, total = column.shape[0], load_ref.shape[0]
    lane = lax.broadcasted_iota(jnp.int32, (listed, total), 1).astype(f32)
    first = (column == lane).astype(f32).astype(bf16)
    listed_ref[...] = first
    wanted_rows = count * blocks.shape[1]
    sent = None
    for copy, rows in zip(load_copies, halves):
        copy.wait()
        part = pick(first[:wanted_rows, rows], load_ref[rows])
        sent = part if sent is None else sent + part
    put_shared(sent, shared_refs)
    sent_copy.wait()


def order_body(subs, listed_ref, load_ref, basis_ref,
               chooser_ref, flipped_ref, basis_high, basis_low, test_high, test_low, ahead_ref, ordered_ref):
    listed, total = listed_ref.shape
    first = listed_ref[...].astype(f32)
    unlisted = 1.0 - jnp.sum(first, axis=0, keepdims=True)
    before = (
        lax.broadcasted_iota(jnp.int32, (total, total), 0)
        < lax.broadcasted_iota(jnp.int32, (total, total), 1)
    ).astype(f32).astype(bf16)
    rank = dot(jnp.broadcast_to(unlisted, (8, total)).astype(bf16), before)[:1]
    slot = lax.broadcasted_iota(jnp.int32, (total - listed, total), 0).astype(f32)
    last = jnp.where(rank == slot, unlisted, 0.0)
    chooser = jnp.concatenate([first, last], axis=0)
    flipped_ref[...] = chooser.T.astype(bf16)
    weighted = (chooser * weight_column(subs, listed // 4, total)).astype(bf16)
    chooser = chooser.astype(bf16)
    chooser_ref[...] = chooser
    ordered = pick(chooser, load_ref[...])
    ordered_ref[...] = ordered
    for part, out, turned in zip(split(basis_ref[...]), (basis_high, basis_low), (test_high, test_low)):
        placed = dot(weighted, part)
        out[...] = placed.astype(bf16)
        turned[...] = placed.T.astype(bf16)
    ahead_ref[...] = dot3((test_high[...], test_low[...]), split(ordered))


def weight_column(subs, width, total):
    parts = [jnp.full((width, 1), jnp.where(here, 0.5, 1.0), f32) for _, _, _, here in sides(subs)]
    return jnp.concatenate(parts + [jnp.ones((total - 4 * width, 1), f32)], axis=0)


def rows_of(columns_ref, place):
    modes = columns_ref.shape[1]
    return columns_ref[pl.ds(pl.multiple_of(place * modes, modes), modes), :]


def solver_body(subs, listed, chooser_ref, solve_ref, solve_high, solve_low):
    chooser = chooser_ref[...]
    weighted = (chooser.astype(f32) * weight_column(subs, listed // 4, chooser.shape[0])).astype(bf16)
    for part, out in zip(split(solve_ref[...] * RELAX), (solve_high, solve_low)):
        out[...] = dot(dot(weighted, part).astype(bf16), weighted, NT).astype(bf16)


def schur_body(chooser_ref, flipped_ref, schur_ref, schur_high, schur_low):
    chooser, flipped = chooser_ref[...], flipped_ref[...]
    for part, out in zip(split(schur_ref[...]), (schur_high, schur_low)):
        out[...] = dot(dot(chooser, part).astype(bf16), flipped).astype(bf16)


def blend_body(columns_ref, other_ref, mix_high, mix_low):
    grp = lax.axis_index("grp")
    away = jnp.concatenate([rows_of(columns_ref, 3 - grp), other_ref[...]], axis=1)
    kept = jnp.concatenate([rows_of(columns_ref, grp), rows_of(columns_ref, grp ^ 1).T], axis=1)
    mix_high[...], mix_low[...] = split(jnp.concatenate([away, kept], axis=0) * RELAX)


def cut():
    return [(sum(PIECES[:place]), width) for place, width in enumerate(PIECES)]


def project_body(subs, count, ahead_ref, test_high, test_low, *refs):
    came = came_in(subs, refs[:count])
    size = came.shape[0]
    projected = ahead_ref[...] + dot3((test_high[:, :size], test_low[:, :size]), split(came))
    for ref, (start, width) in zip(refs[count:], cut()):
        ref[...] = projected[:, start : start + width]


def solve_body(subs, value_ref, solve_high, solve_low, *refs):
    halves = split(add_shared(subs, value_ref[...], refs[:-1]))
    refs[-1][...] = dot3((solve_high[...], solve_low[...]), halves)


def mix_body(own_ref, other_ref, mix_high, mix_low, away_ref, kept_ref):
    modes = away_ref.shape[0]
    pair = jnp.concatenate([own_ref[...], other_ref[...]], axis=0)
    mixed = dot3((mix_high[...], mix_low[...]), split(pair))
    away_ref[...] = mixed[:modes]
    kept_ref[...] = mixed[modes:]


def correct_body(kept_ref, came_ref, fine_ref, basis_high, basis_low, place, *refs):
    coarse = kept_ref[...] + came_ref[...]
    start, width = cut()[place]
    fine = fine_ref[:, start : start + width]
    step = fine + dot3((basis_high[...], basis_low[...]), split(coarse))
    formers = place if len(refs) > 1 else 0
    former_refs, out_ref = refs[:formers], refs[formers]
    out_ref[...] = step
    for at, ref in enumerate(refs[formers + 1 :]):
        size = ref.shape[0]
        rows = slice(at * size, (at + 1) * size)
        ref[...] = jnp.concatenate([former[rows] for former in former_refs] + [step[rows]], axis=1)


def ahead_body(pieces, first, *refs):
    total = jnp.concatenate([ref[...] for ref in refs[:pieces]], axis=1)
    refs = refs[pieces:]
    if not first:
        total = refs[0][...] + total
        refs = refs[1:]
    load_ref, schur_high, schur_low, base_ref, total_ref = refs
    total_ref[...] = total
    base_ref[...] = load_ref[...] - dot3((schur_high[...], schur_low[...]), split(total))


def product_body(subs, count, base_ref, schur_high, schur_low, *refs):
    came = came_in(subs, refs[:count])
    size = came.shape[0]
    part = dot3((schur_high[:size, :size], schur_low[:size, :size]), split(came))
    put_shared(base_ref[:size] - part, refs[count:])


def follow_body(subs, count, last, base_ref, total_ref, schur_high, schur_low, *refs):
    arrived, shared, refs = refs[:count], refs[count : 2 * count], refs[2 * count :]
    came = came_in(subs, arrived)
    size = came.shape[0]
    part = dot3((schur_high[size:, :size], schur_low[size:, :size]), split(came))
    value = jnp.concatenate([ref[...] for ref in shared] + [base_ref[size:] - part], axis=0)
    iterate_ref, value_ref = refs[-2:]
    value_ref[...] = value
    iterate_ref[...] = jnp.concatenate([total_ref[:size] + came, total_ref[size:]], axis=0)
    if not last:
        test_high, test_low, projected_ref = refs[:3]
        projected_ref[...] = dot3((test_high[...], test_low[...]), split(value))


def restore_body(flipped_ref, value_ref, iterate_ref, base_ref, out_ref):
    flipped = flipped_ref[...]
    out_ref[...] = pick(flipped, iterate_ref[...])
    base_ref[...] = pick(flipped, value_ref[...])


def finish_body(subs, flipped_ref, base_ref, *refs):
    *arrived, out_hbm, out_ref, sems = refs
    came = came_in(subs, arrived)
    total = base_ref[...] + pick(flipped_ref[:, : came.shape[0]], came)
    copies = []
    size = out_ref.shape[0] // 4
    for step in range(4):
        rows = slice(step * size, (step + 1) * size)
        out_ref[rows] = total[rows]
        copy = pltpu.make_async_copy(out_ref.at[rows], out_hbm.at[rows], sems.at[step])
        copy.start()
        copies.append(copy)
    for copy in copies:
        copy.wait()


def swaps(count, stride, odd):
    partner = {}
    for low in range(count - stride):
        if (low // stride) % 2 == odd:
            partner[low], partner[low + stride] = low + stride, low
    if not partner:
        return []
    left = [index for index in range(count) if index not in partner]
    half = len(left) // 2
    for low, high in zip(left[:half], left[half:]):
        partner[low], partner[high] = high, low
    return sorted(partner.items())


def local(load_terms, schur_matrix, local_inverse, coarse_modes, cluster_inverse, row_blocks):
    load = load_terms[0, 0]
    basis = coarse_modes[0, 0]
    columns = cluster_inverse[0]
    blocks = row_blocks[0, 0]
    rows, loads = load.shape
    modes = basis.shape[1]
    shared_rows = blocks.shape[1]
    listed = 4 * shared_rows
    subs = lax.axis_size("sub")
    if lax.axis_size("grp") != GROUPS or sum(PIECES) != loads:
        raise ValueError("unexpected sizes")

    plans = [swaps(subs, ROW_SUBS, 0), swaps(subs, 1, 1), swaps(subs, 1, 0), swaps(subs, ROW_SUBS, 1)]
    plans = [plan for plan in plans if plan]
    count = len(plans)

    def exchange(parts):
        return [lax.ppermute(part, "sub", plan) for part, plan in zip(parts, plans)]

    def whole(width, kind=f32):
        return ((rows, width), kind)

    pair_plan = [(0, 1), (1, 0), (2, 3), (3, 2)]
    mirror_plan = [(0, 3), (3, 0), (1, 2), (2, 1)]
    shared = [((shared_rows, loads), f32)] * count
    outside = pl.BlockSpec(memory_space=pltpu.HBM)
    pieces = len(PIECES)
    size = rows * loads
    run = Chain()

    one_hot, load_near, sent, *parts = run(
        lambda *refs: listed_body(subs, count, *refs),
        [((listed, rows), bf16), whole(loads), ((modes, modes), f32)] + shared, 4 * listed * size, 16 * size,
        *[pltpu.with_memory_space_constraint(array, pltpu.HBM) for array in (blocks, load, columns)], ins=[outside] * 3,
        scratch=[pltpu.VMEM(blocks.shape, blocks.dtype), pltpu.SemaphoreType.DMA((2,))]
        + [pltpu.SemaphoreType.DMA] * 2,
    )
    arrived = exchange(parts)
    other = lax.ppermute(sent, "grp", pair_plan)
    chooser, flipped, basis_high, basis_low, test_high, test_low, ahead, ordered = run(
        lambda *refs: order_body(subs, *refs),
        [whole(rows, bf16)] * 2 + [whole(modes, bf16)] * 2 + [((modes, rows), bf16)] * 2
        + [((modes, loads), f32), whole(loads)],
        4 * rows * size, 24 * size, one_hot, load_near, basis,
    )
    value, iterate = ordered, None
    for iteration in range(ITERS):
        first, last = iteration == 0, iteration == ITERS - 1
        shapes = [((modes, width), f32) for width in PIECES]
        own = run(
            lambda *refs: project_body(subs, count, *refs), shapes, 6 * modes * size, 12 * size,
            ahead, test_high, test_low, *arrived,
        )
        theirs = [lax.ppermute(piece, "grp", pair_plan) for piece in own]
        if first:
            mixers = run(blend_body, [((2 * modes, 2 * modes), bf16)] * 2, size, size, columns, other)
        kept, came = [], []
        for place, width in enumerate(PIECES):
            away, keep = run(
                mix_body, [((modes, width), f32)] * 2, HIDE * 24 * modes * modes * width, HIDE * 4 * rows * width,
                own[place], theirs[place], *mixers,
            )
            kept.append(keep)
            came.append(lax.ppermute(away, "grp", mirror_plan))
        if first:
            solve_high, solve_low = run(
                lambda *refs: solver_body(subs, listed, *refs), [whole(rows, bf16)] * 2, 8 * rows**3, 12 * size,
                chooser, local_inverse[0, 0],
            )
        (fine,) = run(
            lambda *refs: solve_body(subs, *refs), [whole(loads)], HIDE * 6 * rows * size, HIDE * 12 * size,
            value, solve_high, solve_low, *arrived,
        )
        steps = []
        for place, width in enumerate(PIECES):
            final = place == pieces - 1
            step, *parts = run(
                lambda kept, came, fine, high, low, *refs: correct_body(kept, came, fine, high, low, place, *refs),
                [whole(width)] + (shared if final else []), 6 * modes * rows * width, 12 * rows * width,
                kept[place], came[place], fine, basis_high, basis_low, *(steps if final else []),
            )
            steps.append(step)
        arrived = exchange(parts)
        if first:
            schur_high, schur_low = run(
                schur_body, [whole(rows, bf16)] * 2, 8 * rows**3, 12 * size, chooser, flipped, schur_matrix[0, 0],
            )
        base, total = run(
            lambda *refs: ahead_body(pieces, first, *refs), [whole(loads)] * 2, 6 * rows * size, 16 * size,
            *steps, *([] if first else [iterate]), ordered, schur_high, schur_low,
        )
        parts = run(
            lambda *refs: product_body(subs, count, *refs), shared, 2 * rows * size, 12 * size,
            base, schur_high, schur_low, *arrived,
        )
        before, arrived = arrived, exchange(parts)
        *projected, iterate, value = run(
            lambda *refs: follow_body(subs, count, last, *refs),
            ([] if last else [((modes, loads), f32)]) + [whole(loads)] * 2, 3 * rows * size, 16 * size,
            base, total, schur_high, schur_low, *before, *parts, *([] if last else [test_high, test_low]),
        )
        ahead = projected[0] if projected else None
    near, solution_rows = run(
        restore_body, [whole(loads)] * 2, 8 * rows * size, 10 * size, flipped, value, iterate,
    )
    (residual_rows,) = run(
        lambda *refs: finish_body(subs, *refs), [whole(loads)], 4 * rows * size, 10 * size,
        flipped, near, *arrived, places=[outside],
        scratch=[pltpu.VMEM((rows, loads), f32), pltpu.SemaphoreType.DMA((4,))],
    )
    return (solution_rows[None, None], residual_rows[None, None])


def solution(mesh):
    return jax.shard_map(
        local,
        mesh=mesh,
        in_specs=(
            P("sub", "grp", None, None),
            P("sub", "grp", None, None),
            P("sub", "grp", None, None),
            P("sub", "grp", None, None),
            P("sub", None, "grp"),
            P("sub", "grp", None, None),
        ),
        out_specs=(P("sub", "grp", None, None), P("sub", "grp", None, None)),
        check_vma=False,
    )
```

```python
import jax
import jax.numpy as jnp
from jax import lax
from jax.experimental import pallas as pl
from jax.experimental.pallas import tpu as pltpu
from jax.sharding import PartitionSpec as P

ITERS = 2
ROW_SUBS = 4
RELAX = 0.5
GROUPS = 4
HIDE = 16
PIECES = (128, 256)
f32 = jnp.float32
bf16 = jnp.bfloat16
NN = (((1,), (0,)), ((), ()))
NT = (((1,), (1,)), ((), ()))


class Chain:
    def __init__(self):
        self.last = None

    def __call__(self, body, outs, flops, moved, *operands, scratch=(), ins=None, places=None):
        count = len(operands)
        specs = [pl.BlockSpec(memory_space=pltpu.VMEM)] * count if ins is None else ins
        extra = []
        if self.last is not None:
            extra = [self.last]
            specs = specs + [pl.BlockSpec(memory_space=pl.ANY)]

        def whole_body(*refs):
            body(*refs[:count], *refs[count + len(extra) :])

        results = pl.pallas_call(
            whole_body,
            out_shape=[jax.ShapeDtypeStruct(shape, kind) for shape, kind in outs],
            in_specs=specs,
            out_specs=[pl.BlockSpec(memory_space=pltpu.VMEM)] * len(outs) if places is None else places,
            scratch_shapes=list(scratch),
            compiler_params=pltpu.CompilerParams(vmem_limit_bytes=24 * 1024 * 1024),
            cost_estimate=pl.CostEstimate(flops=flops, bytes_accessed=moved, transcendentals=0),
        )(*operands, *extra)
        self.last = results[0]
        return results


def dot(left, right, dims=NN):
    return lax.dot_general(left, right, dims, preferred_element_type=f32)


def split(value):
    high = value.astype(bf16)
    return high, (value - high.astype(f32)).astype(bf16)


def dot3(left, right):
    return dot(left[0], right[0]) + (dot(left[0], right[1]) + dot(left[1], right[0]))


def pick(chooser, value):
    high, low = split(value)
    return dot(chooser, high) + dot(chooser, low)


def sides(subs):
    sub = lax.axis_index("sub")
    low_side = sub % 2 == 0
    low_row = (sub // ROW_SUBS) % 2 == 0
    up, down = sub < subs - 1, sub > 0
    over, under = sub < subs - ROW_SUBS, sub >= ROW_SUBS
    return [
        (low_row, 3, 2, jnp.where(low_row, over, under)),
        (low_side, 0, 1, jnp.where(low_side, down, up)),
        (low_side, 1, 0, jnp.where(low_side, up, down)),
        (low_row, 2, 3, jnp.where(low_row, under, over)),
    ]


def put_shared(value, shared_refs):
    for place, ref in enumerate(shared_refs):
        width = ref.shape[0]
        ref[...] = value[place * width : (place + 1) * width]


def came_in(subs, shared_refs):
    return jnp.concatenate(
        [ref[...] * jnp.where(here, 1.0, 0.0) for ref, (_, _, _, here) in zip(shared_refs, sides(subs))], axis=0
    )


def add_shared(subs, value, shared_refs):
    came = came_in(subs, shared_refs)
    count = came.shape[0]
    return jnp.concatenate([value[:count] + came, value[count:]], axis=0)


def listed_body(subs, count, blocks_hbm, load_hbm, columns_hbm, listed_ref, load_ref, sent_ref, *refs):
    *shared_refs, blocks_ref, load_sems, blocks_sem, sent_sem = refs
    modes = sent_ref.shape[0]
    wanted = pl.multiple_of((lax.axis_index("grp") ^ 3) * modes, modes)
    sent_copy = pltpu.make_async_copy(columns_hbm.at[pl.ds(wanted, modes), :], sent_ref, sent_sem)
    half = load_ref.shape[0] // 2
    halves = [slice(0, half), slice(half, 2 * half)]
    load_copies = [
        pltpu.make_async_copy(load_hbm.at[rows], load_ref.at[rows], load_sems.at[place])
        for place, rows in enumerate(halves)
    ]
    blocks_copy = pltpu.make_async_copy(blocks_hbm, blocks_ref, blocks_sem)
    blocks_copy.start()
    for copy in load_copies:
        copy.start()
    sent_copy.start()
    blocks_copy.wait()
    blocks = blocks_ref[...]
    placed = jnp.concatenate(
        [jnp.where(test, blocks[a : a + 1], blocks[b : b + 1]) for test, a, b, _ in sides(subs)], axis=0
    )
    upright = placed.astype(f32).T
    column = jnp.concatenate([upright[:, place : place + 1] for place in range(4)], axis=0)
    listed, total = column.shape[0], load_ref.shape[0]
    lane = lax.broadcasted_iota(jnp.int32, (listed, total), 1).astype(f32)
    first = (column == lane).astype(f32).astype(bf16)
    listed_ref[...] = first
    wanted_rows = count * blocks.shape[1]
    sent = None
    for copy, rows in zip(load_copies, halves):
        copy.wait()
        part = pick(first[:wanted_rows, rows], load_ref[rows])
        sent = part if sent is None else sent + part
    put_shared(sent, shared_refs)
    sent_copy.wait()


def order_body(subs, listed_ref, load_ref, basis_ref,
               chooser_ref, flipped_ref, basis_high, basis_low, test_high, test_low, ahead_ref, ordered_ref):
    listed, total = listed_ref.shape
    first = listed_ref[...].astype(f32)
    unlisted = 1.0 - jnp.sum(first, axis=0, keepdims=True)
    before = (
        lax.broadcasted_iota(jnp.int32, (total, total), 0)
        < lax.broadcasted_iota(jnp.int32, (total, total), 1)
    ).astype(f32).astype(bf16)
    rank = dot(jnp.broadcast_to(unlisted, (8, total)).astype(bf16), before)[:1]
    slot = lax.broadcasted_iota(jnp.int32, (total - listed, total), 0).astype(f32)
    last = jnp.where(rank == slot, unlisted, 0.0)
    chooser = jnp.concatenate([first, last], axis=0)
    flipped_ref[...] = chooser.T.astype(bf16)
    weighted = (chooser * weight_column(subs, listed // 4, total)).astype(bf16)
    chooser = chooser.astype(bf16)
    chooser_ref[...] = chooser
    ordered = pick(chooser, load_ref[...])
    ordered_ref[...] = ordered
    for part, out, turned in zip(split(basis_ref[...]), (basis_high, basis_low), (test_high, test_low)):
        placed = dot(weighted, part)
        out[...] = placed.astype(bf16)
        turned[...] = placed.T.astype(bf16)
    ahead_ref[...] = dot3((test_high[...], test_low[...]), split(ordered))


def weight_column(subs, width, total):
    parts = [jnp.full((width, 1), jnp.where(here, 0.5, 1.0), f32) for _, _, _, here in sides(subs)]
    return jnp.concatenate(parts + [jnp.ones((total - 4 * width, 1), f32)], axis=0)


def rows_of(columns_ref, place):
    modes = columns_ref.shape[1]
    return columns_ref[pl.ds(pl.multiple_of(place * modes, modes), modes), :]


def solver_body(subs, listed, chooser_ref, solve_ref, solve_high, solve_low):
    chooser = chooser_ref[...]
    weighted = (chooser.astype(f32) * weight_column(subs, listed // 4, chooser.shape[0])).astype(bf16)
    for part, out in zip(split(solve_ref[...] * RELAX), (solve_high, solve_low)):
        out[...] = dot(dot(weighted, part).astype(bf16), weighted, NT).astype(bf16)


def schur_body(chooser_ref, flipped_ref, schur_ref, schur_high, schur_low):
    chooser, flipped = chooser_ref[...], flipped_ref[...]
    for part, out in zip(split(schur_ref[...]), (schur_high, schur_low)):
        out[...] = dot(dot(chooser, part).astype(bf16), flipped).astype(bf16)


def blend_body(columns_ref, other_ref, mix_high, mix_low):
    grp = lax.axis_index("grp")
    away = jnp.concatenate([rows_of(columns_ref, grp ^ 2), other_ref[...]], axis=1)
    kept = jnp.concatenate([rows_of(columns_ref, grp), rows_of(columns_ref, grp ^ 1).T], axis=1)
    mix_high[...], mix_low[...] = split(jnp.concatenate([away, kept], axis=0) * RELAX)


def cut():
    return [(sum(PIECES[:place]), width) for place, width in enumerate(PIECES)]


def project_body(subs, count, ahead_ref, test_high, test_low, *refs):
    came = came_in(subs, refs[:count])
    size = came.shape[0]
    projected = ahead_ref[...] + dot3((test_high[:, :size], test_low[:, :size]), split(came))
    for ref, (start, width) in zip(refs[count:], cut()):
        ref[...] = projected[:, start : start + width]


def solve_body(subs, value_ref, solve_high, solve_low, *refs):
    halves = split(add_shared(subs, value_ref[...], refs[:-1]))
    refs[-1][...] = dot3((solve_high[...], solve_low[...]), halves)


def mix_body(own_ref, other_ref, mix_high, mix_low, away_ref, kept_ref):
    modes = away_ref.shape[0]
    pair = jnp.concatenate([own_ref[...], other_ref[...]], axis=0)
    mixed = dot3((mix_high[...], mix_low[...]), split(pair))
    away_ref[...] = mixed[:modes]
    kept_ref[...] = mixed[modes:]


def correct_body(kept_ref, came_ref, fine_ref, basis_high, basis_low, place, *refs):
    coarse = kept_ref[...] + came_ref[...]
    start, width = cut()[place]
    fine = fine_ref[:, start : start + width]
    step = fine + dot3((basis_high[...], basis_low[...]), split(coarse))
    formers = place if len(refs) > 1 else 0
    former_refs, out_ref = refs[:formers], refs[formers]
    out_ref[...] = step
    for at, ref in enumerate(refs[formers + 1 :]):
        size = ref.shape[0]
        rows = slice(at * size, (at + 1) * size)
        ref[...] = jnp.concatenate([former[rows] for former in former_refs] + [step[rows]], axis=1)


def ahead_body(pieces, first, *refs):
    total = jnp.concatenate([ref[...] for ref in refs[:pieces]], axis=1)
    refs = refs[pieces:]
    if not first:
        total = refs[0][...] + total
        refs = refs[1:]
    load_ref, schur_high, schur_low, base_ref, total_ref = refs
    total_ref[...] = total
    base_ref[...] = load_ref[...] - dot3((schur_high[...], schur_low[...]), split(total))


def product_body(subs, count, base_ref, schur_high, schur_low, *refs):
    came = came_in(subs, refs[:count])
    size = came.shape[0]
    part = dot3((schur_high[:size, :size], schur_low[:size, :size]), split(came))
    put_shared(base_ref[:size] - part, refs[count:])


def follow_body(subs, count, last, base_ref, total_ref, schur_high, schur_low, *refs):
    arrived, shared, refs = refs[:count], refs[count : 2 * count], refs[2 * count :]
    came = came_in(subs, arrived)
    size = came.shape[0]
    part = dot3((schur_high[size:, :size], schur_low[size:, :size]), split(came))
    value = jnp.concatenate([ref[...] for ref in shared] + [base_ref[size:] - part], axis=0)
    iterate_ref, value_ref = refs[-2:]
    value_ref[...] = value
    iterate_ref[...] = jnp.concatenate([total_ref[:size] + came, total_ref[size:]], axis=0)
    if not last:
        test_high, test_low, projected_ref = refs[:3]
        projected_ref[...] = dot3((test_high[...], test_low[...]), split(value))


def restore_body(flipped_ref, value_ref, iterate_ref, base_ref, out_ref):
    flipped = flipped_ref[...]
    out_ref[...] = pick(flipped, iterate_ref[...])
    base_ref[...] = pick(flipped, value_ref[...])


def finish_body(subs, flipped_ref, base_ref, *refs):
    *arrived, out_hbm, out_ref, sems = refs
    came = came_in(subs, arrived)
    total = base_ref[...] + pick(flipped_ref[:, : came.shape[0]], came)
    copies = []
    size = out_ref.shape[0] // 4
    for step in range(4):
        rows = slice(step * size, (step + 1) * size)
        out_ref[rows] = total[rows]
        copy = pltpu.make_async_copy(out_ref.at[rows], out_hbm.at[rows], sems.at[step])
        copy.start()
        copies.append(copy)
    for copy in copies:
        copy.wait()


def swaps(count, stride, odd):
    partner = {}
    for low in range(count - stride):
        if (low // stride) % 2 == odd:
            partner[low], partner[low + stride] = low + stride, low
    if not partner:
        return []
    left = [index for index in range(count) if index not in partner]
    half = len(left) // 2
    for low, high in zip(left[:half], left[half:]):
        partner[low], partner[high] = high, low
    return sorted(partner.items())


def local(load_terms, schur_matrix, local_inverse, coarse_modes, cluster_inverse, row_blocks):
    load = load_terms[0, 0]
    basis = coarse_modes[0, 0]
    columns = cluster_inverse[0]
    blocks = row_blocks[0, 0]
    rows, loads = load.shape
    modes = basis.shape[1]
    shared_rows = blocks.shape[1]
    listed = 4 * shared_rows
    subs = lax.axis_size("sub")
    if lax.axis_size("grp") != GROUPS or sum(PIECES) != loads:
        raise ValueError("unexpected sizes")

    plans = [swaps(subs, ROW_SUBS, 0), swaps(subs, 1, 1), swaps(subs, 1, 0), swaps(subs, ROW_SUBS, 1)]
    plans = [plan for plan in plans if plan]
    count = len(plans)

    def exchange(parts):
        return [lax.ppermute(part, "sub", plan) for part, plan in zip(parts, plans)]

    def whole(width, kind=f32):
        return ((rows, width), kind)

    pair_plan = [(0, 1), (1, 0), (2, 3), (3, 2)]
    across_plan = [(0, 2), (1, 3), (2, 0), (3, 1)]
    shared = [((shared_rows, loads), f32)] * count
    outside = pl.BlockSpec(memory_space=pltpu.HBM)
    pieces = len(PIECES)
    size = rows * loads
    run = Chain()

    one_hot, load_near, sent, *parts = run(
        lambda *refs: listed_body(subs, count, *refs),
        [((listed, rows), bf16), whole(loads), ((modes, modes), f32)] + shared, 4 * listed * size, 16 * size,
        *[pltpu.with_memory_space_constraint(array, pltpu.HBM) for array in (blocks, load, columns)], ins=[outside] * 3,
        scratch=[pltpu.VMEM(blocks.shape, blocks.dtype), pltpu.SemaphoreType.DMA((2,))]
        + [pltpu.SemaphoreType.DMA] * 2,
    )
    arrived = exchange(parts)
    other = lax.ppermute(sent, "grp", pair_plan)
    chooser, flipped, basis_high, basis_low, test_high, test_low, ahead, ordered = run(
        lambda *refs: order_body(subs, *refs),
        [whole(rows, bf16)] * 2 + [whole(modes, bf16)] * 2 + [((modes, rows), bf16)] * 2
        + [((modes, loads), f32), whole(loads)],
        4 * rows * size, 24 * size, one_hot, load_near, basis,
    )
    value, iterate = ordered, None
    for iteration in range(ITERS):
        first, last = iteration == 0, iteration == ITERS - 1
        shapes = [((modes, width), f32) for width in PIECES]
        own = run(
            lambda *refs: project_body(subs, count, *refs), shapes, 6 * modes * size, 12 * size,
            ahead, test_high, test_low, *arrived,
        )
        theirs = [lax.ppermute(piece, "grp", pair_plan) for piece in own]
        if first:
            mixers = run(blend_body, [((2 * modes, 2 * modes), bf16)] * 2, size, size, columns, other)
        kept, came = [], []
        for place, width in enumerate(PIECES):
            away, keep = run(
                mix_body, [((modes, width), f32)] * 2, HIDE * 24 * modes * modes * width, HIDE * 4 * rows * width,
                own[place], theirs[place], *mixers,
            )
            kept.append(keep)
            came.append(lax.ppermute(away, "grp", across_plan))
        if first:
            solve_high, solve_low = run(
                lambda *refs: solver_body(subs, listed, *refs), [whole(rows, bf16)] * 2, 8 * rows**3, 12 * size,
                chooser, local_inverse[0, 0],
            )
        (fine,) = run(
            lambda *refs: solve_body(subs, *refs), [whole(loads)], HIDE * 6 * rows * size, HIDE * 12 * size,
            value, solve_high, solve_low, *arrived,
        )
        steps = []
        for place, width in enumerate(PIECES):
            final = place == pieces - 1
            step, *parts = run(
                lambda kept, came, fine, high, low, *refs: correct_body(kept, came, fine, high, low, place, *refs),
                [whole(width)] + (shared if final else []), 6 * modes * rows * width, 12 * rows * width,
                kept[place], came[place], fine, basis_high, basis_low, *(steps if final else []),
            )
            steps.append(step)
        arrived = exchange(parts)
        if first:
            schur_high, schur_low = run(
                schur_body, [whole(rows, bf16)] * 2, 8 * rows**3, 12 * size, chooser, flipped, schur_matrix[0, 0],
            )
        base, total = run(
            lambda *refs: ahead_body(pieces, first, *refs), [whole(loads)] * 2, 6 * rows * size, 16 * size,
            *steps, *([] if first else [iterate]), ordered, schur_high, schur_low,
        )
        parts = run(
            lambda *refs: product_body(subs, count, *refs), shared, 2 * rows * size, 12 * size,
            base, schur_high, schur_low, *arrived,
        )
        before, arrived = arrived, exchange(parts)
        *projected, iterate, value = run(
            lambda *refs: follow_body(subs, count, last, *refs),
            ([] if last else [((modes, loads), f32)]) + [whole(loads)] * 2, 3 * rows * size, 16 * size,
            base, total, schur_high, schur_low, *before, *parts, *([] if last else [test_high, test_low]),
        )
        ahead = projected[0] if projected else None
    near, solution_rows = run(
        restore_body, [whole(loads)] * 2, 8 * rows * size, 10 * size, flipped, value, iterate,
    )
    (residual_rows,) = run(
        lambda *refs: finish_body(subs, *refs), [whole(loads)], 4 * rows * size, 10 * size,
        flipped, near, *arrived, places=[outside],
        scratch=[pltpu.VMEM((rows, loads), f32), pltpu.SemaphoreType.DMA((4,))],
    )
    return (solution_rows[None, None], residual_rows[None, None])


def solution(mesh):
    return jax.shard_map(
        local,
        mesh=mesh,
        in_specs=(
            P("sub", "grp", None, None),
            P("sub", "grp", None, None),
            P("sub", "grp", None, None),
            P("sub", "grp", None, None),
            P("sub", None, "grp"),
            P("sub", "grp", None, None),
        ),
        out_specs=(P("sub", "grp", None, None), P("sub", "grp", None, None)),
        check_vma=False,
    )
```

```python
import jax
import jax.numpy as jnp
from jax import lax
from jax.experimental import pallas as pl
from jax.experimental.pallas import tpu as pltpu
from jax.sharding import PartitionSpec as P

ITERS = 2
ROW_SUBS = 4
RELAX = 0.5
GROUPS = 4
PIECES = (128, 128, 128)
f32 = jnp.float32
bf16 = jnp.bfloat16
NN = (((1,), (0,)), ((), ()))
NT = (((1,), (1,)), ((), ()))


class Chain:
    def __init__(self):
        self.last = None

    def __call__(self, body, outs, flops, moved, *operands, scratch=(), ins=None, places=None):
        count = len(operands)
        specs = [pl.BlockSpec(memory_space=pltpu.VMEM)] * count if ins is None else ins
        extra = []
        if self.last is not None:
            extra = [self.last]
            specs = specs + [pl.BlockSpec(memory_space=pl.ANY)]

        def whole_body(*refs):
            body(*refs[:count], *refs[count + len(extra) :])

        results = pl.pallas_call(
            whole_body,
            out_shape=[jax.ShapeDtypeStruct(shape, kind) for shape, kind in outs],
            in_specs=specs,
            out_specs=[pl.BlockSpec(memory_space=pltpu.VMEM)] * len(outs) if places is None else places,
            scratch_shapes=list(scratch),
            compiler_params=pltpu.CompilerParams(vmem_limit_bytes=24 * 1024 * 1024),
            cost_estimate=pl.CostEstimate(flops=flops, bytes_accessed=moved, transcendentals=0),
        )(*operands, *extra)
        self.last = results[0]
        return results


def dot(left, right, dims=NN):
    return lax.dot_general(left, right, dims, preferred_element_type=f32)


def split(value):
    high = value.astype(bf16)
    return high, (value - high.astype(f32)).astype(bf16)


def dot3(left, right):
    return dot(left[0], right[0]) + (dot(left[0], right[1]) + dot(left[1], right[0]))


def pick(chooser, value):
    high, low = split(value)
    return dot(chooser, high) + dot(chooser, low)


def sides(subs):
    sub = lax.axis_index("sub")
    low_side = sub % 2 == 0
    low_row = (sub // ROW_SUBS) % 2 == 0
    up, down = sub < subs - 1, sub > 0
    over, under = sub < subs - ROW_SUBS, sub >= ROW_SUBS
    return [
        (low_row, 3, 2, jnp.where(low_row, over, under)),
        (low_side, 0, 1, jnp.where(low_side, down, up)),
        (low_side, 1, 0, jnp.where(low_side, up, down)),
        (low_row, 2, 3, jnp.where(low_row, under, over)),
    ]


def put_shared(value, shared_refs):
    for place, ref in enumerate(shared_refs):
        width = ref.shape[0]
        ref[...] = value[place * width : (place + 1) * width]


def came_in(subs, shared_refs):
    return jnp.concatenate(
        [ref[...] * jnp.where(here, 1.0, 0.0) for ref, (_, _, _, here) in zip(shared_refs, sides(subs))], axis=0
    )


def add_shared(subs, value, shared_refs):
    came = came_in(subs, shared_refs)
    count = came.shape[0]
    return jnp.concatenate([value[:count] + came, value[count:]], axis=0)


def listed_body(subs, count, blocks_hbm, load_hbm, columns_hbm, listed_ref, load_ref, sent_ref, *refs):
    *shared_refs, blocks_ref, load_sems, blocks_sem, sent_sem = refs
    modes = sent_ref.shape[0]
    wanted = pl.multiple_of((lax.axis_index("grp") ^ 2) * modes, modes)
    sent_copy = pltpu.make_async_copy(columns_hbm.at[pl.ds(wanted, modes), :], sent_ref, sent_sem)
    half = load_ref.shape[0] // 2
    halves = [slice(0, half), slice(half, 2 * half)]
    load_copies = [
        pltpu.make_async_copy(load_hbm.at[rows], load_ref.at[rows], load_sems.at[place])
        for place, rows in enumerate(halves)
    ]
    blocks_copy = pltpu.make_async_copy(blocks_hbm, blocks_ref, blocks_sem)
    blocks_copy.start()
    for copy in load_copies:
        copy.start()
    sent_copy.start()
    blocks_copy.wait()
    blocks = blocks_ref[...]
    placed = jnp.concatenate(
        [jnp.where(test, blocks[a : a + 1], blocks[b : b + 1]) for test, a, b, _ in sides(subs)], axis=0
    )
    upright = placed.astype(f32).T
    column = jnp.concatenate([upright[:, place : place + 1] for place in range(4)], axis=0)
    listed, total = column.shape[0], load_ref.shape[0]
    lane = lax.broadcasted_iota(jnp.int32, (listed, total), 1).astype(f32)
    first = (column == lane).astype(f32).astype(bf16)
    listed_ref[...] = first
    wanted_rows = count * blocks.shape[1]
    sent = None
    for copy, rows in zip(load_copies, halves):
        copy.wait()
        part = pick(first[:wanted_rows, rows], load_ref[rows])
        sent = part if sent is None else sent + part
    put_shared(sent, shared_refs)
    sent_copy.wait()


def order_body(subs, listed_ref, load_ref, basis_ref,
               chooser_ref, flipped_ref, basis_high, basis_low, test_high, test_low, ahead_ref, ordered_ref):
    listed, total = listed_ref.shape
    first = listed_ref[...].astype(f32)
    unlisted = 1.0 - jnp.sum(first, axis=0, keepdims=True)
    before = (
        lax.broadcasted_iota(jnp.int32, (total, total), 0)
        < lax.broadcasted_iota(jnp.int32, (total, total), 1)
    ).astype(f32).astype(bf16)
    rank = dot(jnp.broadcast_to(unlisted, (8, total)).astype(bf16), before)[:1]
    slot = lax.broadcasted_iota(jnp.int32, (total - listed, total), 0).astype(f32)
    last = jnp.where(rank == slot, unlisted, 0.0)
    chooser = jnp.concatenate([first, last], axis=0)
    flipped_ref[...] = chooser.T.astype(bf16)
    weighted = (chooser * weight_column(subs, listed // 4, total)).astype(bf16)
    chooser = chooser.astype(bf16)
    chooser_ref[...] = chooser
    ordered = pick(chooser, load_ref[...])
    ordered_ref[...] = ordered
    for part, out, turned in zip(split(basis_ref[...]), (basis_high, basis_low), (test_high, test_low)):
        placed = dot(weighted, part)
        out[...] = placed.astype(bf16)
        turned[...] = placed.T.astype(bf16)
    ahead_ref[...] = dot3((test_high[...], test_low[...]), split(ordered))


def weight_column(subs, width, total):
    parts = [jnp.full((width, 1), jnp.where(here, 0.5, 1.0), f32) for _, _, _, here in sides(subs)]
    return jnp.concatenate(parts + [jnp.ones((total - 4 * width, 1), f32)], axis=0)


def rows_of(columns_ref, place):
    modes = columns_ref.shape[1]
    return columns_ref[pl.ds(pl.multiple_of(place * modes, modes), modes), :]


def solver_body(subs, listed, chooser_ref, solve_ref, solve_high, solve_low):
    chooser = chooser_ref[...]
    weighted = (chooser.astype(f32) * weight_column(subs, listed // 4, chooser.shape[0])).astype(bf16)
    for part, out in zip(split(solve_ref[...] * RELAX), (solve_high, solve_low)):
        out[...] = dot(dot(weighted, part).astype(bf16), weighted, NT).astype(bf16)


def schur_body(chooser_ref, flipped_ref, schur_ref, schur_high, schur_low):
    chooser, flipped = chooser_ref[...], flipped_ref[...]
    for part, out in zip(split(schur_ref[...]), (schur_high, schur_low)):
        out[...] = dot(dot(chooser, part).astype(bf16), flipped).astype(bf16)


def blend_body(columns_ref, other_ref, mix_high, mix_low):
    grp = lax.axis_index("grp")
    away = jnp.concatenate([rows_of(columns_ref, grp ^ 1), other_ref[...]], axis=1)
    kept = jnp.concatenate([rows_of(columns_ref, grp), rows_of(columns_ref, grp ^ 3).T], axis=1)
    mix_high[...], mix_low[...] = split(jnp.concatenate([away, kept], axis=0) * RELAX)


def cut():
    return [(sum(PIECES[:place]), width) for place, width in enumerate(PIECES)]


def project_body(subs, count, ahead_ref, test_high, test_low, *refs):
    came = came_in(subs, refs[:count])
    size = came.shape[0]
    projected = ahead_ref[...] + dot3((test_high[:, :size], test_low[:, :size]), split(came))
    for ref, (start, width) in zip(refs[count:], cut()):
        ref[...] = projected[:, start : start + width]


def solve_body(subs, value_ref, solve_high, solve_low, *refs):
    halves = split(add_shared(subs, value_ref[...], refs[:-1]))
    refs[-1][...] = dot3((solve_high[...], solve_low[...]), halves)


def mix_body(own_ref, other_ref, mix_high, mix_low, away_ref, kept_ref):
    modes = away_ref.shape[0]
    pair = jnp.concatenate([own_ref[...], other_ref[...]], axis=0)
    mixed = dot3((mix_high[...], mix_low[...]), split(pair))
    away_ref[...] = mixed[:modes]
    kept_ref[...] = mixed[modes:]


def correct_body(kept_ref, came_ref, fine_ref, basis_high, basis_low, place, *refs):
    coarse = kept_ref[...] + came_ref[...]
    start, width = cut()[place]
    fine = fine_ref[:, start : start + width]
    step = fine + dot3((basis_high[...], basis_low[...]), split(coarse))
    formers = place if len(refs) > 1 else 0
    former_refs, out_ref = refs[:formers], refs[formers]
    out_ref[...] = step
    for at, ref in enumerate(refs[formers + 1 :]):
        size = ref.shape[0]
        rows = slice(at * size, (at + 1) * size)
        ref[...] = jnp.concatenate([former[rows] for former in former_refs] + [step[rows]], axis=1)


def ahead_body(pieces, first, *refs):
    total = jnp.concatenate([ref[...] for ref in refs[:pieces]], axis=1)
    refs = refs[pieces:]
    if not first:
        total = refs[0][...] + total
        refs = refs[1:]
    load_ref, schur_high, schur_low, base_ref, total_ref = refs
    total_ref[...] = total
    base_ref[...] = load_ref[...] - dot3((schur_high[...], schur_low[...]), split(total))


def product_body(subs, count, base_ref, schur_high, schur_low, *refs):
    came = came_in(subs, refs[:count])
    size = came.shape[0]
    part = dot3((schur_high[:size, :size], schur_low[:size, :size]), split(came))
    put_shared(base_ref[:size] - part, refs[count:])


def follow_body(subs, count, last, base_ref, total_ref, schur_high, schur_low, *refs):
    arrived, shared, refs = refs[:count], refs[count : 2 * count], refs[2 * count :]
    came = came_in(subs, arrived)
    size = came.shape[0]
    part = dot3((schur_high[size:, :size], schur_low[size:, :size]), split(came))
    value = jnp.concatenate([ref[...] for ref in shared] + [base_ref[size:] - part], axis=0)
    iterate_ref, value_ref = refs[-2:]
    value_ref[...] = value
    iterate_ref[...] = jnp.concatenate([total_ref[:size] + came, total_ref[size:]], axis=0)
    if not last:
        test_high, test_low, projected_ref = refs[:3]
        projected_ref[...] = dot3((test_high[...], test_low[...]), split(value))


def restore_body(flipped_ref, value_ref, iterate_ref, base_ref, out_ref):
    flipped = flipped_ref[...]
    out_ref[...] = pick(flipped, iterate_ref[...])
    base_ref[...] = pick(flipped, value_ref[...])


def finish_body(subs, flipped_ref, base_ref, *refs):
    *arrived, out_hbm, out_ref, sems = refs
    came = came_in(subs, arrived)
    total = base_ref[...] + pick(flipped_ref[:, : came.shape[0]], came)
    copies = []
    size = out_ref.shape[0] // 4
    for step in range(4):
        rows = slice(step * size, (step + 1) * size)
        out_ref[rows] = total[rows]
        copy = pltpu.make_async_copy(out_ref.at[rows], out_hbm.at[rows], sems.at[step])
        copy.start()
        copies.append(copy)
    for copy in copies:
        copy.wait()


def swaps(count, stride, odd):
    partner = {}
    for low in range(count - stride):
        if (low // stride) % 2 == odd:
            partner[low], partner[low + stride] = low + stride, low
    if not partner:
        return []
    left = [index for index in range(count) if index not in partner]
    half = len(left) // 2
    for low, high in zip(left[:half], left[half:]):
        partner[low], partner[high] = high, low
    return sorted(partner.items())


def local(load_terms, schur_matrix, local_inverse, coarse_modes, cluster_inverse, row_blocks):
    load = load_terms[0, 0]
    basis = coarse_modes[0, 0]
    columns = cluster_inverse[0]
    blocks = row_blocks[0, 0]
    rows, loads = load.shape
    modes = basis.shape[1]
    shared_rows = blocks.shape[1]
    listed = 4 * shared_rows
    subs = lax.axis_size("sub")
    if lax.axis_size("grp") != GROUPS or sum(PIECES) != loads:
        raise ValueError("unexpected sizes")

    plans = [swaps(subs, ROW_SUBS, 0), swaps(subs, 1, 1), swaps(subs, 1, 0), swaps(subs, ROW_SUBS, 1)]
    plans = [plan for plan in plans if plan]
    count = len(plans)

    def exchange(parts):
        return [lax.ppermute(part, "sub", plan) for part, plan in zip(parts, plans)]

    def whole(width, kind=f32):
        return ((rows, width), kind)

    pair_plan = [(0, 1), (1, 0), (2, 3), (3, 2)]
    mirror_plan = [(0, 3), (3, 0), (1, 2), (2, 1)]
    shared = [((shared_rows, loads), f32)] * count
    outside = pl.BlockSpec(memory_space=pltpu.HBM)
    pieces = len(PIECES)
    size = rows * loads
    run = Chain()

    one_hot, load_near, sent, *parts = run(
        lambda *refs: listed_body(subs, count, *refs),
        [((listed, rows), bf16), whole(loads), ((modes, modes), f32)] + shared, 4 * listed * size, 16 * size,
        *[pltpu.with_memory_space_constraint(array, pltpu.HBM) for array in (blocks, load, columns)], ins=[outside] * 3,
        scratch=[pltpu.VMEM(blocks.shape, blocks.dtype), pltpu.SemaphoreType.DMA((2,))]
        + [pltpu.SemaphoreType.DMA] * 2,
    )
    arrived = exchange(parts)
    other = lax.ppermute(sent, "grp", mirror_plan)
    chooser, flipped, basis_high, basis_low, test_high, test_low, ahead, ordered = run(
        lambda *refs: order_body(subs, *refs),
        [whole(rows, bf16)] * 2 + [whole(modes, bf16)] * 2 + [((modes, rows), bf16)] * 2
        + [((modes, loads), f32), whole(loads)],
        4 * rows * size, 24 * size, one_hot, load_near, basis,
    )
    value, iterate = ordered, None
    for iteration in range(ITERS):
        first, last = iteration == 0, iteration == ITERS - 1
        shapes = [((modes, width), f32) for width in PIECES]
        own = run(
            lambda *refs: project_body(subs, count, *refs), shapes, 6 * modes * size, 12 * size,
            ahead, test_high, test_low, *arrived,
        )
        theirs = [lax.ppermute(piece, "grp", mirror_plan) for piece in own]
        if first:
            mixers = run(blend_body, [((2 * modes, 2 * modes), bf16)] * 2, size, size, columns, other)
        kept, came = [], []
        for place, width in enumerate(PIECES):
            away, keep = run(
                mix_body, [((modes, width), f32)] * 2, 24 * modes * modes * width, 4 * rows * width,
                own[place], theirs[place], *mixers,
            )
            kept.append(keep)
            came.append(lax.ppermute(away, "grp", pair_plan))
        if first:
            solve_high, solve_low = run(
                lambda *refs: solver_body(subs, listed, *refs), [whole(rows, bf16)] * 2, 8 * rows**3, 12 * size,
                chooser, local_inverse[0, 0],
            )
        (fine,) = run(
            lambda *refs: solve_body(subs, *refs), [whole(loads)], 6 * rows * size, 12 * size,
            value, solve_high, solve_low, *arrived,
        )
        steps = []
        for place, width in enumerate(PIECES):
            final = place == pieces - 1
            step, *parts = run(
                lambda kept, came, fine, high, low, *refs: correct_body(kept, came, fine, high, low, place, *refs),
                [whole(width)] + (shared if final else []), 6 * modes * rows * width, 12 * rows * width,
                kept[place], came[place], fine, basis_high, basis_low, *(steps if final else []),
            )
            steps.append(step)
        arrived = exchange(parts)
        if first:
            schur_high, schur_low = run(
                schur_body, [whole(rows, bf16)] * 2, 8 * rows**3, 12 * size, chooser, flipped, schur_matrix[0, 0],
            )
        base, total = run(
            lambda *refs: ahead_body(pieces, first, *refs), [whole(loads)] * 2, 6 * rows * size, 16 * size,
            *steps, *([] if first else [iterate]), ordered, schur_high, schur_low,
        )
        parts = run(
            lambda *refs: product_body(subs, count, *refs), shared, 2 * rows * size, 12 * size,
            base, schur_high, schur_low, *arrived,
        )
        before, arrived = arrived, exchange(parts)
        *projected, iterate, value = run(
            lambda *refs: follow_body(subs, count, last, *refs),
            ([] if last else [((modes, loads), f32)]) + [whole(loads)] * 2, 3 * rows * size, 16 * size,
            base, total, schur_high, schur_low, *before, *parts, *([] if last else [test_high, test_low]),
        )
        ahead = projected[0] if projected else None
    near, solution_rows = run(
        restore_body, [whole(loads)] * 2, 8 * rows * size, 10 * size, flipped, value, iterate,
    )
    (residual_rows,) = run(
        lambda *refs: finish_body(subs, *refs), [whole(loads)], 4 * rows * size, 10 * size,
        flipped, near, *arrived, places=[outside],
        scratch=[pltpu.VMEM((rows, loads), f32), pltpu.SemaphoreType.DMA((4,))],
    )
    return (solution_rows[None, None], residual_rows[None, None])


def solution(mesh):
    return jax.shard_map(
        local,
        mesh=mesh,
        in_specs=(
            P("sub", "grp", None, None),
            P("sub", "grp", None, None),
            P("sub", "grp", None, None),
            P("sub", "grp", None, None),
            P("sub", None, "grp"),
            P("sub", "grp", None, None),
        ),
        out_specs=(P("sub", "grp", None, None), P("sub", "grp", None, None)),
        check_vma=False,
    )
```

```python
import jax
import jax.numpy as jnp
from jax import lax
from jax.experimental import pallas as pl
from jax.experimental.pallas import tpu as pltpu
from jax.sharding import PartitionSpec as P

ITERS = 2
ROW_SUBS = 4
RELAX = 0.5
GROUPS = 4
HIDE = 16
PIECES = (128, 256)
f32 = jnp.float32
bf16 = jnp.bfloat16
NN = (((1,), (0,)), ((), ()))
NT = (((1,), (1,)), ((), ()))


class Chain:
    def __init__(self):
        self.last = None

    def __call__(self, body, outs, flops, moved, *operands, scratch=(), ins=None, places=None):
        count = len(operands)
        specs = [pl.BlockSpec(memory_space=pltpu.VMEM)] * count if ins is None else ins
        extra = []
        if self.last is not None:
            extra = [self.last]
            specs = specs + [pl.BlockSpec(memory_space=pl.ANY)]

        def whole_body(*refs):
            body(*refs[:count], *refs[count + len(extra) :])

        results = pl.pallas_call(
            whole_body,
            out_shape=[jax.ShapeDtypeStruct(shape, kind) for shape, kind in outs],
            in_specs=specs,
            out_specs=[pl.BlockSpec(memory_space=pltpu.VMEM)] * len(outs) if places is None else places,
            scratch_shapes=list(scratch),
            compiler_params=pltpu.CompilerParams(vmem_limit_bytes=24 * 1024 * 1024),
            cost_estimate=pl.CostEstimate(flops=flops, bytes_accessed=moved, transcendentals=0),
        )(*operands, *extra)
        self.last = results[0]
        return results


def dot(left, right, dims=NN):
    return lax.dot_general(left, right, dims, preferred_element_type=f32)


def split(value):
    high = value.astype(bf16)
    return high, (value - high.astype(f32)).astype(bf16)


def dot3(left, right):
    return dot(left[0], right[0]) + (dot(left[0], right[1]) + dot(left[1], right[0]))


def join_left(halves):
    return jnp.concatenate([halves[0], halves[0], halves[1]], axis=1)


def join_right(halves):
    return jnp.concatenate([halves[0], halves[1], halves[0]], axis=0)


def pick(chooser, value):
    high, low = split(value)
    return dot(chooser, high) + dot(chooser, low)


def sides(subs):
    sub = lax.axis_index("sub")
    low_side = sub % 2 == 0
    low_row = (sub // ROW_SUBS) % 2 == 0
    up, down = sub < subs - 1, sub > 0
    over, under = sub < subs - ROW_SUBS, sub >= ROW_SUBS
    return [
        (low_row, 3, 2, jnp.where(low_row, over, under)),
        (low_side, 0, 1, jnp.where(low_side, down, up)),
        (low_side, 1, 0, jnp.where(low_side, up, down)),
        (low_row, 2, 3, jnp.where(low_row, under, over)),
    ]


def put_shared(value, shared_refs):
    for place, ref in enumerate(shared_refs):
        width = ref.shape[0]
        ref[...] = value[place * width : (place + 1) * width]


def came_in(subs, shared_refs):
    return jnp.concatenate(
        [ref[...] * jnp.where(here, 1.0, 0.0) for ref, (_, _, _, here) in zip(shared_refs, sides(subs))], axis=0
    )


def add_shared(subs, value, shared_refs):
    came = came_in(subs, shared_refs)
    count = came.shape[0]
    return jnp.concatenate([value[:count] + came, value[count:]], axis=0)


def listed_body(subs, count, blocks_hbm, load_hbm, columns_hbm, listed_ref, load_ref, sent_ref, *refs):
    *shared_refs, blocks_ref, load_sems, blocks_sem, sent_sem = refs
    modes = sent_ref.shape[0]
    wanted = pl.multiple_of((3 - (lax.axis_index("grp") ^ 1)) * modes, modes)
    sent_copy = pltpu.make_async_copy(columns_hbm.at[pl.ds(wanted, modes), :], sent_ref, sent_sem)
    half = load_ref.shape[0] // 2
    halves = [slice(0, half), slice(half, 2 * half)]
    load_copies = [
        pltpu.make_async_copy(load_hbm.at[rows], load_ref.at[rows], load_sems.at[place])
        for place, rows in enumerate(halves)
    ]
    blocks_copy = pltpu.make_async_copy(blocks_hbm, blocks_ref, blocks_sem)
    blocks_copy.start()
    for copy in load_copies:
        copy.start()
    sent_copy.start()
    blocks_copy.wait()
    blocks = blocks_ref[...]
    placed = jnp.concatenate(
        [jnp.where(test, blocks[a : a + 1], blocks[b : b + 1]) for test, a, b, _ in sides(subs)], axis=0
    )
    upright = placed.astype(f32).T
    column = jnp.concatenate([upright[:, place : place + 1] for place in range(4)], axis=0)
    listed, total = column.shape[0], load_ref.shape[0]
    lane = lax.broadcasted_iota(jnp.int32, (listed, total), 1).astype(f32)
    first = (column == lane).astype(f32).astype(bf16)
    listed_ref[...] = first
    wanted_rows = count * blocks.shape[1]
    sent = None
    for copy, rows in zip(load_copies, halves):
        copy.wait()
        part = pick(first[:wanted_rows, rows], load_ref[rows])
        sent = part if sent is None else sent + part
    put_shared(sent, shared_refs)
    sent_copy.wait()


def order_body(subs, count, listed_ref, load_ref, basis_ref, chooser_ref, flipped_ref, twice_ref,
               basis_wide, test_high, test_low, test_wide, ahead_ref, ordered_ref):
    listed, total = listed_ref.shape
    first = listed_ref[...].astype(f32)
    unlisted = 1.0 - jnp.sum(first, axis=0, keepdims=True)
    before = (
        lax.broadcasted_iota(jnp.int32, (total, total), 0)
        < lax.broadcasted_iota(jnp.int32, (total, total), 1)
    ).astype(f32).astype(bf16)
    rank = dot(jnp.broadcast_to(unlisted, (8, total)).astype(bf16), before)[:1]
    slot = lax.broadcasted_iota(jnp.int32, (total - listed, total), 0).astype(f32)
    last = jnp.where(rank == slot, unlisted, 0.0)
    chooser = jnp.concatenate([first, last], axis=0)
    flipped_ref[...] = chooser.T.astype(bf16)
    weighted = (chooser * weight_column(subs, listed // 4, total)).astype(bf16)
    chooser = chooser.astype(bf16)
    chooser_ref[...] = chooser
    ordered = pick(chooser, load_ref[...])
    ordered_ref[...] = ordered
    size = count * listed // 4
    shared = flipped_ref[:, :size]
    twice_ref[...] = jnp.concatenate([shared, shared], axis=1)
    placed = [dot(weighted, part) for part in split(basis_ref[...])]
    basis_wide[...] = join_left([part.astype(bf16) for part in placed])
    for part, turned in zip(placed, (test_high, test_low)):
        turned[...] = part.T.astype(bf16)
    test_wide[...] = join_left([test_high[:, :size], test_low[:, :size]])
    ahead_ref[...] = dot3((test_high[...], test_low[...]), split(ordered))


def weight_column(subs, width, total):
    parts = [jnp.full((width, 1), jnp.where(here, 0.5, 1.0), f32) for _, _, _, here in sides(subs)]
    return jnp.concatenate(parts + [jnp.ones((total - 4 * width, 1), f32)], axis=0)


def rows_of(columns_ref, place):
    modes = columns_ref.shape[1]
    return columns_ref[pl.ds(pl.multiple_of(place * modes, modes), modes), :]


def solver_body(subs, listed, chooser_ref, solve_ref, solve_high, solve_low):
    chooser = chooser_ref[...]
    weighted = (chooser.astype(f32) * weight_column(subs, listed // 4, chooser.shape[0])).astype(bf16)
    for part, out in zip(split(solve_ref[...] * RELAX), (solve_high, solve_low)):
        out[...] = dot(dot(weighted, part).astype(bf16), weighted, NT).astype(bf16)


def schur_body(chooser_ref, flipped_ref, schur_ref, schur_high, schur_low, schur_wide):
    chooser, flipped = chooser_ref[...], flipped_ref[...]
    size = schur_wide.shape[0]
    for part, out in zip(split(schur_ref[...]), (schur_high, schur_low)):
        out[...] = dot(dot(chooser, part).astype(bf16), flipped).astype(bf16)
    schur_wide[...] = join_left([schur_high[:size, :size], schur_low[:size, :size]])


def blend_body(columns_ref, other_ref, mix_high, mix_low):
    grp = lax.axis_index("grp")
    away = jnp.concatenate([rows_of(columns_ref, 3 - grp), other_ref[...]], axis=1)
    kept = jnp.concatenate([rows_of(columns_ref, grp), rows_of(columns_ref, grp ^ 1).T], axis=1)
    mix_high[...], mix_low[...] = split(jnp.concatenate([away, kept], axis=0) * RELAX)


def cut():
    return [(sum(PIECES[:place]), width) for place, width in enumerate(PIECES)]


def project_body(subs, count, ahead_ref, test_wide, *refs):
    halves = split(came_in(subs, refs[:count]))
    projected = ahead_ref[...] + dot(test_wide[...], join_right(halves))
    for ref, (start, width) in zip(refs[count:], cut()):
        ref[...] = projected[:, start : start + width]


def solve_body(subs, value_ref, solve_high, solve_low, *refs):
    halves = split(add_shared(subs, value_ref[...], refs[:-1]))
    refs[-1][...] = dot3((solve_high[...], solve_low[...]), halves)


def mix_body(own_ref, other_ref, mix_high, mix_low, away_ref, kept_ref):
    modes = away_ref.shape[0]
    pair = jnp.concatenate([own_ref[...], other_ref[...]], axis=0)
    mixed = dot3((mix_high[...], mix_low[...]), split(pair))
    away_ref[...] = mixed[:modes]
    kept_ref[...] = mixed[modes:]


def correct_body(kept_ref, came_ref, fine_ref, basis_wide, place, *refs):
    coarse = kept_ref[...] + came_ref[...]
    start, width = cut()[place]
    fine = fine_ref[:, start : start + width]
    step = fine + dot(basis_wide[...], join_right(split(coarse)))
    formers = place if len(refs) > 1 else 0
    former_refs, out_ref = refs[:formers], refs[formers]
    out_ref[...] = step
    for at, ref in enumerate(refs[formers + 1 :]):
        size = ref.shape[0]
        rows = slice(at * size, (at + 1) * size)
        ref[...] = jnp.concatenate([former[rows] for former in former_refs] + [step[rows]], axis=1)


def ahead_body(pieces, first, *refs):
    total = jnp.concatenate([ref[...] for ref in refs[:pieces]], axis=1)
    refs = refs[pieces:]
    if not first:
        total = refs[0][...] + total
        refs = refs[1:]
    load_ref, schur_high, schur_low, base_ref, total_ref = refs
    total_ref[...] = total
    base_ref[...] = load_ref[...] - dot3((schur_high[...], schur_low[...]), split(total))


def product_body(subs, count, base_ref, schur_wide, *refs):
    came = came_in(subs, refs[:count])
    size = came.shape[0]
    part = dot(schur_wide[...], join_right(split(came)))
    put_shared(base_ref[:size] - part, refs[count:])


def follow_body(subs, count, last, base_ref, total_ref, schur_high, schur_low, *refs):
    arrived, shared, refs = refs[:count], refs[count : 2 * count], refs[2 * count :]
    came = came_in(subs, arrived)
    size = came.shape[0]
    part = dot3((schur_high[size:, :size], schur_low[size:, :size]), split(came))
    value = jnp.concatenate([ref[...] for ref in shared] + [base_ref[size:] - part], axis=0)
    iterate_ref, value_ref = refs[-2:]
    value_ref[...] = value
    iterate_ref[...] = jnp.concatenate([total_ref[:size] + came, total_ref[size:]], axis=0)
    if not last:
        test_high, test_low, projected_ref = refs[:3]
        projected_ref[...] = dot3((test_high[...], test_low[...]), split(value))


def restore_body(flipped_ref, value_ref, iterate_ref, base_ref, out_ref):
    flipped = flipped_ref[...]
    out_ref[...] = pick(flipped, iterate_ref[...])
    base_ref[...] = pick(flipped, value_ref[...])


def finish_body(subs, twice_ref, base_ref, *refs):
    *arrived, out_hbm, out_ref, sems = refs
    came = came_in(subs, arrived)
    total = base_ref[...] + dot(twice_ref[...], jnp.concatenate(split(came), axis=0))
    copies = []
    size = out_ref.shape[0] // 4
    for step in range(4):
        rows = slice(step * size, (step + 1) * size)
        out_ref[rows] = total[rows]
        copy = pltpu.make_async_copy(out_ref.at[rows], out_hbm.at[rows], sems.at[step])
        copy.start()
        copies.append(copy)
    for copy in copies:
        copy.wait()


def swaps(count, stride, odd):
    partner = {}
    for low in range(count - stride):
        if (low // stride) % 2 == odd:
            partner[low], partner[low + stride] = low + stride, low
    if not partner:
        return []
    left = [index for index in range(count) if index not in partner]
    half = len(left) // 2
    for low, high in zip(left[:half], left[half:]):
        partner[low], partner[high] = high, low
    return sorted(partner.items())


def local(load_terms, schur_matrix, local_inverse, coarse_modes, cluster_inverse, row_blocks):
    load = load_terms[0, 0]
    basis = coarse_modes[0, 0]
    columns = cluster_inverse[0]
    blocks = row_blocks[0, 0]
    rows, loads = load.shape
    modes = basis.shape[1]
    shared_rows = blocks.shape[1]
    listed = 4 * shared_rows
    subs = lax.axis_size("sub")
    if lax.axis_size("grp") != GROUPS or sum(PIECES) != loads:
        raise ValueError("unexpected sizes")

    plans = [swaps(subs, ROW_SUBS, 0), swaps(subs, 1, 1), swaps(subs, 1, 0), swaps(subs, ROW_SUBS, 1)]
    plans = [plan for plan in plans if plan]
    count = len(plans)

    def exchange(parts):
        return [lax.ppermute(part, "sub", plan) for part, plan in zip(parts, plans)]

    def whole(width, kind=f32):
        return ((rows, width), kind)

    pair_plan = [(0, 1), (1, 0), (2, 3), (3, 2)]
    mirror_plan = [(0, 3), (3, 0), (1, 2), (2, 1)]
    shared = [((shared_rows, loads), f32)] * count
    outside = pl.BlockSpec(memory_space=pltpu.HBM)
    pieces = len(PIECES)
    size = rows * loads
    sent_rows = count * shared_rows
    run = Chain()

    one_hot, load_near, sent, *parts = run(
        lambda *refs: listed_body(subs, count, *refs),
        [((listed, rows), bf16), whole(loads), ((modes, modes), f32)] + shared, 4 * listed * size, 16 * size,
        *[pltpu.with_memory_space_constraint(array, pltpu.HBM) for array in (blocks, load, columns)], ins=[outside] * 3,
        scratch=[pltpu.VMEM(blocks.shape, blocks.dtype), pltpu.SemaphoreType.DMA((2,))]
        + [pltpu.SemaphoreType.DMA] * 2,
    )
    arrived = exchange(parts)
    other = lax.ppermute(sent, "grp", pair_plan)
    chooser, flipped, twice, basis_wide, test_high, test_low, test_wide, ahead, ordered = run(
        lambda *refs: order_body(subs, count, *refs),
        [whole(rows, bf16)] * 2 + [whole(2 * sent_rows, bf16), whole(3 * modes, bf16)]
        + [((modes, rows), bf16)] * 2 + [((modes, 3 * sent_rows), bf16), ((modes, loads), f32), whole(loads)],
        4 * rows * size, 24 * size, one_hot, load_near, basis,
    )
    value, iterate = ordered, None
    for iteration in range(ITERS):
        first, last = iteration == 0, iteration == ITERS - 1
        shapes = [((modes, width), f32) for width in PIECES]
        own = run(
            lambda *refs: project_body(subs, count, *refs), shapes, 6 * modes * size, 12 * size,
            ahead, test_wide, *arrived,
        )
        theirs = [lax.ppermute(piece, "grp", pair_plan) for piece in own]
        if first:
            mixers = run(blend_body, [((2 * modes, 2 * modes), bf16)] * 2, size, size, columns, other)
        kept, came = [], []
        for place, width in enumerate(PIECES):
            away, keep = run(
                mix_body, [((modes, width), f32)] * 2, HIDE * 24 * modes * modes * width, HIDE * 4 * rows * width,
                own[place], theirs[place], *mixers,
            )
            kept.append(keep)
            came.append(lax.ppermute(away, "grp", mirror_plan))
        if first:
            solve_high, solve_low = run(
                lambda *refs: solver_body(subs, listed, *refs), [whole(rows, bf16)] * 2, 8 * rows**3, 12 * size,
                chooser, local_inverse[0, 0],
            )
        (fine,) = run(
            lambda *refs: solve_body(subs, *refs), [whole(loads)], HIDE * 6 * rows * size, HIDE * 12 * size,
            value, solve_high, solve_low, *arrived,
        )
        steps = []
        for place, width in enumerate(PIECES):
            final = place == pieces - 1
            step, *parts = run(
                lambda kept, came, fine, wide, *refs: correct_body(kept, came, fine, wide, place, *refs),
                [whole(width)] + (shared if final else []), 6 * modes * rows * width, 12 * rows * width,
                kept[place], came[place], fine, basis_wide, *(steps if final else []),
            )
            steps.append(step)
        arrived = exchange(parts)
        if first:
            schur_high, schur_low, schur_wide = run(
                schur_body, [whole(rows, bf16)] * 2 + [((sent_rows, 3 * sent_rows), bf16)], 8 * rows**3, 12 * size, chooser, flipped, schur_matrix[0, 0],
            )
        base, total = run(
            lambda *refs: ahead_body(pieces, first, *refs), [whole(loads)] * 2, 6 * rows * size, 16 * size,
            *steps, *([] if first else [iterate]), ordered, schur_high, schur_low,
        )
        parts = run(
            lambda *refs: product_body(subs, count, *refs), shared, 2 * rows * size, 12 * size,
            base, schur_wide, *arrived,
        )
        before, arrived = arrived, exchange(parts)
        *projected, iterate, value = run(
            lambda *refs: follow_body(subs, count, last, *refs),
            ([] if last else [((modes, loads), f32)]) + [whole(loads)] * 2, 3 * rows * size, 16 * size,
            base, total, schur_high, schur_low, *before, *parts, *([] if last else [test_high, test_low]),
        )
        ahead = projected[0] if projected else None
    near, solution_rows = run(
        restore_body, [whole(loads)] * 2, 8 * rows * size, 10 * size, flipped, value, iterate,
    )
    (residual_rows,) = run(
        lambda *refs: finish_body(subs, *refs), [whole(loads)], 4 * rows * size, 10 * size,
        twice, near, *arrived, places=[outside],
        scratch=[pltpu.VMEM((rows, loads), f32), pltpu.SemaphoreType.DMA((4,))],
    )
    return (solution_rows[None, None], residual_rows[None, None])


def solution(mesh):
    return jax.shard_map(
        local,
        mesh=mesh,
        in_specs=(
            P("sub", "grp", None, None),
            P("sub", "grp", None, None),
            P("sub", "grp", None, None),
            P("sub", "grp", None, None),
            P("sub", None, "grp"),
            P("sub", "grp", None, None),
        ),
        out_specs=(P("sub", "grp", None, None), P("sub", "grp", None, None)),
        check_vma=False,
    )
```

```python
import jax
import jax.numpy as jnp
from jax import lax
from jax.experimental import pallas as pl
from jax.experimental.pallas import tpu as pltpu
from jax.sharding import PartitionSpec as P

ITERS = 2
ROW_SUBS = 4
RELAX = 0.5
GROUPS = 4
HIDE = 16
PIECES = (128, 256)
f32 = jnp.float32
bf16 = jnp.bfloat16
NN = (((1,), (0,)), ((), ()))
NT = (((1,), (1,)), ((), ()))


class Chain:
    def __init__(self):
        self.last = None

    def __call__(self, body, outs, flops, moved, *operands, scratch=(), ins=None, places=None):
        count = len(operands)
        specs = [pl.BlockSpec(memory_space=pltpu.VMEM)] * count if ins is None else ins
        extra = []
        if self.last is not None:
            extra = [self.last]
            specs = specs + [pl.BlockSpec(memory_space=pl.ANY)]

        def whole_body(*refs):
            body(*refs[:count], *refs[count + len(extra) :])

        results = pl.pallas_call(
            whole_body,
            out_shape=[jax.ShapeDtypeStruct(shape, kind) for shape, kind in outs],
            in_specs=specs,
            out_specs=[pl.BlockSpec(memory_space=pltpu.VMEM)] * len(outs) if places is None else places,
            scratch_shapes=list(scratch),
            compiler_params=pltpu.CompilerParams(vmem_limit_bytes=24 * 1024 * 1024),
            cost_estimate=pl.CostEstimate(flops=flops, bytes_accessed=moved, transcendentals=0),
        )(*operands, *extra)
        self.last = results[0]
        return results


def dot(left, right, dims=NN):
    return lax.dot_general(left, right, dims, preferred_element_type=f32)


def split(value):
    high = value.astype(bf16)
    return high, (value - high.astype(f32)).astype(bf16)


def dot3(left, right):
    return dot(left[0], right[0]) + (dot(left[0], right[1]) + dot(left[1], right[0]))


def join_left(halves):
    return jnp.concatenate([halves[0], halves[0], halves[1]], axis=1)


def join_right(halves):
    return jnp.concatenate([halves[0], halves[1], halves[0]], axis=0)


def pick(chooser, value):
    high, low = split(value)
    return dot(chooser, high) + dot(chooser, low)


def sides(subs):
    sub = lax.axis_index("sub")
    low_side = sub % 2 == 0
    low_row = (sub // ROW_SUBS) % 2 == 0
    up, down = sub < subs - 1, sub > 0
    over, under = sub < subs - ROW_SUBS, sub >= ROW_SUBS
    return [
        (low_row, 3, 2, jnp.where(low_row, over, under)),
        (low_side, 0, 1, jnp.where(low_side, down, up)),
        (low_side, 1, 0, jnp.where(low_side, up, down)),
        (low_row, 2, 3, jnp.where(low_row, under, over)),
    ]


def put_shared(value, shared_refs):
    for place, ref in enumerate(shared_refs):
        width = ref.shape[0]
        ref[...] = value[place * width : (place + 1) * width]


def came_in(subs, shared_refs):
    return jnp.concatenate(
        [ref[...] * jnp.where(here, 1.0, 0.0) for ref, (_, _, _, here) in zip(shared_refs, sides(subs))], axis=0
    )


def add_shared(subs, value, shared_refs):
    came = came_in(subs, shared_refs)
    count = came.shape[0]
    return jnp.concatenate([value[:count] + came, value[count:]], axis=0)


def listed_body(subs, count, blocks_hbm, load_hbm, columns_hbm, listed_ref, load_ref, sent_ref, *refs):
    *shared_refs, blocks_ref, load_sems, blocks_sem, sent_sem = refs
    modes = sent_ref.shape[0]
    wanted = pl.multiple_of((3 - (lax.axis_index("grp") ^ 1)) * modes, modes)
    sent_copy = pltpu.make_async_copy(columns_hbm.at[pl.ds(wanted, modes), :], sent_ref, sent_sem)
    half = load_ref.shape[0] // 2
    halves = [slice(0, half), slice(half, 2 * half)]
    load_copies = [
        pltpu.make_async_copy(load_hbm.at[rows], load_ref.at[rows], load_sems.at[place])
        for place, rows in enumerate(halves)
    ]
    blocks_copy = pltpu.make_async_copy(blocks_hbm, blocks_ref, blocks_sem)
    blocks_copy.start()
    for copy in load_copies:
        copy.start()
    sent_copy.start()
    blocks_copy.wait()
    blocks = blocks_ref[...]
    placed = jnp.concatenate(
        [jnp.where(test, blocks[a : a + 1], blocks[b : b + 1]) for test, a, b, _ in sides(subs)], axis=0
    )
    upright = placed.astype(f32).T
    column = jnp.concatenate([upright[:, place : place + 1] for place in range(4)], axis=0)
    listed, total = column.shape[0], load_ref.shape[0]
    lane = lax.broadcasted_iota(jnp.int32, (listed, total), 1).astype(f32)
    first = (column == lane).astype(f32).astype(bf16)
    listed_ref[...] = first
    wanted_rows = count * blocks.shape[1]
    sent = None
    for copy, rows in zip(load_copies, halves):
        copy.wait()
        part = pick(first[:wanted_rows, rows], load_ref[rows])
        sent = part if sent is None else sent + part
    put_shared(sent, shared_refs)
    sent_copy.wait()


def order_body(subs, count, listed_ref, load_ref, basis_ref, chooser_ref, flipped_ref, twice_ref,
               basis_wide, test_high, test_low, test_wide, ahead_ref, ordered_ref):
    listed, total = listed_ref.shape
    first = listed_ref[...].astype(f32)
    unlisted = 1.0 - jnp.sum(first, axis=0, keepdims=True)
    before = (
        lax.broadcasted_iota(jnp.int32, (total, total), 0)
        < lax.broadcasted_iota(jnp.int32, (total, total), 1)
    ).astype(f32).astype(bf16)
    rank = dot(jnp.broadcast_to(unlisted, (8, total)).astype(bf16), before)[:1]
    slot = lax.broadcasted_iota(jnp.int32, (total - listed, total), 0).astype(f32)
    last = jnp.where(rank == slot, unlisted, 0.0)
    chooser = jnp.concatenate([first, last], axis=0)
    flipped_ref[...] = chooser.T.astype(bf16)
    weighted = (chooser * weight_column(subs, listed // 4, total)).astype(bf16)
    chooser = chooser.astype(bf16)
    chooser_ref[...] = chooser
    ordered = pick(chooser, load_ref[...])
    ordered_ref[...] = ordered
    size = count * listed // 4
    shared = flipped_ref[:, :size]
    twice_ref[...] = jnp.concatenate([shared, shared], axis=1)
    placed = [dot(weighted, part) for part in split(basis_ref[...])]
    basis_wide[...] = join_left([part.astype(bf16) for part in placed])
    for part, turned in zip(placed, (test_high, test_low)):
        turned[...] = part.T.astype(bf16)
    test_wide[...] = join_left([test_high[:, :size], test_low[:, :size]])
    ahead_ref[...] = dot3((test_high[...], test_low[...]), split(ordered))


def weight_column(subs, width, total):
    parts = [jnp.full((width, 1), jnp.where(here, 0.5, 1.0), f32) for _, _, _, here in sides(subs)]
    return jnp.concatenate(parts + [jnp.ones((total - 4 * width, 1), f32)], axis=0)


def rows_of(columns_ref, place):
    modes = columns_ref.shape[1]
    return columns_ref[pl.ds(pl.multiple_of(place * modes, modes), modes), :]


def solver_body(subs, listed, chooser_ref, solve_ref, later_ref, solve_high, solve_low, passed_ref):
    chooser = chooser_ref[...]
    weighted = (chooser.astype(f32) * weight_column(subs, listed // 4, chooser.shape[0])).astype(bf16)
    passed_ref[...] = later_ref[...]
    for part, out in zip(split(solve_ref[...] * RELAX), (solve_high, solve_low)):
        out[...] = dot(dot(weighted, part).astype(bf16), weighted, NT).astype(bf16)


def schur_body(chooser_ref, flipped_ref, schur_ref, schur_high, schur_low, schur_wide):
    chooser, flipped = chooser_ref[...], flipped_ref[...]
    size = schur_wide.shape[0]
    for part, out in zip(split(schur_ref[...]), (schur_high, schur_low)):
        out[...] = dot(dot(chooser, part).astype(bf16), flipped).astype(bf16)
    schur_wide[...] = join_left([schur_high[:size, :size], schur_low[:size, :size]])


def blend_body(columns_ref, other_ref, mix_high, mix_low):
    grp = lax.axis_index("grp")
    away = jnp.concatenate([rows_of(columns_ref, 3 - grp), other_ref[...]], axis=1)
    kept = jnp.concatenate([rows_of(columns_ref, grp), rows_of(columns_ref, grp ^ 1).T], axis=1)
    mix_high[...], mix_low[...] = split(jnp.concatenate([away, kept], axis=0) * RELAX)


def cut():
    return [(sum(PIECES[:place]), width) for place, width in enumerate(PIECES)]


def project_body(subs, count, ahead_ref, test_wide, *refs):
    halves = split(came_in(subs, refs[:count]))
    projected = ahead_ref[...] + dot(test_wide[...], join_right(halves))
    for ref, (start, width) in zip(refs[count:], cut()):
        ref[...] = projected[:, start : start + width]


def solve_body(subs, value_ref, solve_high, solve_low, *refs):
    halves = split(add_shared(subs, value_ref[...], refs[:-1]))
    refs[-1][...] = dot3((solve_high[...], solve_low[...]), halves)


def mix_body(own_ref, other_ref, mix_high, mix_low, away_ref, kept_ref):
    modes = away_ref.shape[0]
    pair = jnp.concatenate([own_ref[...], other_ref[...]], axis=0)
    mixed = dot3((mix_high[...], mix_low[...]), split(pair))
    away_ref[...] = mixed[:modes]
    kept_ref[...] = mixed[modes:]


def correct_body(kept_ref, came_ref, fine_ref, basis_wide, place, *refs):
    coarse = kept_ref[...] + came_ref[...]
    start, width = cut()[place]
    fine = fine_ref[:, start : start + width]
    step = fine + dot(basis_wide[...], join_right(split(coarse)))
    formers = place if len(refs) > 1 else 0
    former_refs, out_ref = refs[:formers], refs[formers]
    out_ref[...] = step
    for at, ref in enumerate(refs[formers + 1 :]):
        size = ref.shape[0]
        rows = slice(at * size, (at + 1) * size)
        ref[...] = jnp.concatenate([former[rows] for former in former_refs] + [step[rows]], axis=1)


def ahead_body(pieces, first, *refs):
    total = jnp.concatenate([ref[...] for ref in refs[:pieces]], axis=1)
    refs = refs[pieces:]
    if not first:
        total = refs[0][...] + total
        refs = refs[1:]
    load_ref, schur_high, schur_low, base_ref, total_ref = refs
    total_ref[...] = total
    base_ref[...] = load_ref[...] - dot3((schur_high[...], schur_low[...]), split(total))


def product_body(subs, count, base_ref, schur_wide, *refs):
    came = came_in(subs, refs[:count])
    size = came.shape[0]
    part = dot(schur_wide[...], join_right(split(came)))
    put_shared(base_ref[:size] - part, refs[count:])


def follow_body(subs, count, last, base_ref, total_ref, schur_high, schur_low, *refs):
    arrived, shared, refs = refs[:count], refs[count : 2 * count], refs[2 * count :]
    came = came_in(subs, arrived)
    size = came.shape[0]
    part = dot3((schur_high[size:, :size], schur_low[size:, :size]), split(came))
    value = jnp.concatenate([ref[...] for ref in shared] + [base_ref[size:] - part], axis=0)
    iterate_ref, value_ref = refs[-2:]
    value_ref[...] = value
    iterate_ref[...] = jnp.concatenate([total_ref[:size] + came, total_ref[size:]], axis=0)
    if not last:
        test_high, test_low, projected_ref = refs[:3]
        projected_ref[...] = dot3((test_high[...], test_low[...]), split(value))


def restore_body(flipped_ref, value_ref, iterate_ref, base_ref, out_ref):
    flipped = flipped_ref[...]
    out_ref[...] = pick(flipped, iterate_ref[...])
    base_ref[...] = pick(flipped, value_ref[...])


def finish_body(subs, twice_ref, base_ref, *refs):
    *arrived, out_hbm, out_ref, sems = refs
    came = came_in(subs, arrived)
    total = base_ref[...] + dot(twice_ref[...], jnp.concatenate(split(came), axis=0))
    copies = []
    size = out_ref.shape[0] // 4
    for step in range(4):
        rows = slice(step * size, (step + 1) * size)
        out_ref[rows] = total[rows]
        copy = pltpu.make_async_copy(out_ref.at[rows], out_hbm.at[rows], sems.at[step])
        copy.start()
        copies.append(copy)
    for copy in copies:
        copy.wait()


def swaps(count, stride, odd):
    partner = {}
    for low in range(count - stride):
        if (low // stride) % 2 == odd:
            partner[low], partner[low + stride] = low + stride, low
    if not partner:
        return []
    left = [index for index in range(count) if index not in partner]
    half = len(left) // 2
    for low, high in zip(left[:half], left[half:]):
        partner[low], partner[high] = high, low
    return sorted(partner.items())


def local(load_terms, schur_matrix, local_inverse, coarse_modes, cluster_inverse, row_blocks):
    load = load_terms[0, 0]
    basis = coarse_modes[0, 0]
    columns = cluster_inverse[0]
    blocks = row_blocks[0, 0]
    rows, loads = load.shape
    modes = basis.shape[1]
    shared_rows = blocks.shape[1]
    listed = 4 * shared_rows
    subs = lax.axis_size("sub")
    if lax.axis_size("grp") != GROUPS or sum(PIECES) != loads:
        raise ValueError("unexpected sizes")

    plans = [swaps(subs, ROW_SUBS, 0), swaps(subs, 1, 1), swaps(subs, 1, 0), swaps(subs, ROW_SUBS, 1)]
    plans = [plan for plan in plans if plan]
    count = len(plans)

    def exchange(parts):
        return [lax.ppermute(part, "sub", plan) for part, plan in zip(parts, plans)]

    def whole(width, kind=f32):
        return ((rows, width), kind)

    pair_plan = [(0, 1), (1, 0), (2, 3), (3, 2)]
    mirror_plan = [(0, 3), (3, 0), (1, 2), (2, 1)]
    shared = [((shared_rows, loads), f32)] * count
    outside = pl.BlockSpec(memory_space=pltpu.HBM)
    pieces = len(PIECES)
    size = rows * loads
    sent_rows = count * shared_rows
    run = Chain()

    one_hot, load_near, sent, *parts = run(
        lambda *refs: listed_body(subs, count, *refs),
        [((listed, rows), bf16), whole(loads), ((modes, modes), f32)] + shared, 4 * listed * size, 16 * size,
        *[pltpu.with_memory_space_constraint(array, pltpu.HBM) for array in (blocks, load, columns)], ins=[outside] * 3,
        scratch=[pltpu.VMEM(blocks.shape, blocks.dtype), pltpu.SemaphoreType.DMA((2,))]
        + [pltpu.SemaphoreType.DMA] * 2,
    )
    arrived = exchange(parts)
    other = lax.ppermute(sent, "grp", pair_plan)
    chooser, flipped, twice, basis_wide, test_high, test_low, test_wide, ahead, ordered = run(
        lambda *refs: order_body(subs, count, *refs),
        [whole(rows, bf16)] * 2 + [whole(2 * sent_rows, bf16), whole(3 * modes, bf16)]
        + [((modes, rows), bf16)] * 2 + [((modes, 3 * sent_rows), bf16), ((modes, loads), f32), whole(loads)],
        4 * rows * size, 24 * size, one_hot, load_near, basis,
    )
    value, iterate = ordered, None
    for iteration in range(ITERS):
        first, last = iteration == 0, iteration == ITERS - 1
        shapes = [((modes, width), f32) for width in PIECES]
        own = list(run(
            lambda *refs: project_body(subs, count, *refs), shapes, 6 * modes * size, 12 * size,
            ahead, test_wide, *arrived,
        ))
        if first:
            solve_high, solve_low, own[1] = run(
                lambda *refs: solver_body(subs, listed, *refs), [whole(rows, bf16)] * 2 + [shapes[1]],
                8 * rows**3, 12 * size, chooser, local_inverse[0, 0], own[1],
            )
        theirs = [lax.ppermute(piece, "grp", pair_plan) for piece in own]
        if first:
            mixers = run(blend_body, [((2 * modes, 2 * modes), bf16)] * 2, size, size, columns, other)
        kept, came = [], []
        for place, width in enumerate(PIECES):
            away, keep = run(
                mix_body, [((modes, width), f32)] * 2, HIDE * 24 * modes * modes * width, HIDE * 4 * rows * width,
                own[place], theirs[place], *mixers,
            )
            kept.append(keep)
            came.append(lax.ppermute(away, "grp", mirror_plan))
        (fine,) = run(
            lambda *refs: solve_body(subs, *refs), [whole(loads)], HIDE * 6 * rows * size, HIDE * 12 * size,
            value, solve_high, solve_low, *arrived,
        )
        steps = []
        for place, width in enumerate(PIECES):
            final = place == pieces - 1
            step, *parts = run(
                lambda kept, came, fine, wide, *refs: correct_body(kept, came, fine, wide, place, *refs),
                [whole(width)] + (shared if final else []), 6 * modes * rows * width, 12 * rows * width,
                kept[place], came[place], fine, basis_wide, *(steps if final else []),
            )
            steps.append(step)
        arrived = exchange(parts)
        if first:
            schur_high, schur_low, schur_wide = run(
                schur_body, [whole(rows, bf16)] * 2 + [((sent_rows, 3 * sent_rows), bf16)], 8 * rows**3, 12 * size, chooser, flipped, schur_matrix[0, 0],
            )
        base, total = run(
            lambda *refs: ahead_body(pieces, first, *refs), [whole(loads)] * 2, 6 * rows * size, 16 * size,
            *steps, *([] if first else [iterate]), ordered, schur_high, schur_low,
        )
        parts = run(
            lambda *refs: product_body(subs, count, *refs), shared, 2 * rows * size, 12 * size,
            base, schur_wide, *arrived,
        )
        before, arrived = arrived, exchange(parts)
        *projected, iterate, value = run(
            lambda *refs: follow_body(subs, count, last, *refs),
            ([] if last else [((modes, loads), f32)]) + [whole(loads)] * 2, 3 * rows * size, 16 * size,
            base, total, schur_high, schur_low, *before, *parts, *([] if last else [test_high, test_low]),
        )
        ahead = projected[0] if projected else None
    near, solution_rows = run(
        restore_body, [whole(loads)] * 2, 8 * rows * size, 10 * size, flipped, value, iterate,
    )
    (residual_rows,) = run(
        lambda *refs: finish_body(subs, *refs), [whole(loads)], 4 * rows * size, 10 * size,
        twice, near, *arrived, places=[outside],
        scratch=[pltpu.VMEM((rows, loads), f32), pltpu.SemaphoreType.DMA((4,))],
    )
    return (solution_rows[None, None], residual_rows[None, None])


def solution(mesh):
    return jax.shard_map(
        local,
        mesh=mesh,
        in_specs=(
            P("sub", "grp", None, None),
            P("sub", "grp", None, None),
            P("sub", "grp", None, None),
            P("sub", "grp", None, None),
            P("sub", None, "grp"),
            P("sub", "grp", None, None),
        ),
        out_specs=(P("sub", "grp", None, None), P("sub", "grp", None, None)),
        check_vma=False,
    )
```

```python
import jax
import jax.numpy as jnp
from jax import lax
from jax.experimental import pallas as pl
from jax.experimental.pallas import tpu as pltpu
from jax.sharding import PartitionSpec as P

ITERS = 2
ROW_SUBS = 4
RELAX = 0.5
GROUPS = 4
HIDE = 16
PIECES = (128, 256)
f32 = jnp.float32
bf16 = jnp.bfloat16
NN = (((1,), (0,)), ((), ()))
NT = (((1,), (1,)), ((), ()))


class Chain:
    def __init__(self):
        self.last = None

    def __call__(self, body, outs, flops, moved, *operands, scratch=(), ins=None, places=None):
        count = len(operands)
        specs = [pl.BlockSpec(memory_space=pltpu.VMEM)] * count if ins is None else ins
        extra = []
        if self.last is not None:
            extra = [self.last]
            specs = specs + [pl.BlockSpec(memory_space=pl.ANY)]

        def whole_body(*refs):
            body(*refs[:count], *refs[count + len(extra) :])

        results = pl.pallas_call(
            whole_body,
            out_shape=[jax.ShapeDtypeStruct(shape, kind) for shape, kind in outs],
            in_specs=specs,
            out_specs=[pl.BlockSpec(memory_space=pltpu.VMEM)] * len(outs) if places is None else places,
            scratch_shapes=list(scratch),
            compiler_params=pltpu.CompilerParams(vmem_limit_bytes=24 * 1024 * 1024),
            cost_estimate=pl.CostEstimate(flops=flops, bytes_accessed=moved, transcendentals=0),
        )(*operands, *extra)
        self.last = results[0]
        return results


def dot(left, right, dims=NN):
    return lax.dot_general(left, right, dims, preferred_element_type=f32)


def split(value):
    high = value.astype(bf16)
    return high, (value - high.astype(f32)).astype(bf16)


def dot3(left, right):
    return dot(left[0], right[0]) + (dot(left[0], right[1]) + dot(left[1], right[0]))


def join_left(halves):
    return jnp.concatenate([halves[0], halves[0], halves[1]], axis=1)


def join_right(halves):
    return jnp.concatenate([halves[0], halves[1], halves[0]], axis=0)


def pick(chooser, value):
    high, low = split(value)
    return dot(chooser, high) + dot(chooser, low)


def sides(subs):
    sub = lax.axis_index("sub")
    low_side = sub % 2 == 0
    low_row = (sub // ROW_SUBS) % 2 == 0
    up, down = sub < subs - 1, sub > 0
    over, under = sub < subs - ROW_SUBS, sub >= ROW_SUBS
    return [
        (low_row, 3, 2, jnp.where(low_row, over, under)),
        (low_side, 1, 0, jnp.where(low_side, up, down)),
        (low_side, 0, 1, jnp.where(low_side, down, up)),
        (low_row, 2, 3, jnp.where(low_row, under, over)),
    ]


def put_shared(value, shared_refs):
    for place, ref in enumerate(shared_refs):
        width = ref.shape[0]
        ref[...] = value[place * width : (place + 1) * width]


def came_in(subs, shared_refs):
    return jnp.concatenate(
        [ref[...] * jnp.where(here, 1.0, 0.0) for ref, (_, _, _, here) in zip(shared_refs, sides(subs))], axis=0
    )


def add_shared(subs, value, shared_refs):
    came = came_in(subs, shared_refs)
    count = came.shape[0]
    return jnp.concatenate([value[:count] + came, value[count:]], axis=0)


def listed_body(subs, count, blocks_hbm, load_hbm, columns_hbm, listed_ref, load_ref, sent_ref, *refs):
    *shared_refs, blocks_ref, load_sems, blocks_sem, sent_sem = refs
    modes = sent_ref.shape[0]
    wanted = pl.multiple_of((3 - (lax.axis_index("grp") ^ 1)) * modes, modes)
    sent_copy = pltpu.make_async_copy(columns_hbm.at[pl.ds(wanted, modes), :], sent_ref, sent_sem)
    half = load_ref.shape[0] // 2
    halves = [slice(0, half), slice(half, 2 * half)]
    load_copies = [
        pltpu.make_async_copy(load_hbm.at[rows], load_ref.at[rows], load_sems.at[place])
        for place, rows in enumerate(halves)
    ]
    blocks_copy = pltpu.make_async_copy(blocks_hbm, blocks_ref, blocks_sem)
    blocks_copy.start()
    for copy in load_copies:
        copy.start()
    sent_copy.start()
    blocks_copy.wait()
    blocks = blocks_ref[...]
    placed = jnp.concatenate(
        [jnp.where(test, blocks[a : a + 1], blocks[b : b + 1]) for test, a, b, _ in sides(subs)], axis=0
    )
    upright = placed.astype(f32).T
    column = jnp.concatenate([upright[:, place : place + 1] for place in range(4)], axis=0)
    listed, total = column.shape[0], load_ref.shape[0]
    lane = lax.broadcasted_iota(jnp.int32, (listed, total), 1).astype(f32)
    first = (column == lane).astype(f32).astype(bf16)
    listed_ref[...] = first
    wanted_rows = count * blocks.shape[1]
    sent = None
    for copy, rows in zip(load_copies, halves):
        copy.wait()
        part = pick(first[:wanted_rows, rows], load_ref[rows])
        sent = part if sent is None else sent + part
    put_shared(sent, shared_refs)
    sent_copy.wait()


def order_body(subs, count, listed_ref, load_ref, basis_ref, chooser_ref, flipped_ref, twice_ref,
               basis_wide, test_high, test_low, test_wide, ahead_ref, ordered_ref):
    listed, total = listed_ref.shape
    first = listed_ref[...].astype(f32)
    unlisted = 1.0 - jnp.sum(first, axis=0, keepdims=True)
    before = (
        lax.broadcasted_iota(jnp.int32, (total, total), 0)
        < lax.broadcasted_iota(jnp.int32, (total, total), 1)
    ).astype(f32).astype(bf16)
    rank = dot(jnp.broadcast_to(unlisted, (8, total)).astype(bf16), before)[:1]
    slot = lax.broadcasted_iota(jnp.int32, (total - listed, total), 0).astype(f32)
    last = jnp.where(rank == slot, unlisted, 0.0)
    chooser = jnp.concatenate([first, last], axis=0)
    flipped_ref[...] = chooser.T.astype(bf16)
    weighted = (chooser * weight_column(subs, listed // 4, total)).astype(bf16)
    chooser = chooser.astype(bf16)
    chooser_ref[...] = chooser
    ordered = pick(chooser, load_ref[...])
    ordered_ref[...] = ordered
    size = count * listed // 4
    shared = flipped_ref[:, :size]
    twice_ref[...] = jnp.concatenate([shared, shared], axis=1)
    placed = [dot(weighted, part) for part in split(basis_ref[...])]
    basis_wide[...] = join_left([part.astype(bf16) for part in placed])
    for part, turned in zip(placed, (test_high, test_low)):
        turned[...] = part.T.astype(bf16)
    test_wide[...] = join_left([test_high[:, :size], test_low[:, :size]])
    ahead_ref[...] = dot3((test_high[...], test_low[...]), split(ordered))


def weight_column(subs, width, total):
    parts = [jnp.full((width, 1), jnp.where(here, 0.5, 1.0), f32) for _, _, _, here in sides(subs)]
    return jnp.concatenate(parts + [jnp.ones((total - 4 * width, 1), f32)], axis=0)


def rows_of(columns_ref, place):
    modes = columns_ref.shape[1]
    return columns_ref[pl.ds(pl.multiple_of(place * modes, modes), modes), :]


def solver_body(subs, listed, chooser_ref, solve_ref, later_ref, solve_high, solve_low, passed_ref):
    chooser = chooser_ref[...]
    weighted = (chooser.astype(f32) * weight_column(subs, listed // 4, chooser.shape[0])).astype(bf16)
    passed_ref[...] = later_ref[...]
    for part, out in zip(split(solve_ref[...] * RELAX), (solve_high, solve_low)):
        out[...] = dot(dot(weighted, part).astype(bf16), weighted, NT).astype(bf16)


def schur_body(chooser_ref, flipped_ref, schur_ref, schur_high, schur_low, schur_wide):
    chooser, flipped = chooser_ref[...], flipped_ref[...]
    size = schur_wide.shape[0]
    for part, out in zip(split(schur_ref[...]), (schur_high, schur_low)):
        out[...] = dot(dot(chooser, part).astype(bf16), flipped).astype(bf16)
    schur_wide[...] = join_left([schur_high[:size, :size], schur_low[:size, :size]])


def blend_body(columns_ref, other_ref, mix_high, mix_low):
    grp = lax.axis_index("grp")
    away = jnp.concatenate([rows_of(columns_ref, 3 - grp), other_ref[...]], axis=1)
    kept = jnp.concatenate([rows_of(columns_ref, grp), rows_of(columns_ref, grp ^ 1).T], axis=1)
    mix_high[...], mix_low[...] = split(jnp.concatenate([away, kept], axis=0) * RELAX)


def cut():
    return [(sum(PIECES[:place]), width) for place, width in enumerate(PIECES)]


def project_body(subs, count, ahead_ref, test_wide, *refs):
    halves = split(came_in(subs, refs[:count]))
    projected = ahead_ref[...] + dot(test_wide[...], join_right(halves))
    for ref, (start, width) in zip(refs[count:], cut()):
        ref[...] = projected[:, start : start + width]


def solve_body(subs, value_ref, solve_high, solve_low, *refs):
    halves = split(add_shared(subs, value_ref[...], refs[:-1]))
    refs[-1][...] = dot3((solve_high[...], solve_low[...]), halves)


def mix_body(own_ref, other_ref, mix_high, mix_low, away_ref, kept_ref):
    modes = away_ref.shape[0]
    pair = jnp.concatenate([own_ref[...], other_ref[...]], axis=0)
    mixed = dot3((mix_high[...], mix_low[...]), split(pair))
    away_ref[...] = mixed[:modes]
    kept_ref[...] = mixed[modes:]


def correct_body(kept_ref, came_ref, fine_ref, basis_wide, place, *refs):
    coarse = kept_ref[...] + came_ref[...]
    start, width = cut()[place]
    fine = fine_ref[:, start : start + width]
    step = fine + dot(basis_wide[...], join_right(split(coarse)))
    formers = place if len(refs) > 1 else 0
    former_refs, out_ref = refs[:formers], refs[formers]
    out_ref[...] = step
    for at, ref in enumerate(refs[formers + 1 :]):
        size = ref.shape[0]
        rows = slice(at * size, (at + 1) * size)
        ref[...] = jnp.concatenate([former[rows] for former in former_refs] + [step[rows]], axis=1)


def ahead_body(pieces, first, *refs):
    total = jnp.concatenate([ref[...] for ref in refs[:pieces]], axis=1)
    refs = refs[pieces:]
    if not first:
        total = refs[0][...] + total
        refs = refs[1:]
    load_ref, schur_high, schur_low, base_ref, total_ref = refs
    total_ref[...] = total
    base_ref[...] = load_ref[...] - dot3((schur_high[...], schur_low[...]), split(total))


def product_body(subs, count, base_ref, schur_wide, *refs):
    came = came_in(subs, refs[:count])
    size = came.shape[0]
    part = dot(schur_wide[...], join_right(split(came)))
    put_shared(base_ref[:size] - part, refs[count:])


def follow_body(subs, count, last, base_ref, total_ref, schur_high, schur_low, *refs):
    arrived, shared, refs = refs[:count], refs[count : 2 * count], refs[2 * count :]
    came = came_in(subs, arrived)
    size = came.shape[0]
    part = dot3((schur_high[size:, :size], schur_low[size:, :size]), split(came))
    value = jnp.concatenate([ref[...] for ref in shared] + [base_ref[size:] - part], axis=0)
    iterate_ref, value_ref = refs[-2:]
    value_ref[...] = value
    iterate_ref[...] = jnp.concatenate([total_ref[:size] + came, total_ref[size:]], axis=0)
    if not last:
        test_high, test_low, projected_ref = refs[:3]
        projected_ref[...] = dot3((test_high[...], test_low[...]), split(value))


def restore_body(flipped_ref, value_ref, iterate_ref, base_ref, out_ref):
    flipped = flipped_ref[...]
    out_ref[...] = pick(flipped, iterate_ref[...])
    base_ref[...] = pick(flipped, value_ref[...])


def finish_body(subs, twice_ref, base_ref, *refs):
    *arrived, out_hbm, out_ref, sems = refs
    came = came_in(subs, arrived)
    total = base_ref[...] + dot(twice_ref[...], jnp.concatenate(split(came), axis=0))
    copies = []
    size = out_ref.shape[0] // 4
    for step in range(4):
        rows = slice(step * size, (step + 1) * size)
        out_ref[rows] = total[rows]
        copy = pltpu.make_async_copy(out_ref.at[rows], out_hbm.at[rows], sems.at[step])
        copy.start()
        copies.append(copy)
    for copy in copies:
        copy.wait()


def swaps(count, stride, odd):
    partner = {}
    for low in range(count - stride):
        if (low // stride) % 2 == odd:
            partner[low], partner[low + stride] = low + stride, low
    if not partner:
        return []
    left = [index for index in range(count) if index not in partner]
    half = len(left) // 2
    for low, high in zip(left[:half], left[half:]):
        partner[low], partner[high] = high, low
    return sorted(partner.items())


def local(load_terms, schur_matrix, local_inverse, coarse_modes, cluster_inverse, row_blocks):
    load = load_terms[0, 0]
    basis = coarse_modes[0, 0]
    columns = cluster_inverse[0]
    blocks = row_blocks[0, 0]
    rows, loads = load.shape
    modes = basis.shape[1]
    shared_rows = blocks.shape[1]
    listed = 4 * shared_rows
    subs = lax.axis_size("sub")
    if lax.axis_size("grp") != GROUPS or sum(PIECES) != loads:
        raise ValueError("unexpected sizes")

    plans = [swaps(subs, ROW_SUBS, 0), swaps(subs, 1, 0), swaps(subs, 1, 1), swaps(subs, ROW_SUBS, 1)]
    plans = [plan for plan in plans if plan]
    count = len(plans)

    def exchange(parts):
        return [lax.ppermute(part, "sub", plan) for part, plan in zip(parts, plans)]

    def whole(width, kind=f32):
        return ((rows, width), kind)

    pair_plan = [(0, 1), (1, 0), (2, 3), (3, 2)]
    mirror_plan = [(0, 3), (3, 0), (1, 2), (2, 1)]
    shared = [((shared_rows, loads), f32)] * count
    outside = pl.BlockSpec(memory_space=pltpu.HBM)
    pieces = len(PIECES)
    size = rows * loads
    sent_rows = count * shared_rows
    run = Chain()

    one_hot, load_near, sent, *parts = run(
        lambda *refs: listed_body(subs, count, *refs),
        [((listed, rows), bf16), whole(loads), ((modes, modes), f32)] + shared, 4 * listed * size, 16 * size,
        *[pltpu.with_memory_space_constraint(array, pltpu.HBM) for array in (blocks, load, columns)], ins=[outside] * 3,
        scratch=[pltpu.VMEM(blocks.shape, blocks.dtype), pltpu.SemaphoreType.DMA((2,))]
        + [pltpu.SemaphoreType.DMA] * 2,
    )
    arrived = exchange(parts)
    other = lax.ppermute(sent, "grp", pair_plan)
    chooser, flipped, twice, basis_wide, test_high, test_low, test_wide, ahead, ordered = run(
        lambda *refs: order_body(subs, count, *refs),
        [whole(rows, bf16)] * 2 + [whole(2 * sent_rows, bf16), whole(3 * modes, bf16)]
        + [((modes, rows), bf16)] * 2 + [((modes, 3 * sent_rows), bf16), ((modes, loads), f32), whole(loads)],
        4 * rows * size, 24 * size, one_hot, load_near, basis,
    )
    value, iterate = ordered, None
    for iteration in range(ITERS):
        first, last = iteration == 0, iteration == ITERS - 1
        shapes = [((modes, width), f32) for width in PIECES]
        own = list(run(
            lambda *refs: project_body(subs, count, *refs), shapes, 6 * modes * size, 12 * size,
            ahead, test_wide, *arrived,
        ))
        if first:
            solve_high, solve_low, own[1] = run(
                lambda *refs: solver_body(subs, listed, *refs), [whole(rows, bf16)] * 2 + [shapes[1]],
                8 * rows**3, 12 * size, chooser, local_inverse[0, 0], own[1],
            )
        theirs = [lax.ppermute(piece, "grp", pair_plan) for piece in own]
        if first:
            mixers = run(blend_body, [((2 * modes, 2 * modes), bf16)] * 2, size, size, columns, other)
        kept, came = [], []
        for place, width in enumerate(PIECES):
            away, keep = run(
                mix_body, [((modes, width), f32)] * 2, HIDE * 24 * modes * modes * width, HIDE * 4 * rows * width,
                own[place], theirs[place], *mixers,
            )
            kept.append(keep)
            came.append(lax.ppermute(away, "grp", mirror_plan))
        (fine,) = run(
            lambda *refs: solve_body(subs, *refs), [whole(loads)], HIDE * 6 * rows * size, HIDE * 12 * size,
            value, solve_high, solve_low, *arrived,
        )
        steps = []
        for place, width in enumerate(PIECES):
            final = place == pieces - 1
            step, *parts = run(
                lambda kept, came, fine, wide, *refs: correct_body(kept, came, fine, wide, place, *refs),
                [whole(width)] + (shared if final else []), 6 * modes * rows * width, 12 * rows * width,
                kept[place], came[place], fine, basis_wide, *(steps if final else []),
            )
            steps.append(step)
        arrived = exchange(parts)
        if first:
            schur_high, schur_low, schur_wide = run(
                schur_body, [whole(rows, bf16)] * 2 + [((sent_rows, 3 * sent_rows), bf16)], 8 * rows**3, 12 * size, chooser, flipped, schur_matrix[0, 0],
            )
        base, total = run(
            lambda *refs: ahead_body(pieces, first, *refs), [whole(loads)] * 2, 6 * rows * size, 16 * size,
            *steps, *([] if first else [iterate]), ordered, schur_high, schur_low,
        )
        parts = run(
            lambda *refs: product_body(subs, count, *refs), shared, 2 * rows * size, 12 * size,
            base, schur_wide, *arrived,
        )
        before, arrived = arrived, exchange(parts)
        *projected, iterate, value = run(
            lambda *refs: follow_body(subs, count, last, *refs),
            ([] if last else [((modes, loads), f32)]) + [whole(loads)] * 2, 3 * rows * size, 16 * size,
            base, total, schur_high, schur_low, *before, *parts, *([] if last else [test_high, test_low]),
        )
        ahead = projected[0] if projected else None
    near, solution_rows = run(
        restore_body, [whole(loads)] * 2, 8 * rows * size, 10 * size, flipped, value, iterate,
    )
    (residual_rows,) = run(
        lambda *refs: finish_body(subs, *refs), [whole(loads)], 4 * rows * size, 10 * size,
        twice, near, *arrived, places=[outside],
        scratch=[pltpu.VMEM((rows, loads), f32), pltpu.SemaphoreType.DMA((4,))],
    )
    return (solution_rows[None, None], residual_rows[None, None])


def solution(mesh):
    return jax.shard_map(
        local,
        mesh=mesh,
        in_specs=(
            P("sub", "grp", None, None),
            P("sub", "grp", None, None),
            P("sub", "grp", None, None),
            P("sub", "grp", None, None),
            P("sub", None, "grp"),
            P("sub", "grp", None, None),
        ),
        out_specs=(P("sub", "grp", None, None), P("sub", "grp", None, None)),
        check_vma=False,
    )
```

```python
import jax
import jax.numpy as jnp
from jax import lax
from jax.experimental import pallas as pl
from jax.experimental.pallas import tpu as pltpu
from jax.sharding import PartitionSpec as P

ITERS = 2
ROW_SUBS = 4
RELAX = 0.5
GROUPS = 4
HIDE = 16
PIECES = (128, 256)
f32 = jnp.float32
bf16 = jnp.bfloat16
NN = (((1,), (0,)), ((), ()))
NT = (((1,), (1,)), ((), ()))


class Chain:
    def __init__(self):
        self.last = None

    def __call__(self, body, outs, flops, moved, *operands, scratch=(), ins=None, places=None):
        count = len(operands)
        specs = [pl.BlockSpec(memory_space=pltpu.VMEM)] * count if ins is None else ins
        extra = []
        if self.last is not None:
            extra = [self.last]
            specs = specs + [pl.BlockSpec(memory_space=pl.ANY)]

        def whole_body(*refs):
            body(*refs[:count], *refs[count + len(extra) :])

        results = pl.pallas_call(
            whole_body,
            out_shape=[jax.ShapeDtypeStruct(shape, kind) for shape, kind in outs],
            in_specs=specs,
            out_specs=[pl.BlockSpec(memory_space=pltpu.VMEM)] * len(outs) if places is None else places,
            scratch_shapes=list(scratch),
            compiler_params=pltpu.CompilerParams(vmem_limit_bytes=24 * 1024 * 1024),
            cost_estimate=pl.CostEstimate(flops=flops, bytes_accessed=moved, transcendentals=0),
        )(*operands, *extra)
        self.last = results[0]
        return results


def dot(left, right, dims=NN):
    return lax.dot_general(left, right, dims, preferred_element_type=f32)


def split(value):
    high = value.astype(bf16)
    return high, (value - high.astype(f32)).astype(bf16)


def dot3(left, right):
    return dot(left[0], right[0]) + (dot(left[0], right[1]) + dot(left[1], right[0]))


def join_left(halves):
    return jnp.concatenate([halves[0], halves[0], halves[1]], axis=1)


def join_right(halves):
    return jnp.concatenate([halves[0], halves[1], halves[0]], axis=0)


def pick(chooser, value):
    high, low = split(value)
    return dot(chooser, high) + dot(chooser, low)


def sides(subs):
    sub = lax.axis_index("sub")
    low_side = sub % 2 == 0
    low_row = (sub // ROW_SUBS) % 2 == 0
    up, down = sub < subs - 1, sub > 0
    over, under = sub < subs - ROW_SUBS, sub >= ROW_SUBS
    return [
        (low_row, 3, 2, jnp.where(low_row, over, under)),
        (low_side, 0, 1, jnp.where(low_side, down, up)),
        (low_side, 1, 0, jnp.where(low_side, up, down)),
        (low_row, 2, 3, jnp.where(low_row, under, over)),
    ]


def put_shared(value, shared_refs):
    for place, ref in enumerate(shared_refs):
        width = ref.shape[0]
        ref[...] = value[place * width : (place + 1) * width]


def came_in(subs, shared_refs):
    always = (subs % (2 * ROW_SUBS) == 0, False, subs % 2 == 0, False)
    return jnp.concatenate(
        [
            ref[...] if whole else ref[...] * jnp.where(here, 1.0, 0.0)
            for ref, (_, _, _, here), whole in zip(shared_refs, sides(subs), always)
        ],
        axis=0,
    )


def add_shared(subs, value, shared_refs):
    came = came_in(subs, shared_refs)
    count = came.shape[0]
    return jnp.concatenate([value[:count] + came, value[count:]], axis=0)


def listed_body(subs, count, blocks_hbm, load_hbm, columns_hbm, listed_ref, load_ref, sent_ref, *refs):
    *shared_refs, blocks_ref, load_sems, blocks_sem, sent_sem = refs
    modes = sent_ref.shape[0]
    wanted = pl.multiple_of((3 - (lax.axis_index("grp") ^ 1)) * modes, modes)
    sent_copy = pltpu.make_async_copy(columns_hbm.at[pl.ds(wanted, modes), :], sent_ref, sent_sem)
    half = load_ref.shape[0] // 2
    halves = [slice(0, half), slice(half, 2 * half)]
    load_copies = [
        pltpu.make_async_copy(load_hbm.at[rows], load_ref.at[rows], load_sems.at[place])
        for place, rows in enumerate(halves)
    ]
    blocks_copy = pltpu.make_async_copy(blocks_hbm, blocks_ref, blocks_sem)
    blocks_copy.start()
    for copy in load_copies:
        copy.start()
    sent_copy.start()
    blocks_copy.wait()
    blocks = blocks_ref[...]
    placed = jnp.concatenate(
        [jnp.where(test, blocks[a : a + 1], blocks[b : b + 1]) for test, a, b, _ in sides(subs)], axis=0
    )
    upright = placed.astype(f32).T
    column = jnp.concatenate([upright[:, place : place + 1] for place in range(4)], axis=0)
    listed, total = column.shape[0], load_ref.shape[0]
    lane = lax.broadcasted_iota(jnp.int32, (listed, total), 1).astype(f32)
    first = (column == lane).astype(f32).astype(bf16)
    listed_ref[...] = first
    wanted_rows = count * blocks.shape[1]
    sent = None
    for copy, rows in zip(load_copies, halves):
        copy.wait()
        part = pick(first[:wanted_rows, rows], load_ref[rows])
        sent = part if sent is None else sent + part
    put_shared(sent, shared_refs)
    sent_copy.wait()


def order_body(subs, count, listed_ref, load_ref, basis_ref, chooser_ref, flipped_ref, twice_ref,
               basis_wide, test_high, test_low, test_wide, ahead_ref, ordered_ref):
    listed, total = listed_ref.shape
    first = listed_ref[...].astype(f32)
    unlisted = 1.0 - jnp.sum(first, axis=0, keepdims=True)
    before = (
        lax.broadcasted_iota(jnp.int32, (total, total), 0)
        < lax.broadcasted_iota(jnp.int32, (total, total), 1)
    ).astype(f32).astype(bf16)
    rank = dot(jnp.broadcast_to(unlisted, (8, total)).astype(bf16), before)[:1]
    slot = lax.broadcasted_iota(jnp.int32, (total - listed, total), 0).astype(f32)
    last = jnp.where(rank == slot, unlisted, 0.0)
    chooser = jnp.concatenate([first, last], axis=0)
    flipped_ref[...] = chooser.T.astype(bf16)
    weighted = (chooser * weight_column(subs, listed // 4, total)).astype(bf16)
    chooser = chooser.astype(bf16)
    chooser_ref[...] = chooser
    ordered = pick(chooser, load_ref[...])
    ordered_ref[...] = ordered
    size = count * listed // 4
    shared = flipped_ref[:, :size]
    twice_ref[...] = jnp.concatenate([shared, shared], axis=1)
    placed = [dot(weighted, part) for part in split(basis_ref[...])]
    basis_wide[...] = join_left([part.astype(bf16) for part in placed])
    for part, turned in zip(placed, (test_high, test_low)):
        turned[...] = part.T.astype(bf16)
    test_wide[...] = join_left([test_high[:, :size], test_low[:, :size]])
    ahead_ref[...] = dot3((test_high[...], test_low[...]), split(ordered))


def weight_column(subs, width, total):
    parts = [jnp.full((width, 1), jnp.where(here, 0.5, 1.0), f32) for _, _, _, here in sides(subs)]
    return jnp.concatenate(parts + [jnp.ones((total - 4 * width, 1), f32)], axis=0)


def rows_of(columns_ref, place):
    modes = columns_ref.shape[1]
    return columns_ref[pl.ds(pl.multiple_of(place * modes, modes), modes), :]


def solver_body(subs, listed, chooser_ref, solve_ref, later_ref, solve_high, solve_low, passed_ref):
    chooser = chooser_ref[...]
    weighted = (chooser.astype(f32) * weight_column(subs, listed // 4, chooser.shape[0])).astype(bf16)
    passed_ref[...] = later_ref[...]
    for part, out in zip(split(solve_ref[...] * RELAX), (solve_high, solve_low)):
        out[...] = dot(dot(weighted, part).astype(bf16), weighted, NT).astype(bf16)


def schur_body(chooser_ref, flipped_ref, schur_ref, schur_high, schur_low, schur_wide):
    chooser, flipped = chooser_ref[...], flipped_ref[...]
    size = schur_wide.shape[0]
    for part, out in zip(split(schur_ref[...]), (schur_high, schur_low)):
        out[...] = dot(dot(chooser, part).astype(bf16), flipped).astype(bf16)
    schur_wide[...] = join_left([schur_high[:size, :size], schur_low[:size, :size]])


def blend_body(columns_ref, other_ref, mix_high, mix_low):
    grp = lax.axis_index("grp")
    away = jnp.concatenate([rows_of(columns_ref, 3 - grp), other_ref[...]], axis=1)
    kept = jnp.concatenate([rows_of(columns_ref, grp), rows_of(columns_ref, grp ^ 1).T], axis=1)
    mix_high[...], mix_low[...] = split(jnp.concatenate([away, kept], axis=0) * RELAX)


def cut():
    return [(sum(PIECES[:place]), width) for place, width in enumerate(PIECES)]


def project_body(subs, count, ahead_ref, test_wide, *refs):
    halves = split(came_in(subs, refs[:count]))
    projected = ahead_ref[...] + dot(test_wide[...], join_right(halves))
    for ref, (start, width) in zip(refs[count:], cut()):
        ref[...] = projected[:, start : start + width]


def solve_body(subs, value_ref, solve_high, solve_low, *refs):
    halves = split(add_shared(subs, value_ref[...], refs[:-1]))
    refs[-1][...] = dot3((solve_high[...], solve_low[...]), halves)


def mix_body(own_ref, other_ref, mix_high, mix_low, away_ref, kept_ref):
    modes = away_ref.shape[0]
    pair = jnp.concatenate([own_ref[...], other_ref[...]], axis=0)
    mixed = dot3((mix_high[...], mix_low[...]), split(pair))
    away_ref[...] = mixed[:modes]
    kept_ref[...] = mixed[modes:]


def correct_body(kept_ref, came_ref, fine_ref, basis_wide, place, *refs):
    coarse = kept_ref[...] + came_ref[...]
    start, width = cut()[place]
    fine = fine_ref[:, start : start + width]
    step = fine + dot(basis_wide[...], join_right(split(coarse)))
    formers = place if len(refs) > 1 else 0
    former_refs, out_ref = refs[:formers], refs[formers]
    out_ref[...] = step
    for at, ref in enumerate(refs[formers + 1 :]):
        size = ref.shape[0]
        rows = slice(at * size, (at + 1) * size)
        ref[...] = jnp.concatenate([former[rows] for former in former_refs] + [step[rows]], axis=1)


def ahead_body(pieces, first, *refs):
    total = jnp.concatenate([ref[...] for ref in refs[:pieces]], axis=1)
    refs = refs[pieces:]
    if not first:
        total = refs[0][...] + total
        refs = refs[1:]
    load_ref, schur_high, schur_low, base_ref, total_ref = refs
    total_ref[...] = total
    base_ref[...] = load_ref[...] - dot3((schur_high[...], schur_low[...]), split(total))


def product_body(subs, count, base_ref, schur_wide, *refs):
    came = came_in(subs, refs[:count])
    size = came.shape[0]
    part = dot(schur_wide[...], join_right(split(came)))
    put_shared(base_ref[:size] - part, refs[count:])


def follow_body(subs, count, last, base_ref, total_ref, schur_high, schur_low, *refs):
    arrived, shared, refs = refs[:count], refs[count : 2 * count], refs[2 * count :]
    came = came_in(subs, arrived)
    size = came.shape[0]
    part = dot3((schur_high[size:, :size], schur_low[size:, :size]), split(came))
    value = jnp.concatenate([ref[...] for ref in shared] + [base_ref[size:] - part], axis=0)
    iterate_ref, value_ref = refs[-2:]
    value_ref[...] = value
    iterate_ref[...] = jnp.concatenate([total_ref[:size] + came, total_ref[size:]], axis=0)
    if not last:
        test_high, test_low, projected_ref = refs[:3]
        projected_ref[...] = dot3((test_high[...], test_low[...]), split(value))


def restore_body(flipped_ref, value_ref, iterate_ref, base_ref, out_ref):
    flipped = flipped_ref[...]
    out_ref[...] = pick(flipped, iterate_ref[...])
    base_ref[...] = pick(flipped, value_ref[...])


def finish_body(subs, twice_ref, base_ref, *refs):
    *arrived, out_hbm, out_ref, sems = refs
    came = came_in(subs, arrived)
    total = base_ref[...] + dot(twice_ref[...], jnp.concatenate(split(came), axis=0))
    copies = []
    size = out_ref.shape[0] // 4
    for step in range(4):
        rows = slice(step * size, (step + 1) * size)
        out_ref[rows] = total[rows]
        copy = pltpu.make_async_copy(out_ref.at[rows], out_hbm.at[rows], sems.at[step])
        copy.start()
        copies.append(copy)
    for copy in copies:
        copy.wait()


def swaps(count, stride, odd):
    partner = {}
    for low in range(count - stride):
        if (low // stride) % 2 == odd:
            partner[low], partner[low + stride] = low + stride, low
    if not partner:
        return []
    left = [index for index in range(count) if index not in partner]
    half = len(left) // 2
    for low, high in zip(left[:half], left[half:]):
        partner[low], partner[high] = high, low
    return sorted(partner.items())


def local(load_terms, schur_matrix, local_inverse, coarse_modes, cluster_inverse, row_blocks):
    load = load_terms[0, 0]
    basis = coarse_modes[0, 0]
    columns = cluster_inverse[0]
    blocks = row_blocks[0, 0]
    rows, loads = load.shape
    modes = basis.shape[1]
    shared_rows = blocks.shape[1]
    listed = 4 * shared_rows
    subs = lax.axis_size("sub")
    if lax.axis_size("grp") != GROUPS or sum(PIECES) != loads:
        raise ValueError("unexpected sizes")

    plans = [swaps(subs, ROW_SUBS, 0), swaps(subs, 1, 1), swaps(subs, 1, 0), swaps(subs, ROW_SUBS, 1)]
    plans = [plan for plan in plans if plan]
    count = len(plans)

    def exchange(parts):
        return [lax.ppermute(part, "sub", plan) for part, plan in zip(parts, plans)]

    def whole(width, kind=f32):
        return ((rows, width), kind)

    pair_plan = [(0, 1), (1, 0), (2, 3), (3, 2)]
    mirror_plan = [(0, 3), (3, 0), (1, 2), (2, 1)]
    shared = [((shared_rows, loads), f32)] * count
    outside = pl.BlockSpec(memory_space=pltpu.HBM)
    pieces = len(PIECES)
    size = rows * loads
    sent_rows = count * shared_rows
    run = Chain()

    one_hot, load_near, sent, *parts = run(
        lambda *refs: listed_body(subs, count, *refs),
        [((listed, rows), bf16), whole(loads), ((modes, modes), f32)] + shared, 4 * listed * size, 16 * size,
        *[pltpu.with_memory_space_constraint(array, pltpu.HBM) for array in (blocks, load, columns)], ins=[outside] * 3,
        scratch=[pltpu.VMEM(blocks.shape, blocks.dtype), pltpu.SemaphoreType.DMA((2,))]
        + [pltpu.SemaphoreType.DMA] * 2,
    )
    arrived = exchange(parts)
    other = lax.ppermute(sent, "grp", pair_plan)
    chooser, flipped, twice, basis_wide, test_high, test_low, test_wide, ahead, ordered = run(
        lambda *refs: order_body(subs, count, *refs),
        [whole(rows, bf16)] * 2 + [whole(2 * sent_rows, bf16), whole(3 * modes, bf16)]
        + [((modes, rows), bf16)] * 2 + [((modes, 3 * sent_rows), bf16), ((modes, loads), f32), whole(loads)],
        4 * rows * size, 24 * size, one_hot, load_near, basis,
    )
    value, iterate = ordered, None
    for iteration in range(ITERS):
        first, last = iteration == 0, iteration == ITERS - 1
        shapes = [((modes, width), f32) for width in PIECES]
        own = list(run(
            lambda *refs: project_body(subs, count, *refs), shapes, 6 * modes * size, 12 * size,
            ahead, test_wide, *arrived,
        ))
        if first:
            solve_high, solve_low, own[1] = run(
                lambda *refs: solver_body(subs, listed, *refs), [whole(rows, bf16)] * 2 + [shapes[1]],
                8 * rows**3, 12 * size, chooser, local_inverse[0, 0], own[1],
            )
        theirs = [lax.ppermute(piece, "grp", pair_plan) for piece in own]
        if first:
            mixers = run(blend_body, [((2 * modes, 2 * modes), bf16)] * 2, size, size, columns, other)
        kept, came = [], []
        for place, width in enumerate(PIECES):
            away, keep = run(
                mix_body, [((modes, width), f32)] * 2, HIDE * 24 * modes * modes * width, HIDE * 4 * rows * width,
                own[place], theirs[place], *mixers,
            )
            kept.append(keep)
            came.append(lax.ppermute(away, "grp", mirror_plan))
        (fine,) = run(
            lambda *refs: solve_body(subs, *refs), [whole(loads)], HIDE * 6 * rows * size, HIDE * 12 * size,
            value, solve_high, solve_low, *arrived,
        )
        steps = []
        for place, width in enumerate(PIECES):
            final = place == pieces - 1
            step, *parts = run(
                lambda kept, came, fine, wide, *refs: correct_body(kept, came, fine, wide, place, *refs),
                [whole(width)] + (shared if final else []), 6 * modes * rows * width, 12 * rows * width,
                kept[place], came[place], fine, basis_wide, *(steps if final else []),
            )
            steps.append(step)
        arrived = exchange(parts)
        if first:
            schur_high, schur_low, schur_wide = run(
                schur_body, [whole(rows, bf16)] * 2 + [((sent_rows, 3 * sent_rows), bf16)], 8 * rows**3, 12 * size, chooser, flipped, schur_matrix[0, 0],
            )
        base, total = run(
            lambda *refs: ahead_body(pieces, first, *refs), [whole(loads)] * 2, 6 * rows * size, 16 * size,
            *steps, *([] if first else [iterate]), ordered, schur_high, schur_low,
        )
        parts = run(
            lambda *refs: product_body(subs, count, *refs), shared, 2 * rows * size, 12 * size,
            base, schur_wide, *arrived,
        )
        before, arrived = arrived, exchange(parts)
        *projected, iterate, value = run(
            lambda *refs: follow_body(subs, count, last, *refs),
            ([] if last else [((modes, loads), f32)]) + [whole(loads)] * 2, 3 * rows * size, 16 * size,
            base, total, schur_high, schur_low, *before, *parts, *([] if last else [test_high, test_low]),
        )
        ahead = projected[0] if projected else None
    near, solution_rows = run(
        restore_body, [whole(loads)] * 2, 8 * rows * size, 10 * size, flipped, value, iterate,
    )
    (residual_rows,) = run(
        lambda *refs: finish_body(subs, *refs), [whole(loads)], 4 * rows * size, 10 * size,
        twice, near, *arrived, places=[outside],
        scratch=[pltpu.VMEM((rows, loads), f32), pltpu.SemaphoreType.DMA((4,))],
    )
    return (solution_rows[None, None], residual_rows[None, None])


def solution(mesh):
    return jax.shard_map(
        local,
        mesh=mesh,
        in_specs=(
            P("sub", "grp", None, None),
            P("sub", "grp", None, None),
            P("sub", "grp", None, None),
            P("sub", "grp", None, None),
            P("sub", None, "grp"),
            P("sub", "grp", None, None),
        ),
        out_specs=(P("sub", "grp", None, None), P("sub", "grp", None, None)),
        check_vma=False,
    )
```
